32 devices in a mesh: dp: 16 (over z, x, core), seq: 2 (over y).
Axes of the slice: x: 2, y: 2, z: 4, core: 2. Of those that a mesh axis runs over, the one named last changes fastest.
Arguments:
- queries: bfloat16 [4096, 4096], P(('dp', 'seq')), may hold values from -6 to 6
- keys: bfloat16 [4096, 512], P(('dp', 'seq')), may hold values from -6 to 6
- values: bfloat16 [4096, 512], P(('dp', 'seq')), may hold values from -6 to 6
- grad_out: bfloat16 [4096, 4096], P(('dp', 'seq')), may hold values from -6 to 6
- quant_scale: float32 [2, 4, 128], replicated, may hold values from 2 to 8
- doc_lengths: int32 [16, 8], P('dp'), may hold values from 1 to 128, as said below
Outputs:
- attn_out: bfloat16 [4096, 4096], P(('dp', 'seq'))
- grad_queries: bfloat16 [4096, 4096], P(('dp', 'seq'))
- grad_keys: bfloat16 [4096, 512], P(('dp', 'seq'))
- grad_values: bfloat16 [4096, 512], P(('dp', 'seq'))
- grad_scale: float32 [2, 4, 128], replicated
The draws below stay inside these ranges and needn't reach their ends.
Inputs may be any that keep to these rules, and one draw needn't show every extreme that they name: `doc_lengths`: each row sums to 256; its largest length is exactly 128.
All inputs are finite; a program needn't handle non-finite values.
Results may differ from the reference program's by a relative error of at most 0.04.
Values may be sent and summed in bfloat16 or wider, within the bound.
No kernel may reach another device: no remote copies, remote signals or barrier semaphores. Data moves between devices by JAX's collectives and lax.ppermute only.
A program may use at most 64 MiB of HBM per device.

```python
import math
import jax
import jax.numpy as jnp
from jax import lax

HQ = 32
KVH = 4
HD = 128
DOCS = 8
SLAB = 256
ROWS = 4096
N_DP = 16


def doc_table(key):
    key = jax.random.fold_in(key, 101)
    half = SLAB // 2
    rest = SLAB - half

    def one_slab(slab_key):
        pick_key, cut_key = jax.random.split(slab_key)
        biggest = jax.random.randint(pick_key, (), 0, DOCS, dtype=jnp.int32)
        order = jax.random.permutation(cut_key, rest - 1).astype(jnp.int32) + 1
        chosen = order[:DOCS - 2]
        ascending = -lax.top_k(-chosen, DOCS - 2)[0]
        bounds = jnp.concatenate([jnp.zeros((1,), jnp.int32), ascending, jnp.full((1,), rest, jnp.int32)])
        others = bounds[1:] - bounds[:-1]
        index = jnp.arange(DOCS, dtype=jnp.int32)
        source = jnp.clip(jnp.where(index < biggest, index, index - 1), 0, DOCS - 2)
        lengths = jnp.where(index == biggest, half, others[source]).astype(jnp.int32)
        first = jnp.sum(jnp.where(index < biggest, lengths, 0)).astype(jnp.int32)
        return (lengths, first)
    return jax.vmap(one_slab)(jax.random.split(key, N_DP))


def draw_doc_lengths(key, part):
    lengths, starts = doc_table(key)
    return lengths


def draw_queries(key, part):
    key = jax.random.fold_in(key, 3)
    return jax.random.truncated_normal(key, -6.0, 6.0, (ROWS, HQ * HD), jnp.float32).astype(jnp.bfloat16)


def draw_keys(key, part):
    key = jax.random.fold_in(key, 5)
    return jax.random.truncated_normal(key, -6.0, 6.0, (ROWS, KVH * HD), jnp.float32).astype(jnp.bfloat16)


def level_of(own_key, extent, pieces, smallest, top_value):
    factor_of, own = 1.0, jax.random.fold_in(own_key, 6)
    for axis_at, blocks in pieces:
        draws = jnp.exp(jax.random.uniform(jax.random.fold_in(own, axis_at), (blocks,), jnp.float32, smallest / len(pieces), top_value / len(pieces)))
        factor_of = factor_of * jnp.repeat(draws, extent[axis_at] // blocks).reshape([-1 if axis == axis_at else 1 for axis in range(len(extent))])
    return factor_of


def normal_values(rng, shape, deviation, reach, pieces=(), held_as=jnp.bfloat16):
    drawn = deviation * jax.random.normal(rng, shape, jnp.float32)
    if pieces:
        drawn = drawn * level_of(rng, shape, pieces, -0.22, 0.18)
    return jnp.clip(drawn, -reach, reach).astype(held_as)


def setup_inputs(seed: int = 0) -> dict:
    splits = jax.random.split(jax.random.key(seed), 7)
    queries = draw_queries(jax.random.fold_in(splits[6], 71), 0)
    keys = draw_keys(jax.random.fold_in(splits[6], 71), 0)
    values = normal_values(splits[2], (ROWS, KVH * HD), 1.0, 6.0, ((0, 32),))
    grad_out = normal_values(splits[3], (ROWS, HQ * HD), 1.0, 6.0, ((0, 32),))
    quant_scale = jnp.clip(jnp.exp(jax.random.uniform(splits[4], (2, KVH, HD), jnp.float32, math.log(2.0), math.log(8.0))), 2.0, 8.0)
    doc_lengths = draw_doc_lengths(jax.random.fold_in(splits[6], 71), 0)
    return dict(queries=queries, keys=keys, values=values, grad_out=grad_out, quant_scale=quant_scale, doc_lengths=doc_lengths)


two_pi = 2.0 * math.pi

def quantize(source, clip):
    level = 127.0 * jnp.tanh(source / clip)
    return clip / 127.0 * (level - jnp.sin(two_pi * level) / two_pi)

def quant_pair(key_raw, value_raw, clip):
    return (quantize(key_raw, clip[0]), quantize(value_raw, clip[1]))

def segments(lengths, length):
    ends = jnp.cumsum(lengths.astype(jnp.int32))
    positions = jnp.arange(length, dtype=jnp.int32)
    return lax.optimization_barrier(jnp.sum((positions[:, None] >= ends[None, :]).astype(jnp.int32), axis=1))

def attend(query_rows, key_rows, value_rows, grad_rows, segment, row_start, local_kv):
    length = query_rows.shape[0]
    key_len = key_rows.shape[0]
    head_dim = key_rows.shape[1] // local_kv
    per_group = query_rows.shape[1] // (local_kv * head_dim)
    query4 = query_rows.reshape(length, local_kv, per_group, head_dim).astype(jnp.float32)
    grad4 = grad_rows.reshape(length, local_kv, per_group, head_dim)
    key3 = key_rows.reshape(key_len, local_kv, head_dim).astype(jnp.float32)
    value3 = value_rows.reshape(key_len, local_kv, head_dim).astype(jnp.float32)
    block = min(512, length)
    scale = head_dim ** (-0.5)
    columns = jnp.arange(key_len, dtype=jnp.int32)

    def step(carry, index):
        key_acc, value_acc = carry
        start = (index * block).astype(jnp.int32)
        query_blk = lax.dynamic_slice_in_dim(query4, start, block, 0)
        grad_blk = lax.dynamic_slice_in_dim(grad4, start, block, 0)
        row_ids = row_start + start + jnp.arange(block, dtype=jnp.int32)
        row_seg = lax.dynamic_slice_in_dim(segment, row_start + start, block, 0)
        allowed = (columns[None, :] <= row_ids[:, None]) & (segment[None, :] == row_seg[:, None])
        scores = jnp.einsum('qngd,knd->ngqk', query_blk, key3) * scale
        scores = jnp.where(allowed, scores, -1e+30)
        weights = jnp.exp(scores - lax.optimization_barrier(jnp.max(scores, axis=-1, keepdims=True)))
        probs = weights / lax.optimization_barrier(jnp.sum(weights, axis=-1, keepdims=True))
        probs_b = probs.astype(jnp.bfloat16)
        output = jnp.einsum('ngqk,knd->qngd', probs_b.astype(jnp.float32), value3).astype(jnp.bfloat16)
        grad_f = grad_blk.astype(jnp.float32)
        delta = jnp.transpose(lax.optimization_barrier(jnp.sum(grad_f * output.astype(jnp.float32), axis=-1)), (1, 2, 0))
        dprob = jnp.einsum('qngd,knd->ngqk', grad_f, value3)
        dscore = (probs * (dprob - delta[..., None]) * scale).astype(jnp.bfloat16)
        dscore_f = dscore.astype(jnp.float32)
        grad_query = jnp.einsum('ngqk,knd->qngd', dscore_f, key3).astype(jnp.bfloat16)
        key_acc = key_acc + jnp.einsum('ngqk,qngd->knd', dscore_f, query_blk)
        value_acc = value_acc + jnp.einsum('ngqk,qngd->knd', probs_b.astype(jnp.float32), grad_f)
        return ((key_acc, value_acc), (output, grad_query))
    zeros = jnp.zeros((key_len, local_kv, head_dim), jnp.float32)
    (key_grad, value_grad), (outputs, grad_query) = lax.scan(step, (zeros, zeros), jnp.arange(length // block, dtype=jnp.int32))
    return (outputs.reshape(length, -1), grad_query.reshape(length, -1), key_grad.reshape(key_len, -1), value_grad.reshape(key_len, -1))

def reference(queries, keys, values, grad_out, quant_scale, doc_lengths):
    rows = queries.shape[0]
    key_raw = keys.astype(jnp.float32).reshape(rows, KVH, HD)
    value_raw = values.astype(jnp.float32).reshape(rows, KVH, HD)
    (key_q, value_q), pull = jax.vjp(quant_pair, key_raw, value_raw, quant_scale)
    key_b = key_q.astype(jnp.bfloat16).reshape(N_DP, SLAB, KVH * HD)
    value_b = value_q.astype(jnp.bfloat16).reshape(N_DP, SLAB, KVH * HD)

    def per_slab(item):
        query_rows, key_rows, value_rows, grad_rows, lengths = item
        segment = segments(lengths, SLAB)
        return attend(query_rows, key_rows, value_rows, grad_rows, segment, 0, KVH)
    outputs, grad_query, key_grad, value_grad = lax.map(per_slab, (queries.reshape(N_DP, SLAB, HQ * HD), key_b, value_b, grad_out.reshape(N_DP, SLAB, HQ * HD), doc_lengths))
    key_in, value_in, grad_scale = pull((key_grad.reshape(rows, KVH, HD), value_grad.reshape(rows, KVH, HD)))
    return (outputs.reshape(rows, HQ * HD), grad_query.reshape(rows, HQ * HD), key_in.reshape(rows, KVH * HD).astype(jnp.bfloat16), value_in.reshape(rows, KVH * HD).astype(jnp.bfloat16), grad_scale)
```

```python
import functools
import math

import jax
import jax.numpy as jnp
from jax import lax
from jax.experimental import pallas as pl
from jax.experimental.pallas import tpu as pltpu
from jax.sharding import PartitionSpec as P

F32 = jnp.float32
BF16 = jnp.bfloat16
LEVELS = 127.0
NEG = -1e30


def sin_cos_half(u):
    r = (u - jnp.round(u)) * math.pi
    z = r * r
    s = z * (1.0 / 6227020800.0) - 1.0 / 39916800.0
    for c in (1.0 / 362880.0, -1.0 / 5040.0, 1.0 / 120.0, -1.0 / 6.0, 1.0):
        s = s * z + c
    s = s * r
    k = z * (1.0 / 479001600.0) - 1.0 / 3628800.0
    for c in (1.0 / 40320.0, -1.0 / 720.0, 1.0 / 24.0, -0.5, 1.0):
        k = k * z + c
    return s, k


def quant_parts(x, clip):
    inv = 1.0 / clip
    ratio = x * inv
    t = jnp.tanh(ratio)
    u = LEVELS * t
    s, k = sin_cos_half(u)
    level = u - s * k * (1.0 / math.pi)
    unit = level * (1.0 / LEVELS)
    slope = (2.0 * s * s) * (1.0 - t * t)
    return clip * unit, slope, unit - slope * ratio


def prep_kernel(nb, len_ref, key_ref, value_ref, clip_ref, q_ref, slope_ref, dclip_ref, bias_ref):
    rows = key_ref.shape[0]
    kv_heads, hd = clip_ref.shape[1], clip_ref.shape[2]
    base = lax.axis_index("seq") * rows
    for side, src in ((0, key_ref), (1, value_ref)):
        for n in range(kv_heads):
            x = src[:, n * hd:(n + 1) * hd].astype(F32)
            q, slope, dclip = quant_parts(x, clip_ref[side, n:n + 1, :])
            at = slice((side * kv_heads + n) * hd, (side * kv_heads + n + 1) * hd)
            q_ref[:, at] = q.astype(BF16)
            slope_ref[:, at] = slope
            dclip_ref[:, at] = dclip
    row = lax.broadcasted_iota(jnp.int32, (rows, rows), 0)
    col = lax.broadcasted_iota(jnp.int32, (rows, rows), 1)
    start = jnp.zeros((rows, rows), jnp.int32)
    end = jnp.int32(0)
    for d in range(len_ref.shape[1]):
        end = end + len_ref[0, d]
        start = jnp.where(row + base >= end, end, start)
    for b in range(nb):
        if b == 0:
            pos = jnp.where(col <= row, col, col - nb * rows)
        else:
            pos = col - b * rows
        bias_ref[:, b * rows:(b + 1) * rows] = jnp.where(pos + base >= start, 0.0, NEG)


def attend_kernel(nb, q_ref, g_ref, kq_ref, vq_ref, kd_ref, vd_ref, bias_ref, clip_ref, *rest):
    far_k, far_v = rest[:nb], rest[nb:2 * nb]
    out_ref, gq_ref, kg_ref, vg_ref, scale_ref, kf_ref, vf_ref = rest[2 * nb:]
    rows, hd = kq_ref.shape
    heads = q_ref.shape[1] // hd
    kv_heads = clip_ref.shape[1]
    n = pl.program_id(0)
    scale = hd ** -0.5
    log2e = math.log2(math.e)
    k_clip = clip_ref[0, pl.ds(n, 1), :]
    v_clip = clip_ref[1, pl.ds(n, 1), :]
    ks, vs, kd, vd = [kq_ref[...]], [vq_ref[...]], [kd_ref[...]], [vd_ref[...]]
    for d in [nb] + list(range(1, nb)):
        q, _, dc = quant_parts(far_k[d - 1][...].astype(F32), k_clip)
        ks.append(q.astype(BF16))
        kd.append(dc)
        q, _, dc = quant_parts(far_v[d - 1][...].astype(F32), v_clip)
        vs.append(q.astype(BF16))
        vd.append(dc)
    k2 = jnp.concatenate(ks, axis=0)
    v2 = jnp.concatenate(vs, axis=0)
    qs = jnp.concatenate([q_ref[:, h * hd:(h + 1) * hd] for h in range(heads)], axis=0)
    gs = jnp.concatenate([g_ref[:, h * hd:(h + 1) * hd] for h in range(heads)], axis=0)
    across = (((1,), (1,)), ((), ()))
    down = (((0,), (0,)), ((), ()))
    s_all = lax.dot_general(qs, k2, across, preferred_element_type=F32)
    d_all = lax.dot_general(gs, v2, across, preferred_element_type=F32)
    row = lax.broadcasted_iota(jnp.int32, (rows, rows), 0)
    col = lax.broadcasted_iota(jnp.int32, (rows, rows), 1)
    near = col <= row
    near_b = near.astype(F32).astype(BF16)
    far_b = 1.0 - near_b
    bias = bias_ref[...]

    def merge(x):
        first = jnp.where(near, x[:, :rows], x[:, rows:2 * rows])
        return jnp.concatenate([first, x[:, 2 * rows:]], axis=1) if nb > 1 else first

    def split(x):
        first = x[:, :rows]
        parts = [first * near_b, first * far_b]
        if nb > 1:
            parts.append(x[:, rows:])
        return jnp.concatenate(parts, axis=1)

    ps, ds = [], []
    for h in range(heads):
        at = slice(h * rows, (h + 1) * rows)
        s = merge(s_all[at]) * (scale * log2e) + bias
        dp = merge(d_all[at])
        w = jnp.exp2(s - jnp.max(s, axis=1, keepdims=True))
        inv = 1.0 / jnp.sum(w, axis=1, keepdims=True)
        p = w * inv
        delta = jnp.sum(p * dp, axis=1, keepdims=True)
        p2 = split(p.astype(BF16))
        ds2 = split((p * ((dp - delta) * scale)).astype(BF16))
        cols = slice(h * hd, (h + 1) * hd)
        out_ref[:, cols] = jnp.dot(p2, v2, preferred_element_type=F32).astype(BF16)
        gq_ref[:, cols] = jnp.dot(ds2, k2, preferred_element_type=F32).astype(BF16)
        ps.append(p2)
        ds.append(ds2)
    k_grad = lax.dot_general(qs, jnp.concatenate(ds, axis=0), down, preferred_element_type=F32).T
    v_grad = lax.dot_general(gs, jnp.concatenate(ps, axis=0), down, preferred_element_type=F32).T
    kg_ref[...] = k_grad[:rows]
    vg_ref[...] = v_grad[:rows]
    kf_ref[...] = k_grad[rows:].astype(BF16)
    vf_ref[...] = v_grad[rows:].astype(BF16)
    scale_ref[pl.ds(n, 1), :] = jnp.sum(k_grad * jnp.concatenate(kd, axis=0), axis=0, keepdims=True)
    scale_ref[pl.ds(kv_heads + n, 1), :] = jnp.sum(
        v_grad * jnp.concatenate(vd, axis=0), axis=0, keepdims=True
    )


def finish_kernel(nb, kg_ref, vg_ref, slope_ref, *rest):
    backs, (gk_ref, gv_ref) = rest[:2 * nb], rest[2 * nb:]
    width = kg_ref.shape[1]
    for side, own, out in ((0, kg_ref, gk_ref), (1, vg_ref, gv_ref)):
        total = own[...]
        for d in range(nb):
            total = total + backs[side * nb + d][...].astype(F32)
        out[...] = (total * slope_ref[:, side * width:(side + 1) * width]).astype(BF16)


def all_sum(part, axes, count):
    stride = 1
    while stride < count:
        size = min(8, count // stride)
        while (count // stride) % size:
            size //= 2
        terms = [part]
        for k in range(1, size):
            perm = [(i, i ^ (k * stride)) for i in range(count)]
            terms.append(lax.ppermute(part, axes, perm))
        while len(terms) > 1:
            terms = [terms[j] + terms[j + 1] for j in range(0, len(terms), 2)]
        part = terms[0]
        stride *= size
    return part


def on_device(sizes, queries, keys, values, grad_out, quant_scale, doc_lengths):
    dp_count, seq_count = sizes
    nb = max(1, seq_count // 2)
    rows, width = keys.shape
    kv_heads, hd = quant_scale.shape[1], quant_scale.shape[2]
    group = queries.shape[1] // kv_heads
    vmem = functools.partial(pl.BlockSpec, memory_space=pltpu.VMEM)
    params = pltpu.CompilerParams(vmem_limit_bytes=40 * 1024 * 1024)

    def shift(array, d):
        return lax.ppermute(array, "seq", [(r, r + d) for r in range(seq_count - d)])

    def unshift(array, d):
        return lax.ppermute(array, "seq", [(r + d, r) for r in range(seq_count - d)])

    far_k = [shift(keys, d) for d in range(1, nb + 1)]
    far_v = [shift(values, d) for d in range(1, nb + 1)]

    quants, slopes, dclips, bias = pl.pallas_call(
        functools.partial(prep_kernel, nb),
        out_shape=(
            jax.ShapeDtypeStruct((rows, 2 * width), BF16),
            jax.ShapeDtypeStruct((rows, 2 * width), F32),
            jax.ShapeDtypeStruct((rows, 2 * width), F32),
            jax.ShapeDtypeStruct((rows, nb * rows), F32),
        ),
        in_specs=[pl.BlockSpec(memory_space=pltpu.SMEM), vmem(), vmem(), vmem()],
        out_specs=(vmem(), vmem(), vmem(), vmem()),
        compiler_params=params,
        cost_estimate=pl.CostEstimate(
            flops=100 * rows * width, bytes_accessed=16 * rows * width, transcendentals=2 * rows * width
        ),
        name="prep",
    )(doc_lengths, keys, values, quant_scale)

    wide = pl.BlockSpec((rows, group), lambda n: (0, n))
    thin = pl.BlockSpec((rows, hd), lambda n: (0, n))
    thin_v = pl.BlockSpec((rows, hd), lambda n: (0, kv_heads + n))
    whole = lambda shape: pl.BlockSpec(shape, lambda n: (0,) * len(shape))
    attn_out, grad_queries, k_grad, v_grad, scale_part, k_far, v_far = pl.pallas_call(
        functools.partial(attend_kernel, nb),
        grid=(kv_heads,),
        out_shape=(
            jax.ShapeDtypeStruct(queries.shape, BF16),
            jax.ShapeDtypeStruct(queries.shape, BF16),
            jax.ShapeDtypeStruct((rows, width), F32),
            jax.ShapeDtypeStruct((rows, width), F32),
            jax.ShapeDtypeStruct((2 * kv_heads, hd), F32),
            jax.ShapeDtypeStruct((nb * rows, width), BF16),
            jax.ShapeDtypeStruct((nb * rows, width), BF16),
        ),
        in_specs=[wide, wide, thin, thin_v, thin, thin_v, whole((rows, nb * rows)), whole(quant_scale.shape)]
        + [thin] * (2 * nb),
        out_specs=(
            wide,
            wide,
            thin,
            thin,
            whole((2 * kv_heads, hd)),
            pl.BlockSpec((nb * rows, hd), lambda n: (0, n)),
            pl.BlockSpec((nb * rows, hd), lambda n: (0, n)),
        ),
        compiler_params=params,
        cost_estimate=pl.CostEstimate(
            flops=12 * rows * (nb + 1) * rows * queries.shape[1],
            bytes_accessed=8 * rows * queries.shape[1],
            transcendentals=rows * rows * nb * queries.shape[1] // hd,
        ),
        name="attend",
    )(queries, grad_out, quants, quants, dclips, dclips, bias, quant_scale, *far_k, *far_v)

    total = all_sum(scale_part, ("dp", "seq"), dp_count * seq_count)
    grad_scale = total.reshape(quant_scale.shape)

    order = [nb] + list(range(1, nb))
    piece = lambda array, d: lax.slice_in_dim(array, order.index(d) * rows, (order.index(d) + 1) * rows, axis=0)
    backs = [unshift(piece(k_far, d), d) for d in range(1, nb + 1)]
    backs += [unshift(piece(v_far, d), d) for d in range(1, nb + 1)]
    grad_keys, grad_values = pl.pallas_call(
        functools.partial(finish_kernel, nb),
        out_shape=(
            jax.ShapeDtypeStruct((rows, width), BF16),
            jax.ShapeDtypeStruct((rows, width), BF16),
        ),
        in_specs=[vmem()] * (3 + 2 * nb),
        out_specs=(vmem(), vmem()),
        compiler_params=params,
        cost_estimate=pl.CostEstimate(
            flops=6 * rows * width, bytes_accessed=20 * rows * width, transcendentals=0
        ),
        name="finish",
    )(k_grad, v_grad, slopes, *backs)
    return (attn_out, grad_queries, grad_keys, grad_values, grad_scale)


def solution(mesh):
    rows = P(("dp", "seq"), None)
    return jax.shard_map(
        functools.partial(on_device, (mesh.shape["dp"], mesh.shape["seq"])),
        mesh=mesh,
        in_specs=(rows, rows, rows, rows, P(), P("dp", None)),
        out_specs=(rows, rows, rows, rows, P()),
        check_vma=False,
    )
```

```python
import functools
import math

import jax
import jax.numpy as jnp
from jax import lax
from jax.experimental import pallas as pl
from jax.experimental.pallas import tpu as pltpu
from jax.sharding import PartitionSpec as P

F32 = jnp.float32
BF16 = jnp.bfloat16
LEVELS = 127.0
NEG = -1e30


def sin_cos_half(u):
    r = (u - jnp.round(u)) * math.pi
    z = r * r
    s = z * (1.0 / 6227020800.0) - 1.0 / 39916800.0
    for c in (1.0 / 362880.0, -1.0 / 5040.0, 1.0 / 120.0, -1.0 / 6.0, 1.0):
        s = s * z + c
    s = s * r
    k = z * (1.0 / 479001600.0) - 1.0 / 3628800.0
    for c in (1.0 / 40320.0, -1.0 / 720.0, 1.0 / 24.0, -0.5, 1.0):
        k = k * z + c
    return s, k


def quant_parts(x, clip):
    inv = 1.0 / clip
    ratio = x * inv
    t = jnp.tanh(ratio)
    u = LEVELS * t
    s, k = sin_cos_half(u)
    level = u - s * k * (1.0 / math.pi)
    unit = level * (1.0 / LEVELS)
    slope = (2.0 * s * s) * (1.0 - t * t)
    return clip * unit, slope, unit - slope * ratio


def prep_kernel(nb, len_ref, key_ref, value_ref, clip_ref, q_ref, slope_ref, dclip_ref, bias_ref):
    rows = key_ref.shape[0]
    kv_heads, hd = clip_ref.shape[1], clip_ref.shape[2]
    base = lax.axis_index("seq") * rows
    for side, src in ((0, key_ref), (1, value_ref)):
        for n in range(kv_heads):
            x = src[:, n * hd:(n + 1) * hd].astype(F32)
            q, slope, dclip = quant_parts(x, clip_ref[side, n:n + 1, :])
            at = slice((side * kv_heads + n) * hd, (side * kv_heads + n + 1) * hd)
            q_ref[:, at] = q.astype(BF16)
            slope_ref[:, at] = slope
            dclip_ref[:, at] = dclip
    row = lax.broadcasted_iota(jnp.int32, (rows, rows), 0)
    col = lax.broadcasted_iota(jnp.int32, (rows, rows), 1)
    start = jnp.zeros((rows, rows), jnp.int32)
    end = jnp.int32(0)
    for d in range(len_ref.shape[1]):
        end = end + len_ref[0, d]
        start = jnp.where(row + base >= end, end, start)
    for b in range(nb):
        if b == 0:
            pos = jnp.where(col <= row, col, col - nb * rows)
        else:
            pos = col - b * rows
        bias_ref[:, b * rows:(b + 1) * rows] = jnp.where(pos + base >= start, 0.0, NEG)


def attend_kernel(nb, q_ref, g_ref, kq_ref, vq_ref, kd_ref, vd_ref, bias_ref, clip_ref, *rest):
    far_k, far_v = rest[:nb], rest[nb:2 * nb]
    out_ref, gq_ref, kg_ref, vg_ref, scale_ref, kf_ref, vf_ref = rest[2 * nb:]
    rows, hd = kq_ref.shape
    heads = q_ref.shape[1] // hd
    kv_heads = clip_ref.shape[1]
    n = pl.program_id(0)
    scale = hd ** -0.5
    log2e = math.log2(math.e)
    k_clip = clip_ref[0, pl.ds(n, 1), :]
    v_clip = clip_ref[1, pl.ds(n, 1), :]
    ks, vs, kd, vd = [kq_ref[...]], [vq_ref[...]], [kd_ref[...]], [vd_ref[...]]
    for d in [nb] + list(range(1, nb)):
        q, _, dc = quant_parts(far_k[d - 1][...].astype(F32), k_clip)
        ks.append(q.astype(BF16))
        kd.append(dc)
        q, _, dc = quant_parts(far_v[d - 1][...].astype(F32), v_clip)
        vs.append(q.astype(BF16))
        vd.append(dc)
    k2 = jnp.concatenate(ks, axis=0)
    v2 = jnp.concatenate(vs, axis=0)
    qs = jnp.concatenate([q_ref[:, h * hd:(h + 1) * hd] for h in range(heads)], axis=0)
    gs = jnp.concatenate([g_ref[:, h * hd:(h + 1) * hd] for h in range(heads)], axis=0)
    across = (((1,), (1,)), ((), ()))
    down = (((0,), (0,)), ((), ()))
    s_all = lax.dot_general(qs, k2, across, preferred_element_type=F32)
    d_all = lax.dot_general(gs, v2, across, preferred_element_type=F32)
    row = lax.broadcasted_iota(jnp.int32, (rows, rows), 0)
    col = lax.broadcasted_iota(jnp.int32, (rows, rows), 1)
    near = col <= row
    near_b = near.astype(F32).astype(BF16)
    far_b = 1.0 - near_b
    bias = bias_ref[...]

    def merge(x):
        first = jnp.where(near, x[:, :rows], x[:, rows:2 * rows])
        return jnp.concatenate([first, x[:, 2 * rows:]], axis=1) if nb > 1 else first

    def split(x):
        first = x[:, :rows]
        parts = [first * near_b, first * far_b]
        if nb > 1:
            parts.append(x[:, rows:])
        return jnp.concatenate(parts, axis=1)

    ps, ds = [], []
    for h in range(heads):
        at = slice(h * rows, (h + 1) * rows)
        s = merge(s_all[at]) * (scale * log2e) + bias
        dp = merge(d_all[at])
        w = jnp.exp2(s - jnp.max(s, axis=1, keepdims=True))
        inv = 1.0 / jnp.sum(w, axis=1, keepdims=True)
        p = w * inv
        delta = jnp.sum(p * dp, axis=1, keepdims=True)
        p2 = split(p.astype(BF16))
        ds2 = split((p * ((dp - delta) * scale)).astype(BF16))
        cols = slice(h * hd, (h + 1) * hd)
        out_ref[:, cols] = jnp.dot(p2, v2, preferred_element_type=F32).astype(BF16)
        gq_ref[:, cols] = jnp.dot(ds2, k2, preferred_element_type=F32).astype(BF16)
        ps.append(p2)
        ds.append(ds2)
    k_grad = lax.dot_general(qs, jnp.concatenate(ds, axis=0), down, preferred_element_type=F32).T
    v_grad = lax.dot_general(gs, jnp.concatenate(ps, axis=0), down, preferred_element_type=F32).T
    kg_ref[...] = k_grad[:rows]
    vg_ref[...] = v_grad[:rows]
    kf_ref[...] = k_grad[rows:].astype(BF16)
    vf_ref[...] = v_grad[rows:].astype(BF16)
    scale_ref[pl.ds(n, 1), :] = jnp.sum(k_grad * jnp.concatenate(kd, axis=0), axis=0, keepdims=True)
    scale_ref[pl.ds(kv_heads + n, 1), :] = jnp.sum(
        v_grad * jnp.concatenate(vd, axis=0), axis=0, keepdims=True
    )


def finish_kernel(nb, kg_ref, vg_ref, slope_ref, *rest):
    backs, (gk_ref, gv_ref) = rest[:2 * nb], rest[2 * nb:]
    width = kg_ref.shape[1]
    for side, own, out in ((0, kg_ref, gk_ref), (1, vg_ref, gv_ref)):
        total = own[...]
        for d in range(nb):
            total = total + backs[side * nb + d][...].astype(F32)
        out[...] = (total * slope_ref[:, side * width:(side + 1) * width]).astype(BF16)


def all_sum(part, axes, count):
    gathered = lax.all_gather(part, axes, axis=0, tiled=False)
    return jnp.sum(gathered, axis=0)


def on_device(sizes, queries, keys, values, grad_out, quant_scale, doc_lengths):
    dp_count, seq_count = sizes
    nb = max(1, seq_count // 2)
    rows, width = keys.shape
    kv_heads, hd = quant_scale.shape[1], quant_scale.shape[2]
    group = queries.shape[1] // kv_heads
    vmem = functools.partial(pl.BlockSpec, memory_space=pltpu.VMEM)
    params = pltpu.CompilerParams(vmem_limit_bytes=40 * 1024 * 1024)

    def shift(array, d):
        return lax.ppermute(array, "seq", [(r, r + d) for r in range(seq_count - d)])

    def unshift(array, d):
        return lax.ppermute(array, "seq", [(r + d, r) for r in range(seq_count - d)])

    far_k = [shift(keys, d) for d in range(1, nb + 1)]
    far_v = [shift(values, d) for d in range(1, nb + 1)]

    quants, slopes, dclips, bias = pl.pallas_call(
        functools.partial(prep_kernel, nb),
        out_shape=(
            jax.ShapeDtypeStruct((rows, 2 * width), BF16),
            jax.ShapeDtypeStruct((rows, 2 * width), F32),
            jax.ShapeDtypeStruct((rows, 2 * width), F32),
            jax.ShapeDtypeStruct((rows, nb * rows), F32),
        ),
        in_specs=[pl.BlockSpec(memory_space=pltpu.SMEM), vmem(), vmem(), vmem()],
        out_specs=(vmem(), vmem(), vmem(), vmem()),
        compiler_params=params,
        cost_estimate=pl.CostEstimate(
            flops=100 * rows * width, bytes_accessed=16 * rows * width, transcendentals=2 * rows * width
        ),
        name="prep",
    )(doc_lengths, keys, values, quant_scale)

    wide = pl.BlockSpec((rows, group), lambda n: (0, n))
    thin = pl.BlockSpec((rows, hd), lambda n: (0, n))
    thin_v = pl.BlockSpec((rows, hd), lambda n: (0, kv_heads + n))
    whole = lambda shape: pl.BlockSpec(shape, lambda n: (0,) * len(shape))
    attn_out, grad_queries, k_grad, v_grad, scale_part, k_far, v_far = pl.pallas_call(
        functools.partial(attend_kernel, nb),
        grid=(kv_heads,),
        out_shape=(
            jax.ShapeDtypeStruct(queries.shape, BF16),
            jax.ShapeDtypeStruct(queries.shape, BF16),
            jax.ShapeDtypeStruct((rows, width), F32),
            jax.ShapeDtypeStruct((rows, width), F32),
            jax.ShapeDtypeStruct((2 * kv_heads, hd), F32),
            jax.ShapeDtypeStruct((nb * rows, width), BF16),
            jax.ShapeDtypeStruct((nb * rows, width), BF16),
        ),
        in_specs=[wide, wide, thin, thin_v, thin, thin_v, whole((rows, nb * rows)), whole(quant_scale.shape)]
        + [thin] * (2 * nb),
        out_specs=(
            wide,
            wide,
            thin,
            thin,
            whole((2 * kv_heads, hd)),
            pl.BlockSpec((nb * rows, hd), lambda n: (0, n)),
            pl.BlockSpec((nb * rows, hd), lambda n: (0, n)),
        ),
        compiler_params=params,
        cost_estimate=pl.CostEstimate(
            flops=12 * rows * (nb + 1) * rows * queries.shape[1],
            bytes_accessed=8 * rows * queries.shape[1],
            transcendentals=rows * rows * nb * queries.shape[1] // hd,
        ),
        name="attend",
    )(queries, grad_out, quants, quants, dclips, dclips, bias, quant_scale, *far_k, *far_v)

    total = all_sum(scale_part, ("dp", "seq"), dp_count * seq_count)
    grad_scale = total.reshape(quant_scale.shape)

    order = [nb] + list(range(1, nb))
    piece = lambda array, d: lax.slice_in_dim(array, order.index(d) * rows, (order.index(d) + 1) * rows, axis=0)
    backs = [unshift(piece(k_far, d), d) for d in range(1, nb + 1)]
    backs += [unshift(piece(v_far, d), d) for d in range(1, nb + 1)]
    grad_keys, grad_values = pl.pallas_call(
        functools.partial(finish_kernel, nb),
        out_shape=(
            jax.ShapeDtypeStruct((rows, width), BF16),
            jax.ShapeDtypeStruct((rows, width), BF16),
        ),
        in_specs=[vmem()] * (3 + 2 * nb),
        out_specs=(vmem(), vmem()),
        compiler_params=params,
        cost_estimate=pl.CostEstimate(
            flops=6 * rows * width, bytes_accessed=20 * rows * width, transcendentals=0
        ),
        name="finish",
    )(k_grad, v_grad, slopes, *backs)
    return (attn_out, grad_queries, grad_keys, grad_values, grad_scale)


def solution(mesh):
    rows = P(("dp", "seq"), None)
    return jax.shard_map(
        functools.partial(on_device, (mesh.shape["dp"], mesh.shape["seq"])),
        mesh=mesh,
        in_specs=(rows, rows, rows, rows, P(), P("dp", None)),
        out_specs=(rows, rows, rows, rows, P()),
        check_vma=False,
    )
```

```python
import functools
import math

import jax
import jax.numpy as jnp
from jax import lax
from jax.experimental import pallas as pl
from jax.experimental.pallas import tpu as pltpu
from jax.sharding import PartitionSpec as P

F32 = jnp.float32
BF16 = jnp.bfloat16
LEVELS = 127.0
NEG = -1e30


def sin_cos_half(u):
    r = (u - jnp.round(u)) * math.pi
    z = r * r
    s = z * (1.0 / 6227020800.0) - 1.0 / 39916800.0
    for c in (1.0 / 362880.0, -1.0 / 5040.0, 1.0 / 120.0, -1.0 / 6.0, 1.0):
        s = s * z + c
    s = s * r
    k = z * (1.0 / 479001600.0) - 1.0 / 3628800.0
    for c in (1.0 / 40320.0, -1.0 / 720.0, 1.0 / 24.0, -0.5, 1.0):
        k = k * z + c
    return s, k


def quant_parts(x, clip):
    inv = 1.0 / clip
    ratio = x * inv
    t = jnp.tanh(ratio)
    u = LEVELS * t
    s, k = sin_cos_half(u)
    level = u - s * k * (1.0 / math.pi)
    unit = level * (1.0 / LEVELS)
    slope = (2.0 * s * s) * (1.0 - t * t)
    return clip * unit, slope, unit - slope * ratio


def prep_kernel(nb, len_ref, key_ref, value_ref, clip_ref, q_ref, slope_ref, dclip_ref, bias_ref):
    rows = key_ref.shape[0]
    kv_heads, hd = clip_ref.shape[1], clip_ref.shape[2]
    base = lax.axis_index("seq") * rows
    for side, src in ((0, key_ref), (1, value_ref)):
        for n in range(kv_heads):
            x = src[:, n * hd:(n + 1) * hd].astype(F32)
            q, slope, dclip = quant_parts(x, clip_ref[side, n:n + 1, :])
            at = slice((side * kv_heads + n) * hd, (side * kv_heads + n + 1) * hd)
            q_ref[:, at] = q.astype(BF16)
            slope_ref[:, at] = slope
            dclip_ref[:, at] = dclip
    row = lax.broadcasted_iota(jnp.int32, (rows, rows), 0)
    col = lax.broadcasted_iota(jnp.int32, (rows, rows), 1)
    start = jnp.zeros((rows, rows), jnp.int32)
    end = jnp.int32(0)
    for d in range(len_ref.shape[1]):
        end = end + len_ref[0, d]
        start = jnp.where(row + base >= end, end, start)
    for b in range(nb):
        if b == 0:
            pos = jnp.where(col <= row, col, col - nb * rows)
        else:
            pos = col - b * rows
        bias_ref[:, b * rows:(b + 1) * rows] = jnp.where(pos + base >= start, 0.0, NEG)


def attend_kernel(nb, q_ref, g_ref, kq_ref, vq_ref, kd_ref, vd_ref, bias_ref, clip_ref, *rest):
    far_k, far_v = rest[:nb], rest[nb:2 * nb]
    out_ref, gq_ref, kg_ref, vg_ref, scale_ref, kf_ref, vf_ref = rest[2 * nb:]
    rows, hd = kq_ref.shape
    heads = q_ref.shape[1] // hd
    kv_heads = clip_ref.shape[1]
    n = pl.program_id(0)
    scale = hd ** -0.5
    log2e = math.log2(math.e)
    k_clip = clip_ref[0, pl.ds(n, 1), :]
    v_clip = clip_ref[1, pl.ds(n, 1), :]
    ks, vs, kd, vd = [kq_ref[...]], [vq_ref[...]], [kd_ref[...]], [vd_ref[...]]
    for d in [nb] + list(range(1, nb)):
        q, _, dc = quant_parts(far_k[d - 1][...].astype(F32), k_clip)
        ks.append(q.astype(BF16))
        kd.append(dc)
        q, _, dc = quant_parts(far_v[d - 1][...].astype(F32), v_clip)
        vs.append(q.astype(BF16))
        vd.append(dc)
    k2 = jnp.concatenate(ks, axis=0)
    v2 = jnp.concatenate(vs, axis=0)
    qs = jnp.concatenate([q_ref[:, h * hd:(h + 1) * hd] for h in range(heads)], axis=0)
    gs = jnp.concatenate([g_ref[:, h * hd:(h + 1) * hd] for h in range(heads)], axis=0)
    across = (((1,), (1,)), ((), ()))
    down = (((0,), (0,)), ((), ()))
    s_all = lax.dot_general(qs, k2, across, preferred_element_type=F32)
    d_all = lax.dot_general(gs, v2, across, preferred_element_type=F32)
    row = lax.broadcasted_iota(jnp.int32, (rows, rows), 0)
    col = lax.broadcasted_iota(jnp.int32, (rows, rows), 1)
    near = col <= row
    near_b = near.astype(F32).astype(BF16)
    far_b = 1.0 - near_b
    bias = bias_ref[...]

    def merge(x):
        first = jnp.where(near, x[:, :rows], x[:, rows:2 * rows])
        return jnp.concatenate([first, x[:, 2 * rows:]], axis=1) if nb > 1 else first

    def split(x):
        first = x[:, :rows]
        parts = [first * near_b, first * far_b]
        if nb > 1:
            parts.append(x[:, rows:])
        return jnp.concatenate(parts, axis=1)

    ps, ds = [], []
    for h in range(heads):
        at = slice(h * rows, (h + 1) * rows)
        s = merge(s_all[at]) * (scale * log2e) + bias
        dp = merge(d_all[at])
        w = jnp.exp2(s - jnp.max(s, axis=1, keepdims=True))
        inv = 1.0 / jnp.sum(w, axis=1, keepdims=True)
        p = w * inv
        delta = jnp.sum(p * dp, axis=1, keepdims=True)
        p2 = split(p.astype(BF16))
        ds2 = split((p * ((dp - delta) * scale)).astype(BF16))
        cols = slice(h * hd, (h + 1) * hd)
        out_ref[:, cols] = jnp.dot(p2, v2, preferred_element_type=F32).astype(BF16)
        gq_ref[:, cols] = jnp.dot(ds2, k2, preferred_element_type=F32).astype(BF16)
        ps.append(p2)
        ds.append(ds2)
    k_grad = lax.dot_general(qs, jnp.concatenate(ds, axis=0), down, preferred_element_type=F32).T
    v_grad = lax.dot_general(gs, jnp.concatenate(ps, axis=0), down, preferred_element_type=F32).T
    kg_ref[...] = k_grad[:rows]
    vg_ref[...] = v_grad[:rows]
    kf_ref[...] = k_grad[rows:].astype(BF16)
    vf_ref[...] = v_grad[rows:].astype(BF16)
    scale_ref[pl.ds(n, 1), :] = jnp.sum(k_grad * jnp.concatenate(kd, axis=0), axis=0, keepdims=True)
    scale_ref[pl.ds(kv_heads + n, 1), :] = jnp.sum(
        v_grad * jnp.concatenate(vd, axis=0), axis=0, keepdims=True
    )


def finish_kernel(nb, kg_ref, vg_ref, slope_ref, *rest):
    backs, (gk_ref, gv_ref) = rest[:2 * nb], rest[2 * nb:]
    width = kg_ref.shape[1]
    for side, own, out in ((0, kg_ref, gk_ref), (1, vg_ref, gv_ref)):
        total = own[...]
        for d in range(nb):
            total = total + backs[side * nb + d][...].astype(F32)
        out[...] = (total * slope_ref[:, side * width:(side + 1) * width]).astype(BF16)


def all_sum(part, axes, count):
    copies = jnp.broadcast_to(part[None], (count,) + part.shape)
    gathered = lax.all_to_all(copies, axes, split_axis=0, concat_axis=0, tiled=True)
    return jnp.sum(gathered, axis=0)


def on_device(sizes, queries, keys, values, grad_out, quant_scale, doc_lengths):
    dp_count, seq_count = sizes
    nb = max(1, seq_count // 2)
    rows, width = keys.shape
    kv_heads, hd = quant_scale.shape[1], quant_scale.shape[2]
    group = queries.shape[1] // kv_heads
    vmem = functools.partial(pl.BlockSpec, memory_space=pltpu.VMEM)
    params = pltpu.CompilerParams(vmem_limit_bytes=40 * 1024 * 1024)

    def shift(array, d):
        return lax.ppermute(array, "seq", [(r, r + d) for r in range(seq_count - d)])

    def unshift(array, d):
        return lax.ppermute(array, "seq", [(r + d, r) for r in range(seq_count - d)])

    far_k = [shift(keys, d) for d in range(1, nb + 1)]
    far_v = [shift(values, d) for d in range(1, nb + 1)]

    quants, slopes, dclips, bias = pl.pallas_call(
        functools.partial(prep_kernel, nb),
        out_shape=(
            jax.ShapeDtypeStruct((rows, 2 * width), BF16),
            jax.ShapeDtypeStruct((rows, 2 * width), F32),
            jax.ShapeDtypeStruct((rows, 2 * width), F32),
            jax.ShapeDtypeStruct((rows, nb * rows), F32),
        ),
        in_specs=[pl.BlockSpec(memory_space=pltpu.SMEM), vmem(), vmem(), vmem()],
        out_specs=(vmem(), vmem(), vmem(), vmem()),
        compiler_params=params,
        cost_estimate=pl.CostEstimate(
            flops=100 * rows * width, bytes_accessed=16 * rows * width, transcendentals=2 * rows * width
        ),
        name="prep",
    )(doc_lengths, keys, values, quant_scale)

    wide = pl.BlockSpec((rows, group), lambda n: (0, n))
    thin = pl.BlockSpec((rows, hd), lambda n: (0, n))
    thin_v = pl.BlockSpec((rows, hd), lambda n: (0, kv_heads + n))
    whole = lambda shape: pl.BlockSpec(shape, lambda n: (0,) * len(shape))
    attn_out, grad_queries, k_grad, v_grad, scale_part, k_far, v_far = pl.pallas_call(
        functools.partial(attend_kernel, nb),
        grid=(kv_heads,),
        out_shape=(
            jax.ShapeDtypeStruct(queries.shape, BF16),
            jax.ShapeDtypeStruct(queries.shape, BF16),
            jax.ShapeDtypeStruct((rows, width), F32),
            jax.ShapeDtypeStruct((rows, width), F32),
            jax.ShapeDtypeStruct((2 * kv_heads, hd), F32),
            jax.ShapeDtypeStruct((nb * rows, width), BF16),
            jax.ShapeDtypeStruct((nb * rows, width), BF16),
        ),
        in_specs=[wide, wide, thin, thin_v, thin, thin_v, whole((rows, nb * rows)), whole(quant_scale.shape)]
        + [thin] * (2 * nb),
        out_specs=(
            wide,
            wide,
            thin,
            thin,
            whole((2 * kv_heads, hd)),
            pl.BlockSpec((nb * rows, hd), lambda n: (0, n)),
            pl.BlockSpec((nb * rows, hd), lambda n: (0, n)),
        ),
        compiler_params=params,
        cost_estimate=pl.CostEstimate(
            flops=12 * rows * (nb + 1) * rows * queries.shape[1],
            bytes_accessed=8 * rows * queries.shape[1],
            transcendentals=rows * rows * nb * queries.shape[1] // hd,
        ),
        name="attend",
    )(queries, grad_out, quants, quants, dclips, dclips, bias, quant_scale, *far_k, *far_v)

    total = all_sum(scale_part, ("dp", "seq"), dp_count * seq_count)
    grad_scale = total.reshape(quant_scale.shape)

    order = [nb] + list(range(1, nb))
    piece = lambda array, d: lax.slice_in_dim(array, order.index(d) * rows, (order.index(d) + 1) * rows, axis=0)
    backs = [unshift(piece(k_far, d), d) for d in range(1, nb + 1)]
    backs += [unshift(piece(v_far, d), d) for d in range(1, nb + 1)]
    grad_keys, grad_values = pl.pallas_call(
        functools.partial(finish_kernel, nb),
        out_shape=(
            jax.ShapeDtypeStruct((rows, width), BF16),
            jax.ShapeDtypeStruct((rows, width), BF16),
        ),
        in_specs=[vmem()] * (3 + 2 * nb),
        out_specs=(vmem(), vmem()),
        compiler_params=params,
        cost_estimate=pl.CostEstimate(
            flops=6 * rows * width, bytes_accessed=20 * rows * width, transcendentals=0
        ),
        name="finish",
    )(k_grad, v_grad, slopes, *backs)
    return (attn_out, grad_queries, grad_keys, grad_values, grad_scale)


def solution(mesh):
    rows = P(("dp", "seq"), None)
    return jax.shard_map(
        functools.partial(on_device, (mesh.shape["dp"], mesh.shape["seq"])),
        mesh=mesh,
        in_specs=(rows, rows, rows, rows, P(), P("dp", None)),
        out_specs=(rows, rows, rows, rows, P()),
        check_vma=False,
    )
```

```python
import functools
import math

import jax
import jax.numpy as jnp
from jax import lax
from jax.experimental import pallas as pl
from jax.experimental.pallas import tpu as pltpu
from jax.sharding import PartitionSpec as P

F32 = jnp.float32
BF16 = jnp.bfloat16
LEVELS = 127.0
NEG = -1e30


def sin_cos_half(u):
    r = (u - jnp.round(u)) * math.pi
    z = r * r
    s = z * (1.0 / 6227020800.0) - 1.0 / 39916800.0
    for c in (1.0 / 362880.0, -1.0 / 5040.0, 1.0 / 120.0, -1.0 / 6.0, 1.0):
        s = s * z + c
    s = s * r
    k = z * (1.0 / 479001600.0) - 1.0 / 3628800.0
    for c in (1.0 / 40320.0, -1.0 / 720.0, 1.0 / 24.0, -0.5, 1.0):
        k = k * z + c
    return s, k


def quant_parts(x, clip):
    inv = 1.0 / clip
    ratio = x * inv
    t = jnp.tanh(ratio)
    u = LEVELS * t
    s, k = sin_cos_half(u)
    level = u - s * k * (1.0 / math.pi)
    unit = level * (1.0 / LEVELS)
    slope = (2.0 * s * s) * (1.0 - t * t)
    return clip * unit, slope, unit - slope * ratio


def prep_kernel(nb, q_hbm, g_hbm, key_hbm, value_hbm, clip_hbm, len_hbm, q_ref, g_ref, quant_ref, slope_ref,
                dclip_ref, bias_ref, clip_out, key_ref, value_ref, len_ref, sems):
    small = [
        pltpu.make_async_copy(src, dst, sems.at[i])
        for i, (src, dst) in enumerate(
            ((len_hbm, len_ref), (clip_hbm, clip_out), (key_hbm, key_ref), (value_hbm, value_ref))
        )
    ]
    large = [
        pltpu.make_async_copy(q_hbm, q_ref, sems.at[4]),
        pltpu.make_async_copy(g_hbm, g_ref, sems.at[5]),
    ]
    for copy in small + large:
        copy.start()
    rows = key_ref.shape[0]
    kv_heads, hd = clip_out.shape[1], clip_out.shape[2]
    base = lax.axis_index("seq") * rows
    for copy in small:
        copy.wait()
    for side, src in ((0, key_ref), (1, value_ref)):
        for n in range(kv_heads):
            x = src[:, n * hd:(n + 1) * hd].astype(F32)
            q, slope, dclip = quant_parts(x, clip_out[side, n:n + 1, :])
            at = slice((side * kv_heads + n) * hd, (side * kv_heads + n + 1) * hd)
            quant_ref[:, at] = q.astype(BF16)
            slope_ref[:, at] = slope
            dclip_ref[:, at] = dclip
    row = lax.broadcasted_iota(jnp.int32, (rows, rows), 0)
    col = lax.broadcasted_iota(jnp.int32, (rows, rows), 1)
    start = jnp.zeros((rows, rows), jnp.int32)
    end = jnp.int32(0)
    for d in range(len_ref.shape[1]):
        end = end + len_ref[0, d]
        start = jnp.where(row + base >= end, end, start)
    for b in range(nb):
        if b == 0:
            pos = jnp.where(col <= row, col, col - nb * rows)
        else:
            pos = col - b * rows
        bias_ref[:, b * rows:(b + 1) * rows] = jnp.where(pos + base >= start, 0.0, NEG)
    for copy in large:
        copy.wait()


def attend_kernel(nb, q_ref, g_ref, quant_ref, dclip_ref, bias_ref, clip_ref, *rest):
    far_k, far_v = rest[:nb], rest[nb:2 * nb]
    out_hbm, gq_hbm, grad_ref, far_ref, spread_ref, out_ref, gq_ref, scale_ref, sems = rest[2 * nb:]
    kv_heads, hd = clip_ref.shape[1], clip_ref.shape[2]
    rows, group = q_ref.shape[0], q_ref.shape[1] // kv_heads
    heads = group // hd
    width = kv_heads * hd
    scale = hd ** -0.5
    log2e = math.log2(math.e)
    across = (((1,), (1,)), ((), ()))
    down = (((0,), (0,)), ((), ()))
    row = lax.broadcasted_iota(jnp.int32, (rows, rows), 0)
    col = lax.broadcasted_iota(jnp.int32, (rows, rows), 1)
    near = col <= row
    near_b = near.astype(F32).astype(BF16)
    far_b = 1.0 - near_b

    def merge(x):
        first = jnp.where(near, x[:, :rows], x[:, rows:2 * rows])
        return jnp.concatenate([first, x[:, 2 * rows:]], axis=1) if nb > 1 else first

    def split(x):
        first = x[:, :rows]
        parts = [first * near_b, first * far_b]
        if nb > 1:
            parts.append(x[:, rows:])
        return jnp.concatenate(parts, axis=1)

    def copies(n):
        cols = pl.ds(pl.multiple_of(n * group, group), group)
        return (
            pltpu.make_async_copy(out_ref.at[:, cols], out_hbm.at[:, cols], sems.at[0, n]),
            pltpu.make_async_copy(gq_ref.at[:, cols], gq_hbm.at[:, cols], sems.at[1, n]),
        )

    def step(n, carry):
        k_cols = pl.ds(pl.multiple_of(n * hd, hd), hd)
        v_cols = pl.ds(pl.multiple_of(width + n * hd, hd), hd)
        k_clip = clip_ref[0, pl.ds(n, 1), :]
        v_clip = clip_ref[1, pl.ds(n, 1), :]
        ks, vs = [quant_ref[:, k_cols]], [quant_ref[:, v_cols]]
        kd, vd = [dclip_ref[:, k_cols]], [dclip_ref[:, v_cols]]
        for d in [nb] + list(range(1, nb)):
            q, _, dc = quant_parts(far_k[d - 1][:, k_cols].astype(F32), k_clip)
            ks.append(q.astype(BF16))
            kd.append(dc)
            q, _, dc = quant_parts(far_v[d - 1][:, k_cols].astype(F32), v_clip)
            vs.append(q.astype(BF16))
            vd.append(dc)
        k2 = jnp.concatenate(ks, axis=0)
        v2 = jnp.concatenate(vs, axis=0)

        def head_cols(h):
            return pl.ds(pl.multiple_of(n * group + h * hd, hd), hd)

        qs = jnp.concatenate([q_ref[:, head_cols(h)] for h in range(heads)], axis=0)
        gs = jnp.concatenate([g_ref[:, head_cols(h)] for h in range(heads)], axis=0)
        s_all = lax.dot_general(qs, k2, across, preferred_element_type=F32)
        d_all = lax.dot_general(gs, v2, across, preferred_element_type=F32)
        bias = bias_ref[...]
        ps, ds = [], []
        for h in range(heads):
            at = slice(h * rows, (h + 1) * rows)
            s = merge(s_all[at]) * (scale * log2e) + bias
            dp = merge(d_all[at])
            w = jnp.exp2(s - jnp.max(s, axis=1, keepdims=True))
            inv = 1.0 / jnp.sum(w, axis=1, keepdims=True)
            p = w * inv
            delta = jnp.sum(p * dp, axis=1, keepdims=True)
            p2 = split(p.astype(BF16))
            ds2 = split((p * ((dp - delta) * scale)).astype(BF16))
            out_ref[:, head_cols(h)] = jnp.dot(p2, v2, preferred_element_type=F32).astype(BF16)
            gq_ref[:, head_cols(h)] = jnp.dot(ds2, k2, preferred_element_type=F32).astype(BF16)
            ps.append(p2)
            ds.append(ds2)
        for copy in copies(n):
            copy.start()
        k_grad = lax.dot_general(qs, jnp.concatenate(ds, axis=0), down, preferred_element_type=F32).T
        v_grad = lax.dot_general(gs, jnp.concatenate(ps, axis=0), down, preferred_element_type=F32).T
        grad_ref[:, k_cols] = k_grad[:rows]
        grad_ref[:, v_cols] = v_grad[:rows]
        far_ref[:, k_cols] = k_grad[rows:].astype(BF16)
        far_ref[:, v_cols] = v_grad[rows:].astype(BF16)
        scale_ref[pl.ds(n, 1), :] = jnp.sum(k_grad * jnp.concatenate(kd, axis=0), axis=0, keepdims=True)
        scale_ref[pl.ds(kv_heads + n, 1), :] = jnp.sum(
            v_grad * jnp.concatenate(vd, axis=0), axis=0, keepdims=True
        )
        return carry

    lax.fori_loop(0, kv_heads, step, 0)
    part = scale_ref[...]

    def spread(i, carry):
        spread_ref[i] = part
        return carry

    lax.fori_loop(0, spread_ref.shape[0], spread, 0)
    for n in range(kv_heads):
        for copy in copies(n):
            copy.wait()


def finish_kernel(nb, grad_ref, slope_ref, *rest):
    backs, (gk_ref, gv_ref) = rest[:nb], rest[nb:]
    width = gk_ref.shape[1]
    for side, out in ((0, gk_ref), (1, gv_ref)):
        at = slice(side * width, (side + 1) * width)
        total = grad_ref[:, at]
        for back in backs:
            total = total + back[:, at].astype(F32)
        out[...] = (total * slope_ref[:, at]).astype(BF16)


def on_device(sizes, queries, keys, values, grad_out, quant_scale, doc_lengths):
    dp_count, seq_count = sizes
    count = dp_count * seq_count
    nb = max(1, seq_count // 2)
    rows, width = keys.shape
    kv_heads, hd = quant_scale.shape[1], quant_scale.shape[2]
    vmem = pl.BlockSpec(memory_space=pltpu.VMEM)
    hbm = pl.BlockSpec(memory_space=pltpu.HBM)
    params = pltpu.CompilerParams(vmem_limit_bytes=40 * 1024 * 1024)
    shape = jax.ShapeDtypeStruct

    def shift(array, d):
        return lax.ppermute(array, "seq", [(r, r + d) for r in range(seq_count - d)])

    def unshift(array, d):
        return lax.ppermute(array, "seq", [(r + d, r) for r in range(seq_count - d)])

    far_k = [shift(keys, d) for d in range(1, nb + 1)]
    far_v = [shift(values, d) for d in range(1, nb + 1)]

    q_near, g_near, quants, slopes, dclips, bias, clips = pl.pallas_call(
        functools.partial(prep_kernel, nb),
        out_shape=(
            shape(queries.shape, BF16),
            shape(queries.shape, BF16),
            shape((rows, 2 * width), BF16),
            shape((rows, 2 * width), F32),
            shape((rows, 2 * width), F32),
            shape((rows, nb * rows), F32),
            shape(quant_scale.shape, F32),
        ),
        in_specs=[hbm] * 6,
        out_specs=(vmem,) * 7,
        scratch_shapes=[
            pltpu.VMEM(keys.shape, BF16),
            pltpu.VMEM(values.shape, BF16),
            pltpu.SMEM(doc_lengths.shape, jnp.int32),
            pltpu.SemaphoreType.DMA((6,)),
        ],
        compiler_params=params,
        cost_estimate=pl.CostEstimate(
            flops=100 * rows * width, bytes_accessed=16 * rows * width, transcendentals=2 * rows * width
        ),
        name="prep",
    )(*[pltpu.with_memory_space_constraint(x, pltpu.HBM) for x in (queries, grad_out, keys, values, quant_scale, doc_lengths)])

    attn_out, grad_queries, grads, far_grads, spread = pl.pallas_call(
        functools.partial(attend_kernel, nb),
        out_shape=(
            shape(queries.shape, BF16),
            shape(queries.shape, BF16),
            shape((rows, 2 * width), F32),
            shape((nb * rows, 2 * width), BF16),
            shape((count, 2 * kv_heads, hd), F32),
        ),
        in_specs=[vmem] * (6 + 2 * nb),
        out_specs=(hbm, hbm, vmem, vmem, vmem),
        scratch_shapes=[
            pltpu.VMEM(queries.shape, BF16),
            pltpu.VMEM(queries.shape, BF16),
            pltpu.VMEM((2 * kv_heads, hd), F32),
            pltpu.SemaphoreType.DMA((2, kv_heads)),
        ],
        compiler_params=params,
        cost_estimate=pl.CostEstimate(
            flops=12 * rows * (nb + 1) * rows * queries.shape[1],
            bytes_accessed=8 * rows * queries.shape[1],
            transcendentals=rows * rows * nb * queries.shape[1] // hd,
        ),
        name="attend",
    )(q_near, g_near, quants, dclips, bias, clips, *far_k, *far_v)

    order = [nb] + list(range(1, nb))
    backs = []
    for d in range(1, nb + 1):
        at = order.index(d) * rows
        backs.append(unshift(lax.slice_in_dim(far_grads, at, at + rows, axis=0), d))
    gathered = lax.all_to_all(spread, ("dp", "seq"), split_axis=0, concat_axis=0, tiled=True)
    grad_scale = jnp.sum(gathered, axis=0).reshape(quant_scale.shape)

    grad_keys, grad_values = pl.pallas_call(
        functools.partial(finish_kernel, nb),
        out_shape=(shape((rows, width), BF16), shape((rows, width), BF16)),
        in_specs=[vmem] * (2 + nb),
        out_specs=(vmem, vmem),
        compiler_params=params,
        cost_estimate=pl.CostEstimate(
            flops=6 * rows * width, bytes_accessed=20 * rows * width, transcendentals=0
        ),
        name="finish",
    )(grads, slopes, *backs)
    return (attn_out, grad_queries, grad_keys, grad_values, grad_scale)


def solution(mesh):
    rows = P(("dp", "seq"), None)
    return jax.shard_map(
        functools.partial(on_device, (mesh.shape["dp"], mesh.shape["seq"])),
        mesh=mesh,
        in_specs=(rows, rows, rows, rows, P(), P("dp", None)),
        out_specs=(rows, rows, rows, rows, P()),
        check_vma=False,
    )
```

```python
import functools
import math

import jax
import jax.numpy as jnp
from jax import lax
from jax.experimental import pallas as pl
from jax.experimental.pallas import tpu as pltpu
from jax.sharding import PartitionSpec as P

F32 = jnp.float32
BF16 = jnp.bfloat16
LEVELS = 127.0
NEG = -1e30


def sin_cos_half(u):
    r = (u - jnp.round(u)) * math.pi
    z = r * r
    s = z * (1.0 / 6227020800.0) - 1.0 / 39916800.0
    for c in (1.0 / 362880.0, -1.0 / 5040.0, 1.0 / 120.0, -1.0 / 6.0, 1.0):
        s = s * z + c
    s = s * r
    k = z * (1.0 / 479001600.0) - 1.0 / 3628800.0
    for c in (1.0 / 40320.0, -1.0 / 720.0, 1.0 / 24.0, -0.5, 1.0):
        k = k * z + c
    return s, k


def quant_parts(x, clip):
    inv = 1.0 / clip
    ratio = x * inv
    t = jnp.tanh(ratio)
    u = LEVELS * t
    s, k = sin_cos_half(u)
    level = u - s * k * (1.0 / math.pi)
    unit = level * (1.0 / LEVELS)
    slope = (2.0 * s * s) * (1.0 - t * t)
    return clip * unit, slope, unit - slope * ratio


def prep_kernel(nb, q_hbm, g_hbm, key_hbm, value_hbm, clip_hbm, len_hbm, q_ref, g_ref, quant_ref, slope_ref,
                dclip_ref, bias_ref, clip_out, key_ref, value_ref, len_ref, sems):
    small = [
        pltpu.make_async_copy(src, dst, sems.at[i])
        for i, (src, dst) in enumerate(
            ((len_hbm, len_ref), (clip_hbm, clip_out), (key_hbm, key_ref), (value_hbm, value_ref))
        )
    ]
    large = [
        pltpu.make_async_copy(q_hbm, q_ref, sems.at[4]),
        pltpu.make_async_copy(g_hbm, g_ref, sems.at[5]),
    ]
    for copy in small + large:
        copy.start()
    rows = key_ref.shape[0]
    kv_heads, hd = clip_out.shape[1], clip_out.shape[2]
    base = lax.axis_index("seq") * rows
    for copy in small:
        copy.wait()
    for side, src in ((0, key_ref), (1, value_ref)):
        for n in range(kv_heads):
            x = src[:, n * hd:(n + 1) * hd].astype(F32)
            q, slope, dclip = quant_parts(x, clip_out[side, n:n + 1, :])
            at = slice((side * kv_heads + n) * hd, (side * kv_heads + n + 1) * hd)
            quant_ref[:, at] = q.astype(BF16)
            slope_ref[:, at] = slope
            dclip_ref[:, at] = dclip
    row = lax.broadcasted_iota(jnp.int32, (rows, rows), 0)
    col = lax.broadcasted_iota(jnp.int32, (rows, rows), 1)
    start = jnp.zeros((rows, rows), jnp.int32)
    end = jnp.int32(0)
    for d in range(len_ref.shape[1]):
        end = end + len_ref[0, d]
        start = jnp.where(row + base >= end, end, start)
    for b in range(nb):
        if b == 0:
            pos = jnp.where(col <= row, col, col - nb * rows)
        else:
            pos = col - b * rows
        bias_ref[:, b * rows:(b + 1) * rows] = jnp.where(pos + base >= start, 0.0, NEG)
    for copy in large:
        copy.wait()


def attend_kernel(nb, q_ref, g_ref, quant_ref, dclip_ref, bias_ref, clip_ref, *rest):
    far_k, far_v = rest[:nb], rest[nb:2 * nb]
    out_hbm, gq_hbm, grad_ref, far_ref, spread_ref, out_ref, gq_ref, scale_ref, sems = rest[2 * nb:]
    kv_heads, hd = clip_ref.shape[1], clip_ref.shape[2]
    rows, group = q_ref.shape[0], q_ref.shape[1] // kv_heads
    heads = group // hd
    width = kv_heads * hd
    scale = hd ** -0.5
    log2e = math.log2(math.e)
    across = (((1,), (1,)), ((), ()))
    down = (((0,), (0,)), ((), ()))
    row = lax.broadcasted_iota(jnp.int32, (rows, rows), 0)
    col = lax.broadcasted_iota(jnp.int32, (rows, rows), 1)
    near = col <= row
    near_b = near.astype(F32).astype(BF16)
    far_b = 1.0 - near_b

    def merge(x):
        first = jnp.where(near, x[:, :rows], x[:, rows:2 * rows])
        return jnp.concatenate([first, x[:, 2 * rows:]], axis=1) if nb > 1 else first

    def split(x):
        first = x[:, :rows]
        parts = [first * near_b, first * far_b]
        if nb > 1:
            parts.append(x[:, rows:])
        return jnp.concatenate(parts, axis=1)

    def copies(n):
        cols = pl.ds(pl.multiple_of(n * group, group), group)
        return (
            pltpu.make_async_copy(out_ref.at[:, cols], out_hbm.at[:, cols], sems.at[0, n]),
            pltpu.make_async_copy(gq_ref.at[:, cols], gq_hbm.at[:, cols], sems.at[1, n]),
        )

    def step(n, carry):
        k_cols = pl.ds(pl.multiple_of(n * hd, hd), hd)
        v_cols = pl.ds(pl.multiple_of(width + n * hd, hd), hd)
        k_clip = clip_ref[0, pl.ds(n, 1), :]
        v_clip = clip_ref[1, pl.ds(n, 1), :]
        ks, vs = [quant_ref[:, k_cols]], [quant_ref[:, v_cols]]
        kd, vd = [dclip_ref[:, k_cols]], [dclip_ref[:, v_cols]]
        for d in [nb] + list(range(1, nb)):
            q, _, dc = quant_parts(far_k[d - 1][:, k_cols].astype(F32), k_clip)
            ks.append(q.astype(BF16))
            kd.append(dc)
            q, _, dc = quant_parts(far_v[d - 1][:, k_cols].astype(F32), v_clip)
            vs.append(q.astype(BF16))
            vd.append(dc)
        k2 = jnp.concatenate(ks, axis=0)
        v2 = jnp.concatenate(vs, axis=0)

        def head_cols(h):
            return pl.ds(pl.multiple_of(n * group + h * hd, hd), hd)

        qs = jnp.concatenate([q_ref[:, head_cols(h)] for h in range(heads)], axis=0)
        gs = jnp.concatenate([g_ref[:, head_cols(h)] for h in range(heads)], axis=0)
        s_all = lax.dot_general(qs, k2, across, preferred_element_type=F32)
        d_all = lax.dot_general(gs, v2, across, preferred_element_type=F32)
        bias = bias_ref[...]
        ps, ds = [], []
        for h in range(heads):
            at = slice(h * rows, (h + 1) * rows)
            s = merge(s_all[at]) * (scale * log2e) + bias
            dp = merge(d_all[at])
            w = jnp.exp2(s - jnp.max(s, axis=1, keepdims=True))
            inv = 1.0 / jnp.sum(w, axis=1, keepdims=True)
            p = w * inv
            delta = jnp.sum(p * dp, axis=1, keepdims=True)
            p2 = split(p.astype(BF16))
            ds2 = split((p * ((dp - delta) * scale)).astype(BF16))
            out_ref[:, head_cols(h)] = jnp.dot(p2, v2, preferred_element_type=F32).astype(BF16)
            gq_ref[:, head_cols(h)] = jnp.dot(ds2, k2, preferred_element_type=F32).astype(BF16)
            ps.append(p2)
            ds.append(ds2)
        for copy in copies(n):
            copy.start()
        k_grad = lax.dot_general(qs, jnp.concatenate(ds, axis=0), down, preferred_element_type=F32).T
        v_grad = lax.dot_general(gs, jnp.concatenate(ps, axis=0), down, preferred_element_type=F32).T
        grad_ref[:, k_cols] = k_grad[:rows]
        grad_ref[:, v_cols] = v_grad[:rows]
        far_ref[:, k_cols] = k_grad[rows:].astype(BF16)
        far_ref[:, v_cols] = v_grad[rows:].astype(BF16)
        scale_ref[pl.ds(n, 1), :] = jnp.sum(k_grad * jnp.concatenate(kd, axis=0), axis=0, keepdims=True)
        scale_ref[pl.ds(kv_heads + n, 1), :] = jnp.sum(
            v_grad * jnp.concatenate(vd, axis=0), axis=0, keepdims=True
        )
        return carry

    lax.fori_loop(0, kv_heads, step, 0)
    part = scale_ref[...]

    def spread(i, carry):
        spread_ref[i] = part
        return carry

    lax.fori_loop(0, spread_ref.shape[0], spread, 0)
    for n in range(kv_heads):
        for copy in copies(n):
            copy.wait()


def finish_kernel(nb, grad_ref, slope_ref, *rest):
    backs, (gk_ref, gv_ref) = rest[:nb], rest[nb:]
    width = gk_ref.shape[1]
    for side, out in ((0, gk_ref), (1, gv_ref)):
        at = slice(side * width, (side + 1) * width)
        total = grad_ref[:, at]
        for back in backs:
            total = total + back[:, at].astype(F32)
        out[...] = (total * slope_ref[:, at]).astype(BF16)


def total_kernel(parts_ref, after_ref, out_ref):
    del after_ref
    out_ref[...] = jnp.sum(parts_ref[...], axis=0)


def on_device(sizes, queries, keys, values, grad_out, quant_scale, doc_lengths):
    dp_count, seq_count = sizes
    count = dp_count * seq_count
    nb = max(1, seq_count // 2)
    rows, width = keys.shape
    kv_heads, hd = quant_scale.shape[1], quant_scale.shape[2]
    vmem = pl.BlockSpec(memory_space=pltpu.VMEM)
    hbm = pl.BlockSpec(memory_space=pltpu.HBM)
    params = pltpu.CompilerParams(vmem_limit_bytes=40 * 1024 * 1024)
    shape = jax.ShapeDtypeStruct

    def shift(array, d):
        return lax.ppermute(array, "seq", [(r, r + d) for r in range(seq_count - d)])

    def unshift(array, d):
        return lax.ppermute(array, "seq", [(r + d, r) for r in range(seq_count - d)])

    far_k = [shift(keys, d) for d in range(1, nb + 1)]
    far_v = [shift(values, d) for d in range(1, nb + 1)]

    q_near, g_near, quants, slopes, dclips, bias, clips = pl.pallas_call(
        functools.partial(prep_kernel, nb),
        out_shape=(
            shape(queries.shape, BF16),
            shape(queries.shape, BF16),
            shape((rows, 2 * width), BF16),
            shape((rows, 2 * width), F32),
            shape((rows, 2 * width), F32),
            shape((rows, nb * rows), F32),
            shape(quant_scale.shape, F32),
        ),
        in_specs=[hbm] * 6,
        out_specs=(vmem,) * 7,
        scratch_shapes=[
            pltpu.VMEM(keys.shape, BF16),
            pltpu.VMEM(values.shape, BF16),
            pltpu.SMEM(doc_lengths.shape, jnp.int32),
            pltpu.SemaphoreType.DMA((6,)),
        ],
        compiler_params=params,
        cost_estimate=pl.CostEstimate(
            flops=100 * rows * width, bytes_accessed=16 * rows * width, transcendentals=2 * rows * width
        ),
        name="prep",
    )(*[pltpu.with_memory_space_constraint(x, pltpu.HBM) for x in (queries, grad_out, keys, values, quant_scale, doc_lengths)])

    attn_out, grad_queries, grads, far_grads, spread = pl.pallas_call(
        functools.partial(attend_kernel, nb),
        out_shape=(
            shape(queries.shape, BF16),
            shape(queries.shape, BF16),
            shape((rows, 2 * width), F32),
            shape((nb * rows, 2 * width), BF16),
            shape((count, 2 * kv_heads, hd), F32),
        ),
        in_specs=[vmem] * (6 + 2 * nb),
        out_specs=(hbm, hbm, vmem, vmem, vmem),
        scratch_shapes=[
            pltpu.VMEM(queries.shape, BF16),
            pltpu.VMEM(queries.shape, BF16),
            pltpu.VMEM((2 * kv_heads, hd), F32),
            pltpu.SemaphoreType.DMA((2, kv_heads)),
        ],
        compiler_params=params,
        cost_estimate=pl.CostEstimate(
            flops=12 * rows * (nb + 1) * rows * queries.shape[1],
            bytes_accessed=8 * rows * queries.shape[1],
            transcendentals=rows * rows * nb * queries.shape[1] // hd,
        ),
        name="attend",
    )(q_near, g_near, quants, dclips, bias, clips, *far_k, *far_v)

    order = [nb] + list(range(1, nb))
    backs = []
    for d in range(1, nb + 1):
        at = order.index(d) * rows
        backs.append(unshift(lax.slice_in_dim(far_grads, at, at + rows, axis=0), d))
    gathered = lax.all_to_all(spread, ("dp", "seq"), split_axis=0, concat_axis=0, tiled=True)
    grad_keys, grad_values = pl.pallas_call(
        functools.partial(finish_kernel, nb),
        out_shape=(shape((rows, width), BF16), shape((rows, width), BF16)),
        in_specs=[vmem] * (2 + nb),
        out_specs=(vmem, vmem),
        compiler_params=params,
        cost_estimate=pl.CostEstimate(
            flops=6 * rows * width, bytes_accessed=20 * rows * width, transcendentals=0
        ),
        name="finish",
    )(grads, slopes, *backs)
    grad_scale = pl.pallas_call(
        total_kernel,
        out_shape=shape((2 * kv_heads, hd), F32),
        in_specs=[vmem, hbm],
        out_specs=vmem,
        compiler_params=params,
        name="total",
    )(gathered, pltpu.with_memory_space_constraint(grad_keys, pltpu.HBM))
    return (attn_out, grad_queries, grad_keys, grad_values, grad_scale.reshape(quant_scale.shape))


def solution(mesh):
    rows = P(("dp", "seq"), None)
    return jax.shard_map(
        functools.partial(on_device, (mesh.shape["dp"], mesh.shape["seq"])),
        mesh=mesh,
        in_specs=(rows, rows, rows, rows, P(), P("dp", None)),
        out_specs=(rows, rows, rows, rows, P()),
        check_vma=False,
    )
```

```python
import functools
import math

import jax
import jax.numpy as jnp
from jax import lax
from jax.experimental import pallas as pl
from jax.experimental.pallas import tpu as pltpu
from jax.sharding import PartitionSpec as P

F32 = jnp.float32
BF16 = jnp.bfloat16
LEVELS = 127.0
NEG = -1e30


def sin_cos_half(u):
    r = (u - jnp.round(u)) * math.pi
    z = r * r
    s = z * (1.0 / 6227020800.0) - 1.0 / 39916800.0
    for c in (1.0 / 362880.0, -1.0 / 5040.0, 1.0 / 120.0, -1.0 / 6.0, 1.0):
        s = s * z + c
    s = s * r
    k = z * (1.0 / 479001600.0) - 1.0 / 3628800.0
    for c in (1.0 / 40320.0, -1.0 / 720.0, 1.0 / 24.0, -0.5, 1.0):
        k = k * z + c
    return s, k


def quant_parts(x, clip):
    inv = 1.0 / clip
    ratio = x * inv
    t = jnp.tanh(ratio)
    u = LEVELS * t
    s, k = sin_cos_half(u)
    level = u - s * k * (1.0 / math.pi)
    unit = level * (1.0 / LEVELS)
    slope = (2.0 * s * s) * (1.0 - t * t)
    return clip * unit, slope, unit - slope * ratio


def prep_kernel(nb, q_hbm, g_hbm, key_hbm, value_hbm, clip_hbm, len_hbm, q_ref, g_ref, quant_ref, slope_ref,
                dclip_ref, bias_ref, clip_out, key_ref, value_ref, len_ref, sems):
    small = [
        pltpu.make_async_copy(src, dst, sems.at[i])
        for i, (src, dst) in enumerate(
            ((len_hbm, len_ref), (clip_hbm, clip_out), (key_hbm, key_ref), (value_hbm, value_ref))
        )
    ]
    large = [
        pltpu.make_async_copy(q_hbm, q_ref, sems.at[4]),
        pltpu.make_async_copy(g_hbm, g_ref, sems.at[5]),
    ]
    for copy in small + large:
        copy.start()
    rows = key_ref.shape[0]
    kv_heads, hd = clip_out.shape[1], clip_out.shape[2]
    base = lax.axis_index("seq") * rows
    for copy in small:
        copy.wait()
    for side, src in ((0, key_ref), (1, value_ref)):
        for n in range(kv_heads):
            x = src[:, n * hd:(n + 1) * hd].astype(F32)
            q, slope, dclip = quant_parts(x, clip_out[side, n:n + 1, :])
            at = slice((side * kv_heads + n) * hd, (side * kv_heads + n + 1) * hd)
            quant_ref[:, at] = q.astype(BF16)
            slope_ref[:, at] = slope
            dclip_ref[:, at] = dclip
    row = lax.broadcasted_iota(jnp.int32, (rows, rows), 0)
    col = lax.broadcasted_iota(jnp.int32, (rows, rows), 1)
    start = jnp.zeros((rows, rows), jnp.int32)
    end = jnp.int32(0)
    for d in range(len_ref.shape[1]):
        end = end + len_ref[0, d]
        start = jnp.where(row + base >= end, end, start)
    for b in range(nb):
        if b == 0:
            pos = jnp.where(col <= row, col, col - nb * rows)
        else:
            pos = col - b * rows
        bias_ref[:, b * rows:(b + 1) * rows] = jnp.where(pos + base >= start, 0.0, NEG)
    for copy in large:
        copy.wait()


def attend_kernel(nb, q_ref, g_ref, quant_ref, dclip_ref, bias_ref, clip_ref, *rest):
    far_k, far_v = rest[:nb], rest[nb:2 * nb]
    out_hbm, gq_hbm, grad_ref, far_ref, scale_ref, out_ref, gq_ref, sems = rest[2 * nb:]
    kv_heads, hd = clip_ref.shape[1], clip_ref.shape[2]
    rows, group = q_ref.shape[0], q_ref.shape[1] // kv_heads
    heads = group // hd
    width = kv_heads * hd
    scale = hd ** -0.5
    log2e = math.log2(math.e)
    across = (((1,), (1,)), ((), ()))
    down = (((0,), (0,)), ((), ()))
    row = lax.broadcasted_iota(jnp.int32, (rows, rows), 0)
    col = lax.broadcasted_iota(jnp.int32, (rows, rows), 1)
    near = col <= row
    near_b = near.astype(F32).astype(BF16)
    far_b = 1.0 - near_b

    def merge(x):
        first = jnp.where(near, x[:, :rows], x[:, rows:2 * rows])
        return jnp.concatenate([first, x[:, 2 * rows:]], axis=1) if nb > 1 else first

    def split(x):
        first = x[:, :rows]
        parts = [first * near_b, first * far_b]
        if nb > 1:
            parts.append(x[:, rows:])
        return jnp.concatenate(parts, axis=1)

    def copies(n):
        cols = pl.ds(pl.multiple_of(n * group, group), group)
        return (
            pltpu.make_async_copy(out_ref.at[:, cols], out_hbm.at[:, cols], sems.at[0, n]),
            pltpu.make_async_copy(gq_ref.at[:, cols], gq_hbm.at[:, cols], sems.at[1, n]),
        )

    def step(n, carry):
        k_cols = pl.ds(pl.multiple_of(n * hd, hd), hd)
        v_cols = pl.ds(pl.multiple_of(width + n * hd, hd), hd)
        k_clip = clip_ref[0, pl.ds(n, 1), :]
        v_clip = clip_ref[1, pl.ds(n, 1), :]
        ks, vs = [quant_ref[:, k_cols]], [quant_ref[:, v_cols]]
        kd, vd = [dclip_ref[:, k_cols]], [dclip_ref[:, v_cols]]
        for d in [nb] + list(range(1, nb)):
            q, _, dc = quant_parts(far_k[d - 1][:, k_cols].astype(F32), k_clip)
            ks.append(q.astype(BF16))
            kd.append(dc)
            q, _, dc = quant_parts(far_v[d - 1][:, k_cols].astype(F32), v_clip)
            vs.append(q.astype(BF16))
            vd.append(dc)
        k2 = jnp.concatenate(ks, axis=0)
        v2 = jnp.concatenate(vs, axis=0)

        def head_cols(h):
            return pl.ds(pl.multiple_of(n * group + h * hd, hd), hd)

        qs = jnp.concatenate([q_ref[:, head_cols(h)] for h in range(heads)], axis=0)
        gs = jnp.concatenate([g_ref[:, head_cols(h)] for h in range(heads)], axis=0)
        s_all = lax.dot_general(qs, k2, across, preferred_element_type=F32)
        d_all = lax.dot_general(gs, v2, across, preferred_element_type=F32)
        bias = bias_ref[...]
        ps, ds = [], []
        for h in range(heads):
            at = slice(h * rows, (h + 1) * rows)
            s = merge(s_all[at]) * (scale * log2e) + bias
            dp = merge(d_all[at])
            w = jnp.exp2(s - jnp.max(s, axis=1, keepdims=True))
            inv = 1.0 / jnp.sum(w, axis=1, keepdims=True)
            p = w * inv
            delta = jnp.sum(p * dp, axis=1, keepdims=True)
            p2 = split(p.astype(BF16))
            ds2 = split((p * ((dp - delta) * scale)).astype(BF16))
            out_ref[:, head_cols(h)] = jnp.dot(p2, v2, preferred_element_type=F32).astype(BF16)
            gq_ref[:, head_cols(h)] = jnp.dot(ds2, k2, preferred_element_type=F32).astype(BF16)
            ps.append(p2)
            ds.append(ds2)
        for copy in copies(n):
            copy.start()
        k_grad = lax.dot_general(qs, jnp.concatenate(ds, axis=0), down, preferred_element_type=F32).T
        v_grad = lax.dot_general(gs, jnp.concatenate(ps, axis=0), down, preferred_element_type=F32).T
        grad_ref[:, k_cols] = k_grad[:rows]
        grad_ref[:, v_cols] = v_grad[:rows]
        far_ref[:, k_cols] = k_grad[rows:].astype(BF16)
        far_ref[:, v_cols] = v_grad[rows:].astype(BF16)
        scale_ref[pl.ds(n, 1), :] = jnp.sum(k_grad * jnp.concatenate(kd, axis=0), axis=0, keepdims=True)
        scale_ref[pl.ds(kv_heads + n, 1), :] = jnp.sum(
            v_grad * jnp.concatenate(vd, axis=0), axis=0, keepdims=True
        )
        return carry

    lax.fori_loop(0, kv_heads, step, 0)
    for n in range(kv_heads):
        for copy in copies(n):
            copy.wait()


def finish_kernel(nb, part_ref, other_ref, grad_ref, slope_ref, *rest):
    backs, (gk_ref, gv_ref, gs_ref) = rest[:nb], rest[nb:]
    gs_ref[...] = part_ref[...] + other_ref[...]
    width = gk_ref.shape[1]
    for side, out in ((0, gk_ref), (1, gv_ref)):
        at = slice(side * width, (side + 1) * width)
        total = grad_ref[:, at]
        for back in backs:
            total = total + back[:, at].astype(F32)
        out[...] = (total * slope_ref[:, at]).astype(BF16)


def all_sum(part, dp_count, seq_count):
    count = dp_count * seq_count
    strides = [seq_count << b for b in range(dp_count.bit_length() - 1)]
    strides += [1 << b for b in range(seq_count.bit_length() - 1)]
    for stride in strides:
        other = lax.ppermute(part, ("dp", "seq"), [(i, i ^ stride) for i in range(count)])
        if stride == strides[-1]:
            return part, other
        part = part + other


def on_device(sizes, queries, keys, values, grad_out, quant_scale, doc_lengths):
    dp_count, seq_count = sizes
    nb = max(1, seq_count // 2)
    rows, width = keys.shape
    kv_heads, hd = quant_scale.shape[1], quant_scale.shape[2]
    vmem = pl.BlockSpec(memory_space=pltpu.VMEM)
    hbm = pl.BlockSpec(memory_space=pltpu.HBM)
    params = pltpu.CompilerParams(vmem_limit_bytes=40 * 1024 * 1024)
    shape = jax.ShapeDtypeStruct

    def shift(array, d):
        return lax.ppermute(array, "seq", [(r, r + d) for r in range(seq_count - d)])

    def unshift(array, d):
        return lax.ppermute(array, "seq", [(r + d, r) for r in range(seq_count - d)])

    far_k = [shift(keys, d) for d in range(1, nb + 1)]
    far_v = [shift(values, d) for d in range(1, nb + 1)]

    q_near, g_near, quants, slopes, dclips, bias, clips = pl.pallas_call(
        functools.partial(prep_kernel, nb),
        out_shape=(
            shape(queries.shape, BF16),
            shape(queries.shape, BF16),
            shape((rows, 2 * width), BF16),
            shape((rows, 2 * width), F32),
            shape((rows, 2 * width), F32),
            shape((rows, nb * rows), F32),
            shape(quant_scale.shape, F32),
        ),
        in_specs=[hbm] * 6,
        out_specs=(vmem,) * 7,
        scratch_shapes=[
            pltpu.VMEM(keys.shape, BF16),
            pltpu.VMEM(values.shape, BF16),
            pltpu.SMEM(doc_lengths.shape, jnp.int32),
            pltpu.SemaphoreType.DMA((6,)),
        ],
        compiler_params=params,
        cost_estimate=pl.CostEstimate(
            flops=100 * rows * width, bytes_accessed=16 * rows * width, transcendentals=2 * rows * width
        ),
        name="prep",
    )(*[pltpu.with_memory_space_constraint(x, pltpu.HBM) for x in (queries, grad_out, keys, values, quant_scale, doc_lengths)])

    attn_out, grad_queries, grads, far_grads, scale_part = pl.pallas_call(
        functools.partial(attend_kernel, nb),
        out_shape=(
            shape(queries.shape, BF16),
            shape(queries.shape, BF16),
            shape((rows, 2 * width), F32),
            shape((nb * rows, 2 * width), BF16),
            shape((2 * kv_heads, hd), F32),
        ),
        in_specs=[vmem] * (6 + 2 * nb),
        out_specs=(hbm, hbm, vmem, vmem, vmem),
        scratch_shapes=[
            pltpu.VMEM(queries.shape, BF16),
            pltpu.VMEM(queries.shape, BF16),
            pltpu.SemaphoreType.DMA((2, kv_heads)),
        ],
        compiler_params=params,
        cost_estimate=pl.CostEstimate(
            flops=12 * rows * (nb + 1) * rows * queries.shape[1],
            bytes_accessed=8 * rows * queries.shape[1],
            transcendentals=rows * rows * nb * queries.shape[1] // hd,
        ),
        name="attend",
    )(q_near, g_near, quants, dclips, bias, clips, *far_k, *far_v)

    order = [nb] + list(range(1, nb))
    backs = []
    for d in range(1, nb + 1):
        at = order.index(d) * rows
        backs.append(unshift(lax.slice_in_dim(far_grads, at, at + rows, axis=0), d))
    part, other = all_sum(scale_part, dp_count, seq_count)

    grad_keys, grad_values, grad_scale = pl.pallas_call(
        functools.partial(finish_kernel, nb),
        out_shape=(shape((rows, width), BF16), shape((rows, width), BF16), shape(part.shape, F32)),
        in_specs=[vmem] * (4 + nb),
        out_specs=(vmem, vmem, vmem),
        compiler_params=params,
        cost_estimate=pl.CostEstimate(
            flops=6 * rows * width, bytes_accessed=20 * rows * width, transcendentals=0
        ),
        name="finish",
    )(part, other, grads, slopes, *backs)
    return (attn_out, grad_queries, grad_keys, grad_values, grad_scale.reshape(quant_scale.shape))


def solution(mesh):
    rows = P(("dp", "seq"), None)
    return jax.shard_map(
        functools.partial(on_device, (mesh.shape["dp"], mesh.shape["seq"])),
        mesh=mesh,
        in_specs=(rows, rows, rows, rows, P(), P("dp", None)),
        out_specs=(rows, rows, rows, rows, P()),
        check_vma=False,
    )
```

```python
import functools
import math

import jax
import jax.numpy as jnp
from jax import lax
from jax.experimental import pallas as pl
from jax.experimental.pallas import tpu as pltpu
from jax.sharding import PartitionSpec as P

F32 = jnp.float32
BF16 = jnp.bfloat16
LEVELS = 127.0
NEG = -1e30


def sin_cos_half(u):
    r = (u - jnp.round(u)) * math.pi
    z = r * r
    s = z * (1.0 / 6227020800.0) - 1.0 / 39916800.0
    for c in (1.0 / 362880.0, -1.0 / 5040.0, 1.0 / 120.0, -1.0 / 6.0, 1.0):
        s = s * z + c
    s = s * r
    k = z * (1.0 / 479001600.0) - 1.0 / 3628800.0
    for c in (1.0 / 40320.0, -1.0 / 720.0, 1.0 / 24.0, -0.5, 1.0):
        k = k * z + c
    return s, k


def quant_parts(x, clip):
    inv = 1.0 / clip
    ratio = x * inv
    t = jnp.tanh(ratio)
    u = LEVELS * t
    s, k = sin_cos_half(u)
    level = u - s * k * (1.0 / math.pi)
    unit = level * (1.0 / LEVELS)
    slope = (2.0 * s * s) * (1.0 - t * t)
    return clip * unit, slope, unit - slope * ratio


def prep_kernel(nb, q_hbm, g_hbm, key_hbm, value_hbm, clip_hbm, len_hbm, q_ref, g_ref, quant_ref, slope_ref,
                dclip_ref, bias_ref, clip_out, key_ref, value_ref, len_ref, sems):
    small = [
        pltpu.make_async_copy(src, dst, sems.at[i])
        for i, (src, dst) in enumerate(
            ((len_hbm, len_ref), (clip_hbm, clip_out), (key_hbm, key_ref), (value_hbm, value_ref))
        )
    ]
    large = [
        pltpu.make_async_copy(q_hbm, q_ref, sems.at[4]),
        pltpu.make_async_copy(g_hbm, g_ref, sems.at[5]),
    ]
    for copy in small + large:
        copy.start()
    rows = key_ref.shape[0]
    kv_heads, hd = clip_out.shape[1], clip_out.shape[2]
    base = lax.axis_index("seq") * rows
    for copy in small:
        copy.wait()
    for side, src in ((0, key_ref), (1, value_ref)):
        for n in range(kv_heads):
            x = src[:, n * hd:(n + 1) * hd].astype(F32)
            q, slope, dclip = quant_parts(x, clip_out[side, n:n + 1, :])
            at = slice((side * kv_heads + n) * hd, (side * kv_heads + n + 1) * hd)
            quant_ref[:, at] = q.astype(BF16)
            slope_ref[:, at] = slope
            dclip_ref[:, at] = dclip
    row = lax.broadcasted_iota(jnp.int32, (rows, rows), 0)
    col = lax.broadcasted_iota(jnp.int32, (rows, rows), 1)
    start = jnp.zeros((rows, rows), jnp.int32)
    end = jnp.int32(0)
    for d in range(len_ref.shape[1]):
        end = end + len_ref[0, d]
        start = jnp.where(row + base >= end, end, start)
    for b in range(nb):
        if b == 0:
            pos = jnp.where(col <= row, col, col - nb * rows)
        else:
            pos = col - b * rows
        bias_ref[:, b * rows:(b + 1) * rows] = jnp.where(pos + base >= start, 0.0, NEG)
    for copy in large:
        copy.wait()


def attend_kernel(nb, q_ref, g_ref, quant_ref, dclip_ref, bias_ref, clip_ref, *rest):
    far_k, far_v = rest[:nb], rest[nb:2 * nb]
    out_hbm, gq_hbm, grad_ref, far_ref, scale_ref, out_ref, gq_ref, sems = rest[2 * nb:]
    kv_heads, hd = clip_ref.shape[1], clip_ref.shape[2]
    rows, group = q_ref.shape[0], q_ref.shape[1] // kv_heads
    heads = group // hd
    width = kv_heads * hd
    scale = hd ** -0.5
    log2e = math.log2(math.e)
    across = (((1,), (1,)), ((), ()))
    down = (((0,), (0,)), ((), ()))
    row = lax.broadcasted_iota(jnp.int32, (rows, rows), 0)
    col = lax.broadcasted_iota(jnp.int32, (rows, rows), 1)
    near = col <= row
    near_b = near.astype(F32).astype(BF16)
    far_b = 1.0 - near_b

    def merge(x):
        first = jnp.where(near, x[:, :rows], x[:, rows:2 * rows])
        return jnp.concatenate([first, x[:, 2 * rows:]], axis=1) if nb > 1 else first

    def split(x):
        first = x[:, :rows]
        parts = [first * near_b, first * far_b]
        if nb > 1:
            parts.append(x[:, rows:])
        return jnp.concatenate(parts, axis=1)

    def copies(n):
        cols = pl.ds(pl.multiple_of(n * group, group), group)
        return (
            pltpu.make_async_copy(out_ref.at[:, cols], out_hbm.at[:, cols], sems.at[0, n]),
            pltpu.make_async_copy(gq_ref.at[:, cols], gq_hbm.at[:, cols], sems.at[1, n]),
        )

    def step(n, carry):
        k_cols = pl.ds(pl.multiple_of(n * hd, hd), hd)
        v_cols = pl.ds(pl.multiple_of(width + n * hd, hd), hd)
        k_clip = clip_ref[0, pl.ds(n, 1), :]
        v_clip = clip_ref[1, pl.ds(n, 1), :]
        ks, vs = [quant_ref[:, k_cols]], [quant_ref[:, v_cols]]
        kd, vd = [dclip_ref[:, k_cols]], [dclip_ref[:, v_cols]]
        for d in [nb] + list(range(1, nb)):
            q, _, dc = quant_parts(far_k[d - 1][:, k_cols].astype(F32), k_clip)
            ks.append(q.astype(BF16))
            kd.append(dc)
            q, _, dc = quant_parts(far_v[d - 1][:, k_cols].astype(F32), v_clip)
            vs.append(q.astype(BF16))
            vd.append(dc)
        k2 = jnp.concatenate(ks, axis=0)
        v2 = jnp.concatenate(vs, axis=0)

        def head_cols(h):
            return pl.ds(pl.multiple_of(n * group + h * hd, hd), hd)

        qs = jnp.concatenate([q_ref[:, head_cols(h)] for h in range(heads)], axis=0)
        gs = jnp.concatenate([g_ref[:, head_cols(h)] for h in range(heads)], axis=0)
        s_all = lax.dot_general(qs, k2, across, preferred_element_type=F32)
        d_all = lax.dot_general(gs, v2, across, preferred_element_type=F32)
        bias = bias_ref[...]
        ps, ds = [], []
        for h in range(heads):
            at = slice(h * rows, (h + 1) * rows)
            s = merge(s_all[at]) * (scale * log2e) + bias
            dp = merge(d_all[at])
            w = jnp.exp2(s - jnp.max(s, axis=1, keepdims=True))
            inv = 1.0 / jnp.sum(w, axis=1, keepdims=True)
            p = w * inv
            delta = jnp.sum(p * dp, axis=1, keepdims=True)
            p2 = split(p.astype(BF16))
            ds2 = split((p * ((dp - delta) * scale)).astype(BF16))
            out_ref[:, head_cols(h)] = jnp.dot(p2, v2, preferred_element_type=F32).astype(BF16)
            gq_ref[:, head_cols(h)] = jnp.dot(ds2, k2, preferred_element_type=F32).astype(BF16)
            ps.append(p2)
            ds.append(ds2)
        for copy in copies(n):
            copy.start()
        k_grad = lax.dot_general(qs, jnp.concatenate(ds, axis=0), down, preferred_element_type=F32).T
        v_grad = lax.dot_general(gs, jnp.concatenate(ps, axis=0), down, preferred_element_type=F32).T
        grad_ref[:, k_cols] = k_grad[:rows]
        grad_ref[:, v_cols] = v_grad[:rows]
        far_ref[:, k_cols] = k_grad[rows:].astype(BF16)
        far_ref[:, v_cols] = v_grad[rows:].astype(BF16)
        scale_ref[pl.ds(n, 1), :] = jnp.sum(k_grad * jnp.concatenate(kd, axis=0), axis=0, keepdims=True)
        scale_ref[pl.ds(kv_heads + n, 1), :] = jnp.sum(
            v_grad * jnp.concatenate(vd, axis=0), axis=0, keepdims=True
        )
        return carry

    lax.fori_loop(0, kv_heads, step, 0)
    for n in range(kv_heads):
        for copy in copies(n):
            copy.wait()


def finish_kernel(nb, part_ref, other_ref, grad_ref, slope_ref, *rest):
    backs, (gk_ref, gv_ref, gs_ref) = rest[:nb], rest[nb:]
    gs_ref[...] = part_ref[...] + other_ref[...]
    width = gk_ref.shape[1]
    for side, out in ((0, gk_ref), (1, gv_ref)):
        at = slice(side * width, (side + 1) * width)
        total = grad_ref[:, at]
        for back in backs:
            total = total + back[:, at].astype(F32)
        out[...] = (total * slope_ref[:, at]).astype(BF16)


def all_sum(part, dp_count, seq_count):
    copies = jnp.broadcast_to(part[None], (dp_count,) + part.shape)
    part = jnp.sum(lax.all_to_all(copies, "dp", split_axis=0, concat_axis=0, tiled=True), axis=0)
    other = jnp.zeros_like(part)
    for b in range(seq_count.bit_length() - 1):
        part = part + other
        other = lax.ppermute(part, "seq", [(i, i ^ (1 << b)) for i in range(seq_count)])
    return part, other


def on_device(sizes, queries, keys, values, grad_out, quant_scale, doc_lengths):
    dp_count, seq_count = sizes
    nb = max(1, seq_count // 2)
    rows, width = keys.shape
    kv_heads, hd = quant_scale.shape[1], quant_scale.shape[2]
    vmem = pl.BlockSpec(memory_space=pltpu.VMEM)
    hbm = pl.BlockSpec(memory_space=pltpu.HBM)
    params = pltpu.CompilerParams(vmem_limit_bytes=40 * 1024 * 1024)
    shape = jax.ShapeDtypeStruct

    def shift(array, d):
        return lax.ppermute(array, "seq", [(r, r + d) for r in range(seq_count - d)])

    def unshift(array, d):
        return lax.ppermute(array, "seq", [(r + d, r) for r in range(seq_count - d)])

    far_k = [shift(keys, d) for d in range(1, nb + 1)]
    far_v = [shift(values, d) for d in range(1, nb + 1)]

    q_near, g_near, quants, slopes, dclips, bias, clips = pl.pallas_call(
        functools.partial(prep_kernel, nb),
        out_shape=(
            shape(queries.shape, BF16),
            shape(queries.shape, BF16),
            shape((rows, 2 * width), BF16),
            shape((rows, 2 * width), F32),
            shape((rows, 2 * width), F32),
            shape((rows, nb * rows), F32),
            shape(quant_scale.shape, F32),
        ),
        in_specs=[hbm] * 6,
        out_specs=(vmem,) * 7,
        scratch_shapes=[
            pltpu.VMEM(keys.shape, BF16),
            pltpu.VMEM(values.shape, BF16),
            pltpu.SMEM(doc_lengths.shape, jnp.int32),
            pltpu.SemaphoreType.DMA((6,)),
        ],
        compiler_params=params,
        cost_estimate=pl.CostEstimate(
            flops=100 * rows * width, bytes_accessed=16 * rows * width, transcendentals=2 * rows * width
        ),
        name="prep",
    )(*[pltpu.with_memory_space_constraint(x, pltpu.HBM) for x in (queries, grad_out, keys, values, quant_scale, doc_lengths)])

    attn_out, grad_queries, grads, far_grads, scale_part = pl.pallas_call(
        functools.partial(attend_kernel, nb),
        out_shape=(
            shape(queries.shape, BF16),
            shape(queries.shape, BF16),
            shape((rows, 2 * width), F32),
            shape((nb * rows, 2 * width), BF16),
            shape((2 * kv_heads, hd), F32),
        ),
        in_specs=[vmem] * (6 + 2 * nb),
        out_specs=(hbm, hbm, vmem, vmem, vmem),
        scratch_shapes=[
            pltpu.VMEM(queries.shape, BF16),
            pltpu.VMEM(queries.shape, BF16),
            pltpu.SemaphoreType.DMA((2, kv_heads)),
        ],
        compiler_params=params,
        cost_estimate=pl.CostEstimate(
            flops=12 * rows * (nb + 1) * rows * queries.shape[1],
            bytes_accessed=8 * rows * queries.shape[1],
            transcendentals=rows * rows * nb * queries.shape[1] // hd,
        ),
        name="attend",
    )(q_near, g_near, quants, dclips, bias, clips, *far_k, *far_v)

    order = [nb] + list(range(1, nb))
    backs = []
    for d in range(1, nb + 1):
        at = order.index(d) * rows
        backs.append(unshift(lax.slice_in_dim(far_grads, at, at + rows, axis=0), d))
    part, other = all_sum(scale_part, dp_count, seq_count)

    grad_keys, grad_values, grad_scale = pl.pallas_call(
        functools.partial(finish_kernel, nb),
        out_shape=(shape((rows, width), BF16), shape((rows, width), BF16), shape(part.shape, F32)),
        in_specs=[vmem] * (4 + nb),
        out_specs=(vmem, vmem, vmem),
        compiler_params=params,
        cost_estimate=pl.CostEstimate(
            flops=6 * rows * width, bytes_accessed=20 * rows * width, transcendentals=0
        ),
        name="finish",
    )(part, other, grads, slopes, *backs)
    return (attn_out, grad_queries, grad_keys, grad_values, grad_scale.reshape(quant_scale.shape))


def solution(mesh):
    rows = P(("dp", "seq"), None)
    return jax.shard_map(
        functools.partial(on_device, (mesh.shape["dp"], mesh.shape["seq"])),
        mesh=mesh,
        in_specs=(rows, rows, rows, rows, P(), P("dp", None)),
        out_specs=(rows, rows, rows, rows, P()),
        check_vma=False,
    )
```

```python
import functools
import math

import jax
import jax.numpy as jnp
from jax import lax
from jax.experimental import pallas as pl
from jax.experimental.pallas import tpu as pltpu
from jax.sharding import PartitionSpec as P

F32 = jnp.float32
BF16 = jnp.bfloat16
LEVELS = 127.0
NEG = -1e30


def sin_cos_half(u):
    r = (u - jnp.round(u)) * math.pi
    z = r * r
    s = z * (1.0 / 6227020800.0) - 1.0 / 39916800.0
    for c in (1.0 / 362880.0, -1.0 / 5040.0, 1.0 / 120.0, -1.0 / 6.0, 1.0):
        s = s * z + c
    s = s * r
    k = z * (1.0 / 479001600.0) - 1.0 / 3628800.0
    for c in (1.0 / 40320.0, -1.0 / 720.0, 1.0 / 24.0, -0.5, 1.0):
        k = k * z + c
    return s, k


def quant_parts(x, clip):
    inv = 1.0 / clip
    ratio = x * inv
    t = jnp.tanh(ratio)
    u = LEVELS * t
    s, k = sin_cos_half(u)
    level = u - s * k * (1.0 / math.pi)
    unit = level * (1.0 / LEVELS)
    slope = (2.0 * s * s) * (1.0 - t * t)
    return clip * unit, slope, unit - slope * ratio


def prep_kernel(nb, q_hbm, g_hbm, key_hbm, value_hbm, clip_hbm, len_hbm, q_ref, g_ref, quant_ref, slope_ref,
                dclip_ref, bias_ref, clip_out, key_ref, value_ref, len_ref, sems):
    small = [
        pltpu.make_async_copy(src, dst, sems.at[i])
        for i, (src, dst) in enumerate(
            ((len_hbm, len_ref), (clip_hbm, clip_out), (key_hbm, key_ref), (value_hbm, value_ref))
        )
    ]
    large = [
        pltpu.make_async_copy(q_hbm, q_ref, sems.at[4]),
        pltpu.make_async_copy(g_hbm, g_ref, sems.at[5]),
    ]
    for copy in small + large:
        copy.start()
    rows = key_ref.shape[0]
    kv_heads, hd = clip_out.shape[1], clip_out.shape[2]
    base = lax.axis_index("seq") * rows
    for copy in small:
        copy.wait()
    for side, src in ((0, key_ref), (1, value_ref)):
        for n in range(kv_heads):
            x = src[:, n * hd:(n + 1) * hd].astype(F32)
            q, slope, dclip = quant_parts(x, clip_out[side, n:n + 1, :])
            at = slice((side * kv_heads + n) * hd, (side * kv_heads + n + 1) * hd)
            quant_ref[:, at] = q.astype(BF16)
            slope_ref[:, at] = slope
            dclip_ref[:, at] = dclip
    row = lax.broadcasted_iota(jnp.int32, (rows, rows), 0)
    col = lax.broadcasted_iota(jnp.int32, (rows, rows), 1)
    start = jnp.zeros((rows, rows), jnp.int32)
    end = jnp.int32(0)
    for d in range(len_ref.shape[1]):
        end = end + len_ref[0, d]
        start = jnp.where(row + base >= end, end, start)
    for b in range(nb):
        if b == 0:
            pos = jnp.where(col <= row, col, col - nb * rows)
        else:
            pos = col - b * rows
        bias_ref[:, b * rows:(b + 1) * rows] = jnp.where(pos + base >= start, 0.0, NEG)
    for copy in large:
        copy.wait()


def attend_kernel(nb, q_ref, g_ref, quant_ref, dclip_ref, bias_ref, clip_ref, *rest):
    far_k, far_v = rest[:nb], rest[nb:2 * nb]
    out_hbm, gq_hbm, grad_ref, far_ref, scale_ref, out_ref, gq_ref, sems = rest[2 * nb:]
    kv_heads, hd = clip_ref.shape[1], clip_ref.shape[2]
    rows, group = q_ref.shape[0], q_ref.shape[1] // kv_heads
    heads = group // hd
    width = kv_heads * hd
    scale = hd ** -0.5
    log2e = math.log2(math.e)
    across = (((1,), (1,)), ((), ()))
    down = (((0,), (0,)), ((), ()))
    row = lax.broadcasted_iota(jnp.int32, (rows, rows), 0)
    col = lax.broadcasted_iota(jnp.int32, (rows, rows), 1)
    near = col <= row
    near_b = near.astype(F32).astype(BF16)
    far_b = 1.0 - near_b

    def merge(x):
        first = jnp.where(near, x[:, :rows], x[:, rows:2 * rows])
        return jnp.concatenate([first, x[:, 2 * rows:]], axis=1) if nb > 1 else first

    def split(x):
        first = x[:, :rows]
        parts = [first * near_b, first * far_b]
        if nb > 1:
            parts.append(x[:, rows:])
        return jnp.concatenate(parts, axis=1)

    def copies(n):
        cols = pl.ds(pl.multiple_of(n * group, group), group)
        return (
            pltpu.make_async_copy(out_ref.at[:, cols], out_hbm.at[:, cols], sems.at[0, n]),
            pltpu.make_async_copy(gq_ref.at[:, cols], gq_hbm.at[:, cols], sems.at[1, n]),
        )

    def step(n, carry):
        k_cols = pl.ds(pl.multiple_of(n * hd, hd), hd)
        v_cols = pl.ds(pl.multiple_of(width + n * hd, hd), hd)
        k_clip = clip_ref[0, pl.ds(n, 1), :]
        v_clip = clip_ref[1, pl.ds(n, 1), :]
        ks, vs = [quant_ref[:, k_cols]], [quant_ref[:, v_cols]]
        kd, vd = [dclip_ref[:, k_cols]], [dclip_ref[:, v_cols]]
        for d in [nb] + list(range(1, nb)):
            q, _, dc = quant_parts(far_k[d - 1][:, k_cols].astype(F32), k_clip)
            ks.append(q.astype(BF16))
            kd.append(dc)
            q, _, dc = quant_parts(far_v[d - 1][:, k_cols].astype(F32), v_clip)
            vs.append(q.astype(BF16))
            vd.append(dc)
        k2 = jnp.concatenate(ks, axis=0)
        v2 = jnp.concatenate(vs, axis=0)

        def head_cols(h):
            return pl.ds(pl.multiple_of(n * group + h * hd, hd), hd)

        qs = jnp.concatenate([q_ref[:, head_cols(h)] for h in range(heads)], axis=0)
        gs = jnp.concatenate([g_ref[:, head_cols(h)] for h in range(heads)], axis=0)
        s_all = lax.dot_general(qs, k2, across, preferred_element_type=F32)
        d_all = lax.dot_general(gs, v2, across, preferred_element_type=F32)
        bias = bias_ref[...]
        ps, ds = [], []
        for h in range(heads):
            at = slice(h * rows, (h + 1) * rows)
            s = merge(s_all[at]) * (scale * log2e) + bias
            dp = merge(d_all[at])
            w = jnp.exp2(s - jnp.max(s, axis=1, keepdims=True))
            inv = 1.0 / jnp.sum(w, axis=1, keepdims=True)
            p = w * inv
            delta = jnp.sum(p * dp, axis=1, keepdims=True)
            p2 = split(p.astype(BF16))
            ds2 = split((p * ((dp - delta) * scale)).astype(BF16))
            out_ref[:, head_cols(h)] = jnp.dot(p2, v2, preferred_element_type=F32).astype(BF16)
            gq_ref[:, head_cols(h)] = jnp.dot(ds2, k2, preferred_element_type=F32).astype(BF16)
            ps.append(p2)
            ds.append(ds2)
        for copy in copies(n):
            copy.start()
        k_grad = lax.dot_general(qs, jnp.concatenate(ds, axis=0), down, preferred_element_type=F32).T
        v_grad = lax.dot_general(gs, jnp.concatenate(ps, axis=0), down, preferred_element_type=F32).T
        grad_ref[:, k_cols] = k_grad[:rows]
        grad_ref[:, v_cols] = v_grad[:rows]
        far_ref[:, k_cols] = k_grad[rows:].astype(BF16)
        far_ref[:, v_cols] = v_grad[rows:].astype(BF16)
        scale_ref[pl.ds(n, 1), :] = jnp.sum(k_grad * jnp.concatenate(kd, axis=0), axis=0, keepdims=True)
        scale_ref[pl.ds(kv_heads + n, 1), :] = jnp.sum(
            v_grad * jnp.concatenate(vd, axis=0), axis=0, keepdims=True
        )
        return carry

    lax.fori_loop(0, kv_heads, step, 0)
    for n in range(kv_heads):
        for copy in copies(n):
            copy.wait()


def finish_kernel(nb, part_ref, other_ref, grad_ref, slope_ref, *rest):
    backs, (gk_ref, gv_ref, gs_ref) = rest[:nb], rest[nb:]
    gs_ref[...] = part_ref[...] + other_ref[...]
    width = gk_ref.shape[1]
    for side, out in ((0, gk_ref), (1, gv_ref)):
        at = slice(side * width, (side + 1) * width)
        total = grad_ref[:, at]
        for back in backs:
            total = total + back[:, at].astype(F32)
        out[...] = (total * slope_ref[:, at]).astype(BF16)


def all_sum(part, dp_count, seq_count):
    axes = ("dp", "seq")
    count = dp_count * seq_count
    core = seq_count
    bits = [1 << b for b in range(count.bit_length() - 1) if (1 << b) != core]
    fields = [bits[j:j + 2] for j in range(0, len(bits), 2)]
    part = part + lax.ppermute(part, axes, [(i, i ^ core) for i in range(count)])
    active = [i for i in range(count) if i & core]
    levels = []
    for field in fields:
        steps = [sum(c) for c in ([field[0]], field[1:], field) if c][:2 ** len(field) - 1]
        mask = sum(field)
        root = 0 if field[0] < core else field[0]
        leaves = [(k, [i for i in active if (i ^ k) & mask == root]) for k in steps]
        terms = [part] + [lax.ppermute(part, axes, [(i, i ^ k) for i in group]) for k, group in leaves]
        part = functools.reduce(jnp.add, terms)
        levels.append(leaves)
        active = [i for i in active if i & mask == root]
    total = jnp.where(lax.axis_index(axes) == active[0], part, jnp.zeros_like(part))
    for leaves in reversed(levels):
        terms = [total] + [lax.ppermute(total, axes, [(i ^ k, i) for i in group]) for k, group in leaves]
        total = functools.reduce(jnp.add, terms)
    other = lax.ppermute(total, axes, [(i, i ^ core) for i in range(count) if i & core])
    return total, other


def on_device(sizes, queries, keys, values, grad_out, quant_scale, doc_lengths):
    dp_count, seq_count = sizes
    nb = max(1, seq_count // 2)
    rows, width = keys.shape
    kv_heads, hd = quant_scale.shape[1], quant_scale.shape[2]
    vmem = pl.BlockSpec(memory_space=pltpu.VMEM)
    hbm = pl.BlockSpec(memory_space=pltpu.HBM)
    params = pltpu.CompilerParams(vmem_limit_bytes=40 * 1024 * 1024)
    shape = jax.ShapeDtypeStruct

    def shift(array, d):
        return lax.ppermute(array, "seq", [(r, (r + d) % seq_count) for r in range(seq_count)])

    def unshift(array, d):
        return lax.ppermute(array, "seq", [((r + d) % seq_count, r) for r in range(seq_count)])

    far_k = [shift(keys, d) for d in range(1, nb + 1)]
    far_v = [shift(values, d) for d in range(1, nb + 1)]

    q_near, g_near, quants, slopes, dclips, bias, clips = pl.pallas_call(
        functools.partial(prep_kernel, nb),
        out_shape=(
            shape(queries.shape, BF16),
            shape(queries.shape, BF16),
            shape((rows, 2 * width), BF16),
            shape((rows, 2 * width), F32),
            shape((rows, 2 * width), F32),
            shape((rows, nb * rows), F32),
            shape(quant_scale.shape, F32),
        ),
        in_specs=[hbm] * 6,
        out_specs=(vmem,) * 7,
        scratch_shapes=[
            pltpu.VMEM(keys.shape, BF16),
            pltpu.VMEM(values.shape, BF16),
            pltpu.SMEM(doc_lengths.shape, jnp.int32),
            pltpu.SemaphoreType.DMA((6,)),
        ],
        compiler_params=params,
        cost_estimate=pl.CostEstimate(
            flops=100 * rows * width, bytes_accessed=16 * rows * width, transcendentals=2 * rows * width
        ),
        name="prep",
    )(*[pltpu.with_memory_space_constraint(x, pltpu.HBM) for x in (queries, grad_out, keys, values, quant_scale, doc_lengths)])

    attn_out, grad_queries, grads, far_grads, scale_part = pl.pallas_call(
        functools.partial(attend_kernel, nb),
        out_shape=(
            shape(queries.shape, BF16),
            shape(queries.shape, BF16),
            shape((rows, 2 * width), F32),
            shape((nb * rows, 2 * width), BF16),
            shape((2 * kv_heads, hd), F32),
        ),
        in_specs=[vmem] * (6 + 2 * nb),
        out_specs=(hbm, hbm, vmem, vmem, vmem),
        scratch_shapes=[
            pltpu.VMEM(queries.shape, BF16),
            pltpu.VMEM(queries.shape, BF16),
            pltpu.SemaphoreType.DMA((2, kv_heads)),
        ],
        compiler_params=params,
        cost_estimate=pl.CostEstimate(
            flops=12 * rows * (nb + 1) * rows * queries.shape[1],
            bytes_accessed=8 * rows * queries.shape[1],
            transcendentals=rows * rows * nb * queries.shape[1] // hd,
        ),
        name="attend",
    )(q_near, g_near, quants, dclips, bias, clips, *far_k, *far_v)

    order = [nb] + list(range(1, nb))
    backs = []
    for d in range(1, nb + 1):
        at = order.index(d) * rows
        backs.append(unshift(lax.slice_in_dim(far_grads, at, at + rows, axis=0), d))
    part, other = all_sum(scale_part, dp_count, seq_count)

    grad_keys, grad_values, grad_scale = pl.pallas_call(
        functools.partial(finish_kernel, nb),
        out_shape=(shape((rows, width), BF16), shape((rows, width), BF16), shape(part.shape, F32)),
        in_specs=[vmem] * (4 + nb),
        out_specs=(vmem, vmem, vmem),
        compiler_params=params,
        cost_estimate=pl.CostEstimate(
            flops=6 * rows * width, bytes_accessed=20 * rows * width, transcendentals=0
        ),
        name="finish",
    )(part, other, grads, slopes, *backs)
    return (attn_out, grad_queries, grad_keys, grad_values, grad_scale.reshape(quant_scale.shape))


def solution(mesh):
    rows = P(("dp", "seq"), None)
    return jax.shard_map(
        functools.partial(on_device, (mesh.shape["dp"], mesh.shape["seq"])),
        mesh=mesh,
        in_specs=(rows, rows, rows, rows, P(), P("dp", None)),
        out_specs=(rows, rows, rows, rows, P()),
        check_vma=False,
    )
```

```python
import functools
import math

import jax
import jax.numpy as jnp
from jax import lax
from jax.experimental import pallas as pl
from jax.experimental.pallas import tpu as pltpu
from jax.sharding import PartitionSpec as P

F32 = jnp.float32
BF16 = jnp.bfloat16
LEVELS = 127.0
NEG = -1e30


def sin_cos_half(u):
    r = (u - jnp.round(u)) * math.pi
    z = r * r
    s = z * (1.0 / 6227020800.0) - 1.0 / 39916800.0
    for c in (1.0 / 362880.0, -1.0 / 5040.0, 1.0 / 120.0, -1.0 / 6.0, 1.0):
        s = s * z + c
    s = s * r
    k = z * (1.0 / 479001600.0) - 1.0 / 3628800.0
    for c in (1.0 / 40320.0, -1.0 / 720.0, 1.0 / 24.0, -0.5, 1.0):
        k = k * z + c
    return s, k


def quant_parts(x, clip):
    inv = 1.0 / clip
    ratio = x * inv
    t = jnp.tanh(ratio)
    u = LEVELS * t
    s, k = sin_cos_half(u)
    level = u - s * k * (1.0 / math.pi)
    unit = level * (1.0 / LEVELS)
    slope = (2.0 * s * s) * (1.0 - t * t)
    return clip * unit, slope, unit - slope * ratio


def prep_kernel(nb, q_hbm, g_hbm, key_hbm, value_hbm, clip_hbm, len_hbm, q_ref, g_ref, qt_ref, gt_ref, quant_ref,
                slope_ref, dclip_ref, bias_ref, clip_out, key_ref, value_ref, len_ref, sems):
    small = [
        pltpu.make_async_copy(src, dst, sems.at[i])
        for i, (src, dst) in enumerate(
            ((len_hbm, len_ref), (clip_hbm, clip_out), (key_hbm, key_ref), (value_hbm, value_ref))
        )
    ]
    large = [
        pltpu.make_async_copy(q_hbm, q_ref, sems.at[4]),
        pltpu.make_async_copy(g_hbm, g_ref, sems.at[5]),
    ]
    for copy in small + large:
        copy.start()
    rows = key_ref.shape[0]
    kv_heads, hd = clip_out.shape[1], clip_out.shape[2]
    group = q_ref.shape[1] // kv_heads
    base = lax.axis_index("seq") * rows
    for copy in small:
        copy.wait()
    for side, src in ((0, key_ref), (1, value_ref)):
        for n in range(kv_heads):
            x = src[:, n * hd:(n + 1) * hd].astype(F32)
            q, slope, dclip = quant_parts(x, clip_out[side, n:n + 1, :])
            at = slice((side * kv_heads + n) * hd, (side * kv_heads + n + 1) * hd)
            quant_ref[:, at] = q.astype(BF16)
            slope_ref[:, at] = slope
            dclip_ref[:, at] = dclip
    row = lax.broadcasted_iota(jnp.int32, (rows, rows), 0)
    col = lax.broadcasted_iota(jnp.int32, (rows, rows), 1)
    start = jnp.zeros((rows, rows), jnp.int32)
    end = jnp.int32(0)
    for d in range(len_ref.shape[1]):
        end = end + len_ref[0, d]
        start = jnp.where(row + base >= end, end, start)
    for b in range(nb):
        if b == 0:
            pos = jnp.where(col <= row, col, col - nb * rows)
        else:
            pos = col - b * rows
        bias_ref[:, b * rows:(b + 1) * rows] = jnp.where(pos + base >= start, 0.0, NEG)
    for copy, src, dst in zip(large, (q_ref, g_ref), (qt_ref, gt_ref)):
        copy.wait()
        for n in range(kv_heads):
            for h in range(group // hd):
                at = n * group + h * hd
                dst[n * hd:(n + 1) * hd, h * rows:(h + 1) * rows] = src[:, at:at + hd].T


ACROSS = (((1,), (1,)), ((), ()))


def far_order(nb):
    return [nb] + list(range(1, nb))


def score_kernel(nb, q_ref, gt_ref, quant_ref, bias_ref, clip_ref, *rest):
    far, (p_ref, p2_ref, k2_ref, dclip_ref, vgrad_ref) = rest[:nb], rest[nb:]
    kv_heads, hd = clip_ref.shape[1], clip_ref.shape[2]
    rows, group = q_ref.shape[0], q_ref.shape[1] // kv_heads
    heads = group // hd
    factor = hd ** -0.5 * math.log2(math.e)
    near = near_mask(rows)
    near_b = near.astype(F32).astype(BF16)
    far_b = 1.0 - near_b

    def step(n, carry):
        cols = pl.ds(pl.multiple_of(n * hd, hd), hd)
        clip = clip_ref[0, pl.ds(n, 1), :]
        k2_ref[:rows, cols] = quant_ref[:, cols]
        for j, d in enumerate(far_order(nb)):
            q, _, dclip = quant_parts(far[d - 1][:, cols].astype(F32), clip)
            k2_ref[(j + 1) * rows:(j + 2) * rows, cols] = q.astype(BF16)
            dclip_ref[j * rows:(j + 1) * rows, cols] = dclip
        k2 = k2_ref[:, cols]
        qs = jnp.concatenate(
            [q_ref[:, pl.ds(pl.multiple_of(n * group + h * hd, hd), hd)] for h in range(heads)], axis=0
        )
        s_all = lax.dot_general(qs, k2, ACROSS, preferred_element_type=F32)
        bias = bias_ref[...]
        for h in range(heads):
            s = merge(near, s_all[h * rows:(h + 1) * rows], nb) * factor + bias
            w = jnp.exp2(s - jnp.max(s, axis=1, keepdims=True))
            p = (w * (1.0 / jnp.sum(w, axis=1, keepdims=True))).astype(BF16)
            at = pl.ds(pl.multiple_of(n * heads * rows + h * rows, rows), rows)
            p_ref[at, :] = p
            p2_ref[at, :] = split(near_b, far_b, p, nb)
        p2 = p2_ref[pl.ds(pl.multiple_of(n * heads * rows, rows), heads * rows), :]
        at = pl.ds(pl.multiple_of(n * hd, hd), hd)
        vgrad_ref[:, cols] = jnp.dot(gt_ref[at, :], p2, preferred_element_type=F32).T
        return carry

    lax.fori_loop(0, kv_heads, step, 0)


def near_mask(rows):
    row = lax.broadcasted_iota(jnp.int32, (rows, rows), 0)
    col = lax.broadcasted_iota(jnp.int32, (rows, rows), 1)
    return col <= row


def merge(near, x, nb):
    rows = near.shape[0]
    first = jnp.where(near, x[:, :rows], x[:, rows:2 * rows])
    return jnp.concatenate([first, x[:, 2 * rows:]], axis=1) if nb > 1 else first


def split(near_b, far_b, x, nb):
    rows = near_b.shape[0]
    parts = [x[:, :rows] * near_b, x[:, :rows] * far_b]
    if nb > 1:
        parts.append(x[:, rows:])
    return jnp.concatenate(parts, axis=1)


def dscore_kernel(nb, g_ref, qt_ref, quant_ref, dclip_ref, clip_ref, p_ref, kdclip_ref, vgrad_ref, *rest):
    far, (ds2_ref, v2_ref, grad_ref, far_ref, scale_ref) = rest[:nb], rest[nb:]
    kv_heads, hd = clip_ref.shape[1], clip_ref.shape[2]
    rows, group = g_ref.shape[0], g_ref.shape[1] // kv_heads
    heads = group // hd
    width = kv_heads * hd
    scale = hd ** -0.5
    near = near_mask(rows)
    near_b = near.astype(F32).astype(BF16)
    far_b = 1.0 - near_b

    def step(n, carry):
        cols = pl.ds(pl.multiple_of(n * hd, hd), hd)
        v_cols = pl.ds(pl.multiple_of(width + n * hd, hd), hd)
        clip = clip_ref[1, pl.ds(n, 1), :]
        v2_ref[:rows, cols] = quant_ref[:, v_cols]
        vdclips = [dclip_ref[:, v_cols]]
        for j, d in enumerate(far_order(nb)):
            q, _, dclip = quant_parts(far[d - 1][:, cols].astype(F32), clip)
            v2_ref[(j + 1) * rows:(j + 2) * rows, cols] = q.astype(BF16)
            vdclips.append(dclip)
        v2 = v2_ref[:, cols]
        gs = jnp.concatenate(
            [g_ref[:, pl.ds(pl.multiple_of(n * group + h * hd, hd), hd)] for h in range(heads)], axis=0
        )
        d_all = lax.dot_general(gs, v2, ACROSS, preferred_element_type=F32)
        for h in range(heads):
            at = pl.ds(pl.multiple_of(n * heads * rows + h * rows, rows), rows)
            dp = merge(near, d_all[h * rows:(h + 1) * rows], nb)
            p = p_ref[at, :].astype(F32)
            delta = jnp.sum(p * dp, axis=1, keepdims=True)
            ds = (p * ((dp - delta) * scale)).astype(BF16)
            ds2_ref[at, :] = split(near_b, far_b, ds, nb)
        ds2 = ds2_ref[pl.ds(pl.multiple_of(n * heads * rows, rows), heads * rows), :]
        at = pl.ds(pl.multiple_of(n * hd, hd), hd)
        k_grad = jnp.dot(qt_ref[at, :], ds2, preferred_element_type=F32).T
        v_grad = vgrad_ref[:, cols]
        grad_ref[:, cols] = k_grad[:rows]
        grad_ref[:, v_cols] = v_grad[:rows]
        far_ref[:, cols] = k_grad[rows:].astype(BF16)
        far_ref[:, v_cols] = v_grad[rows:].astype(BF16)
        scale_ref[pl.ds(n, 1), :] = jnp.sum(k_grad[:rows] * dclip_ref[:, cols], axis=0, keepdims=True) + jnp.sum(
            k_grad[rows:] * kdclip_ref[:, cols], axis=0, keepdims=True
        )
        scale_ref[pl.ds(kv_heads + n, 1), :] = jnp.sum(
            v_grad * jnp.concatenate(vdclips, axis=0), axis=0, keepdims=True
        )
        return carry

    lax.fori_loop(0, kv_heads, step, 0)


def output_kernel(p2_ref, v2_ref, ds2_ref, k2_ref, out_hbm, gq_hbm, out_ref, gq_ref, sems):
    kv_heads = sems.shape[1]
    group = out_ref.shape[1] // kv_heads
    hd = v2_ref.shape[1] // kv_heads
    rows = out_ref.shape[0]
    heads = group // hd

    def copies(n):
        cols = pl.ds(pl.multiple_of(n * group, group), group)
        return (
            pltpu.make_async_copy(out_ref.at[:, cols], out_hbm.at[:, cols], sems.at[0, n]),
            pltpu.make_async_copy(gq_ref.at[:, cols], gq_hbm.at[:, cols], sems.at[1, n]),
        )

    def step(n, carry):
        cols = pl.ds(pl.multiple_of(n * hd, hd), hd)
        at = pl.ds(pl.multiple_of(n * heads * rows, rows), heads * rows)
        for left, right, dst in ((p2_ref, v2_ref, out_ref), (ds2_ref, k2_ref, gq_ref)):
            y = jnp.dot(left[at, :], right[:, cols], preferred_element_type=F32).astype(BF16)
            for h in range(heads):
                dst[:, pl.ds(pl.multiple_of(n * group + h * hd, hd), hd)] = y[h * rows:(h + 1) * rows]
        for copy in copies(n):
            copy.start()
        return carry

    lax.fori_loop(0, kv_heads, step, 0)
    for n in range(kv_heads):
        for copy in copies(n):
            copy.wait()


def finish_kernel(nb, part_ref, other_ref, grad_ref, slope_ref, *rest):
    backs, (gk_ref, gv_ref, gs_ref) = rest[:nb], rest[nb:]
    first_core = lax.axis_index("dp") % 2 == 0
    gs_ref[...] = jnp.where(first_core, other_ref[...], part_ref[...])
    width = gk_ref.shape[1]
    for side, out in ((0, gk_ref), (1, gv_ref)):
        at = slice(side * width, (side + 1) * width)
        total = grad_ref[:, at]
        for back in backs:
            total = total + back[:, at].astype(F32)
        out[...] = (total * slope_ref[:, at]).astype(BF16)


def all_sum(part, dp_count, seq_count):
    axes = ("dp", "seq")
    count = dp_count * seq_count
    core = seq_count
    part = part + lax.ppermute(part, axes, [(i, i ^ core) for i in range(count)])
    strides = [seq_count << b for b in range(1, dp_count.bit_length() - 1)]
    strides += [1 << b for b in range(seq_count.bit_length() - 1)]
    for stride in strides:
        part = part + lax.ppermute(part, axes, [(i, i ^ stride if i & core else i) for i in range(count)])
    return part, lax.ppermute(part, axes, [(i, i ^ core) for i in range(count)])


def on_device(sizes, queries, keys, values, grad_out, quant_scale, doc_lengths):
    dp_count, seq_count = sizes
    nb = max(1, seq_count // 2)
    rows, width = keys.shape
    kv_heads, hd = quant_scale.shape[1], quant_scale.shape[2]
    heads = queries.shape[1] // hd
    vmem = pl.BlockSpec(memory_space=pltpu.VMEM)
    hbm = pl.BlockSpec(memory_space=pltpu.HBM)
    params = pltpu.CompilerParams(vmem_limit_bytes=36 * 1024 * 1024)
    shape = jax.ShapeDtypeStruct
    work = rows * rows * queries.shape[1]

    def call(kernel, name, flops, args, outs, in_specs=None, out_specs=None, scratch=()):
        return pl.pallas_call(
            kernel,
            out_shape=outs,
            in_specs=in_specs or [vmem] * len(args),
            out_specs=out_specs or (vmem,) * len(outs),
            scratch_shapes=scratch,
            compiler_params=params,
            cost_estimate=pl.CostEstimate(flops=flops, bytes_accessed=16 * rows * width, transcendentals=0),
            name=name,
        )(*args)

    def shift(array, d):
        return lax.ppermute(array, "seq", [(r, (r + d) % seq_count) for r in range(seq_count)])

    def unshift(array, d):
        return lax.ppermute(array, "seq", [((r + d) % seq_count, r) for r in range(seq_count)])

    far_k = [shift(keys, d) for d in range(1, nb + 1)]
    far_v = [shift(values, d) for d in range(1, nb + 1)]

    raw = (queries, grad_out, keys, values, quant_scale, doc_lengths)
    q, g, qt, gt, quants, slopes, dclips, bias, clips = call(
        functools.partial(prep_kernel, nb),
        "prep",
        2 * work,
        [pltpu.with_memory_space_constraint(x, pltpu.HBM) for x in raw],
        (
            shape(queries.shape, BF16),
            shape(queries.shape, BF16),
            shape((width, heads // kv_heads * rows), BF16),
            shape((width, heads // kv_heads * rows), BF16),
            shape((rows, 2 * width), BF16),
            shape((rows, 2 * width), F32),
            shape((rows, 2 * width), F32),
            shape((rows, nb * rows), F32),
            shape(quant_scale.shape, F32),
        ),
        in_specs=[hbm] * 6,
        scratch=[
            pltpu.VMEM(keys.shape, BF16),
            pltpu.VMEM(values.shape, BF16),
            pltpu.SMEM(doc_lengths.shape, jnp.int32),
            pltpu.SemaphoreType.DMA((6,)),
        ],
    )
    p, p2, k2, kdclips, v_grads = call(
        functools.partial(score_kernel, nb),
        "score",
        4 * (nb + 1) * work,
        (q, gt, quants, bias, clips, *far_k),
        (
            shape((heads * rows, nb * rows), BF16),
            shape((heads * rows, (nb + 1) * rows), BF16),
            shape(((nb + 1) * rows, width), BF16),
            shape((nb * rows, width), F32),
            shape(((nb + 1) * rows, width), F32),
        ),
    )
    ds2, v2, grads, far_grads, scale_part = call(
        functools.partial(dscore_kernel, nb),
        "dscore",
        4 * (nb + 1) * work,
        (g, qt, quants, dclips, clips, p, kdclips, v_grads, *far_v),
        (
            shape((heads * rows, (nb + 1) * rows), BF16),
            shape(((nb + 1) * rows, width), BF16),
            shape((rows, 2 * width), F32),
            shape((nb * rows, 2 * width), BF16),
            shape((2 * kv_heads, hd), F32),
        ),
    )
    backs = []
    for d in range(1, nb + 1):
        at = far_order(nb).index(d) * rows
        backs.append(unshift(lax.slice_in_dim(far_grads, at, at + rows, axis=0), d))
    part, other = all_sum(scale_part, dp_count, seq_count)
    attn_out, grad_queries = call(
        output_kernel,
        "output",
        4 * (nb + 1) * work,
        (p2, v2, ds2, k2),
        (shape(queries.shape, BF16), shape(queries.shape, BF16)),
        out_specs=(hbm, hbm),
        scratch=[
            pltpu.VMEM(queries.shape, BF16),
            pltpu.VMEM(queries.shape, BF16),
            pltpu.SemaphoreType.DMA((2, kv_heads)),
        ],
    )
    grad_keys, grad_values, grad_scale = call(
        functools.partial(finish_kernel, nb),
        "finish",
        6 * rows * width,
        (part, other, grads, slopes, *backs),
        (shape((rows, width), BF16), shape((rows, width), BF16), shape(part.shape, F32)),
    )
    return (attn_out, grad_queries, grad_keys, grad_values, grad_scale.reshape(quant_scale.shape))


def solution(mesh):
    rows = P(("dp", "seq"), None)
    return jax.shard_map(
        functools.partial(on_device, (mesh.shape["dp"], mesh.shape["seq"])),
        mesh=mesh,
        in_specs=(rows, rows, rows, rows, P(), P("dp", None)),
        out_specs=(rows, rows, rows, rows, P()),
        check_vma=False,
    )
```

```python
import functools
import math

import jax
import jax.numpy as jnp
from jax import lax
from jax.experimental import pallas as pl
from jax.experimental.pallas import tpu as pltpu
from jax.sharding import PartitionSpec as P

F32 = jnp.float32
BF16 = jnp.bfloat16
LEVELS = 127.0
NEG = -1e30


def sin_cos_half(u):
    r = (u - jnp.round(u)) * math.pi
    z = r * r
    s = z * (1.0 / 6227020800.0) - 1.0 / 39916800.0
    for c in (1.0 / 362880.0, -1.0 / 5040.0, 1.0 / 120.0, -1.0 / 6.0, 1.0):
        s = s * z + c
    s = s * r
    k = z * (1.0 / 479001600.0) - 1.0 / 3628800.0
    for c in (1.0 / 40320.0, -1.0 / 720.0, 1.0 / 24.0, -0.5, 1.0):
        k = k * z + c
    return s, k


def quant_parts(x, clip):
    inv = 1.0 / clip
    ratio = x * inv
    t = jnp.tanh(ratio)
    u = LEVELS * t
    s, k = sin_cos_half(u)
    level = u - s * k * (1.0 / math.pi)
    unit = level * (1.0 / LEVELS)
    slope = (2.0 * s * s) * (1.0 - t * t)
    return clip * unit, slope, unit - slope * ratio


def prep_kernel(nb, q_hbm, g_hbm, key_hbm, value_hbm, clip_hbm, len_hbm, q_ref, g_ref, qt_ref, gt_ref, quant_ref,
                slope_ref, dclip_ref, bias_ref, clip_out, key_ref, value_ref, len_ref, sems):
    small = [
        pltpu.make_async_copy(src, dst, sems.at[i])
        for i, (src, dst) in enumerate(
            ((len_hbm, len_ref), (clip_hbm, clip_out), (key_hbm, key_ref), (value_hbm, value_ref))
        )
    ]
    large = [
        pltpu.make_async_copy(q_hbm, q_ref, sems.at[4]),
        pltpu.make_async_copy(g_hbm, g_ref, sems.at[5]),
    ]
    for copy in small + large:
        copy.start()
    rows = key_ref.shape[0]
    kv_heads, hd = clip_out.shape[1], clip_out.shape[2]
    group = q_ref.shape[1] // kv_heads
    base = lax.axis_index("seq") * rows
    for copy in small:
        copy.wait()
    for side, src in ((0, key_ref), (1, value_ref)):
        for n in range(kv_heads):
            x = src[:, n * hd:(n + 1) * hd].astype(F32)
            q, slope, dclip = quant_parts(x, clip_out[side, n:n + 1, :])
            at = slice((side * kv_heads + n) * hd, (side * kv_heads + n + 1) * hd)
            quant_ref[:, at] = q.astype(BF16)
            slope_ref[:, at] = slope
            dclip_ref[:, at] = dclip
    row = lax.broadcasted_iota(jnp.int32, (rows, rows), 0)
    col = lax.broadcasted_iota(jnp.int32, (rows, rows), 1)
    start = jnp.zeros((rows, rows), jnp.int32)
    end = jnp.int32(0)
    for d in range(len_ref.shape[1]):
        end = end + len_ref[0, d]
        start = jnp.where(row + base >= end, end, start)
    for b in range(nb):
        if b == 0:
            pos = jnp.where(col <= row, col, col - nb * rows)
        else:
            pos = col - b * rows
        bias_ref[:, b * rows:(b + 1) * rows] = jnp.where(pos + base >= start, 0.0, NEG)
    for copy, src, dst in zip(large, (q_ref, g_ref), (qt_ref, gt_ref)):
        copy.wait()
        for n in range(kv_heads):
            for h in range(group // hd):
                at = n * group + h * hd
                dst[n * hd:(n + 1) * hd, h * rows:(h + 1) * rows] = src[:, at:at + hd].T


ACROSS = (((1,), (1,)), ((), ()))


def far_order(nb):
    return [nb] + list(range(1, nb))


def near_mask(rows):
    row = lax.broadcasted_iota(jnp.int32, (rows, rows), 0)
    col = lax.broadcasted_iota(jnp.int32, (rows, rows), 1)
    return col <= row


def merge(near, x, nb):
    rows = near.shape[0]
    first = jnp.where(near, x[:, :rows], x[:, rows:2 * rows])
    return jnp.concatenate([first, x[:, 2 * rows:]], axis=1) if nb > 1 else first


def split(near_b, far_b, x, nb):
    rows = near_b.shape[0]
    parts = [x[:, :rows] * near_b, x[:, :rows] * far_b]
    if nb > 1:
        parts.append(x[:, rows:])
    return jnp.concatenate(parts, axis=1)


def attend_kernel(nb, q_ref, g_ref, qt_ref, gt_ref, quant_ref, dclip_ref, bias_ref, clip_ref, *rest):
    far_k, far_v = rest[:nb], rest[nb:2 * nb]
    out_hbm, gq_hbm, grad_ref, far_ref, scale_ref, out_ref, gq_ref, sems = rest[2 * nb:]
    kv_heads, hd = clip_ref.shape[1], clip_ref.shape[2]
    rows, group = q_ref.shape[0], q_ref.shape[1] // kv_heads
    heads = group // hd
    width = kv_heads * hd
    scale = hd ** -0.5
    log2e = math.log2(math.e)
    near = near_mask(rows)
    near_b = near.astype(F32).astype(BF16)
    far_b = 1.0 - near_b

    def copies(n):
        cols = pl.ds(pl.multiple_of(n * group, group), group)
        return (
            pltpu.make_async_copy(out_ref.at[:, cols], out_hbm.at[:, cols], sems.at[0, n]),
            pltpu.make_async_copy(gq_ref.at[:, cols], gq_hbm.at[:, cols], sems.at[1, n]),
        )

    def step(n, carry):
        k_cols = pl.ds(pl.multiple_of(n * hd, hd), hd)
        v_cols = pl.ds(pl.multiple_of(width + n * hd, hd), hd)
        k_clip = clip_ref[0, pl.ds(n, 1), :]
        v_clip = clip_ref[1, pl.ds(n, 1), :]
        ks, vs = [quant_ref[:, k_cols]], [quant_ref[:, v_cols]]
        kd, vd = [dclip_ref[:, k_cols]], [dclip_ref[:, v_cols]]
        for d in far_order(nb):
            q, _, dc = quant_parts(far_k[d - 1][:, k_cols].astype(F32), k_clip)
            ks.append(q.astype(BF16))
            kd.append(dc)
            q, _, dc = quant_parts(far_v[d - 1][:, k_cols].astype(F32), v_clip)
            vs.append(q.astype(BF16))
            vd.append(dc)
        k2 = jnp.concatenate(ks, axis=0)
        v2 = jnp.concatenate(vs, axis=0)

        def head_cols(h):
            return pl.ds(pl.multiple_of(n * group + h * hd, hd), hd)

        qs = jnp.concatenate([q_ref[:, head_cols(h)] for h in range(heads)], axis=0)
        gs = jnp.concatenate([g_ref[:, head_cols(h)] for h in range(heads)], axis=0)
        s_all = lax.dot_general(qs, k2, ACROSS, preferred_element_type=F32)
        d_all = lax.dot_general(gs, v2, ACROSS, preferred_element_type=F32)
        bias = bias_ref[...]
        ps, ds = [], []
        for h in range(heads):
            at = slice(h * rows, (h + 1) * rows)
            s = merge(near, s_all[at], nb) * (scale * log2e) + bias
            dp = merge(near, d_all[at], nb)
            w = jnp.exp2(s - jnp.max(s, axis=1, keepdims=True))
            inv = 1.0 / jnp.sum(w, axis=1, keepdims=True)
            p = w * inv
            delta = jnp.sum(p * dp, axis=1, keepdims=True)
            p2 = split(near_b, far_b, p.astype(BF16), nb)
            ds2 = split(near_b, far_b, (p * ((dp - delta) * scale)).astype(BF16), nb)
            out_ref[:, head_cols(h)] = jnp.dot(p2, v2, preferred_element_type=F32).astype(BF16)
            gq_ref[:, head_cols(h)] = jnp.dot(ds2, k2, preferred_element_type=F32).astype(BF16)
            ps.append(p2)
            ds.append(ds2)
        for copy in copies(n):
            copy.start()
        k_grad = jnp.dot(qt_ref[k_cols, :], jnp.concatenate(ds, axis=0), preferred_element_type=F32).T
        v_grad = jnp.dot(gt_ref[k_cols, :], jnp.concatenate(ps, axis=0), preferred_element_type=F32).T
        grad_ref[:, k_cols] = k_grad[:rows]
        grad_ref[:, v_cols] = v_grad[:rows]
        far_ref[:, k_cols] = k_grad[rows:].astype(BF16)
        far_ref[:, v_cols] = v_grad[rows:].astype(BF16)
        scale_ref[pl.ds(n, 1), :] = jnp.sum(k_grad * jnp.concatenate(kd, axis=0), axis=0, keepdims=True)
        scale_ref[pl.ds(kv_heads + n, 1), :] = jnp.sum(
            v_grad * jnp.concatenate(vd, axis=0), axis=0, keepdims=True
        )
        return carry

    lax.fori_loop(0, kv_heads, step, 0, unroll=True)
    for n in range(kv_heads):
        for copy in copies(n):
            copy.wait()


def finish_kernel(nb, grad_ref, slope_ref, part_ref, *rest):
    others, backs, (gk_ref, gv_ref, gs_ref) = rest[:3], rest[3:3 + nb], rest[3 + nb:]
    gs_ref[...] = (part_ref[...] + others[0][...]) + (others[1][...] + others[2][...])
    width = gk_ref.shape[1]
    for side, out in ((0, gk_ref), (1, gv_ref)):
        at = slice(side * width, (side + 1) * width)
        total = grad_ref[:, at]
        for back in backs:
            total = total + back[:, at].astype(F32)
        out[...] = (total * slope_ref[:, at]).astype(BF16)


def all_sum(part, dp_count, seq_count):
    axes = ("dp", "seq")
    count = dp_count * seq_count

    def exchange(array, mask):
        return lax.ppermute(array, axes, [(i, i ^ mask) for i in range(count)])

    core = seq_count
    bits = [1 << b for b in range(count.bit_length() - 1) if (1 << b) != core]
    part = part + exchange(part, core)
    if len(bits) % 2:
        part = part + exchange(part, bits[0])
        bits = bits[1:]
    for low, high in zip(bits[::2], bits[1::2]):
        far, mid, near = exchange(part, low | high), exchange(part, high), exchange(part, low)
        terms = [part, near, mid, far]
        part = (part + near) + (mid + far)
    return terms


def on_device(sizes, queries, keys, values, grad_out, quant_scale, doc_lengths):
    dp_count, seq_count = sizes
    nb = max(1, seq_count // 2)
    rows, width = keys.shape
    kv_heads, hd = quant_scale.shape[1], quant_scale.shape[2]
    heads = queries.shape[1] // hd
    vmem = pl.BlockSpec(memory_space=pltpu.VMEM)
    hbm = pl.BlockSpec(memory_space=pltpu.HBM)
    params = pltpu.CompilerParams(vmem_limit_bytes=36 * 1024 * 1024)
    shape = jax.ShapeDtypeStruct
    work = rows * rows * queries.shape[1]

    def call(kernel, name, flops, args, outs, in_specs=None, out_specs=None, scratch=()):
        return pl.pallas_call(
            kernel,
            out_shape=outs,
            in_specs=in_specs or [vmem] * len(args),
            out_specs=out_specs or (vmem,) * len(outs),
            scratch_shapes=scratch,
            compiler_params=params,
            cost_estimate=pl.CostEstimate(flops=flops, bytes_accessed=16 * rows * width, transcendentals=0),
            name=name,
        )(*args)

    def shift(array, d):
        return lax.ppermute(array, "seq", [(r, (r + d) % seq_count) for r in range(seq_count)])

    def unshift(array, d):
        return lax.ppermute(array, "seq", [((r + d) % seq_count, r) for r in range(seq_count)])

    far_k = [shift(keys, d) for d in range(1, nb + 1)]
    far_v = [shift(values, d) for d in range(1, nb + 1)]

    raw = (queries, grad_out, keys, values, quant_scale, doc_lengths)
    q, g, qt, gt, quants, slopes, dclips, bias, clips = call(
        functools.partial(prep_kernel, nb),
        "prep",
        2 * work,
        [pltpu.with_memory_space_constraint(x, pltpu.HBM) for x in raw],
        (
            shape(queries.shape, BF16),
            shape(queries.shape, BF16),
            shape((width, heads // kv_heads * rows), BF16),
            shape((width, heads // kv_heads * rows), BF16),
            shape((rows, 2 * width), BF16),
            shape((rows, 2 * width), F32),
            shape((rows, 2 * width), F32),
            shape((rows, nb * rows), F32),
            shape(quant_scale.shape, F32),
        ),
        in_specs=[hbm] * 6,
        scratch=[
            pltpu.VMEM(keys.shape, BF16),
            pltpu.VMEM(values.shape, BF16),
            pltpu.SMEM(doc_lengths.shape, jnp.int32),
            pltpu.SemaphoreType.DMA((6,)),
        ],
    )
    attn_out, grad_queries, grads, far_grads, scale_part = call(
        functools.partial(attend_kernel, nb),
        "attend",
        12 * (nb + 1) * work,
        (q, g, qt, gt, quants, dclips, bias, clips, *far_k, *far_v),
        (
            shape(queries.shape, BF16),
            shape(queries.shape, BF16),
            shape((rows, 2 * width), F32),
            shape((nb * rows, 2 * width), BF16),
            shape((2 * kv_heads, hd), F32),
        ),
        out_specs=(hbm, hbm, vmem, vmem, vmem),
        scratch=[
            pltpu.VMEM(queries.shape, BF16),
            pltpu.VMEM(queries.shape, BF16),
            pltpu.SemaphoreType.DMA((2, kv_heads)),
        ],
    )
    backs = []
    for d in range(1, nb + 1):
        at = far_order(nb).index(d) * rows
        backs.append(unshift(lax.slice_in_dim(far_grads, at, at + rows, axis=0), d))
    terms = all_sum(scale_part, dp_count, seq_count)
    grad_keys, grad_values, grad_scale = call(
        functools.partial(finish_kernel, nb),
        "finish",
        6 * rows * width,
        (grads, slopes, *terms, *backs),
        (shape((rows, width), BF16), shape((rows, width), BF16), shape(scale_part.shape, F32)),
    )
    return (attn_out, grad_queries, grad_keys, grad_values, grad_scale.reshape(quant_scale.shape))


def solution(mesh):
    rows = P(("dp", "seq"), None)
    return jax.shard_map(
        functools.partial(on_device, (mesh.shape["dp"], mesh.shape["seq"])),
        mesh=mesh,
        in_specs=(rows, rows, rows, rows, P(), P("dp", None)),
        out_specs=(rows, rows, rows, rows, P()),
        check_vma=False,
    )
```

```python
import functools
import math

import jax
import jax.numpy as jnp
from jax import lax
from jax.experimental import pallas as pl
from jax.experimental.pallas import tpu as pltpu
from jax.sharding import PartitionSpec as P

F32 = jnp.float32
BF16 = jnp.bfloat16
LEVELS = 127.0
NEG = -1e30


def sin_cos_half(u):
    r = (u - jnp.round(u)) * math.pi
    z = r * r
    s = z * (1.0 / 6227020800.0) - 1.0 / 39916800.0
    for c in (1.0 / 362880.0, -1.0 / 5040.0, 1.0 / 120.0, -1.0 / 6.0, 1.0):
        s = s * z + c
    s = s * r
    k = z * (1.0 / 479001600.0) - 1.0 / 3628800.0
    for c in (1.0 / 40320.0, -1.0 / 720.0, 1.0 / 24.0, -0.5, 1.0):
        k = k * z + c
    return s, k


def quant_parts(x, clip):
    inv = 1.0 / clip
    ratio = x * inv
    t = jnp.tanh(ratio)
    u = LEVELS * t
    s, k = sin_cos_half(u)
    level = u - s * k * (1.0 / math.pi)
    unit = level * (1.0 / LEVELS)
    slope = (2.0 * s * s) * (1.0 - t * t)
    return clip * unit, slope, unit - slope * ratio


def prep_kernel(nb, q_hbm, g_hbm, key_hbm, value_hbm, clip_hbm, len_hbm, q_ref, g_ref, qt_ref, gt_ref, quant_ref,
                slope_ref, dclip_ref, bias_ref, clip_out, key_ref, value_ref, len_ref, sems):
    small = [
        pltpu.make_async_copy(src, dst, sems.at[i])
        for i, (src, dst) in enumerate(
            ((len_hbm, len_ref), (clip_hbm, clip_out), (key_hbm, key_ref), (value_hbm, value_ref))
        )
    ]
    large = [
        pltpu.make_async_copy(q_hbm, q_ref, sems.at[4]),
        pltpu.make_async_copy(g_hbm, g_ref, sems.at[5]),
    ]
    for copy in small + large:
        copy.start()
    rows = key_ref.shape[0]
    kv_heads, hd = clip_out.shape[1], clip_out.shape[2]
    group = q_ref.shape[1] // kv_heads
    base = lax.axis_index("seq") * rows
    for copy in small:
        copy.wait()
    for side, src in ((0, key_ref), (1, value_ref)):
        for n in range(kv_heads):
            x = src[:, n * hd:(n + 1) * hd].astype(F32)
            q, slope, dclip = quant_parts(x, clip_out[side, n:n + 1, :])
            at = slice((side * kv_heads + n) * hd, (side * kv_heads + n + 1) * hd)
            quant_ref[:, at] = q.astype(BF16)
            slope_ref[:, at] = slope
            dclip_ref[:, at] = dclip
    row = lax.broadcasted_iota(jnp.int32, (rows, rows), 0)
    col = lax.broadcasted_iota(jnp.int32, (rows, rows), 1)
    start = jnp.zeros((rows, rows), jnp.int32)
    end = jnp.int32(0)
    for d in range(len_ref.shape[1]):
        end = end + len_ref[0, d]
        start = jnp.where(row + base >= end, end, start)
    for b in range(nb):
        if b == 0:
            pos = jnp.where(col <= row, col, col - nb * rows)
        else:
            pos = col - b * rows
        bias_ref[:, b * rows:(b + 1) * rows] = jnp.where(pos + base >= start, 0.0, NEG)
    for copy, src, dst in zip(large, (q_ref, g_ref), (qt_ref, gt_ref)):
        copy.wait()
        for n in range(kv_heads):
            for h in range(group // hd):
                at = n * group + h * hd
                dst[n * hd:(n + 1) * hd, h * rows:(h + 1) * rows] = src[:, at:at + hd].T


ACROSS = (((1,), (1,)), ((), ()))


def far_order(nb):
    return [nb] + list(range(1, nb))


def near_mask(rows):
    row = lax.broadcasted_iota(jnp.int32, (rows, rows), 0)
    col = lax.broadcasted_iota(jnp.int32, (rows, rows), 1)
    return col <= row


def merge(near, x, nb):
    rows = near.shape[0]
    first = jnp.where(near, x[:, :rows], x[:, rows:2 * rows])
    return jnp.concatenate([first, x[:, 2 * rows:]], axis=1) if nb > 1 else first


def split(near_b, far_b, x, nb):
    rows = near_b.shape[0]
    parts = [x[:, :rows] * near_b, x[:, :rows] * far_b]
    if nb > 1:
        parts.append(x[:, rows:])
    return jnp.concatenate(parts, axis=1)


def attend_kernel(nb, q_ref, g_ref, qt_ref, gt_ref, quant_ref, dclip_ref, bias_ref, clip_ref, *rest):
    far_k, far_v = rest[:nb], rest[nb:2 * nb]
    out_hbm, gq_hbm, grad_ref, far_ref, scale_ref, out_ref, gq_ref, sems = rest[2 * nb:]
    kv_heads, hd = clip_ref.shape[1], clip_ref.shape[2]
    rows, group = q_ref.shape[0], q_ref.shape[1] // kv_heads
    heads = group // hd
    width = kv_heads * hd
    scale = hd ** -0.5
    log2e = math.log2(math.e)
    near = near_mask(rows)
    near_b = near.astype(F32).astype(BF16)
    far_b = 1.0 - near_b

    def copies(n):
        cols = pl.ds(pl.multiple_of(n * group, group), group)
        return (
            pltpu.make_async_copy(out_ref.at[:, cols], out_hbm.at[:, cols], sems.at[0, n]),
            pltpu.make_async_copy(gq_ref.at[:, cols], gq_hbm.at[:, cols], sems.at[1, n]),
        )

    def step(n, carry):
        k_cols = pl.ds(pl.multiple_of(n * hd, hd), hd)
        v_cols = pl.ds(pl.multiple_of(width + n * hd, hd), hd)
        k_clip = clip_ref[0, pl.ds(n, 1), :]
        v_clip = clip_ref[1, pl.ds(n, 1), :]
        ks, vs = [quant_ref[:, k_cols]], [quant_ref[:, v_cols]]
        kd, vd = [dclip_ref[:, k_cols]], [dclip_ref[:, v_cols]]
        for d in far_order(nb):
            q, _, dc = quant_parts(far_k[d - 1][:, k_cols].astype(F32), k_clip)
            ks.append(q.astype(BF16))
            kd.append(dc)
            q, _, dc = quant_parts(far_v[d - 1][:, k_cols].astype(F32), v_clip)
            vs.append(q.astype(BF16))
            vd.append(dc)
        k2 = jnp.concatenate(ks, axis=0)
        v2 = jnp.concatenate(vs, axis=0)

        def head_cols(h):
            return pl.ds(pl.multiple_of(n * group + h * hd, hd), hd)

        qs = jnp.concatenate([q_ref[:, head_cols(h)] for h in range(heads)], axis=0)
        gs = jnp.concatenate([g_ref[:, head_cols(h)] for h in range(heads)], axis=0)
        s_all = lax.dot_general(qs, k2, ACROSS, preferred_element_type=F32)
        d_all = lax.dot_general(gs, v2, ACROSS, preferred_element_type=F32)
        bias = bias_ref[...]
        ps, ds = [], []
        for h in range(heads):
            at = slice(h * rows, (h + 1) * rows)
            s = merge(near, s_all[at], nb) * (scale * log2e) + bias
            dp = merge(near, d_all[at], nb)
            w = jnp.exp2(s - jnp.max(s, axis=1, keepdims=True))
            inv = 1.0 / jnp.sum(w, axis=1, keepdims=True)
            p = w * inv
            delta = jnp.sum(p * dp, axis=1, keepdims=True)
            p2 = split(near_b, far_b, p.astype(BF16), nb)
            ds2 = split(near_b, far_b, (p * ((dp - delta) * scale)).astype(BF16), nb)
            out_ref[:, head_cols(h)] = jnp.dot(p2, v2, preferred_element_type=F32).astype(BF16)
            gq_ref[:, head_cols(h)] = jnp.dot(ds2, k2, preferred_element_type=F32).astype(BF16)
            ps.append(p2)
            ds.append(ds2)
        for copy in copies(n):
            copy.start()
        k_grad = jnp.dot(qt_ref[k_cols, :], jnp.concatenate(ds, axis=0), preferred_element_type=F32).T
        v_grad = jnp.dot(gt_ref[k_cols, :], jnp.concatenate(ps, axis=0), preferred_element_type=F32).T
        grad_ref[:, k_cols] = k_grad[:rows]
        grad_ref[:, v_cols] = v_grad[:rows]
        far_ref[:, k_cols] = k_grad[rows:].astype(BF16)
        far_ref[:, v_cols] = v_grad[rows:].astype(BF16)
        scale_ref[pl.ds(n, 1), :] = jnp.sum(k_grad * jnp.concatenate(kd, axis=0), axis=0, keepdims=True)
        scale_ref[pl.ds(kv_heads + n, 1), :] = jnp.sum(
            v_grad * jnp.concatenate(vd, axis=0), axis=0, keepdims=True
        )
        return carry

    lax.fori_loop(0, kv_heads, step, 0, unroll=True)
    for n in range(kv_heads):
        for copy in copies(n):
            copy.wait()


def finish_kernel(nb, grad_ref, slope_ref, part_ref, *rest):
    others, backs, (gk_ref, gv_ref, gs_ref) = rest[:3], rest[3:3 + nb], rest[3 + nb:]
    gs_ref[...] = (part_ref[...] + others[0][...]) + (others[1][...] + others[2][...])
    width = gk_ref.shape[1]
    for side, out in ((0, gk_ref), (1, gv_ref)):
        at = slice(side * width, (side + 1) * width)
        total = grad_ref[:, at]
        for back in backs:
            total = total + back[:, at].astype(F32)
        out[...] = (total * slope_ref[:, at]).astype(BF16)


def all_sum(part, dp_count, seq_count):
    axes = ("dp", "seq")
    count = dp_count * seq_count

    def exchange(array, mask):
        return lax.ppermute(array, axes, [(i, i ^ mask) for i in range(count)])

    core = seq_count
    bits = [1 << b for b in range(count.bit_length() - 1) if (1 << b) != core]
    part = part + exchange(part, core)
    if len(bits) % 2:
        part = part + exchange(part, bits[0])
        bits = bits[1:]
    for low, high in reversed(list(zip(bits[::2], bits[1::2]))):
        far, mid, near = exchange(part, low | high), exchange(part, high), exchange(part, low)
        terms = [part, near, mid, far]
        part = (part + near) + (mid + far)
    return terms


def on_device(sizes, queries, keys, values, grad_out, quant_scale, doc_lengths):
    dp_count, seq_count = sizes
    nb = max(1, seq_count // 2)
    rows, width = keys.shape
    kv_heads, hd = quant_scale.shape[1], quant_scale.shape[2]
    heads = queries.shape[1] // hd
    vmem = pl.BlockSpec(memory_space=pltpu.VMEM)
    hbm = pl.BlockSpec(memory_space=pltpu.HBM)
    params = pltpu.CompilerParams(vmem_limit_bytes=36 * 1024 * 1024)
    shape = jax.ShapeDtypeStruct
    work = rows * rows * queries.shape[1]

    def call(kernel, name, flops, args, outs, in_specs=None, out_specs=None, scratch=()):
        return pl.pallas_call(
            kernel,
            out_shape=outs,
            in_specs=in_specs or [vmem] * len(args),
            out_specs=out_specs or (vmem,) * len(outs),
            scratch_shapes=scratch,
            compiler_params=params,
            cost_estimate=pl.CostEstimate(flops=flops, bytes_accessed=16 * rows * width, transcendentals=0),
            name=name,
        )(*args)

    def shift(array, d):
        return lax.ppermute(array, "seq", [(r, (r + d) % seq_count) for r in range(seq_count)])

    def unshift(array, d):
        return lax.ppermute(array, "seq", [((r + d) % seq_count, r) for r in range(seq_count)])

    far_k = [shift(keys, d) for d in range(1, nb + 1)]
    far_v = [shift(values, d) for d in range(1, nb + 1)]

    raw = (queries, grad_out, keys, values, quant_scale, doc_lengths)
    q, g, qt, gt, quants, slopes, dclips, bias, clips = call(
        functools.partial(prep_kernel, nb),
        "prep",
        2 * work,
        [pltpu.with_memory_space_constraint(x, pltpu.HBM) for x in raw],
        (
            shape(queries.shape, BF16),
            shape(queries.shape, BF16),
            shape((width, heads // kv_heads * rows), BF16),
            shape((width, heads // kv_heads * rows), BF16),
            shape((rows, 2 * width), BF16),
            shape((rows, 2 * width), F32),
            shape((rows, 2 * width), F32),
            shape((rows, nb * rows), F32),
            shape(quant_scale.shape, F32),
        ),
        in_specs=[hbm] * 6,
        scratch=[
            pltpu.VMEM(keys.shape, BF16),
            pltpu.VMEM(values.shape, BF16),
            pltpu.SMEM(doc_lengths.shape, jnp.int32),
            pltpu.SemaphoreType.DMA((6,)),
        ],
    )
    attn_out, grad_queries, grads, far_grads, scale_part = call(
        functools.partial(attend_kernel, nb),
        "attend",
        12 * (nb + 1) * work,
        (q, g, qt, gt, quants, dclips, bias, clips, *far_k, *far_v),
        (
            shape(queries.shape, BF16),
            shape(queries.shape, BF16),
            shape((rows, 2 * width), F32),
            shape((nb * rows, 2 * width), BF16),
            shape((2 * kv_heads, hd), F32),
        ),
        out_specs=(hbm, hbm, vmem, vmem, vmem),
        scratch=[
            pltpu.VMEM(queries.shape, BF16),
            pltpu.VMEM(queries.shape, BF16),
            pltpu.SemaphoreType.DMA((2, kv_heads)),
        ],
    )
    backs = []
    for d in range(1, nb + 1):
        at = far_order(nb).index(d) * rows
        backs.append(unshift(lax.slice_in_dim(far_grads, at, at + rows, axis=0), d))
    terms = all_sum(scale_part, dp_count, seq_count)
    grad_keys, grad_values, grad_scale = call(
        functools.partial(finish_kernel, nb),
        "finish",
        6 * rows * width,
        (grads, slopes, *terms, *backs),
        (shape((rows, width), BF16), shape((rows, width), BF16), shape(scale_part.shape, F32)),
    )
    return (attn_out, grad_queries, grad_keys, grad_values, grad_scale.reshape(quant_scale.shape))


def solution(mesh):
    rows = P(("dp", "seq"), None)
    return jax.shard_map(
        functools.partial(on_device, (mesh.shape["dp"], mesh.shape["seq"])),
        mesh=mesh,
        in_specs=(rows, rows, rows, rows, P(), P("dp", None)),
        out_specs=(rows, rows, rows, rows, P()),
        check_vma=False,
    )
```

```python
import functools
import math

import jax
import jax.numpy as jnp
from jax import lax
from jax.experimental import pallas as pl
from jax.experimental.pallas import tpu as pltpu
from jax.sharding import PartitionSpec as P

F32 = jnp.float32
BF16 = jnp.bfloat16
LEVELS = 127.0
NEG = -1e30


def sin_cos_half(u):
    r = (u - jnp.round(u)) * math.pi
    z = r * r
    s = z * (1.0 / 6227020800.0) - 1.0 / 39916800.0
    for c in (1.0 / 362880.0, -1.0 / 5040.0, 1.0 / 120.0, -1.0 / 6.0, 1.0):
        s = s * z + c
    s = s * r
    k = z * (1.0 / 479001600.0) - 1.0 / 3628800.0
    for c in (1.0 / 40320.0, -1.0 / 720.0, 1.0 / 24.0, -0.5, 1.0):
        k = k * z + c
    return s, k


def quant_parts(x, clip):
    inv = 1.0 / clip
    ratio = x * inv
    t = jnp.tanh(ratio)
    u = LEVELS * t
    s, k = sin_cos_half(u)
    level = u - s * k * (1.0 / math.pi)
    unit = level * (1.0 / LEVELS)
    slope = (2.0 * s * s) * (1.0 - t * t)
    return clip * unit, slope, unit - slope * ratio


def prep_kernel(nb, q_hbm, g_hbm, key_hbm, value_hbm, clip_hbm, len_hbm, q_ref, g_ref, qt_ref, gt_ref, quant_ref,
                slope_ref, dclip_ref, bias_ref, clip_out, key_ref, value_ref, len_ref, sems):
    small = [
        pltpu.make_async_copy(src, dst, sems.at[i])
        for i, (src, dst) in enumerate(
            ((len_hbm, len_ref), (clip_hbm, clip_out), (key_hbm, key_ref), (value_hbm, value_ref))
        )
    ]
    large = [
        pltpu.make_async_copy(q_hbm, q_ref, sems.at[4]),
        pltpu.make_async_copy(g_hbm, g_ref, sems.at[5]),
    ]
    for copy in small + large:
        copy.start()
    rows = key_ref.shape[0]
    kv_heads, hd = clip_out.shape[1], clip_out.shape[2]
    group = q_ref.shape[1] // kv_heads
    base = lax.axis_index("seq") * rows
    for copy in small:
        copy.wait()
    for side, src in ((0, key_ref), (1, value_ref)):
        for n in range(kv_heads):
            x = src[:, n * hd:(n + 1) * hd].astype(F32)
            q, slope, dclip = quant_parts(x, clip_out[side, n:n + 1, :])
            at = slice((side * kv_heads + n) * hd, (side * kv_heads + n + 1) * hd)
            quant_ref[:, at] = q.astype(BF16)
            slope_ref[:, at] = slope
            dclip_ref[:, at] = dclip
    row = lax.broadcasted_iota(jnp.int32, (rows, rows), 0)
    col = lax.broadcasted_iota(jnp.int32, (rows, rows), 1)
    start = jnp.zeros((rows, rows), jnp.int32)
    end = jnp.int32(0)
    for d in range(len_ref.shape[1]):
        end = end + len_ref[0, d]
        start = jnp.where(row + base >= end, end, start)
    for b in range(nb):
        if b == 0:
            pos = jnp.where(col <= row, col, col - nb * rows)
        else:
            pos = col - b * rows
        bias_ref[:, b * rows:(b + 1) * rows] = jnp.where(pos + base >= start, 0.0, NEG)
    for copy, src, dst in zip(large, (q_ref, g_ref), (qt_ref, gt_ref)):
        copy.wait()
        for n in range(kv_heads):
            for h in range(group // hd):
                at = n * group + h * hd
                dst[n * hd:(n + 1) * hd, h * rows:(h + 1) * rows] = src[:, at:at + hd].T


ACROSS = (((1,), (1,)), ((), ()))


def far_order(nb):
    return [nb] + list(range(1, nb))


def near_mask(rows):
    row = lax.broadcasted_iota(jnp.int32, (rows, rows), 0)
    col = lax.broadcasted_iota(jnp.int32, (rows, rows), 1)
    return col <= row


def merge(near, x, nb):
    rows = near.shape[0]
    first = jnp.where(near, x[:, :rows], x[:, rows:2 * rows])
    return jnp.concatenate([first, x[:, 2 * rows:]], axis=1) if nb > 1 else first


def split(near_b, far_b, x, nb):
    rows = near_b.shape[0]
    parts = [x[:, :rows] * near_b, x[:, :rows] * far_b]
    if nb > 1:
        parts.append(x[:, rows:])
    return jnp.concatenate(parts, axis=1)


def attend_kernel(nb, q_ref, g_ref, qt_ref, gt_ref, quant_ref, dclip_ref, bias_ref, clip_ref, *rest):
    far_k, far_v = rest[:nb], rest[nb:2 * nb]
    out_hbm, gq_hbm, grad_ref, far_ref, spread_ref, out_ref, gq_ref, scale_ref, sems = rest[2 * nb:]
    kv_heads, hd = clip_ref.shape[1], clip_ref.shape[2]
    rows, group = q_ref.shape[0], q_ref.shape[1] // kv_heads
    heads = group // hd
    width = kv_heads * hd
    scale = hd ** -0.5
    log2e = math.log2(math.e)
    near = near_mask(rows)
    near_b = near.astype(F32).astype(BF16)
    far_b = 1.0 - near_b

    def copies(n):
        cols = pl.ds(pl.multiple_of(n * group, group), group)
        return (
            pltpu.make_async_copy(out_ref.at[:, cols], out_hbm.at[:, cols], sems.at[0, n]),
            pltpu.make_async_copy(gq_ref.at[:, cols], gq_hbm.at[:, cols], sems.at[1, n]),
        )

    def step(n, carry):
        k_cols = pl.ds(pl.multiple_of(n * hd, hd), hd)
        v_cols = pl.ds(pl.multiple_of(width + n * hd, hd), hd)
        k_clip = clip_ref[0, pl.ds(n, 1), :]
        v_clip = clip_ref[1, pl.ds(n, 1), :]
        ks, vs = [quant_ref[:, k_cols]], [quant_ref[:, v_cols]]
        kd, vd = [dclip_ref[:, k_cols]], [dclip_ref[:, v_cols]]
        for d in far_order(nb):
            q, _, dc = quant_parts(far_k[d - 1][:, k_cols].astype(F32), k_clip)
            ks.append(q.astype(BF16))
            kd.append(dc)
            q, _, dc = quant_parts(far_v[d - 1][:, k_cols].astype(F32), v_clip)
            vs.append(q.astype(BF16))
            vd.append(dc)
        k2 = jnp.concatenate(ks, axis=0)
        v2 = jnp.concatenate(vs, axis=0)

        def head_cols(h):
            return pl.ds(pl.multiple_of(n * group + h * hd, hd), hd)

        qs = jnp.concatenate([q_ref[:, head_cols(h)] for h in range(heads)], axis=0)
        gs = jnp.concatenate([g_ref[:, head_cols(h)] for h in range(heads)], axis=0)
        s_all = lax.dot_general(qs, k2, ACROSS, preferred_element_type=F32)
        d_all = lax.dot_general(gs, v2, ACROSS, preferred_element_type=F32)
        bias = bias_ref[...]
        ps, ds = [], []
        for h in range(heads):
            at = slice(h * rows, (h + 1) * rows)
            s = merge(near, s_all[at], nb) * (scale * log2e) + bias
            dp = merge(near, d_all[at], nb)
            w = jnp.exp2(s - jnp.max(s, axis=1, keepdims=True))
            inv = 1.0 / jnp.sum(w, axis=1, keepdims=True)
            p = w * inv
            delta = jnp.sum(p * dp, axis=1, keepdims=True)
            p2 = split(near_b, far_b, p.astype(BF16), nb)
            ds2 = split(near_b, far_b, (p * ((dp - delta) * scale)).astype(BF16), nb)
            out_ref[:, head_cols(h)] = jnp.dot(p2, v2, preferred_element_type=F32).astype(BF16)
            gq_ref[:, head_cols(h)] = jnp.dot(ds2, k2, preferred_element_type=F32).astype(BF16)
            ps.append(p2)
            ds.append(ds2)
        for copy in copies(n):
            copy.start()
        k_grad = jnp.dot(qt_ref[k_cols, :], jnp.concatenate(ds, axis=0), preferred_element_type=F32).T
        v_grad = jnp.dot(gt_ref[k_cols, :], jnp.concatenate(ps, axis=0), preferred_element_type=F32).T
        grad_ref[:, k_cols] = k_grad[:rows]
        grad_ref[:, v_cols] = v_grad[:rows]
        far_ref[:, k_cols] = k_grad[rows:].astype(BF16)
        far_ref[:, v_cols] = v_grad[rows:].astype(BF16)
        scale_ref[pl.ds(n, 1), :] = jnp.sum(k_grad * jnp.concatenate(kd, axis=0), axis=0, keepdims=True)
        scale_ref[pl.ds(kv_heads + n, 1), :] = jnp.sum(
            v_grad * jnp.concatenate(vd, axis=0), axis=0, keepdims=True
        )
        return carry

    lax.fori_loop(0, kv_heads, step, 0, unroll=True)
    part = scale_ref[...]

    def spread(i, carry):
        spread_ref[i] = part
        return carry

    lax.fori_loop(0, spread_ref.shape[0], spread, 0)
    for n in range(kv_heads):
        for copy in copies(n):
            copy.wait()


def finish_kernel(nb, grad_ref, slope_ref, parts_ref, *rest):
    backs, (gk_ref, gv_ref, gs_ref) = rest[:nb], rest[nb:]
    gs_ref[...] = jnp.sum(parts_ref[...], axis=0)
    width = gk_ref.shape[1]
    for side, out in ((0, gk_ref), (1, gv_ref)):
        at = slice(side * width, (side + 1) * width)
        total = grad_ref[:, at]
        for back in backs:
            total = total + back[:, at].astype(F32)
        out[...] = (total * slope_ref[:, at]).astype(BF16)


def on_device(sizes, queries, keys, values, grad_out, quant_scale, doc_lengths):
    dp_count, seq_count = sizes
    nb = max(1, seq_count // 2)
    rows, width = keys.shape
    kv_heads, hd = quant_scale.shape[1], quant_scale.shape[2]
    heads = queries.shape[1] // hd
    vmem = pl.BlockSpec(memory_space=pltpu.VMEM)
    hbm = pl.BlockSpec(memory_space=pltpu.HBM)
    params = pltpu.CompilerParams(vmem_limit_bytes=36 * 1024 * 1024)
    shape = jax.ShapeDtypeStruct
    work = rows * rows * queries.shape[1]

    def call(kernel, name, flops, args, outs, in_specs=None, out_specs=None, scratch=()):
        return pl.pallas_call(
            kernel,
            out_shape=outs,
            in_specs=in_specs or [vmem] * len(args),
            out_specs=out_specs or (vmem,) * len(outs),
            scratch_shapes=scratch,
            compiler_params=params,
            cost_estimate=pl.CostEstimate(flops=flops, bytes_accessed=16 * rows * width, transcendentals=0),
            name=name,
        )(*args)

    def shift(array, d):
        return lax.ppermute(array, "seq", [(r, (r + d) % seq_count) for r in range(seq_count)])

    def unshift(array, d):
        return lax.ppermute(array, "seq", [((r + d) % seq_count, r) for r in range(seq_count)])

    far_k = [shift(keys, d) for d in range(1, nb + 1)]
    far_v = [shift(values, d) for d in range(1, nb + 1)]

    raw = (queries, grad_out, keys, values, quant_scale, doc_lengths)
    q, g, qt, gt, quants, slopes, dclips, bias, clips = call(
        functools.partial(prep_kernel, nb),
        "prep",
        2 * work,
        [pltpu.with_memory_space_constraint(x, pltpu.HBM) for x in raw],
        (
            shape(queries.shape, BF16),
            shape(queries.shape, BF16),
            shape((width, heads // kv_heads * rows), BF16),
            shape((width, heads // kv_heads * rows), BF16),
            shape((rows, 2 * width), BF16),
            shape((rows, 2 * width), F32),
            shape((rows, 2 * width), F32),
            shape((rows, nb * rows), F32),
            shape(quant_scale.shape, F32),
        ),
        in_specs=[hbm] * 6,
        scratch=[
            pltpu.VMEM(keys.shape, BF16),
            pltpu.VMEM(values.shape, BF16),
            pltpu.SMEM(doc_lengths.shape, jnp.int32),
            pltpu.SemaphoreType.DMA((6,)),
        ],
    )
    attn_out, grad_queries, grads, far_grads, spread = call(
        functools.partial(attend_kernel, nb),
        "attend",
        12 * (nb + 1) * work,
        (q, g, qt, gt, quants, dclips, bias, clips, *far_k, *far_v),
        (
            shape(queries.shape, BF16),
            shape(queries.shape, BF16),
            shape((rows, 2 * width), F32),
            shape((nb * rows, 2 * width), BF16),
            shape((dp_count * seq_count, 2 * kv_heads, hd), F32),
        ),
        out_specs=(hbm, hbm, vmem, vmem, vmem),
        scratch=[
            pltpu.VMEM(queries.shape, BF16),
            pltpu.VMEM(queries.shape, BF16),
            pltpu.VMEM((2 * kv_heads, hd), F32),
            pltpu.SemaphoreType.DMA((2, kv_heads)),
        ],
    )
    backs = []
    for d in range(1, nb + 1):
        at = far_order(nb).index(d) * rows
        backs.append(unshift(lax.slice_in_dim(far_grads, at, at + rows, axis=0), d))
    parts = lax.all_to_all(spread, ("dp", "seq"), split_axis=0, concat_axis=0, tiled=True)
    grad_keys, grad_values, grad_scale = call(
        functools.partial(finish_kernel, nb),
        "finish",
        6 * rows * width,
        (grads, slopes, parts, *backs),
        (shape((rows, width), BF16), shape((rows, width), BF16), shape(parts.shape[1:], F32)),
    )
    return (attn_out, grad_queries, grad_keys, grad_values, grad_scale.reshape(quant_scale.shape))


def solution(mesh):
    rows = P(("dp", "seq"), None)
    return jax.shard_map(
        functools.partial(on_device, (mesh.shape["dp"], mesh.shape["seq"])),
        mesh=mesh,
        in_specs=(rows, rows, rows, rows, P(), P("dp", None)),
        out_specs=(rows, rows, rows, rows, P()),
        check_vma=False,
    )
```

```python
import functools
import math

import jax
import jax.numpy as jnp
from jax import lax
from jax.experimental import pallas as pl
from jax.experimental.pallas import tpu as pltpu
from jax.sharding import PartitionSpec as P

F32 = jnp.float32
BF16 = jnp.bfloat16
LEVELS = 127.0
NEG = -1e30


def sin_cos_half(u):
    r = (u - jnp.round(u)) * math.pi
    z = r * r
    s = z * (1.0 / 6227020800.0) - 1.0 / 39916800.0
    for c in (1.0 / 362880.0, -1.0 / 5040.0, 1.0 / 120.0, -1.0 / 6.0, 1.0):
        s = s * z + c
    s = s * r
    k = z * (1.0 / 479001600.0) - 1.0 / 3628800.0
    for c in (1.0 / 40320.0, -1.0 / 720.0, 1.0 / 24.0, -0.5, 1.0):
        k = k * z + c
    return s, k


def quant_parts(x, clip):
    inv = 1.0 / clip
    ratio = x * inv
    t = jnp.tanh(ratio)
    u = LEVELS * t
    s, k = sin_cos_half(u)
    level = u - s * k * (1.0 / math.pi)
    unit = level * (1.0 / LEVELS)
    slope = (2.0 * s * s) * (1.0 - t * t)
    return clip * unit, slope, unit - slope * ratio


def prep_kernel(nb, q_hbm, g_hbm, key_hbm, value_hbm, clip_hbm, len_hbm, q_ref, g_ref, qt_ref, gt_ref, quant_ref,
                slope_ref, dclip_ref, bias_ref, clip_out, key_ref, value_ref, len_ref, sems):
    small = [
        pltpu.make_async_copy(src, dst, sems.at[i])
        for i, (src, dst) in enumerate(
            ((len_hbm, len_ref), (clip_hbm, clip_out), (key_hbm, key_ref), (value_hbm, value_ref))
        )
    ]
    large = [
        pltpu.make_async_copy(q_hbm, q_ref, sems.at[4]),
        pltpu.make_async_copy(g_hbm, g_ref, sems.at[5]),
    ]
    for copy in small + large:
        copy.start()
    rows = key_ref.shape[0]
    kv_heads, hd = clip_out.shape[1], clip_out.shape[2]
    group = q_ref.shape[1] // kv_heads
    base = lax.axis_index("seq") * rows
    for copy in small:
        copy.wait()
    for side, src in ((0, key_ref), (1, value_ref)):
        for n in range(kv_heads):
            x = src[:, n * hd:(n + 1) * hd].astype(F32)
            q, slope, dclip = quant_parts(x, clip_out[side, n:n + 1, :])
            at = slice((side * kv_heads + n) * hd, (side * kv_heads + n + 1) * hd)
            quant_ref[:, at] = q.astype(BF16)
            slope_ref[:, at] = slope
            dclip_ref[:, at] = dclip
    row = lax.broadcasted_iota(jnp.int32, (rows, rows), 0)
    col = lax.broadcasted_iota(jnp.int32, (rows, rows), 1)
    start = jnp.zeros((rows, rows), jnp.int32)
    end = jnp.int32(0)
    for d in range(len_ref.shape[1]):
        end = end + len_ref[0, d]
        start = jnp.where(row + base >= end, end, start)
    for b in range(nb):
        if b == 0:
            pos = jnp.where(col <= row, col, col - nb * rows)
        else:
            pos = col - b * rows
        bias_ref[:, b * rows:(b + 1) * rows] = jnp.where(pos + base >= start, 0.0, NEG)
    for copy, src, dst in zip(large, (q_ref, g_ref), (qt_ref, gt_ref)):
        copy.wait()
        for n in range(kv_heads):
            for h in range(group // hd):
                at = n * group + h * hd
                dst[n * hd:(n + 1) * hd, h * rows:(h + 1) * rows] = src[:, at:at + hd].T


ACROSS = (((1,), (1,)), ((), ()))


def far_order(nb):
    return [nb] + list(range(1, nb))


def near_mask(rows):
    row = lax.broadcasted_iota(jnp.int32, (rows, rows), 0)
    col = lax.broadcasted_iota(jnp.int32, (rows, rows), 1)
    return col <= row


def merge(near, x, nb):
    rows = near.shape[0]
    first = jnp.where(near, x[:, :rows], x[:, rows:2 * rows])
    return jnp.concatenate([first, x[:, 2 * rows:]], axis=1) if nb > 1 else first


def split(near_b, far_b, x, nb):
    rows = near_b.shape[0]
    parts = [x[:, :rows] * near_b, x[:, :rows] * far_b]
    if nb > 1:
        parts.append(x[:, rows:])
    return jnp.concatenate(parts, axis=1)


def score_kernel(nb, q_ref, quant_ref, bias_ref, clip_ref, *rest):
    far, (p_ref, k2_ref, dclip_ref) = rest[:nb], rest[nb:]
    kv_heads, hd = clip_ref.shape[1], clip_ref.shape[2]
    rows, group = q_ref.shape[0], q_ref.shape[1] // kv_heads
    heads = group // hd
    factor = hd ** -0.5 * math.log2(math.e)
    near = near_mask(rows)

    def step(n, carry):
        cols = pl.ds(pl.multiple_of(n * hd, hd), hd)
        clip = clip_ref[0, pl.ds(n, 1), :]
        ks = [quant_ref[:, cols]]
        for j, d in enumerate(far_order(nb)):
            q, _, dclip = quant_parts(far[d - 1][:, cols].astype(F32), clip)
            ks.append(q.astype(BF16))
            dclip_ref[j * rows:(j + 1) * rows, cols] = dclip
        k2 = jnp.concatenate(ks, axis=0)
        k2_ref[:, cols] = k2
        qs = jnp.concatenate(
            [q_ref[:, pl.ds(pl.multiple_of(n * group + h * hd, hd), hd)] for h in range(heads)], axis=0
        )
        s_all = lax.dot_general(qs, k2, ACROSS, preferred_element_type=F32)
        bias = bias_ref[...]
        for h in range(heads):
            s = merge(near, s_all[h * rows:(h + 1) * rows], nb) * factor + bias
            w = jnp.exp2(s - jnp.max(s, axis=1, keepdims=True))
            at = pl.ds(pl.multiple_of((n * heads + h) * rows, rows), rows)
            p_ref[at, :] = (w * (1.0 / jnp.sum(w, axis=1, keepdims=True))).astype(BF16)
        return carry

    lax.fori_loop(0, kv_heads, step, 0, unroll=True)


def attend_kernel(nb, g_ref, qt_ref, gt_ref, quant_ref, dclip_ref, clip_ref, p_ref, k2_ref, kdclip_ref, *rest):
    far_v = rest[:nb]
    out_hbm, gq_hbm, grad_ref, far_ref, spread_ref, out_ref, gq_ref, scale_ref, sems = rest[nb:]
    kv_heads, hd = clip_ref.shape[1], clip_ref.shape[2]
    rows, group = g_ref.shape[0], g_ref.shape[1] // kv_heads
    heads = group // hd
    width = kv_heads * hd
    scale = hd ** -0.5
    near = near_mask(rows)
    near_b = near.astype(F32).astype(BF16)
    far_b = 1.0 - near_b

    def copies(n):
        cols = pl.ds(pl.multiple_of(n * group, group), group)
        return (
            pltpu.make_async_copy(out_ref.at[:, cols], out_hbm.at[:, cols], sems.at[0, n]),
            pltpu.make_async_copy(gq_ref.at[:, cols], gq_hbm.at[:, cols], sems.at[1, n]),
        )

    def step(n, carry):
        k_cols = pl.ds(pl.multiple_of(n * hd, hd), hd)
        v_cols = pl.ds(pl.multiple_of(width + n * hd, hd), hd)
        v_clip = clip_ref[1, pl.ds(n, 1), :]
        vs, vd = [quant_ref[:, v_cols]], [dclip_ref[:, v_cols]]
        for d in far_order(nb):
            q, _, dc = quant_parts(far_v[d - 1][:, k_cols].astype(F32), v_clip)
            vs.append(q.astype(BF16))
            vd.append(dc)
        k2 = k2_ref[:, k_cols]
        v2 = jnp.concatenate(vs, axis=0)

        def head_cols(h):
            return pl.ds(pl.multiple_of(n * group + h * hd, hd), hd)

        gs = jnp.concatenate([g_ref[:, head_cols(h)] for h in range(heads)], axis=0)
        d_all = lax.dot_general(gs, v2, ACROSS, preferred_element_type=F32)
        ps, ds = [], []
        for h in range(heads):
            at = slice(h * rows, (h + 1) * rows)
            dp = merge(near, d_all[at], nb)
            p_b = p_ref[pl.ds(pl.multiple_of((n * heads + h) * rows, rows), rows), :]
            p = p_b.astype(F32)
            delta = jnp.sum(p * dp, axis=1, keepdims=True)
            p2 = split(near_b, far_b, p_b, nb)
            ds2 = split(near_b, far_b, (p * ((dp - delta) * scale)).astype(BF16), nb)
            out_ref[:, head_cols(h)] = jnp.dot(p2, v2, preferred_element_type=F32).astype(BF16)
            gq_ref[:, head_cols(h)] = jnp.dot(ds2, k2, preferred_element_type=F32).astype(BF16)
            ps.append(p2)
            ds.append(ds2)
        for copy in copies(n):
            copy.start()
        k_grad = jnp.dot(qt_ref[k_cols, :], jnp.concatenate(ds, axis=0), preferred_element_type=F32).T
        v_grad = jnp.dot(gt_ref[k_cols, :], jnp.concatenate(ps, axis=0), preferred_element_type=F32).T
        grad_ref[:, k_cols] = k_grad[:rows]
        grad_ref[:, v_cols] = v_grad[:rows]
        far_ref[:, k_cols] = k_grad[rows:].astype(BF16)
        far_ref[:, v_cols] = v_grad[rows:].astype(BF16)
        scale_ref[pl.ds(n, 1), :] = jnp.sum(k_grad[:rows] * dclip_ref[:, k_cols], axis=0, keepdims=True) + jnp.sum(
            k_grad[rows:] * kdclip_ref[:, k_cols], axis=0, keepdims=True
        )
        scale_ref[pl.ds(kv_heads + n, 1), :] = jnp.sum(
            v_grad * jnp.concatenate(vd, axis=0), axis=0, keepdims=True
        )
        return carry

    lax.fori_loop(0, kv_heads, step, 0, unroll=True)
    part = scale_ref[...].astype(BF16)

    def spread(i, carry):
        spread_ref[i] = part
        return carry

    lax.fori_loop(0, spread_ref.shape[0], spread, 0)
    for n in range(kv_heads):
        for copy in copies(n):
            copy.wait()


def finish_kernel(nb, grad_ref, slope_ref, parts_ref, *rest):
    backs, (gk_ref, gv_ref, gs_ref) = rest[:nb], rest[nb:]
    gs_ref[...] = jnp.sum(parts_ref[...].astype(F32), axis=0)
    width = gk_ref.shape[1]
    for side, out in ((0, gk_ref), (1, gv_ref)):
        at = slice(side * width, (side + 1) * width)
        total = grad_ref[:, at]
        for back in backs:
            total = total + back[:, at].astype(F32)
        out[...] = (total * slope_ref[:, at]).astype(BF16)


def on_device(sizes, queries, keys, values, grad_out, quant_scale, doc_lengths):
    dp_count, seq_count = sizes
    nb = max(1, seq_count // 2)
    rows, width = keys.shape
    kv_heads, hd = quant_scale.shape[1], quant_scale.shape[2]
    heads = queries.shape[1] // hd
    vmem = pl.BlockSpec(memory_space=pltpu.VMEM)
    hbm = pl.BlockSpec(memory_space=pltpu.HBM)
    params = pltpu.CompilerParams(vmem_limit_bytes=36 * 1024 * 1024)
    shape = jax.ShapeDtypeStruct
    work = rows * rows * queries.shape[1]

    def call(kernel, name, flops, args, outs, in_specs=None, out_specs=None, scratch=()):
        return pl.pallas_call(
            kernel,
            out_shape=outs,
            in_specs=in_specs or [vmem] * len(args),
            out_specs=out_specs or (vmem,) * len(outs),
            scratch_shapes=scratch,
            compiler_params=params,
            cost_estimate=pl.CostEstimate(flops=flops, bytes_accessed=16 * rows * width, transcendentals=0),
            name=name,
        )(*args)

    def shift(array, d):
        return lax.ppermute(array, "seq", [(r, (r + d) % seq_count) for r in range(seq_count)])

    def unshift(array, d):
        return lax.ppermute(array, "seq", [((r + d) % seq_count, r) for r in range(seq_count)])

    far_k = [shift(keys, d) for d in range(1, nb + 1)]
    far_v = [shift(values, d) for d in range(1, nb + 1)]

    raw = (queries, grad_out, keys, values, quant_scale, doc_lengths)
    q, g, qt, gt, quants, slopes, dclips, bias, clips = call(
        functools.partial(prep_kernel, nb),
        "prep",
        2 * work,
        [pltpu.with_memory_space_constraint(x, pltpu.HBM) for x in raw],
        (
            shape(queries.shape, BF16),
            shape(queries.shape, BF16),
            shape((width, heads // kv_heads * rows), BF16),
            shape((width, heads // kv_heads * rows), BF16),
            shape((rows, 2 * width), BF16),
            shape((rows, 2 * width), F32),
            shape((rows, 2 * width), F32),
            shape((rows, nb * rows), F32),
            shape(quant_scale.shape, F32),
        ),
        in_specs=[hbm] * 6,
        scratch=[
            pltpu.VMEM(keys.shape, BF16),
            pltpu.VMEM(values.shape, BF16),
            pltpu.SMEM(doc_lengths.shape, jnp.int32),
            pltpu.SemaphoreType.DMA((6,)),
        ],
    )
    p, k2, kdclips = call(
        functools.partial(score_kernel, nb),
        "score",
        2 * (nb + 1) * work,
        (q, quants, bias, clips, *far_k),
        (
            shape((heads * rows, nb * rows), BF16),
            shape(((nb + 1) * rows, width), BF16),
            shape((nb * rows, width), F32),
        ),
    )
    attn_out, grad_queries, grads, far_grads, spread = call(
        functools.partial(attend_kernel, nb),
        "attend",
        10 * (nb + 1) * work,
        (g, qt, gt, quants, dclips, clips, p, k2, kdclips, *far_v),
        (
            shape(queries.shape, BF16),
            shape(queries.shape, BF16),
            shape((rows, 2 * width), F32),
            shape((nb * rows, 2 * width), BF16),
            shape((dp_count * seq_count, 2 * kv_heads, hd), BF16),
        ),
        out_specs=(hbm, hbm, vmem, vmem, vmem),
        scratch=[
            pltpu.VMEM(queries.shape, BF16),
            pltpu.VMEM(queries.shape, BF16),
            pltpu.VMEM((2 * kv_heads, hd), F32),
            pltpu.SemaphoreType.DMA((2, kv_heads)),
        ],
    )
    backs = []
    for d in range(1, nb + 1):
        at = far_order(nb).index(d) * rows
        backs.append(unshift(lax.slice_in_dim(far_grads, at, at + rows, axis=0), d))
    parts = lax.all_to_all(spread, ("dp", "seq"), split_axis=0, concat_axis=0, tiled=True)
    grad_keys, grad_values, grad_scale = call(
        functools.partial(finish_kernel, nb),
        "finish",
        6 * rows * width,
        (grads, slopes, parts, *backs),
        (shape((rows, width), BF16), shape((rows, width), BF16), shape(parts.shape[1:], F32)),
    )
    return (attn_out, grad_queries, grad_keys, grad_values, grad_scale.reshape(quant_scale.shape))


def solution(mesh):
    rows = P(("dp", "seq"), None)
    return jax.shard_map(
        functools.partial(on_device, (mesh.shape["dp"], mesh.shape["seq"])),
        mesh=mesh,
        in_specs=(rows, rows, rows, rows, P(), P("dp", None)),
        out_specs=(rows, rows, rows, rows, P()),
        check_vma=False,
    )
```

```python
import functools
import math

import jax
import jax.numpy as jnp
from jax import lax
from jax.experimental import pallas as pl
from jax.experimental.pallas import tpu as pltpu
from jax.sharding import PartitionSpec as P

F32 = jnp.float32
BF16 = jnp.bfloat16
LEVELS = 127.0
NEG = -1e30


def sin_cos_half(u):
    r = (u - jnp.round(u)) * math.pi
    z = r * r
    s = z * (1.0 / 6227020800.0) - 1.0 / 39916800.0
    for c in (1.0 / 362880.0, -1.0 / 5040.0, 1.0 / 120.0, -1.0 / 6.0, 1.0):
        s = s * z + c
    s = s * r
    k = z * (1.0 / 479001600.0) - 1.0 / 3628800.0
    for c in (1.0 / 40320.0, -1.0 / 720.0, 1.0 / 24.0, -0.5, 1.0):
        k = k * z + c
    return s, k


def quant_parts(x, clip):
    inv = 1.0 / clip
    ratio = x * inv
    t = jnp.tanh(ratio)
    u = LEVELS * t
    s, k = sin_cos_half(u)
    level = u - s * k * (1.0 / math.pi)
    unit = level * (1.0 / LEVELS)
    slope = (2.0 * s * s) * (1.0 - t * t)
    return clip * unit, slope, unit - slope * ratio


def prep_kernel(nb, q_hbm, g_hbm, key_hbm, value_hbm, clip_hbm, len_hbm, q_ref, g_ref, qt_ref, gt_ref, quant_ref,
                slope_ref, dclip_ref, bias_ref, clip_out, key_ref, value_ref, len_ref, sems):
    small = [
        pltpu.make_async_copy(src, dst, sems.at[i])
        for i, (src, dst) in enumerate(
            ((len_hbm, len_ref), (clip_hbm, clip_out), (key_hbm, key_ref), (value_hbm, value_ref))
        )
    ]
    large = [
        pltpu.make_async_copy(q_hbm, q_ref, sems.at[4]),
        pltpu.make_async_copy(g_hbm, g_ref, sems.at[5]),
    ]
    for copy in small + large:
        copy.start()
    rows = key_ref.shape[0]
    kv_heads, hd = clip_out.shape[1], clip_out.shape[2]
    group = q_ref.shape[1] // kv_heads
    base = lax.axis_index("seq") * rows
    for copy in small:
        copy.wait()
    for side, src in ((0, key_ref), (1, value_ref)):
        for n in range(kv_heads):
            x = src[:, n * hd:(n + 1) * hd].astype(F32)
            q, slope, dclip = quant_parts(x, clip_out[side, n:n + 1, :])
            at = slice((side * kv_heads + n) * hd, (side * kv_heads + n + 1) * hd)
            quant_ref[:, at] = q.astype(BF16)
            slope_ref[:, at] = slope
            dclip_ref[:, at] = dclip
    key = lax.broadcasted_iota(jnp.int32, (rows, rows), 0)
    row = lax.broadcasted_iota(jnp.int32, (rows, rows), 1)
    start = jnp.zeros((rows, rows), jnp.int32)
    end = jnp.int32(0)
    for d in range(len_ref.shape[1]):
        end = end + len_ref[0, d]
        start = jnp.where(row + base >= end, end, start)
    for b in range(nb):
        pos = jnp.where(key <= row, key, key - nb * rows) if b == 0 else key - b * rows
        bias_ref[b * rows:(b + 1) * rows, :] = jnp.where(pos + base >= start, 0.0, NEG)
    for copy, src, dst in zip(large, (q_ref, g_ref), (qt_ref, gt_ref)):
        copy.wait()
        for n in range(kv_heads):
            for h in range(group // hd):
                at = n * group + h * hd
                dst[n * hd:(n + 1) * hd, h * rows:(h + 1) * rows] = src[:, at:at + hd].T


def far_order(nb):
    return [nb] + list(range(1, nb))


def near_mask(rows):
    key = lax.broadcasted_iota(jnp.int32, (rows, rows), 0)
    row = lax.broadcasted_iota(jnp.int32, (rows, rows), 1)
    return key <= row


def merge(near, x, nb):
    rows = near.shape[0]
    first = jnp.where(near, x[:rows], x[rows:2 * rows])
    return jnp.concatenate([first, x[2 * rows:]], axis=0) if nb > 1 else first


def split(near_b, far_b, x, nb):
    rows = near_b.shape[0]
    parts = [x[:rows] * near_b, x[:rows] * far_b]
    if nb > 1:
        parts.append(x[rows:])
    return jnp.concatenate(parts, axis=0)


def score_kernel(nb, qt_ref, quant_ref, bias_ref, clip_ref, *rest):
    far, (p_ref, k2_ref, dclip_ref) = rest[:nb], rest[nb:]
    kv_heads, hd = clip_ref.shape[1], clip_ref.shape[2]
    rows, span = bias_ref.shape[1], qt_ref.shape[1]
    factor = hd ** -0.5 * math.log2(math.e)
    near = near_mask(rows)

    def step(n, carry):
        cols = pl.ds(pl.multiple_of(n * hd, hd), hd)
        clip = clip_ref[0, pl.ds(n, 1), :]
        ks = [quant_ref[:, cols]]
        for j, d in enumerate(far_order(nb)):
            q, _, dclip = quant_parts(far[d - 1][:, cols].astype(F32), clip)
            ks.append(q.astype(BF16))
            dclip_ref[j * rows:(j + 1) * rows, cols] = dclip
        k2 = jnp.concatenate(ks, axis=0)
        k2_ref[:, cols] = k2
        s_all = jnp.dot(k2, qt_ref[cols, :], preferred_element_type=F32)
        bias = bias_ref[...]
        for h in range(span // rows):
            s = merge(near, s_all[:, h * rows:(h + 1) * rows], nb) * factor + bias
            w = jnp.exp2(s - jnp.max(s, axis=0, keepdims=True))
            p = w * (1.0 / jnp.sum(w, axis=0, keepdims=True))
            p_ref[:, pl.ds(pl.multiple_of(n * span + h * rows, rows), rows)] = p.astype(BF16)
        return carry

    lax.fori_loop(0, kv_heads, step, 0, unroll=True)


def attend_kernel(nb, q_ref, g_ref, gt_ref, quant_ref, dclip_ref, clip_ref, p_ref, k2_ref, kdclip_ref, *rest):
    far_v = rest[:nb]
    out_hbm, gq_hbm, grad_ref, far_ref, spread_ref, out_ref, gq_ref, scale_ref, sems = rest[nb:]
    kv_heads, hd = clip_ref.shape[1], clip_ref.shape[2]
    rows, group = g_ref.shape[0], g_ref.shape[1] // kv_heads
    heads = group // hd
    span = heads * rows
    width = kv_heads * hd
    scale = hd ** -0.5
    near = near_mask(rows)
    near_b = near.astype(F32).astype(BF16)
    far_b = 1.0 - near_b

    def copies(n):
        cols = pl.ds(pl.multiple_of(n * group, group), group)
        return (
            pltpu.make_async_copy(out_ref.at[:, cols], out_hbm.at[:, cols], sems.at[0, n]),
            pltpu.make_async_copy(gq_ref.at[:, cols], gq_hbm.at[:, cols], sems.at[1, n]),
        )

    def step(n, carry):
        k_cols = pl.ds(pl.multiple_of(n * hd, hd), hd)
        v_cols = pl.ds(pl.multiple_of(width + n * hd, hd), hd)
        v_clip = clip_ref[1, pl.ds(n, 1), :]
        vs, vd = [quant_ref[:, v_cols]], [dclip_ref[:, v_cols]]
        for d in far_order(nb):
            q, _, dc = quant_parts(far_v[d - 1][:, k_cols].astype(F32), v_clip)
            vs.append(q.astype(BF16))
            vd.append(dc)
        k2 = k2_ref[:, k_cols]
        v2 = jnp.concatenate(vs, axis=0)

        def head_cols(h):
            return pl.ds(pl.multiple_of(n * group + h * hd, hd), hd)

        d_all = jnp.dot(v2, gt_ref[k_cols, :], preferred_element_type=F32)
        ps, ds = [], []
        for h in range(heads):
            dp = merge(near, d_all[:, h * rows:(h + 1) * rows], nb)
            p_b = p_ref[:, pl.ds(pl.multiple_of(n * span + h * rows, rows), rows)]
            p = p_b.astype(F32)
            delta = jnp.sum(p * dp, axis=0, keepdims=True)
            ps.append(split(near_b, far_b, p_b, nb))
            ds.append(split(near_b, far_b, (p * ((dp - delta) * scale)).astype(BF16), nb))
        p2 = jnp.concatenate(ps, axis=1)
        ds2 = jnp.concatenate(ds, axis=1)
        for left, right, dst in ((v2, p2, out_ref), (k2, ds2, gq_ref)):
            y = jnp.dot(left.T, right, preferred_element_type=F32).astype(BF16)
            for h in range(heads):
                dst[:, head_cols(h)] = y[:, h * rows:(h + 1) * rows].T
        for copy in copies(n):
            copy.start()
        qs = jnp.concatenate([q_ref[:, head_cols(h)] for h in range(heads)], axis=0)
        gs = jnp.concatenate([g_ref[:, head_cols(h)] for h in range(heads)], axis=0)
        k_grad = jnp.dot(ds2, qs, preferred_element_type=F32)
        v_grad = jnp.dot(p2, gs, preferred_element_type=F32)
        grad_ref[:, k_cols] = k_grad[:rows]
        grad_ref[:, v_cols] = v_grad[:rows]
        far_ref[:, k_cols] = k_grad[rows:].astype(BF16)
        far_ref[:, v_cols] = v_grad[rows:].astype(BF16)
        scale_ref[pl.ds(n, 1), :] = jnp.sum(k_grad[:rows] * dclip_ref[:, k_cols], axis=0, keepdims=True) + jnp.sum(
            k_grad[rows:] * kdclip_ref[:, k_cols], axis=0, keepdims=True
        )
        scale_ref[pl.ds(kv_heads + n, 1), :] = jnp.sum(
            v_grad * jnp.concatenate(vd, axis=0), axis=0, keepdims=True
        )
        return carry

    lax.fori_loop(0, kv_heads, step, 0, unroll=True)
    part = scale_ref[...].astype(BF16)

    def spread(i, carry):
        spread_ref[i] = part
        return carry

    lax.fori_loop(0, spread_ref.shape[0], spread, 0)
    for n in range(kv_heads):
        for copy in copies(n):
            copy.wait()


def finish_kernel(nb, grad_ref, slope_ref, parts_ref, *rest):
    backs, (gk_ref, gv_ref, gs_ref) = rest[:nb], rest[nb:]
    gs_ref[...] = jnp.sum(parts_ref[...].astype(F32), axis=0)
    width = gk_ref.shape[1]
    for side, out in ((0, gk_ref), (1, gv_ref)):
        at = slice(side * width, (side + 1) * width)
        total = grad_ref[:, at]
        for back in backs:
            total = total + back[:, at].astype(F32)
        out[...] = (total * slope_ref[:, at]).astype(BF16)


def on_device(sizes, queries, keys, values, grad_out, quant_scale, doc_lengths):
    dp_count, seq_count = sizes
    nb = max(1, seq_count // 2)
    rows, width = keys.shape
    kv_heads, hd = quant_scale.shape[1], quant_scale.shape[2]
    heads = queries.shape[1] // hd
    vmem = pl.BlockSpec(memory_space=pltpu.VMEM)
    hbm = pl.BlockSpec(memory_space=pltpu.HBM)
    params = pltpu.CompilerParams(vmem_limit_bytes=36 * 1024 * 1024)
    shape = jax.ShapeDtypeStruct
    work = rows * rows * queries.shape[1]

    def call(kernel, name, flops, args, outs, in_specs=None, out_specs=None, scratch=()):
        return pl.pallas_call(
            kernel,
            out_shape=outs,
            in_specs=in_specs or [vmem] * len(args),
            out_specs=out_specs or (vmem,) * len(outs),
            scratch_shapes=scratch,
            compiler_params=params,
            cost_estimate=pl.CostEstimate(flops=flops, bytes_accessed=16 * rows * width, transcendentals=0),
            name=name,
        )(*args)

    def shift(array, d):
        return lax.ppermute(array, "seq", [(r, (r + d) % seq_count) for r in range(seq_count)])

    def unshift(array, d):
        return lax.ppermute(array, "seq", [((r + d) % seq_count, r) for r in range(seq_count)])

    far_k = [shift(keys, d) for d in range(1, nb + 1)]
    far_v = [shift(values, d) for d in range(1, nb + 1)]

    raw = (queries, grad_out, keys, values, quant_scale, doc_lengths)
    q, g, qt, gt, quants, slopes, dclips, bias, clips = call(
        functools.partial(prep_kernel, nb),
        "prep",
        2 * work,
        [pltpu.with_memory_space_constraint(x, pltpu.HBM) for x in raw],
        (
            shape(queries.shape, BF16),
            shape(queries.shape, BF16),
            shape((width, heads // kv_heads * rows), BF16),
            shape((width, heads // kv_heads * rows), BF16),
            shape((rows, 2 * width), BF16),
            shape((rows, 2 * width), F32),
            shape((rows, 2 * width), F32),
            shape((nb * rows, rows), F32),
            shape(quant_scale.shape, F32),
        ),
        in_specs=[hbm] * 6,
        scratch=[
            pltpu.VMEM(keys.shape, BF16),
            pltpu.VMEM(values.shape, BF16),
            pltpu.SMEM(doc_lengths.shape, jnp.int32),
            pltpu.SemaphoreType.DMA((6,)),
        ],
    )
    p, k2, kdclips = call(
        functools.partial(score_kernel, nb),
        "score",
        2 * (nb + 1) * work,
        (qt, quants, bias, clips, *far_k),
        (
            shape((nb * rows, heads * rows), BF16),
            shape(((nb + 1) * rows, width), BF16),
            shape((nb * rows, width), F32),
        ),
    )
    attn_out, grad_queries, grads, far_grads, spread = call(
        functools.partial(attend_kernel, nb),
        "attend",
        10 * (nb + 1) * work,
        (q, g, gt, quants, dclips, clips, p, k2, kdclips, *far_v),
        (
            shape(queries.shape, BF16),
            shape(queries.shape, BF16),
            shape((rows, 2 * width), F32),
            shape((nb * rows, 2 * width), BF16),
            shape((dp_count * seq_count, 2 * kv_heads, hd), BF16),
        ),
        out_specs=(hbm, hbm, vmem, vmem, vmem),
        scratch=[
            pltpu.VMEM(queries.shape, BF16),
            pltpu.VMEM(queries.shape, BF16),
            pltpu.VMEM((2 * kv_heads, hd), F32),
            pltpu.SemaphoreType.DMA((2, kv_heads)),
        ],
    )
    backs = []
    for d in range(1, nb + 1):
        at = far_order(nb).index(d) * rows
        backs.append(unshift(lax.slice_in_dim(far_grads, at, at + rows, axis=0), d))
    parts = lax.all_to_all(spread, ("dp", "seq"), split_axis=0, concat_axis=0, tiled=True)
    grad_keys, grad_values, grad_scale = call(
        functools.partial(finish_kernel, nb),
        "finish",
        6 * rows * width,
        (grads, slopes, parts, *backs),
        (shape((rows, width), BF16), shape((rows, width), BF16), shape(parts.shape[1:], F32)),
    )
    return (attn_out, grad_queries, grad_keys, grad_values, grad_scale.reshape(quant_scale.shape))


def solution(mesh):
    rows = P(("dp", "seq"), None)
    return jax.shard_map(
        functools.partial(on_device, (mesh.shape["dp"], mesh.shape["seq"])),
        mesh=mesh,
        in_specs=(rows, rows, rows, rows, P(), P("dp", None)),
        out_specs=(rows, rows, rows, rows, P()),
        check_vma=False,
    )
```

```python
import functools
import math

import jax
import jax.numpy as jnp
from jax import lax
from jax.experimental import pallas as pl
from jax.experimental.pallas import tpu as pltpu
from jax.sharding import PartitionSpec as P

F32 = jnp.float32
BF16 = jnp.bfloat16
LEVELS = 127.0
NEG = -1e30


def sin_cos_half(u):
    r = (u - jnp.round(u)) * math.pi
    z = r * r
    s = z * (1.0 / 6227020800.0) - 1.0 / 39916800.0
    for c in (1.0 / 362880.0, -1.0 / 5040.0, 1.0 / 120.0, -1.0 / 6.0, 1.0):
        s = s * z + c
    s = s * r
    k = z * (1.0 / 479001600.0) - 1.0 / 3628800.0
    for c in (1.0 / 40320.0, -1.0 / 720.0, 1.0 / 24.0, -0.5, 1.0):
        k = k * z + c
    return s, k


def quant_parts(x, clip):
    inv = 1.0 / clip
    ratio = x * inv
    t = jnp.tanh(ratio)
    u = LEVELS * t
    s, k = sin_cos_half(u)
    level = u - s * k * (1.0 / math.pi)
    unit = level * (1.0 / LEVELS)
    slope = (2.0 * s * s) * (1.0 - t * t)
    return clip * unit, slope, unit - slope * ratio


def prep_kernel(nb, q_hbm, g_hbm, key_hbm, value_hbm, clip_hbm, len_hbm, q_ref, g_ref, qt_ref, gt_ref, quant_ref,
                slope_ref, dclip_ref, bias_ref, clip_out, key_ref, value_ref, len_ref, sems):
    small = [
        pltpu.make_async_copy(src, dst, sems.at[i])
        for i, (src, dst) in enumerate(
            ((len_hbm, len_ref), (clip_hbm, clip_out), (key_hbm, key_ref), (value_hbm, value_ref))
        )
    ]
    large = [
        pltpu.make_async_copy(q_hbm, q_ref, sems.at[4]),
        pltpu.make_async_copy(g_hbm, g_ref, sems.at[5]),
    ]
    for copy in small + large:
        copy.start()
    rows = key_ref.shape[0]
    kv_heads, hd = clip_out.shape[1], clip_out.shape[2]
    group = q_ref.shape[1] // kv_heads
    base = lax.axis_index("seq") * rows
    for copy in small:
        copy.wait()
    for side, src in ((0, key_ref), (1, value_ref)):
        for n in range(kv_heads):
            x = src[:, n * hd:(n + 1) * hd].astype(F32)
            q, slope, dclip = quant_parts(x, clip_out[side, n:n + 1, :])
            at = slice((side * kv_heads + n) * hd, (side * kv_heads + n + 1) * hd)
            quant_ref[:, at] = q.astype(BF16)
            slope_ref[:, at] = slope
            dclip_ref[:, at] = dclip
    key = lax.broadcasted_iota(jnp.int32, (rows, rows), 0)
    row = lax.broadcasted_iota(jnp.int32, (rows, rows), 1)
    start = jnp.zeros((rows, rows), jnp.int32)
    end = jnp.int32(0)
    for d in range(len_ref.shape[1]):
        end = end + len_ref[0, d]
        start = jnp.where(row + base >= end, end, start)
    for b in range(nb):
        pos = jnp.where(key <= row, key, key - nb * rows) if b == 0 else key - b * rows
        bias_ref[b * rows:(b + 1) * rows, :] = jnp.where(pos + base >= start, 0.0, NEG)
    for copy, src, dst in zip(large, (q_ref, g_ref), (qt_ref, gt_ref)):
        copy.wait()
        for n in range(kv_heads):
            for h in range(group // hd):
                at = n * group + h * hd
                dst[n * hd:(n + 1) * hd, h * rows:(h + 1) * rows] = src[:, at:at + hd].T


def far_order(nb):
    return [nb] + list(range(1, nb))


def near_mask(rows):
    key = lax.broadcasted_iota(jnp.int32, (rows, rows), 0)
    row = lax.broadcasted_iota(jnp.int32, (rows, rows), 1)
    return key <= row


def merge(near, x, nb):
    rows = near.shape[0]
    first = jnp.where(near, x[:rows], x[rows:2 * rows])
    return jnp.concatenate([first, x[2 * rows:]], axis=0) if nb > 1 else first


def split(near_b, far_b, x, nb):
    rows = near_b.shape[0]
    parts = [x[:rows] * near_b, x[:rows] * far_b]
    if nb > 1:
        parts.append(x[rows:])
    return jnp.concatenate(parts, axis=0)


def score_kernel(nb, qt_ref, quant_ref, bias_ref, clip_ref, *rest):
    far, (p_ref, k2_ref, dclip_ref) = rest[:nb], rest[nb:]
    kv_heads, hd = clip_ref.shape[1], clip_ref.shape[2]
    rows, span = bias_ref.shape[1], qt_ref.shape[1]
    factor = hd ** -0.5 * math.log2(math.e)
    near = near_mask(rows)

    def step(n, carry):
        cols = pl.ds(pl.multiple_of(n * hd, hd), hd)
        clip = clip_ref[0, pl.ds(n, 1), :]
        ks = [quant_ref[:, cols]]
        for j, d in enumerate(far_order(nb)):
            q, _, dclip = quant_parts(far[d - 1][:, cols].astype(F32), clip)
            ks.append(q.astype(BF16))
            dclip_ref[j * rows:(j + 1) * rows, cols] = dclip
        k2 = jnp.concatenate(ks, axis=0)
        k2_ref[:, cols] = k2
        s_all = jnp.dot(k2, qt_ref[cols, :], preferred_element_type=F32)
        bias = bias_ref[...]
        for h in range(span // rows):
            s = merge(near, s_all[:, h * rows:(h + 1) * rows], nb) * factor + bias
            w = jnp.exp2(s - jnp.max(s, axis=0, keepdims=True))
            p = w * (1.0 / jnp.sum(w, axis=0, keepdims=True))
            p_ref[:, pl.ds(pl.multiple_of(n * span + h * rows, rows), rows)] = p.astype(BF16)
        return carry

    lax.fori_loop(0, kv_heads, step, 0, unroll=True)


def grad_kernel(nb, q_ref, g_ref, gt_ref, quant_ref, dclip_ref, clip_ref, p_ref, kdclip_ref, *rest):
    far_v, (ds_ref, v2_ref, grad_ref, far_ref, spread_ref, scale_ref) = rest[:nb], rest[nb:]
    kv_heads, hd = clip_ref.shape[1], clip_ref.shape[2]
    rows, group = g_ref.shape[0], g_ref.shape[1] // kv_heads
    heads = group // hd
    span = heads * rows
    width = kv_heads * hd
    scale = hd ** -0.5
    near = near_mask(rows)
    near_b = near.astype(F32).astype(BF16)
    far_b = 1.0 - near_b

    def step(n, carry):
        k_cols = pl.ds(pl.multiple_of(n * hd, hd), hd)
        v_cols = pl.ds(pl.multiple_of(width + n * hd, hd), hd)
        v_clip = clip_ref[1, pl.ds(n, 1), :]
        vs, vd = [quant_ref[:, v_cols]], [dclip_ref[:, v_cols]]
        for d in far_order(nb):
            q, _, dc = quant_parts(far_v[d - 1][:, k_cols].astype(F32), v_clip)
            vs.append(q.astype(BF16))
            vd.append(dc)
        v2 = jnp.concatenate(vs, axis=0)
        v2_ref[:, k_cols] = v2

        def head_cols(h):
            return pl.ds(pl.multiple_of(n * group + h * hd, hd), hd)

        d_all = jnp.dot(v2, gt_ref[k_cols, :], preferred_element_type=F32)
        ps, ds = [], []
        for h in range(heads):
            dp = merge(near, d_all[:, h * rows:(h + 1) * rows], nb)
            at = pl.ds(pl.multiple_of(n * span + h * rows, rows), rows)
            p_b = p_ref[:, at]
            p = p_b.astype(F32)
            delta = jnp.sum(p * dp, axis=0, keepdims=True)
            ds_b = (p * ((dp - delta) * scale)).astype(BF16)
            ds_ref[:, at] = ds_b
            ps.append(split(near_b, far_b, p_b, nb))
            ds.append(split(near_b, far_b, ds_b, nb))
        p2 = jnp.concatenate(ps, axis=1)
        ds2 = jnp.concatenate(ds, axis=1)
        qs = jnp.concatenate([q_ref[:, head_cols(h)] for h in range(heads)], axis=0)
        gs = jnp.concatenate([g_ref[:, head_cols(h)] for h in range(heads)], axis=0)
        k_grad = jnp.dot(ds2, qs, preferred_element_type=F32)
        v_grad = jnp.dot(p2, gs, preferred_element_type=F32)
        grad_ref[:, k_cols] = k_grad[:rows]
        grad_ref[:, v_cols] = v_grad[:rows]
        far_ref[:, k_cols] = k_grad[rows:].astype(BF16)
        far_ref[:, v_cols] = v_grad[rows:].astype(BF16)
        scale_ref[pl.ds(n, 1), :] = jnp.sum(k_grad[:rows] * dclip_ref[:, k_cols], axis=0, keepdims=True) + jnp.sum(
            k_grad[rows:] * kdclip_ref[:, k_cols], axis=0, keepdims=True
        )
        scale_ref[pl.ds(kv_heads + n, 1), :] = jnp.sum(
            v_grad * jnp.concatenate(vd, axis=0), axis=0, keepdims=True
        )
        return carry

    lax.fori_loop(0, kv_heads, step, 0, unroll=True)
    part = scale_ref[...].astype(BF16)

    def spread(i, carry):
        spread_ref[i] = part
        return carry

    lax.fori_loop(0, spread_ref.shape[0], spread, 0)


def output_kernel(nb, p_ref, ds_ref, k2_ref, v2_ref, out_hbm, gq_hbm, out_ref, gq_ref, sems):
    kv_heads = sems.shape[1]
    rows, group = out_ref.shape[0], out_ref.shape[1] // kv_heads
    hd = k2_ref.shape[1] // kv_heads
    heads = group // hd
    near_b = near_mask(rows).astype(F32).astype(BF16)
    far_b = 1.0 - near_b

    def copies(n):
        cols = pl.ds(pl.multiple_of(n * group, group), group)
        return (
            pltpu.make_async_copy(out_ref.at[:, cols], out_hbm.at[:, cols], sems.at[0, n]),
            pltpu.make_async_copy(gq_ref.at[:, cols], gq_hbm.at[:, cols], sems.at[1, n]),
        )

    def step(n, carry):
        cols = pl.ds(pl.multiple_of(n * hd, hd), hd)
        for left, right, dst in ((v2_ref, p_ref, out_ref), (k2_ref, ds_ref, gq_ref)):
            at = pl.ds(pl.multiple_of(n * heads * rows, rows), heads * rows)
            x = right[:, at]
            x2 = jnp.concatenate(
                [split(near_b, far_b, x[:, h * rows:(h + 1) * rows], nb) for h in range(heads)], axis=1
            )
            y = jnp.dot(left[:, cols].T, x2, preferred_element_type=F32).astype(BF16)
            for h in range(heads):
                dst[:, pl.ds(pl.multiple_of(n * group + h * hd, hd), hd)] = y[:, h * rows:(h + 1) * rows].T
        for copy in copies(n):
            copy.start()
        return carry

    lax.fori_loop(0, kv_heads, step, 0, unroll=True)
    for n in range(kv_heads):
        for copy in copies(n):
            copy.wait()


def finish_kernel(nb, grad_ref, slope_ref, parts_ref, *rest):
    backs, (gk_ref, gv_ref, gs_ref) = rest[:nb], rest[nb:]
    gs_ref[...] = jnp.sum(parts_ref[...].astype(F32), axis=0)
    width = gk_ref.shape[1]
    for side, out in ((0, gk_ref), (1, gv_ref)):
        at = slice(side * width, (side + 1) * width)
        total = grad_ref[:, at]
        for back in backs:
            total = total + back[:, at].astype(F32)
        out[...] = (total * slope_ref[:, at]).astype(BF16)


def on_device(sizes, queries, keys, values, grad_out, quant_scale, doc_lengths):
    dp_count, seq_count = sizes
    nb = max(1, seq_count // 2)
    rows, width = keys.shape
    kv_heads, hd = quant_scale.shape[1], quant_scale.shape[2]
    heads = queries.shape[1] // hd
    vmem = pl.BlockSpec(memory_space=pltpu.VMEM)
    hbm = pl.BlockSpec(memory_space=pltpu.HBM)
    params = pltpu.CompilerParams(vmem_limit_bytes=36 * 1024 * 1024)
    shape = jax.ShapeDtypeStruct
    work = rows * rows * queries.shape[1]

    def call(kernel, name, flops, args, outs, in_specs=None, out_specs=None, scratch=()):
        return pl.pallas_call(
            kernel,
            out_shape=outs,
            in_specs=in_specs or [vmem] * len(args),
            out_specs=out_specs or (vmem,) * len(outs),
            scratch_shapes=scratch,
            compiler_params=params,
            cost_estimate=pl.CostEstimate(flops=flops, bytes_accessed=16 * rows * width, transcendentals=0),
            name=name,
        )(*args)

    def shift(array, d):
        return lax.ppermute(array, "seq", [(r, (r + d) % seq_count) for r in range(seq_count)])

    def unshift(array, d):
        return lax.ppermute(array, "seq", [((r + d) % seq_count, r) for r in range(seq_count)])

    far_k = [shift(keys, d) for d in range(1, nb + 1)]
    far_v = [shift(values, d) for d in range(1, nb + 1)]

    raw = (queries, grad_out, keys, values, quant_scale, doc_lengths)
    q, g, qt, gt, quants, slopes, dclips, bias, clips = call(
        functools.partial(prep_kernel, nb),
        "prep",
        2 * work,
        [pltpu.with_memory_space_constraint(x, pltpu.HBM) for x in raw],
        (
            shape(queries.shape, BF16),
            shape(queries.shape, BF16),
            shape((width, heads // kv_heads * rows), BF16),
            shape((width, heads // kv_heads * rows), BF16),
            shape((rows, 2 * width), BF16),
            shape((rows, 2 * width), F32),
            shape((rows, 2 * width), F32),
            shape((nb * rows, rows), F32),
            shape(quant_scale.shape, F32),
        ),
        in_specs=[hbm] * 6,
        scratch=[
            pltpu.VMEM(keys.shape, BF16),
            pltpu.VMEM(values.shape, BF16),
            pltpu.SMEM(doc_lengths.shape, jnp.int32),
            pltpu.SemaphoreType.DMA((6,)),
        ],
    )
    p, k2, kdclips = call(
        functools.partial(score_kernel, nb),
        "score",
        2 * (nb + 1) * work,
        (qt, quants, bias, clips, *far_k),
        (
            shape((nb * rows, heads * rows), BF16),
            shape(((nb + 1) * rows, width), BF16),
            shape((nb * rows, width), F32),
        ),
    )
    ds, v2, grads, far_grads, spread = call(
        functools.partial(grad_kernel, nb),
        "grad",
        6 * (nb + 1) * work,
        (q, g, gt, quants, dclips, clips, p, kdclips, *far_v),
        (
            shape((nb * rows, heads * rows), BF16),
            shape(((nb + 1) * rows, width), BF16),
            shape((rows, 2 * width), F32),
            shape((nb * rows, 2 * width), BF16),
            shape((dp_count * seq_count, 2 * kv_heads, hd), BF16),
        ),
        scratch=[pltpu.VMEM((2 * kv_heads, hd), F32)],
    )
    backs = []
    for d in range(1, nb + 1):
        at = far_order(nb).index(d) * rows
        backs.append(unshift(lax.slice_in_dim(far_grads, at, at + rows, axis=0), d))
    parts = lax.all_to_all(spread, ("dp", "seq"), split_axis=0, concat_axis=0, tiled=True)
    attn_out, grad_queries = call(
        functools.partial(output_kernel, nb),
        "output",
        4 * (nb + 1) * work,
        (p, ds, k2, v2),
        (shape(queries.shape, BF16), shape(queries.shape, BF16)),
        out_specs=(hbm, hbm),
        scratch=[
            pltpu.VMEM(queries.shape, BF16),
            pltpu.VMEM(queries.shape, BF16),
            pltpu.SemaphoreType.DMA((2, kv_heads)),
        ],
    )
    grad_keys, grad_values, grad_scale = call(
        functools.partial(finish_kernel, nb),
        "finish",
        6 * rows * width,
        (grads, slopes, parts, *backs),
        (shape((rows, width), BF16), shape((rows, width), BF16), shape(parts.shape[1:], F32)),
    )
    return (attn_out, grad_queries, grad_keys, grad_values, grad_scale.reshape(quant_scale.shape))


def solution(mesh):
    rows = P(("dp", "seq"), None)
    return jax.shard_map(
        functools.partial(on_device, (mesh.shape["dp"], mesh.shape["seq"])),
        mesh=mesh,
        in_specs=(rows, rows, rows, rows, P(), P("dp", None)),
        out_specs=(rows, rows, rows, rows, P()),
        check_vma=False,
    )
```

```python
import functools
import math

import jax
import jax.numpy as jnp
from jax import lax
from jax.experimental import pallas as pl
from jax.experimental.pallas import tpu as pltpu
from jax.sharding import PartitionSpec as P

F32 = jnp.float32
BF16 = jnp.bfloat16
LEVELS = 127.0
NEG = -1e30


def sin_cos_half(u):
    r = (u - jnp.round(u)) * math.pi
    z = r * r
    s = z * (1.0 / 6227020800.0) - 1.0 / 39916800.0
    for c in (1.0 / 362880.0, -1.0 / 5040.0, 1.0 / 120.0, -1.0 / 6.0, 1.0):
        s = s * z + c
    s = s * r
    k = z * (1.0 / 479001600.0) - 1.0 / 3628800.0
    for c in (1.0 / 40320.0, -1.0 / 720.0, 1.0 / 24.0, -0.5, 1.0):
        k = k * z + c
    return s, k


def quant_parts(x, clip):
    inv = 1.0 / clip
    ratio = x * inv
    t = jnp.tanh(ratio)
    u = LEVELS * t
    s, k = sin_cos_half(u)
    level = u - s * k * (1.0 / math.pi)
    unit = level * (1.0 / LEVELS)
    slope = (2.0 * s * s) * (1.0 - t * t)
    return clip * unit, slope, unit - slope * ratio


def prep_kernel(nb, q_hbm, g_hbm, key_hbm, value_hbm, clip_hbm, len_hbm, qt_ref, gt_ref, quant_ref, slope_ref,
                dclip_ref, bias_ref, clip_out, q_ref, g_ref, key_ref, value_ref, len_ref, sems):
    small = [
        pltpu.make_async_copy(src, dst, sems.at[i])
        for i, (src, dst) in enumerate(
            ((len_hbm, len_ref), (clip_hbm, clip_out), (key_hbm, key_ref), (value_hbm, value_ref))
        )
    ]
    large = [
        pltpu.make_async_copy(q_hbm, q_ref, sems.at[4]),
        pltpu.make_async_copy(g_hbm, g_ref, sems.at[5]),
    ]
    for copy in small + large:
        copy.start()
    rows = key_ref.shape[0]
    kv_heads, hd = clip_out.shape[1], clip_out.shape[2]
    group = q_ref.shape[1] // kv_heads
    base = lax.axis_index("seq") * rows
    for copy in small:
        copy.wait()
    for side, src in ((0, key_ref), (1, value_ref)):
        for n in range(kv_heads):
            x = src[:, n * hd:(n + 1) * hd].astype(F32)
            q, slope, dclip = quant_parts(x, clip_out[side, n:n + 1, :])
            at = slice((side * kv_heads + n) * hd, (side * kv_heads + n + 1) * hd)
            quant_ref[:, at] = q.astype(BF16)
            slope_ref[:, at] = slope
            dclip_ref[:, at] = dclip
    key = lax.broadcasted_iota(jnp.int32, (rows, rows), 0)
    row = lax.broadcasted_iota(jnp.int32, (rows, rows), 1)
    start = jnp.zeros((rows, rows), jnp.int32)
    end = jnp.int32(0)
    for d in range(len_ref.shape[1]):
        end = end + len_ref[0, d]
        start = jnp.where(row + base >= end, end, start)
    for b in range(nb):
        pos = jnp.where(key <= row, key, key - nb * rows) if b == 0 else key - b * rows
        bias_ref[b * rows:(b + 1) * rows, :] = jnp.where(pos + base >= start, 0.0, NEG)
    for copy, src, dst in zip(large, (q_ref, g_ref), (qt_ref, gt_ref)):
        copy.wait()
        for n in range(kv_heads):
            for h in range(group // hd):
                at = n * group + h * hd
                dst[n * hd:(n + 1) * hd, h * rows:(h + 1) * rows] = src[:, at:at + hd].T


ACROSS = (((1,), (1,)), ((), ()))


def far_order(nb):
    return [nb] + list(range(1, nb))


def near_mask(rows):
    key = lax.broadcasted_iota(jnp.int32, (rows, rows), 0)
    row = lax.broadcasted_iota(jnp.int32, (rows, rows), 1)
    return key <= row


def merge(near, x, nb):
    rows = near.shape[0]
    first = jnp.where(near, x[:rows], x[rows:2 * rows])
    return jnp.concatenate([first, x[2 * rows:]], axis=0) if nb > 1 else first


def split(near_b, far_b, x, nb):
    rows = near_b.shape[0]
    parts = [x[:rows] * near_b, x[:rows] * far_b]
    if nb > 1:
        parts.append(x[rows:])
    return jnp.concatenate(parts, axis=0)


def score_kernel(nb, qt_ref, quant_ref, bias_ref, clip_ref, *rest):
    far, (p_ref, k2_ref, dclip_ref) = rest[:nb], rest[nb:]
    kv_heads, hd = clip_ref.shape[1], clip_ref.shape[2]
    rows, span = bias_ref.shape[1], qt_ref.shape[1]
    factor = hd ** -0.5 * math.log2(math.e)
    near = near_mask(rows)

    def step(n, carry):
        cols = pl.ds(pl.multiple_of(n * hd, hd), hd)
        clip = clip_ref[0, pl.ds(n, 1), :]
        ks = [quant_ref[:, cols]]
        for j, d in enumerate(far_order(nb)):
            q, _, dclip = quant_parts(far[d - 1][:, cols].astype(F32), clip)
            ks.append(q.astype(BF16))
            dclip_ref[j * rows:(j + 1) * rows, cols] = dclip
        k2 = jnp.concatenate(ks, axis=0)
        k2_ref[:, cols] = k2
        s_all = jnp.dot(k2, qt_ref[cols, :], preferred_element_type=F32)
        bias = bias_ref[...]
        for h in range(span // rows):
            s = merge(near, s_all[:, h * rows:(h + 1) * rows], nb) * factor + bias
            w = jnp.exp2(s - jnp.max(s, axis=0, keepdims=True))
            p = w * (1.0 / jnp.sum(w, axis=0, keepdims=True))
            p_ref[:, pl.ds(pl.multiple_of(n * span + h * rows, rows), rows)] = p.astype(BF16)
        return carry

    lax.fori_loop(0, kv_heads, step, 0, unroll=True)


def grad_kernel(nb, qt_ref, gt_ref, quant_ref, dclip_ref, clip_ref, p_ref, kdclip_ref, *rest):
    far_v, (ds_ref, v2_ref, grad_ref, far_ref, spread_ref, scale_ref) = rest[:nb], rest[nb:]
    kv_heads, hd = clip_ref.shape[1], clip_ref.shape[2]
    rows, span = dclip_ref.shape[0], gt_ref.shape[1]
    heads = span // rows
    width = kv_heads * hd
    scale = hd ** -0.5
    near = near_mask(rows)
    near_b = near.astype(F32).astype(BF16)
    far_b = 1.0 - near_b

    def step(n, carry):
        k_cols = pl.ds(pl.multiple_of(n * hd, hd), hd)
        v_cols = pl.ds(pl.multiple_of(width + n * hd, hd), hd)
        v_clip = clip_ref[1, pl.ds(n, 1), :]
        vs, vd = [quant_ref[:, v_cols]], [dclip_ref[:, v_cols]]
        for d in far_order(nb):
            q, _, dc = quant_parts(far_v[d - 1][:, k_cols].astype(F32), v_clip)
            vs.append(q.astype(BF16))
            vd.append(dc)
        v2 = jnp.concatenate(vs, axis=0)
        v2_ref[:, k_cols] = v2
        d_all = jnp.dot(v2, gt_ref[k_cols, :], preferred_element_type=F32)
        ps, ds = [], []
        for h in range(heads):
            dp = merge(near, d_all[:, h * rows:(h + 1) * rows], nb)
            at = pl.ds(pl.multiple_of(n * span + h * rows, rows), rows)
            p_b = p_ref[:, at]
            p = p_b.astype(F32)
            delta = jnp.sum(p * dp, axis=0, keepdims=True)
            ds_b = (p * (dp - delta)).astype(BF16)
            ds_ref[:, at] = ds_b
            ps.append(split(near_b, far_b, p_b, nb))
            ds.append(split(near_b, far_b, ds_b, nb))
        p2 = jnp.concatenate(ps, axis=1)
        ds2 = jnp.concatenate(ds, axis=1)
        k_grad = (lax.dot_general(qt_ref[k_cols, :], ds2, ACROSS, preferred_element_type=F32) * scale).T
        v_grad = lax.dot_general(gt_ref[k_cols, :], p2, ACROSS, preferred_element_type=F32).T
        grad_ref[:, k_cols] = k_grad[:rows]
        grad_ref[:, v_cols] = v_grad[:rows]
        far_ref[:, k_cols] = k_grad[rows:].astype(BF16)
        far_ref[:, v_cols] = v_grad[rows:].astype(BF16)
        scale_ref[pl.ds(n, 1), :] = jnp.sum(k_grad[:rows] * dclip_ref[:, k_cols], axis=0, keepdims=True) + jnp.sum(
            k_grad[rows:] * kdclip_ref[:, k_cols], axis=0, keepdims=True
        )
        scale_ref[pl.ds(kv_heads + n, 1), :] = jnp.sum(
            v_grad * jnp.concatenate(vd, axis=0), axis=0, keepdims=True
        )
        return carry

    lax.fori_loop(0, kv_heads, step, 0, unroll=True)
    part = scale_ref[...].astype(BF16)

    def spread(i, carry):
        spread_ref[i] = part
        return carry

    lax.fori_loop(0, spread_ref.shape[0], spread, 0)


def output_kernel(nb, p_ref, ds_ref, k2_ref, v2_ref, out_hbm, gq_hbm, out_ref, gq_ref, sems):
    kv_heads = sems.shape[1]
    rows, group = out_ref.shape[0], out_ref.shape[1] // kv_heads
    hd = k2_ref.shape[1] // kv_heads
    heads = group // hd
    near_b = near_mask(rows).astype(F32).astype(BF16)
    far_b = 1.0 - near_b

    def copies(n):
        cols = pl.ds(pl.multiple_of(n * group, group), group)
        return (
            pltpu.make_async_copy(out_ref.at[:, cols], out_hbm.at[:, cols], sems.at[0, n]),
            pltpu.make_async_copy(gq_ref.at[:, cols], gq_hbm.at[:, cols], sems.at[1, n]),
        )

    def step(n, carry):
        cols = pl.ds(pl.multiple_of(n * hd, hd), hd)
        for left, right, dst, scale in ((v2_ref, p_ref, out_ref, None), (k2_ref, ds_ref, gq_ref, hd ** -0.5)):
            at = pl.ds(pl.multiple_of(n * heads * rows, rows), heads * rows)
            x = right[:, at]
            x2 = jnp.concatenate(
                [split(near_b, far_b, x[:, h * rows:(h + 1) * rows], nb) for h in range(heads)], axis=1
            )
            y = jnp.dot(left[:, cols].T, x2, preferred_element_type=F32)
            y = (y if scale is None else y * scale).astype(BF16)
            for h in range(heads):
                dst[:, pl.ds(pl.multiple_of(n * group + h * hd, hd), hd)] = y[:, h * rows:(h + 1) * rows].T
        for copy in copies(n):
            copy.start()
        return carry

    lax.fori_loop(0, kv_heads, step, 0, unroll=True)
    for n in range(kv_heads):
        for copy in copies(n):
            copy.wait()


def total_kernel(parts_ref, after_ref, out_ref):
    del after_ref
    out_ref[...] = jnp.sum(parts_ref[...].astype(F32), axis=0)


def finish_kernel(nb, grad_ref, slope_ref, *rest):
    backs, (gk_ref, gv_ref) = rest[:nb], rest[nb:]
    width = gk_ref.shape[1]
    for side, out in ((0, gk_ref), (1, gv_ref)):
        at = slice(side * width, (side + 1) * width)
        total = grad_ref[:, at]
        for back in backs:
            total = total + back[:, at].astype(F32)
        out[...] = (total * slope_ref[:, at]).astype(BF16)


def on_device(sizes, queries, keys, values, grad_out, quant_scale, doc_lengths):
    dp_count, seq_count = sizes
    nb = max(1, seq_count // 2)
    rows, width = keys.shape
    kv_heads, hd = quant_scale.shape[1], quant_scale.shape[2]
    heads = queries.shape[1] // hd
    vmem = pl.BlockSpec(memory_space=pltpu.VMEM)
    hbm = pl.BlockSpec(memory_space=pltpu.HBM)
    params = pltpu.CompilerParams(vmem_limit_bytes=36 * 1024 * 1024)
    shape = jax.ShapeDtypeStruct
    work = rows * rows * queries.shape[1]

    def call(kernel, name, flops, args, outs, in_specs=None, out_specs=None, scratch=()):
        return pl.pallas_call(
            kernel,
            out_shape=outs,
            in_specs=in_specs or [vmem] * len(args),
            out_specs=out_specs or (vmem,) * len(outs),
            scratch_shapes=scratch,
            compiler_params=params,
            cost_estimate=pl.CostEstimate(flops=flops, bytes_accessed=16 * rows * width, transcendentals=0),
            name=name,
        )(*args)

    def shift(array, d):
        return lax.ppermute(array, "seq", [(r, (r + d) % seq_count) for r in range(seq_count)])

    def unshift(array, d):
        return lax.ppermute(array, "seq", [((r + d) % seq_count, r) for r in range(seq_count)])

    far_k = [shift(keys, d) for d in range(1, nb + 1)]
    far_v = [shift(values, d) for d in range(1, nb + 1)]

    raw = (queries, grad_out, keys, values, quant_scale, doc_lengths)
    qt, gt, quants, slopes, dclips, bias, clips = call(
        functools.partial(prep_kernel, nb),
        "prep",
        2 * work,
        [pltpu.with_memory_space_constraint(x, pltpu.HBM) for x in raw],
        (
            shape((width, heads // kv_heads * rows), BF16),
            shape((width, heads // kv_heads * rows), BF16),
            shape((rows, 2 * width), BF16),
            shape((rows, 2 * width), F32),
            shape((rows, 2 * width), F32),
            shape((nb * rows, rows), F32),
            shape(quant_scale.shape, F32),
        ),
        in_specs=[hbm] * 6,
        scratch=[
            pltpu.VMEM(queries.shape, BF16),
            pltpu.VMEM(queries.shape, BF16),
            pltpu.VMEM(keys.shape, BF16),
            pltpu.VMEM(values.shape, BF16),
            pltpu.SMEM(doc_lengths.shape, jnp.int32),
            pltpu.SemaphoreType.DMA((6,)),
        ],
    )
    p, k2, kdclips = call(
        functools.partial(score_kernel, nb),
        "score",
        2 * (nb + 1) * work,
        (qt, quants, bias, clips, *far_k),
        (
            shape((nb * rows, heads * rows), BF16),
            shape(((nb + 1) * rows, width), BF16),
            shape((nb * rows, width), F32),
        ),
    )
    ds, v2, grads, far_grads, spread = call(
        functools.partial(grad_kernel, nb),
        "grad",
        6 * (nb + 1) * work,
        (qt, gt, quants, dclips, clips, p, kdclips, *far_v),
        (
            shape((nb * rows, heads * rows), BF16),
            shape(((nb + 1) * rows, width), BF16),
            shape((rows, 2 * width), F32),
            shape((nb * rows, 2 * width), BF16),
            shape((dp_count * seq_count, 2 * kv_heads, hd), BF16),
        ),
        scratch=[pltpu.VMEM((2 * kv_heads, hd), F32)],
    )
    backs = []
    for d in range(1, nb + 1):
        at = far_order(nb).index(d) * rows
        backs.append(unshift(lax.slice_in_dim(far_grads, at, at + rows, axis=0), d))
    parts = lax.all_to_all(spread, ("dp", "seq"), split_axis=0, concat_axis=0, tiled=True)
    attn_out, grad_queries = call(
        functools.partial(output_kernel, nb),
        "output",
        4 * (nb + 1) * work,
        (p, ds, k2, v2),
        (shape(queries.shape, BF16), shape(queries.shape, BF16)),
        out_specs=(hbm, hbm),
        scratch=[
            pltpu.VMEM(queries.shape, BF16),
            pltpu.VMEM(queries.shape, BF16),
            pltpu.SemaphoreType.DMA((2, kv_heads)),
        ],
    )
    grad_keys, grad_values = call(
        functools.partial(finish_kernel, nb),
        "finish",
        6 * rows * width,
        (grads, slopes, *backs),
        (shape((rows, width), BF16), shape((rows, width), BF16)),
    )
    (grad_scale,) = call(
        total_kernel,
        "total",
        parts.size,
        (parts, pltpu.with_memory_space_constraint(grad_keys, pltpu.HBM)),
        (shape(parts.shape[1:], F32),),
        in_specs=[vmem, hbm],
    )
    return (attn_out, grad_queries, grad_keys, grad_values, grad_scale.reshape(quant_scale.shape))


def solution(mesh):
    rows = P(("dp", "seq"), None)
    return jax.shard_map(
        functools.partial(on_device, (mesh.shape["dp"], mesh.shape["seq"])),
        mesh=mesh,
        in_specs=(rows, rows, rows, rows, P(), P("dp", None)),
        out_specs=(rows, rows, rows, rows, P()),
        check_vma=False,
    )
```

```python
import functools
import math

import jax
import jax.numpy as jnp
from jax import lax
from jax.experimental import pallas as pl
from jax.experimental.pallas import tpu as pltpu
from jax.sharding import PartitionSpec as P

F32 = jnp.float32
BF16 = jnp.bfloat16
LEVELS = 127.0
NEG = -1e30


def sin_cos_half(u):
    r = (u - jnp.round(u)) * math.pi
    z = r * r
    s = z * (1.0 / 6227020800.0) - 1.0 / 39916800.0
    for c in (1.0 / 362880.0, -1.0 / 5040.0, 1.0 / 120.0, -1.0 / 6.0, 1.0):
        s = s * z + c
    s = s * r
    k = z * (1.0 / 479001600.0) - 1.0 / 3628800.0
    for c in (1.0 / 40320.0, -1.0 / 720.0, 1.0 / 24.0, -0.5, 1.0):
        k = k * z + c
    return s, k


def quant_parts(x, clip):
    inv = 1.0 / clip
    ratio = x * inv
    t = jnp.tanh(ratio)
    u = LEVELS * t
    s, k = sin_cos_half(u)
    level = u - s * k * (1.0 / math.pi)
    unit = level * (1.0 / LEVELS)
    slope = (2.0 * s * s) * (1.0 - t * t)
    return clip * unit, slope, unit - slope * ratio


def prep_kernel(nb, q_hbm, g_hbm, key_hbm, value_hbm, clip_hbm, len_hbm, qt_ref, gt_ref, quant_ref, slope_hbm,
                dclip_ref, bias_ref, clip_out, q_ref, g_ref, key_ref, value_ref, len_ref, slope_ref, sems):
    small = [
        pltpu.make_async_copy(src, dst, sems.at[i])
        for i, (src, dst) in enumerate(
            ((len_hbm, len_ref), (clip_hbm, clip_out), (key_hbm, key_ref), (value_hbm, value_ref))
        )
    ]
    large = [
        pltpu.make_async_copy(q_hbm, q_ref, sems.at[4]),
        pltpu.make_async_copy(g_hbm, g_ref, sems.at[5]),
    ]
    for copy in small + large:
        copy.start()
    rows = key_ref.shape[0]
    kv_heads, hd = clip_out.shape[1], clip_out.shape[2]
    group = q_ref.shape[1] // kv_heads
    base = lax.axis_index("seq") * rows
    for copy in small:
        copy.wait()
    for side, src in ((0, key_ref), (1, value_ref)):
        for n in range(kv_heads):
            x = src[:, n * hd:(n + 1) * hd].astype(F32)
            q, slope, dclip = quant_parts(x, clip_out[side, n:n + 1, :])
            at = slice((side * kv_heads + n) * hd, (side * kv_heads + n + 1) * hd)
            quant_ref[:, at] = q.astype(BF16)
            slope_ref[:, at] = slope
            dclip_ref[:, at] = dclip
    slope_copy = pltpu.make_async_copy(slope_ref, slope_hbm, sems.at[6])
    slope_copy.start()
    key = lax.broadcasted_iota(jnp.int32, (rows, rows), 0)
    row = lax.broadcasted_iota(jnp.int32, (rows, rows), 1)
    start = jnp.zeros((rows, rows), jnp.int32)
    end = jnp.int32(0)
    for d in range(len_ref.shape[1]):
        end = end + len_ref[0, d]
        start = jnp.where(row + base >= end, end, start)
    for b in range(nb):
        pos = jnp.where(key <= row, key, key - nb * rows) if b == 0 else key - b * rows
        bias_ref[b * rows:(b + 1) * rows, :] = jnp.where(pos + base >= start, 0.0, NEG)
    for copy, src, dst in zip(large, (q_ref, g_ref), (qt_ref, gt_ref)):
        copy.wait()
        for n in range(kv_heads):
            for h in range(group // hd):
                at = n * group + h * hd
                dst[n * hd:(n + 1) * hd, h * rows:(h + 1) * rows] = src[:, at:at + hd].T
    slope_copy.wait()


ACROSS = (((1,), (1,)), ((), ()))


def far_order(nb):
    return [nb] + list(range(1, nb))


def near_mask(rows):
    key = lax.broadcasted_iota(jnp.int32, (rows, rows), 0)
    row = lax.broadcasted_iota(jnp.int32, (rows, rows), 1)
    return key <= row


def merge(near, x, nb):
    rows = near.shape[0]
    first = jnp.where(near, x[:rows], x[rows:2 * rows])
    return jnp.concatenate([first, x[2 * rows:]], axis=0) if nb > 1 else first


def split(near_b, far_b, x, nb):
    rows = near_b.shape[0]
    parts = [x[:rows] * near_b, x[:rows] * far_b]
    if nb > 1:
        parts.append(x[rows:])
    return jnp.concatenate(parts, axis=0)


def score_kernel(nb, qt_ref, quant_ref, bias_ref, clip_ref, *rest):
    far, (p_ref, k2_ref, dclip_ref) = rest[:nb], rest[nb:]
    kv_heads, hd = clip_ref.shape[1], clip_ref.shape[2]
    rows, span = bias_ref.shape[1], qt_ref.shape[1]
    factor = hd ** -0.5 * math.log2(math.e)
    near = near_mask(rows)

    bias = bias_ref[...]

    def scores(n):
        cols = slice(n * hd, (n + 1) * hd)
        ks = [quant_ref[:, cols]]
        for j, d in enumerate(far_order(nb)):
            q, _, dclip = quant_parts(far[d - 1][:, cols].astype(F32), clip_ref[0, n:n + 1, :])
            ks.append(q.astype(BF16))
            dclip_ref[j * rows:(j + 1) * rows, cols] = dclip
        k2 = jnp.concatenate(ks, axis=0)
        k2_ref[:, cols] = k2
        return jnp.dot(k2, qt_ref[cols, :], preferred_element_type=F32)

    ahead = scores(0)
    for n in range(kv_heads):
        s_all, ahead = ahead, scores(n + 1) if n + 1 < kv_heads else None
        for h in range(span // rows):
            s = merge(near, s_all[:, h * rows:(h + 1) * rows], nb) * factor + bias
            w = jnp.exp2(s - jnp.max(s, axis=0, keepdims=True))
            p = w * (1.0 / jnp.sum(w, axis=0, keepdims=True))
            p_ref[:, n * span + h * rows:n * span + (h + 1) * rows] = p.astype(BF16)


def grad_kernel(nb, qt_ref, gt_ref, quant_ref, dclip_ref, clip_ref, p_ref, kdclip_ref, *rest):
    far_v, (ds_ref, v2_ref, grad_ref, far_ref, spread_ref, scale_ref) = rest[:nb], rest[nb:]
    kv_heads, hd = clip_ref.shape[1], clip_ref.shape[2]
    rows, span = dclip_ref.shape[0], gt_ref.shape[1]
    heads = span // rows
    width = kv_heads * hd
    scale = hd ** -0.5
    near = near_mask(rows)
    near_b = near.astype(F32).astype(BF16)
    far_b = 1.0 - near_b

    def k_cols(n):
        return slice(n * hd, (n + 1) * hd)

    def v_cols(n):
        return slice(width + n * hd, width + (n + 1) * hd)

    def value_side(n):
        p2 = jnp.concatenate(
            [split(near_b, far_b, p_ref[:, n * span + h * rows:n * span + (h + 1) * rows], nb) for h in range(heads)],
            axis=1,
        )
        v_grad = lax.dot_general(gt_ref[k_cols(n), :], p2, ACROSS, preferred_element_type=F32).T
        vs, vd = [quant_ref[:, v_cols(n)]], [dclip_ref[:, v_cols(n)]]
        for d in far_order(nb):
            q, _, dc = quant_parts(far_v[d - 1][:, k_cols(n)].astype(F32), clip_ref[1, n:n + 1, :])
            vs.append(q.astype(BF16))
            vd.append(dc)
        v2 = jnp.concatenate(vs, axis=0)
        v2_ref[:, k_cols(n)] = v2
        grad_ref[:, v_cols(n)] = v_grad[:rows].astype(BF16)
        far_ref[:, v_cols(n)] = v_grad[rows:].astype(BF16)
        scale_ref[kv_heads + n:kv_heads + n + 1, :] = jnp.sum(
            v_grad * jnp.concatenate(vd, axis=0), axis=0, keepdims=True
        )
        return jnp.dot(v2, gt_ref[k_cols(n), :], preferred_element_type=F32)

    def score_side(n, d_all):
        ds = []
        for h in range(heads):
            dp = merge(near, d_all[:, h * rows:(h + 1) * rows], nb)
            at = slice(n * span + h * rows, n * span + (h + 1) * rows)
            p = p_ref[:, at].astype(F32)
            delta = jnp.sum(p * dp, axis=0, keepdims=True)
            ds_b = (p * (dp - delta)).astype(BF16)
            ds_ref[:, at] = ds_b
            ds.append(split(near_b, far_b, ds_b, nb))
        return jnp.concatenate(ds, axis=1)

    def key_side(n, ds2):
        k_grad = (lax.dot_general(qt_ref[k_cols(n), :], ds2, ACROSS, preferred_element_type=F32) * scale).T
        grad_ref[:, k_cols(n)] = k_grad[:rows].astype(BF16)
        far_ref[:, k_cols(n)] = k_grad[rows:].astype(BF16)
        scale_ref[n:n + 1, :] = jnp.sum(k_grad[:rows] * dclip_ref[:, k_cols(n)], axis=0, keepdims=True) + jnp.sum(
            k_grad[rows:] * kdclip_ref[:, k_cols(n)], axis=0, keepdims=True
        )

    ahead, behind = value_side(0), None
    for n in range(kv_heads):
        d_all, ahead = ahead, value_side(n + 1) if n + 1 < kv_heads else None
        ds2 = score_side(n, d_all)
        if behind is not None:
            key_side(n - 1, behind)
        behind = ds2
    key_side(kv_heads - 1, behind)
    part = scale_ref[...].astype(BF16)

    def spread(i, carry):
        spread_ref[i] = part
        return carry

    lax.fori_loop(0, spread_ref.shape[0], spread, 0, unroll=8)


def output_kernel(nb, p_ref, ds_ref, k2_ref, v2_ref, out_hbm, gq_hbm, out_ref, gq_ref, sems):
    kv_heads = sems.shape[1]
    rows, group = out_ref.shape[0], out_ref.shape[1] // kv_heads
    hd = k2_ref.shape[1] // kv_heads
    heads = group // hd
    near_b = near_mask(rows).astype(F32).astype(BF16)
    far_b = 1.0 - near_b

    def copies(n):
        cols = pl.ds(pl.multiple_of(n * group, group), group)
        return (
            pltpu.make_async_copy(out_ref.at[:, cols], out_hbm.at[:, cols], sems.at[0, n]),
            pltpu.make_async_copy(gq_ref.at[:, cols], gq_hbm.at[:, cols], sems.at[1, n]),
        )

    def step(n, carry):
        cols = pl.ds(pl.multiple_of(n * hd, hd), hd)
        for left, right, dst, scale in ((v2_ref, p_ref, out_ref, None), (k2_ref, ds_ref, gq_ref, hd ** -0.5)):
            at = pl.ds(pl.multiple_of(n * heads * rows, rows), heads * rows)
            x = right[:, at]
            x2 = jnp.concatenate(
                [split(near_b, far_b, x[:, h * rows:(h + 1) * rows], nb) for h in range(heads)], axis=1
            )
            y = jnp.dot(left[:, cols].T, x2, preferred_element_type=F32)
            y = (y if scale is None else y * scale).astype(BF16)
            for h in range(heads):
                dst[:, pl.ds(pl.multiple_of(n * group + h * hd, hd), hd)] = y[:, h * rows:(h + 1) * rows].T
        for copy in copies(n):
            copy.start()
        return carry

    lax.fori_loop(0, kv_heads, step, 0, unroll=True)
    for n in range(kv_heads):
        for copy in copies(n):
            copy.wait()


def total_kernel(parts_ref, after_ref, out_ref):
    del after_ref
    out_ref[...] = jnp.sum(parts_ref[...].astype(F32), axis=0)


def finish_kernel(nb, grad_ref, slope_ref, *rest):
    backs, (gk_ref, gv_ref) = rest[:nb], rest[nb:]
    width = gk_ref.shape[1]
    for side, out in ((0, gk_ref), (1, gv_ref)):
        at = slice(side * width, (side + 1) * width)
        total = grad_ref[:, at].astype(F32)
        for back in backs:
            total = total + back[:, at].astype(F32)
        out[...] = (total * slope_ref[:, at]).astype(BF16)


def on_device(sizes, queries, keys, values, grad_out, quant_scale, doc_lengths):
    dp_count, seq_count = sizes
    nb = max(1, seq_count // 2)
    rows, width = keys.shape
    kv_heads, hd = quant_scale.shape[1], quant_scale.shape[2]
    heads = queries.shape[1] // hd
    vmem = pl.BlockSpec(memory_space=pltpu.VMEM)
    hbm = pl.BlockSpec(memory_space=pltpu.HBM)
    params = pltpu.CompilerParams(vmem_limit_bytes=36 * 1024 * 1024)
    shape = jax.ShapeDtypeStruct
    work = rows * rows * queries.shape[1]

    def call(kernel, name, flops, args, outs, in_specs=None, out_specs=None, scratch=()):
        return pl.pallas_call(
            kernel,
            out_shape=outs,
            in_specs=in_specs or [vmem] * len(args),
            out_specs=out_specs or (vmem,) * len(outs),
            scratch_shapes=scratch,
            compiler_params=params,
            cost_estimate=pl.CostEstimate(flops=flops, bytes_accessed=16 * rows * width, transcendentals=0),
            name=name,
        )(*args)

    def shift(array, d):
        return lax.ppermute(array, "seq", [(r, (r + d) % seq_count) for r in range(seq_count)])

    def unshift(array, d):
        return lax.ppermute(array, "seq", [((r + d) % seq_count, r) for r in range(seq_count)])

    far_k = [shift(keys, d) for d in range(1, nb + 1)]
    far_v = [shift(values, d) for d in range(1, nb + 1)]

    raw = (queries, grad_out, keys, values, quant_scale, doc_lengths)
    qt, gt, quants, slopes, dclips, bias, clips = call(
        functools.partial(prep_kernel, nb),
        "prep",
        2 * work,
        [pltpu.with_memory_space_constraint(x, pltpu.HBM) for x in raw],
        (
            shape((width, heads // kv_heads * rows), BF16),
            shape((width, heads // kv_heads * rows), BF16),
            shape((rows, 2 * width), BF16),
            pltpu.HBM((rows, 2 * width), F32),
            shape((rows, 2 * width), F32),
            shape((nb * rows, rows), F32),
            shape(quant_scale.shape, F32),
        ),
        in_specs=[hbm] * 6,
        out_specs=(vmem, vmem, vmem, hbm, vmem, vmem, vmem),
        scratch=[
            pltpu.VMEM(queries.shape, BF16),
            pltpu.VMEM(queries.shape, BF16),
            pltpu.VMEM(keys.shape, BF16),
            pltpu.VMEM(values.shape, BF16),
            pltpu.SMEM(doc_lengths.shape, jnp.int32),
            pltpu.VMEM((rows, 2 * width), F32),
            pltpu.SemaphoreType.DMA((7,)),
        ],
    )
    p, k2, kdclips = call(
        functools.partial(score_kernel, nb),
        "score",
        2 * (nb + 1) * work,
        (qt, quants, bias, clips, *far_k),
        (
            shape((nb * rows, heads * rows), BF16),
            shape(((nb + 1) * rows, width), BF16),
            shape((nb * rows, width), F32),
        ),
    )
    ds, v2, grads, far_grads, spread = call(
        functools.partial(grad_kernel, nb),
        "grad",
        6 * (nb + 1) * work,
        (qt, gt, quants, dclips, clips, p, kdclips, *far_v),
        (
            shape((nb * rows, heads * rows), BF16),
            shape(((nb + 1) * rows, width), BF16),
            shape((rows, 2 * width), BF16),
            shape((nb * rows, 2 * width), BF16),
            shape((dp_count * seq_count, 2 * kv_heads, hd), BF16),
        ),
        scratch=[pltpu.VMEM((2 * kv_heads, hd), F32)],
    )
    backs = []
    for d in range(1, nb + 1):
        at = far_order(nb).index(d) * rows
        backs.append(unshift(lax.slice_in_dim(far_grads, at, at + rows, axis=0), d))
    parts = lax.all_to_all(spread, ("dp", "seq"), split_axis=0, concat_axis=0, tiled=True)
    attn_out, grad_queries = call(
        functools.partial(output_kernel, nb),
        "output",
        4 * (nb + 1) * work,
        (p, ds, k2, v2),
        (shape(queries.shape, BF16), shape(queries.shape, BF16)),
        out_specs=(hbm, hbm),
        scratch=[
            pltpu.VMEM(queries.shape, BF16),
            pltpu.VMEM(queries.shape, BF16),
            pltpu.SemaphoreType.DMA((2, kv_heads)),
        ],
    )
    grad_keys, grad_values = call(
        functools.partial(finish_kernel, nb),
        "finish",
        6 * rows * width,
        (grads, pltpu.with_memory_space_constraint(slopes, pltpu.HBM), *backs),
        (shape((rows, width), BF16), shape((rows, width), BF16)),
    )
    (grad_scale,) = call(
        total_kernel,
        "total",
        parts.size,
        (parts, pltpu.with_memory_space_constraint(grad_keys, pltpu.HBM)),
        (shape(parts.shape[1:], F32),),
        in_specs=[vmem, hbm],
    )
    return (attn_out, grad_queries, grad_keys, grad_values, grad_scale.reshape(quant_scale.shape))


def solution(mesh):
    rows = P(("dp", "seq"), None)
    return jax.shard_map(
        functools.partial(on_device, (mesh.shape["dp"], mesh.shape["seq"])),
        mesh=mesh,
        in_specs=(rows, rows, rows, rows, P(), P("dp", None)),
        out_specs=(rows, rows, rows, rows, P()),
        check_vma=False,
    )
```

```python
import functools
import math

import jax
import jax.numpy as jnp
from jax import lax
from jax.experimental import pallas as pl
from jax.experimental.pallas import tpu as pltpu
from jax.sharding import PartitionSpec as P

F32 = jnp.float32
BF16 = jnp.bfloat16
LEVELS = 127.0
NEG = -1e30


def sin_cos_half(u):
    r = (u - jnp.round(u)) * math.pi
    z = r * r
    s = z * (1.0 / 6227020800.0) - 1.0 / 39916800.0
    for c in (1.0 / 362880.0, -1.0 / 5040.0, 1.0 / 120.0, -1.0 / 6.0, 1.0):
        s = s * z + c
    s = s * r
    k = z * (1.0 / 479001600.0) - 1.0 / 3628800.0
    for c in (1.0 / 40320.0, -1.0 / 720.0, 1.0 / 24.0, -0.5, 1.0):
        k = k * z + c
    return s, k


def quant_parts(x, clip):
    inv = 1.0 / clip
    ratio = x * inv
    t = jnp.tanh(ratio)
    u = LEVELS * t
    s, k = sin_cos_half(u)
    level = u - s * k * (1.0 / math.pi)
    unit = level * (1.0 / LEVELS)
    slope = (2.0 * s * s) * (1.0 - t * t)
    return clip * unit, slope, unit - slope * ratio


def prep_kernel(nb, q_hbm, g_hbm, key_hbm, value_hbm, clip_hbm, len_hbm, qt_ref, gt_ref, quant_ref, slope_hbm,
                dclip_ref, bias_ref, clip_out, q_ref, g_ref, key_ref, value_ref, len_ref, slope_ref, sems):
    small = [
        pltpu.make_async_copy(src, dst, sems.at[i])
        for i, (src, dst) in enumerate(
            ((len_hbm, len_ref), (clip_hbm, clip_out), (key_hbm, key_ref), (value_hbm, value_ref))
        )
    ]
    large = [
        pltpu.make_async_copy(q_hbm, q_ref, sems.at[4]),
        pltpu.make_async_copy(g_hbm, g_ref, sems.at[5]),
    ]
    for copy in small + large:
        copy.start()
    rows = key_ref.shape[0]
    kv_heads, hd = clip_out.shape[1], clip_out.shape[2]
    group = q_ref.shape[1] // kv_heads
    base = lax.axis_index("seq") * rows
    for copy in small:
        copy.wait()
    for side, src in ((0, key_ref), (1, value_ref)):
        for n in range(kv_heads):
            x = src[:, n * hd:(n + 1) * hd].astype(F32)
            q, slope, dclip = quant_parts(x, clip_out[side, n:n + 1, :])
            at = slice((side * kv_heads + n) * hd, (side * kv_heads + n + 1) * hd)
            quant_ref[:, at] = q.astype(BF16)
            slope_ref[:, at] = slope
            dclip_ref[:, at] = dclip
    slope_copy = pltpu.make_async_copy(slope_ref, slope_hbm, sems.at[6])
    slope_copy.start()
    key = lax.broadcasted_iota(jnp.int32, (rows, rows), 0)
    row = lax.broadcasted_iota(jnp.int32, (rows, rows), 1)
    start = jnp.zeros((rows, rows), jnp.int32)
    end = jnp.int32(0)
    for d in range(len_ref.shape[1]):
        end = end + len_ref[0, d]
        start = jnp.where(row + base >= end, end, start)
    for b in range(nb):
        pos = jnp.where(key <= row, key, key - nb * rows) if b == 0 else key - b * rows
        bias_ref[b * rows:(b + 1) * rows, :] = jnp.where(pos + base >= start, 0.0, NEG)
    for copy, src, dst in zip(large, (q_ref, g_ref), (qt_ref, gt_ref)):
        copy.wait()
        for n in range(kv_heads):
            for h in range(group // hd):
                at = n * group + h * hd
                dst[n * hd:(n + 1) * hd, h * rows:(h + 1) * rows] = src[:, at:at + hd].T
    slope_copy.wait()


ACROSS = (((1,), (1,)), ((), ()))


def far_order(nb):
    return [nb] + list(range(1, nb))


def near_mask(rows):
    key = lax.broadcasted_iota(jnp.int32, (rows, rows), 0)
    row = lax.broadcasted_iota(jnp.int32, (rows, rows), 1)
    return key <= row


def merge(near, x, nb):
    rows = near.shape[0]
    first = jnp.where(near, x[:rows], x[rows:2 * rows])
    return jnp.concatenate([first, x[2 * rows:]], axis=0) if nb > 1 else first


def split(near_b, far_b, x, nb):
    rows = near_b.shape[0]
    parts = [x[:rows] * near_b, x[:rows] * far_b]
    if nb > 1:
        parts.append(x[rows:])
    return jnp.concatenate(parts, axis=0)


def score_kernel(nb, qt_ref, quant_ref, bias_ref, clip_ref, *rest):
    far, (p_ref, k2_ref, dclip_ref) = rest[:nb], rest[nb:]
    kv_heads, hd = clip_ref.shape[1], clip_ref.shape[2]
    rows, span = bias_ref.shape[1], qt_ref.shape[1]
    factor = hd ** -0.5 * math.log2(math.e)
    near = near_mask(rows)

    bias = bias_ref[...]

    def scores(n):
        cols = slice(n * hd, (n + 1) * hd)
        ks = [quant_ref[:, cols]]
        for j, d in enumerate(far_order(nb)):
            q, _, dclip = quant_parts(far[d - 1][:, cols].astype(F32), clip_ref[0, n:n + 1, :])
            ks.append(q.astype(BF16))
            dclip_ref[j * rows:(j + 1) * rows, cols] = dclip
        k2 = jnp.concatenate(ks, axis=0)
        k2_ref[:, cols] = k2
        return jnp.dot(k2, qt_ref[cols, :], preferred_element_type=F32)

    ahead = scores(0)
    for n in range(kv_heads):
        s_all, ahead = ahead, scores(n + 1) if n + 1 < kv_heads else None
        for h in range(span // rows):
            s = merge(near, s_all[:, h * rows:(h + 1) * rows], nb) * factor + bias
            w = jnp.exp2(s - jnp.max(s, axis=0, keepdims=True))
            p = w * (1.0 / jnp.sum(w, axis=0, keepdims=True))
            p_ref[:, n * span + h * rows:n * span + (h + 1) * rows] = p.astype(BF16)


def grad_kernel(nb, qt_ref, gt_ref, quant_ref, dclip_ref, clip_ref, p_ref, kdclip_ref, *rest):
    far_v, (ds_ref, v2_ref, grad_ref, far_ref, scale_ref) = rest[:nb], rest[nb:]
    kv_heads, hd = clip_ref.shape[1], clip_ref.shape[2]
    rows, span = dclip_ref.shape[0], gt_ref.shape[1]
    heads = span // rows
    width = kv_heads * hd
    scale = hd ** -0.5
    near = near_mask(rows)
    near_b = near.astype(F32).astype(BF16)
    far_b = 1.0 - near_b

    def k_cols(n):
        return slice(n * hd, (n + 1) * hd)

    def v_cols(n):
        return slice(width + n * hd, width + (n + 1) * hd)

    def value_side(n):
        p2 = jnp.concatenate(
            [split(near_b, far_b, p_ref[:, n * span + h * rows:n * span + (h + 1) * rows], nb) for h in range(heads)],
            axis=1,
        )
        v_grad = lax.dot_general(gt_ref[k_cols(n), :], p2, ACROSS, preferred_element_type=F32).T
        vs, vd = [quant_ref[:, v_cols(n)]], [dclip_ref[:, v_cols(n)]]
        for d in far_order(nb):
            q, _, dc = quant_parts(far_v[d - 1][:, k_cols(n)].astype(F32), clip_ref[1, n:n + 1, :])
            vs.append(q.astype(BF16))
            vd.append(dc)
        v2 = jnp.concatenate(vs, axis=0)
        v2_ref[:, k_cols(n)] = v2
        grad_ref[:, v_cols(n)] = v_grad[:rows].astype(BF16)
        far_ref[:, v_cols(n)] = v_grad[rows:].astype(BF16)
        scale_ref[kv_heads + n:kv_heads + n + 1, :] = jnp.sum(
            v_grad * jnp.concatenate(vd, axis=0), axis=0, keepdims=True
        )
        return jnp.dot(v2, gt_ref[k_cols(n), :], preferred_element_type=F32)

    def score_side(n, d_all):
        ds = []
        for h in range(heads):
            dp = merge(near, d_all[:, h * rows:(h + 1) * rows], nb)
            at = slice(n * span + h * rows, n * span + (h + 1) * rows)
            p = p_ref[:, at].astype(F32)
            delta = jnp.sum(p * dp, axis=0, keepdims=True)
            ds_b = (p * (dp - delta)).astype(BF16)
            ds_ref[:, at] = ds_b
            ds.append(split(near_b, far_b, ds_b, nb))
        return jnp.concatenate(ds, axis=1)

    def key_side(n, ds2):
        k_grad = (lax.dot_general(qt_ref[k_cols(n), :], ds2, ACROSS, preferred_element_type=F32) * scale).T
        grad_ref[:, k_cols(n)] = k_grad[:rows].astype(BF16)
        far_ref[:, k_cols(n)] = k_grad[rows:].astype(BF16)
        scale_ref[n:n + 1, :] = jnp.sum(k_grad[:rows] * dclip_ref[:, k_cols(n)], axis=0, keepdims=True) + jnp.sum(
            k_grad[rows:] * kdclip_ref[:, k_cols(n)], axis=0, keepdims=True
        )

    ahead, behind = value_side(0), None
    for n in range(kv_heads):
        d_all, ahead = ahead, value_side(n + 1) if n + 1 < kv_heads else None
        ds2 = score_side(n, d_all)
        if behind is not None:
            key_side(n - 1, behind)
        behind = ds2
    key_side(kv_heads - 1, behind)


def output_kernel(nb, p_ref, ds_ref, k2_ref, v2_ref, out_hbm, gq_hbm, out_ref, gq_ref, sems):
    kv_heads = sems.shape[1]
    rows, group = out_ref.shape[0], out_ref.shape[1] // kv_heads
    hd = k2_ref.shape[1] // kv_heads
    heads = group // hd
    near_b = near_mask(rows).astype(F32).astype(BF16)
    far_b = 1.0 - near_b

    def copies(n):
        cols = pl.ds(pl.multiple_of(n * group, group), group)
        return (
            pltpu.make_async_copy(out_ref.at[:, cols], out_hbm.at[:, cols], sems.at[0, n]),
            pltpu.make_async_copy(gq_ref.at[:, cols], gq_hbm.at[:, cols], sems.at[1, n]),
        )

    def step(n, carry):
        cols = pl.ds(pl.multiple_of(n * hd, hd), hd)
        for left, right, dst, scale in ((v2_ref, p_ref, out_ref, None), (k2_ref, ds_ref, gq_ref, hd ** -0.5)):
            at = pl.ds(pl.multiple_of(n * heads * rows, rows), heads * rows)
            x = right[:, at]
            x2 = jnp.concatenate(
                [split(near_b, far_b, x[:, h * rows:(h + 1) * rows], nb) for h in range(heads)], axis=1
            )
            y = jnp.dot(left[:, cols].T, x2, preferred_element_type=F32)
            y = (y if scale is None else y * scale).astype(BF16)
            for h in range(heads):
                dst[:, pl.ds(pl.multiple_of(n * group + h * hd, hd), hd)] = y[:, h * rows:(h + 1) * rows].T
        for copy in copies(n):
            copy.start()
        return carry

    lax.fori_loop(0, kv_heads, step, 0, unroll=True)
    for n in range(kv_heads):
        for copy in copies(n):
            copy.wait()


def chip_sums(part, dp_count, seq_count):
    axes = ("dp", "seq")
    count = dp_count * seq_count
    core = seq_count
    part = part + lax.ppermute(part, axes, [(i, i ^ core) for i in range(count)])
    groups = [[i for i in reversed(range(count)) if bool(i & core) == second] for second in (False, True)]
    copies = jnp.broadcast_to(part.astype(BF16)[None], (count // 2,) + part.shape)
    parts = lax.all_to_all(copies, axes, split_axis=0, concat_axis=0, axis_index_groups=groups, tiled=True)
    return parts, part


def total_kernel(parts_ref, after_ref, out_ref):
    del after_ref
    out_ref[...] = jnp.sum(parts_ref[...].astype(F32), axis=0)


def finish_kernel(nb, grad_ref, slope_ref, *rest):
    backs, (gk_ref, gv_ref) = rest[:nb], rest[nb:]
    width = gk_ref.shape[1]
    for side, out in ((0, gk_ref), (1, gv_ref)):
        at = slice(side * width, (side + 1) * width)
        total = grad_ref[:, at].astype(F32)
        for back in backs:
            total = total + back[:, at].astype(F32)
        out[...] = (total * slope_ref[:, at]).astype(BF16)


def on_device(sizes, queries, keys, values, grad_out, quant_scale, doc_lengths):
    dp_count, seq_count = sizes
    nb = max(1, seq_count // 2)
    rows, width = keys.shape
    kv_heads, hd = quant_scale.shape[1], quant_scale.shape[2]
    heads = queries.shape[1] // hd
    vmem = pl.BlockSpec(memory_space=pltpu.VMEM)
    hbm = pl.BlockSpec(memory_space=pltpu.HBM)
    params = pltpu.CompilerParams(vmem_limit_bytes=36 * 1024 * 1024)
    shape = jax.ShapeDtypeStruct
    work = rows * rows * queries.shape[1]

    def call(kernel, name, flops, args, outs, in_specs=None, out_specs=None, scratch=()):
        return pl.pallas_call(
            kernel,
            out_shape=outs,
            in_specs=in_specs or [vmem] * len(args),
            out_specs=out_specs or (vmem,) * len(outs),
            scratch_shapes=scratch,
            compiler_params=params,
            cost_estimate=pl.CostEstimate(flops=flops, bytes_accessed=16 * rows * width, transcendentals=0),
            name=name,
        )(*args)

    def shift(array, d):
        return lax.ppermute(array, "seq", [(r, (r + d) % seq_count) for r in range(seq_count)])

    def unshift(array, d):
        return lax.ppermute(array, "seq", [((r + d) % seq_count, r) for r in range(seq_count)])

    far_k = [shift(keys, d) for d in range(1, nb + 1)]
    far_v = [shift(values, d) for d in range(1, nb + 1)]

    raw = (queries, grad_out, keys, values, quant_scale, doc_lengths)
    qt, gt, quants, slopes, dclips, bias, clips = call(
        functools.partial(prep_kernel, nb),
        "prep",
        2 * work,
        [pltpu.with_memory_space_constraint(x, pltpu.HBM) for x in raw],
        (
            shape((width, heads // kv_heads * rows), BF16),
            shape((width, heads // kv_heads * rows), BF16),
            shape((rows, 2 * width), BF16),
            pltpu.HBM((rows, 2 * width), F32),
            shape((rows, 2 * width), F32),
            shape((nb * rows, rows), F32),
            shape(quant_scale.shape, F32),
        ),
        in_specs=[hbm] * 6,
        out_specs=(vmem, vmem, vmem, hbm, vmem, vmem, vmem),
        scratch=[
            pltpu.VMEM(queries.shape, BF16),
            pltpu.VMEM(queries.shape, BF16),
            pltpu.VMEM(keys.shape, BF16),
            pltpu.VMEM(values.shape, BF16),
            pltpu.SMEM(doc_lengths.shape, jnp.int32),
            pltpu.VMEM((rows, 2 * width), F32),
            pltpu.SemaphoreType.DMA((7,)),
        ],
    )
    p, k2, kdclips = call(
        functools.partial(score_kernel, nb),
        "score",
        2 * (nb + 1) * work,
        (qt, quants, bias, clips, *far_k),
        (
            shape((nb * rows, heads * rows), BF16),
            shape(((nb + 1) * rows, width), BF16),
            shape((nb * rows, width), F32),
        ),
    )
    ds, v2, grads, far_grads, scale_part = call(
        functools.partial(grad_kernel, nb),
        "grad",
        6 * (nb + 1) * work,
        (qt, gt, quants, dclips, clips, p, kdclips, *far_v),
        (
            shape((nb * rows, heads * rows), BF16),
            shape(((nb + 1) * rows, width), BF16),
            shape((rows, 2 * width), BF16),
            shape((nb * rows, 2 * width), BF16),
            shape((2 * kv_heads, hd), F32),
        ),
    )
    backs = []
    for d in range(1, nb + 1):
        at = far_order(nb).index(d) * rows
        backs.append(unshift(lax.slice_in_dim(far_grads, at, at + rows, axis=0), d))
    parts, chip_part = chip_sums(scale_part, dp_count, seq_count)
    k2, _ = lax.optimization_barrier((k2, chip_part))
    attn_out, grad_queries = call(
        functools.partial(output_kernel, nb),
        "output",
        4 * (nb + 1) * work,
        (p, ds, k2, v2),
        (shape(queries.shape, BF16), shape(queries.shape, BF16)),
        out_specs=(hbm, hbm),
        scratch=[
            pltpu.VMEM(queries.shape, BF16),
            pltpu.VMEM(queries.shape, BF16),
            pltpu.SemaphoreType.DMA((2, kv_heads)),
        ],
    )
    grad_keys, grad_values = call(
        functools.partial(finish_kernel, nb),
        "finish",
        6 * rows * width,
        (grads, pltpu.with_memory_space_constraint(slopes, pltpu.HBM), *backs),
        (shape((rows, width), BF16), shape((rows, width), BF16)),
    )
    (grad_scale,) = call(
        total_kernel,
        "total",
        parts.size,
        (parts, pltpu.with_memory_space_constraint(grad_keys, pltpu.HBM)),
        (shape(parts.shape[1:], F32),),
        in_specs=[vmem, hbm],
    )
    return (attn_out, grad_queries, grad_keys, grad_values, grad_scale.reshape(quant_scale.shape))


def solution(mesh):
    rows = P(("dp", "seq"), None)
    return jax.shard_map(
        functools.partial(on_device, (mesh.shape["dp"], mesh.shape["seq"])),
        mesh=mesh,
        in_specs=(rows, rows, rows, rows, P(), P("dp", None)),
        out_specs=(rows, rows, rows, rows, P()),
        check_vma=False,
    )
```

```python
import functools
import math

import jax
import jax.numpy as jnp
from jax import lax
from jax.experimental import pallas as pl
from jax.experimental.pallas import tpu as pltpu
from jax.sharding import PartitionSpec as P

F32 = jnp.float32
BF16 = jnp.bfloat16
LEVELS = 127.0
NEG = -1e30


def sin_cos_half(u):
    r = (u - jnp.round(u)) * math.pi
    z = r * r
    s = z * (1.0 / 6227020800.0) - 1.0 / 39916800.0
    for c in (1.0 / 362880.0, -1.0 / 5040.0, 1.0 / 120.0, -1.0 / 6.0, 1.0):
        s = s * z + c
    s = s * r
    k = z * (1.0 / 479001600.0) - 1.0 / 3628800.0
    for c in (1.0 / 40320.0, -1.0 / 720.0, 1.0 / 24.0, -0.5, 1.0):
        k = k * z + c
    return s, k


def quant_parts(x, clip):
    inv = 1.0 / clip
    ratio = x * inv
    t = jnp.tanh(ratio)
    u = LEVELS * t
    s, k = sin_cos_half(u)
    level = u - s * k * (1.0 / math.pi)
    unit = level * (1.0 / LEVELS)
    slope = (2.0 * s * s) * (1.0 - t * t)
    return clip * unit, slope, unit - slope * ratio


def prep_kernel(nb, q_hbm, g_hbm, key_hbm, value_hbm, clip_hbm, len_hbm, qt_ref, gt_ref, quant_ref, slope_hbm,
                dclip_ref, bias_ref, clip_out, q_ref, g_ref, key_ref, value_ref, len_ref, slope_ref, sems):
    small = [
        pltpu.make_async_copy(src, dst, sems.at[i])
        for i, (src, dst) in enumerate(
            ((len_hbm, len_ref), (clip_hbm, clip_out), (key_hbm, key_ref), (value_hbm, value_ref))
        )
    ]
    large = [
        pltpu.make_async_copy(q_hbm, q_ref, sems.at[4]),
        pltpu.make_async_copy(g_hbm, g_ref, sems.at[5]),
    ]
    for copy in small + large:
        copy.start()
    rows = key_ref.shape[0]
    kv_heads, hd = clip_out.shape[1], clip_out.shape[2]
    group = q_ref.shape[1] // kv_heads
    base = lax.axis_index("seq") * rows
    for copy in small:
        copy.wait()
    for side, src in ((0, key_ref), (1, value_ref)):
        for n in range(kv_heads):
            x = src[:, n * hd:(n + 1) * hd].astype(F32)
            q, slope, dclip = quant_parts(x, clip_out[side, n:n + 1, :])
            at = slice((side * kv_heads + n) * hd, (side * kv_heads + n + 1) * hd)
            quant_ref[:, at] = q.astype(BF16)
            slope_ref[:, at] = slope
            dclip_ref[:, at] = dclip
    slope_copy = pltpu.make_async_copy(slope_ref, slope_hbm, sems.at[6])
    slope_copy.start()
    key = lax.broadcasted_iota(jnp.int32, (rows, rows), 0)
    row = lax.broadcasted_iota(jnp.int32, (rows, rows), 1)
    start = jnp.zeros((rows, rows), jnp.int32)
    end = jnp.int32(0)
    for d in range(len_ref.shape[1]):
        end = end + len_ref[0, d]
        start = jnp.where(row + base >= end, end, start)
    for b in range(nb):
        pos = jnp.where(key <= row, key, key - nb * rows) if b == 0 else key - b * rows
        bias_ref[b * rows:(b + 1) * rows, :] = jnp.where(pos + base >= start, 0.0, NEG)
    for copy, src, dst in zip(large, (q_ref, g_ref), (qt_ref, gt_ref)):
        copy.wait()
        for n in range(kv_heads):
            for h in range(group // hd):
                at = n * group + h * hd
                dst[n * hd:(n + 1) * hd, h * rows:(h + 1) * rows] = src[:, at:at + hd].T
    slope_copy.wait()


ACROSS = (((1,), (1,)), ((), ()))


def far_order(nb):
    return [nb] + list(range(1, nb))


def near_mask(rows):
    key = lax.broadcasted_iota(jnp.int32, (rows, rows), 0)
    row = lax.broadcasted_iota(jnp.int32, (rows, rows), 1)
    return key <= row


def merge(near, x, nb):
    rows = near.shape[0]
    first = jnp.where(near, x[:rows], x[rows:2 * rows])
    return jnp.concatenate([first, x[2 * rows:]], axis=0) if nb > 1 else first


def split(near_b, far_b, x, nb):
    rows = near_b.shape[0]
    parts = [x[:rows] * near_b, x[:rows] * far_b]
    if nb > 1:
        parts.append(x[rows:])
    return jnp.concatenate(parts, axis=0)


def score_kernel(nb, qt_ref, quant_ref, bias_ref, clip_ref, *rest):
    far, (p_ref, k2_ref, dclip_ref) = rest[:nb], rest[nb:]
    kv_heads, hd = clip_ref.shape[1], clip_ref.shape[2]
    rows, span = bias_ref.shape[1], qt_ref.shape[1]
    factor = hd ** -0.5 * math.log2(math.e)
    near = near_mask(rows)

    bias = bias_ref[...]

    def scores(n):
        cols = slice(n * hd, (n + 1) * hd)
        ks = [quant_ref[:, cols]]
        for j, d in enumerate(far_order(nb)):
            q, _, dclip = quant_parts(far[d - 1][:, cols].astype(F32), clip_ref[0, n:n + 1, :])
            ks.append(q.astype(BF16))
            dclip_ref[j * rows:(j + 1) * rows, cols] = dclip
        k2 = jnp.concatenate(ks, axis=0)
        k2_ref[:, cols] = k2
        return jnp.dot(k2, qt_ref[cols, :], preferred_element_type=F32)

    ahead = scores(0)
    for n in range(kv_heads):
        s_all, ahead = ahead, scores(n + 1) if n + 1 < kv_heads else None
        for h in range(span // rows):
            s = merge(near, s_all[:, h * rows:(h + 1) * rows], nb) * factor + bias
            w = jnp.exp2(s - jnp.max(s, axis=0, keepdims=True))
            p = w * (1.0 / jnp.sum(w, axis=0, keepdims=True))
            p_ref[:, n * span + h * rows:n * span + (h + 1) * rows] = p.astype(BF16)


def grad_kernel(nb, qt_ref, gt_ref, quant_ref, dclip_ref, clip_ref, p_ref, kdclip_ref, *rest):
    far_v, (ds_ref, v2_ref, grad_ref, far_ref, spread_ref, scale_ref) = rest[:nb], rest[nb:]
    kv_heads, hd = clip_ref.shape[1], clip_ref.shape[2]
    rows, span = dclip_ref.shape[0], gt_ref.shape[1]
    heads = span // rows
    width = kv_heads * hd
    scale = hd ** -0.5
    near = near_mask(rows)
    near_b = near.astype(F32).astype(BF16)
    far_b = 1.0 - near_b

    def k_cols(n):
        return slice(n * hd, (n + 1) * hd)

    def v_cols(n):
        return slice(width + n * hd, width + (n + 1) * hd)

    def value_side(n):
        p2 = jnp.concatenate(
            [split(near_b, far_b, p_ref[:, n * span + h * rows:n * span + (h + 1) * rows], nb) for h in range(heads)],
            axis=1,
        )
        v_grad = lax.dot_general(gt_ref[k_cols(n), :], p2, ACROSS, preferred_element_type=F32).T
        vs, vd = [quant_ref[:, v_cols(n)]], [dclip_ref[:, v_cols(n)]]
        for d in far_order(nb):
            q, _, dc = quant_parts(far_v[d - 1][:, k_cols(n)].astype(F32), clip_ref[1, n:n + 1, :])
            vs.append(q.astype(BF16))
            vd.append(dc)
        v2 = jnp.concatenate(vs, axis=0)
        v2_ref[:, k_cols(n)] = v2
        grad_ref[:, v_cols(n)] = v_grad[:rows].astype(BF16)
        far_ref[:, v_cols(n)] = v_grad[rows:].astype(BF16)
        scale_ref[kv_heads + n:kv_heads + n + 1, :] = jnp.sum(
            v_grad * jnp.concatenate(vd, axis=0), axis=0, keepdims=True
        )
        return jnp.dot(v2, gt_ref[k_cols(n), :], preferred_element_type=F32)

    def score_side(n, d_all):
        ds = []
        for h in range(heads):
            dp = merge(near, d_all[:, h * rows:(h + 1) * rows], nb)
            at = slice(n * span + h * rows, n * span + (h + 1) * rows)
            p = p_ref[:, at].astype(F32)
            delta = jnp.sum(p * dp, axis=0, keepdims=True)
            ds_b = (p * (dp - delta)).astype(BF16)
            ds_ref[:, at] = ds_b
            ds.append(split(near_b, far_b, ds_b, nb))
        return jnp.concatenate(ds, axis=1)

    def key_side(n, ds2):
        k_grad = (lax.dot_general(qt_ref[k_cols(n), :], ds2, ACROSS, preferred_element_type=F32) * scale).T
        grad_ref[:, k_cols(n)] = k_grad[:rows].astype(BF16)
        far_ref[:, k_cols(n)] = k_grad[rows:].astype(BF16)
        scale_ref[n:n + 1, :] = jnp.sum(k_grad[:rows] * dclip_ref[:, k_cols(n)], axis=0, keepdims=True) + jnp.sum(
            k_grad[rows:] * kdclip_ref[:, k_cols(n)], axis=0, keepdims=True
        )

    ahead, behind = value_side(0), None
    for n in range(kv_heads):
        d_all, ahead = ahead, value_side(n + 1) if n + 1 < kv_heads else None
        ds2 = score_side(n, d_all)
        if behind is not None:
            key_side(n - 1, behind)
        behind = ds2
    key_side(kv_heads - 1, behind)
    part = scale_ref[...].astype(BF16)

    def spread(i, carry):
        spread_ref[i] = part
        return carry

    lax.fori_loop(0, spread_ref.shape[0], spread, 0, unroll=8)


def output_kernel(nb, p_ref, ds_ref, k2_ref, v2_ref, grad_ref, slope_hbm, *rest):
    backs, rest = rest[:nb], rest[nb:]
    out_hbm, gq_hbm, gk_hbm, gv_hbm, out_ref, gq_ref, gk_ref, gv_ref, slope_ref, back_ref, sems, more_sems = rest
    loads = [pltpu.make_async_copy(slope_hbm, slope_ref, more_sems.at[2])]
    loads += [pltpu.make_async_copy(back, back_ref.at[d], more_sems.at[3 + d]) for d, back in enumerate(backs)]
    for copy in loads:
        copy.start()
    kv_heads = sems.shape[1]
    rows, group = out_ref.shape[0], out_ref.shape[1] // kv_heads
    hd = k2_ref.shape[1] // kv_heads
    heads = group // hd
    near_b = near_mask(rows).astype(F32).astype(BF16)
    far_b = 1.0 - near_b

    def copies(n):
        cols = pl.ds(pl.multiple_of(n * group, group), group)
        return (
            pltpu.make_async_copy(out_ref.at[:, cols], out_hbm.at[:, cols], sems.at[0, n]),
            pltpu.make_async_copy(gq_ref.at[:, cols], gq_hbm.at[:, cols], sems.at[1, n]),
        )

    def step(n, carry):
        cols = pl.ds(pl.multiple_of(n * hd, hd), hd)
        for left, right, dst, scale in ((v2_ref, p_ref, out_ref, None), (k2_ref, ds_ref, gq_ref, hd ** -0.5)):
            at = pl.ds(pl.multiple_of(n * heads * rows, rows), heads * rows)
            x = right[:, at]
            x2 = jnp.concatenate(
                [split(near_b, far_b, x[:, h * rows:(h + 1) * rows], nb) for h in range(heads)], axis=1
            )
            y = jnp.dot(left[:, cols].T, x2, preferred_element_type=F32)
            y = (y if scale is None else y * scale).astype(BF16)
            for h in range(heads):
                dst[:, pl.ds(pl.multiple_of(n * group + h * hd, hd), hd)] = y[:, h * rows:(h + 1) * rows].T
        for copy in copies(n):
            copy.start()
        return carry

    lax.fori_loop(0, kv_heads, step, 0, unroll=True)
    for copy in loads:
        copy.wait()
    stores = []
    width = gk_ref.shape[1]
    for side, ref, dst in ((0, gk_ref, gk_hbm), (1, gv_ref, gv_hbm)):
        at = slice(side * width, (side + 1) * width)
        total = grad_ref[:, at].astype(F32)
        for d in range(nb):
            total = total + back_ref[d, :, at].astype(F32)
        ref[...] = (total * slope_ref[:, at]).astype(BF16)
        stores.append(pltpu.make_async_copy(ref, dst, more_sems.at[side]))
        stores[-1].start()
    for n in range(kv_heads):
        for copy in copies(n):
            copy.wait()
    for copy in stores:
        copy.wait()


def total_kernel(parts_ref, after_ref, out_ref):
    del after_ref
    out_ref[...] = jnp.sum(parts_ref[...].astype(F32), axis=0)


def on_device(sizes, queries, keys, values, grad_out, quant_scale, doc_lengths):
    dp_count, seq_count = sizes
    count = dp_count * seq_count
    nb = max(1, seq_count // 2)
    rows, width = keys.shape
    kv_heads, hd = quant_scale.shape[1], quant_scale.shape[2]
    heads = queries.shape[1] // hd
    vmem = pl.BlockSpec(memory_space=pltpu.VMEM)
    hbm = pl.BlockSpec(memory_space=pltpu.HBM)
    params = pltpu.CompilerParams(vmem_limit_bytes=36 * 1024 * 1024)
    shape = jax.ShapeDtypeStruct
    work = rows * rows * queries.shape[1]

    def call(kernel, name, flops, args, outs, in_specs=None, out_specs=None, scratch=()):
        return pl.pallas_call(
            kernel,
            out_shape=outs,
            in_specs=in_specs or [vmem] * len(args),
            out_specs=out_specs or (vmem,) * len(outs),
            scratch_shapes=scratch,
            compiler_params=params,
            cost_estimate=pl.CostEstimate(flops=flops, bytes_accessed=16 * rows * width, transcendentals=0),
            name=name,
        )(*args)

    def shift(array, d):
        return lax.ppermute(array, "seq", [(r, (r + d) % seq_count) for r in range(seq_count)])

    def unshift(array, d):
        return lax.ppermute(array, "seq", [((r + d) % seq_count, r) for r in range(seq_count)])

    far_k = [shift(keys, d) for d in range(1, nb + 1)]
    far_v = [shift(values, d) for d in range(1, nb + 1)]

    raw = (queries, grad_out, keys, values, quant_scale, doc_lengths)
    qt, gt, quants, slopes, dclips, bias, clips = call(
        functools.partial(prep_kernel, nb),
        "prep",
        2 * work,
        [pltpu.with_memory_space_constraint(x, pltpu.HBM) for x in raw],
        (
            shape((width, heads // kv_heads * rows), BF16),
            shape((width, heads // kv_heads * rows), BF16),
            shape((rows, 2 * width), BF16),
            pltpu.HBM((rows, 2 * width), F32),
            shape((rows, 2 * width), F32),
            shape((nb * rows, rows), F32),
            shape(quant_scale.shape, F32),
        ),
        in_specs=[hbm] * 6,
        out_specs=(vmem, vmem, vmem, hbm, vmem, vmem, vmem),
        scratch=[
            pltpu.VMEM(queries.shape, BF16),
            pltpu.VMEM(queries.shape, BF16),
            pltpu.VMEM(keys.shape, BF16),
            pltpu.VMEM(values.shape, BF16),
            pltpu.SMEM(doc_lengths.shape, jnp.int32),
            pltpu.VMEM((rows, 2 * width), F32),
            pltpu.SemaphoreType.DMA((7,)),
        ],
    )
    p, k2, kdclips = call(
        functools.partial(score_kernel, nb),
        "score",
        2 * (nb + 1) * work,
        (qt, quants, bias, clips, *far_k),
        (
            shape((nb * rows, heads * rows), BF16),
            shape(((nb + 1) * rows, width), BF16),
            shape((nb * rows, width), F32),
        ),
    )
    ds, v2, grads, far_grads, spread = call(
        functools.partial(grad_kernel, nb),
        "grad",
        6 * (nb + 1) * work,
        (qt, gt, quants, dclips, clips, p, kdclips, *far_v),
        (
            shape((nb * rows, heads * rows), BF16),
            shape(((nb + 1) * rows, width), BF16),
            shape((rows, 2 * width), BF16),
            shape((nb * rows, 2 * width), BF16),
            pltpu.VMEM((count, 2 * kv_heads, hd), BF16),
        ),
        scratch=[pltpu.VMEM((2 * kv_heads, hd), F32)],
    )
    backs = []
    for d in range(1, nb + 1):
        at = far_order(nb).index(d) * rows
        backs.append(unshift(lax.slice_in_dim(far_grads, at, at + rows, axis=0), d))
    parts = lax.all_to_all(
        spread,
        ("dp", "seq"),
        split_axis=0,
        concat_axis=0,
        axis_index_groups=[list(reversed(range(count)))],
        tiled=True,
    )
    pinned = pltpu.with_memory_space_constraint(slopes, pltpu.HBM)
    attn_out, grad_queries, grad_keys, grad_values = call(
        functools.partial(output_kernel, nb),
        "output",
        4 * (nb + 1) * work,
        (p, ds, k2, v2, grads, pinned, *backs),
        (
            shape(queries.shape, BF16),
            shape(queries.shape, BF16),
            shape((rows, width), BF16),
            shape((rows, width), BF16),
        ),
        in_specs=[vmem] * 5 + [hbm] + [pl.BlockSpec(memory_space=pl.ANY)] * nb,
        out_specs=(hbm,) * 4,
        scratch=[
            pltpu.VMEM(queries.shape, BF16),
            pltpu.VMEM(queries.shape, BF16),
            pltpu.VMEM((rows, width), BF16),
            pltpu.VMEM((rows, width), BF16),
            pltpu.VMEM((rows, 2 * width), F32),
            pltpu.VMEM((nb, rows, 2 * width), BF16),
            pltpu.SemaphoreType.DMA((2, kv_heads)),
            pltpu.SemaphoreType.DMA((3 + nb,)),
        ],
    )
    (grad_scale,) = call(
        total_kernel,
        "total",
        parts.size,
        (parts, pltpu.with_memory_space_constraint(grad_keys, pltpu.HBM)),
        (shape(parts.shape[1:], F32),),
        in_specs=[vmem, hbm],
    )
    return (attn_out, grad_queries, grad_keys, grad_values, grad_scale.reshape(quant_scale.shape))


def solution(mesh):
    rows = P(("dp", "seq"), None)
    return jax.shard_map(
        functools.partial(on_device, (mesh.shape["dp"], mesh.shape["seq"])),
        mesh=mesh,
        in_specs=(rows, rows, rows, rows, P(), P("dp", None)),
        out_specs=(rows, rows, rows, rows, P()),
        check_vma=False,
    )
```

```python
import functools
import math

import jax
import jax.numpy as jnp
from jax import lax
from jax.experimental import pallas as pl
from jax.experimental.pallas import tpu as pltpu
from jax.sharding import PartitionSpec as P

F32 = jnp.float32
BF16 = jnp.bfloat16
LEVELS = 127.0
NEG = -1e30


def sin_cos_half(u):
    r = (u - jnp.round(u)) * math.pi
    z = r * r
    s = z * (1.0 / 6227020800.0) - 1.0 / 39916800.0
    for c in (1.0 / 362880.0, -1.0 / 5040.0, 1.0 / 120.0, -1.0 / 6.0, 1.0):
        s = s * z + c
    s = s * r
    k = z * (1.0 / 479001600.0) - 1.0 / 3628800.0
    for c in (1.0 / 40320.0, -1.0 / 720.0, 1.0 / 24.0, -0.5, 1.0):
        k = k * z + c
    return s, k


def quant_parts(x, clip):
    inv = 1.0 / clip
    ratio = x * inv
    t = jnp.tanh(ratio)
    u = LEVELS * t
    s, k = sin_cos_half(u)
    level = u - s * k * (1.0 / math.pi)
    unit = level * (1.0 / LEVELS)
    slope = (2.0 * s * s) * (1.0 - t * t)
    return clip * unit, slope, unit - slope * ratio


def prep_kernel(nb, key_hbm, value_hbm, clip_hbm, len_hbm, quant_ref, slope_hbm, dclip_ref, bias_ref, clip_out,
                key_ref, value_ref, len_ref, slope_ref, sems):
    loads = [
        pltpu.make_async_copy(src, dst, sems.at[i])
        for i, (src, dst) in enumerate(
            ((len_hbm, len_ref), (clip_hbm, clip_out), (key_hbm, key_ref), (value_hbm, value_ref))
        )
    ]
    for copy in loads:
        copy.start()
    rows = key_ref.shape[0]
    kv_heads, hd = clip_out.shape[1], clip_out.shape[2]
    base = lax.axis_index("seq") * rows
    for copy in loads:
        copy.wait()
    for side, src in ((0, key_ref), (1, value_ref)):
        for n in range(kv_heads):
            x = src[:, n * hd:(n + 1) * hd].astype(F32)
            q, slope, dclip = quant_parts(x, clip_out[side, n:n + 1, :])
            at = slice((side * kv_heads + n) * hd, (side * kv_heads + n + 1) * hd)
            quant_ref[:, at] = q.astype(BF16)
            slope_ref[:, at] = slope
            dclip_ref[:, at] = dclip
    slope_copy = pltpu.make_async_copy(slope_ref, slope_hbm, sems.at[4])
    slope_copy.start()
    key = lax.broadcasted_iota(jnp.int32, (rows, rows), 0)
    row = lax.broadcasted_iota(jnp.int32, (rows, rows), 1)
    start = jnp.zeros((rows, rows), jnp.int32)
    end = jnp.int32(0)
    for d in range(len_ref.shape[1]):
        end = end + len_ref[0, d]
        start = jnp.where(row + base >= end, end, start)
    for b in range(nb):
        pos = jnp.where(key <= row, key, key - nb * rows) if b == 0 else key - b * rows
        bias_ref[b * rows:(b + 1) * rows, :] = jnp.where(pos + base >= start, 0.0, NEG)
    slope_copy.wait()


def turn_kernel(kv_heads, q_hbm, g_hbm, qt_ref, gt_ref, q_ref, g_ref, sems):
    rows, group = q_ref.shape[0], q_ref.shape[1] // kv_heads
    hd = qt_ref.shape[0] // kv_heads
    loads = []
    for side, (src, dst) in enumerate(((q_hbm, q_ref), (g_hbm, g_ref))):
        for n in range(kv_heads):
            cols = slice(n * group, (n + 1) * group)
            loads.append(pltpu.make_async_copy(src.at[:, cols], dst.at[:, cols], sems.at[side, n]))
            loads[-1].start()
    for side, (src, dst) in enumerate(((q_ref, qt_ref), (g_ref, gt_ref))):
        for n in range(kv_heads):
            loads[side * kv_heads + n].wait()
            for h in range(group // hd):
                at = n * group + h * hd
                dst[n * hd:(n + 1) * hd, h * rows:(h + 1) * rows] = src[:, at:at + hd].T


ACROSS = (((1,), (1,)), ((), ()))


def far_order(nb):
    return [nb] + list(range(1, nb))


def near_mask(rows):
    key = lax.broadcasted_iota(jnp.int32, (rows, rows), 0)
    row = lax.broadcasted_iota(jnp.int32, (rows, rows), 1)
    return key <= row


def merge(near, x, nb):
    rows = near.shape[0]
    first = jnp.where(near, x[:rows], x[rows:2 * rows])
    return jnp.concatenate([first, x[2 * rows:]], axis=0) if nb > 1 else first


def split(near_b, far_b, x, nb):
    rows = near_b.shape[0]
    parts = [x[:rows] * near_b, x[:rows] * far_b]
    if nb > 1:
        parts.append(x[rows:])
    return jnp.concatenate(parts, axis=0)


def score_kernel(nb, qt_ref, gt_ref, quant_ref, bias_ref, clip_ref, *rest):
    far, (p_ref, k2_ref, dclip_ref, vgrad_ref) = rest[:nb], rest[nb:]
    kv_heads, hd = clip_ref.shape[1], clip_ref.shape[2]
    rows, span = bias_ref.shape[1], qt_ref.shape[1]
    factor = hd ** -0.5 * math.log2(math.e)
    near = near_mask(rows)
    near_b = near.astype(F32).astype(BF16)
    far_b = 1.0 - near_b

    bias = bias_ref[...]

    def scores(n):
        cols = slice(n * hd, (n + 1) * hd)
        ks = [quant_ref[:, cols]]
        for j, d in enumerate(far_order(nb)):
            q, _, dclip = quant_parts(far[d - 1][:, cols].astype(F32), clip_ref[0, n:n + 1, :])
            ks.append(q.astype(BF16))
            dclip_ref[j * rows:(j + 1) * rows, cols] = dclip
        k2 = jnp.concatenate(ks, axis=0)
        k2_ref[:, cols] = k2
        return jnp.dot(k2, qt_ref[cols, :], preferred_element_type=F32)

    def softmax(n, s_all):
        ps = []
        for h in range(span // rows):
            s = merge(near, s_all[:, h * rows:(h + 1) * rows], nb) * factor + bias
            w = jnp.exp2(s - jnp.max(s, axis=0, keepdims=True))
            p = (w * (1.0 / jnp.sum(w, axis=0, keepdims=True))).astype(BF16)
            p_ref[:, n * span + h * rows:n * span + (h + 1) * rows] = p
            ps.append(split(near_b, far_b, p, nb))
        return jnp.concatenate(ps, axis=1)

    def value_grad(n, p2):
        cols = slice(n * hd, (n + 1) * hd)
        vgrad_ref[:, cols] = lax.dot_general(gt_ref[cols, :], p2, ACROSS, preferred_element_type=F32).T

    ahead, behind = scores(0), None
    for n in range(kv_heads):
        s_all, ahead = ahead, scores(n + 1) if n + 1 < kv_heads else None
        p2 = softmax(n, s_all)
        if behind is not None:
            value_grad(n - 1, behind)
        behind = p2
    value_grad(kv_heads - 1, behind)


def grad_kernel(nb, qt_ref, gt_ref, quant_ref, dclip_ref, clip_ref, p_ref, kdclip_ref, vgrad_ref, *rest):
    far_v, (ds_ref, v2_ref, grad_ref, far_ref, spread_ref, scale_ref) = rest[:nb], rest[nb:]
    kv_heads, hd = clip_ref.shape[1], clip_ref.shape[2]
    rows, span = dclip_ref.shape[0], gt_ref.shape[1]
    heads = span // rows
    width = kv_heads * hd
    scale = hd ** -0.5
    near = near_mask(rows)
    near_b = near.astype(F32).astype(BF16)
    far_b = 1.0 - near_b

    def k_cols(n):
        return slice(n * hd, (n + 1) * hd)

    def v_cols(n):
        return slice(width + n * hd, width + (n + 1) * hd)

    def value_side(n):
        v_grad = vgrad_ref[:, k_cols(n)]
        vs, vd = [quant_ref[:, v_cols(n)]], [dclip_ref[:, v_cols(n)]]
        for d in far_order(nb):
            q, _, dc = quant_parts(far_v[d - 1][:, k_cols(n)].astype(F32), clip_ref[1, n:n + 1, :])
            vs.append(q.astype(BF16))
            vd.append(dc)
        v2 = jnp.concatenate(vs, axis=0)
        v2_ref[:, k_cols(n)] = v2
        grad_ref[:, v_cols(n)] = v_grad[:rows].astype(BF16)
        far_ref[:, v_cols(n)] = v_grad[rows:].astype(BF16)
        scale_ref[kv_heads + n:kv_heads + n + 1, :] = jnp.sum(
            v_grad * jnp.concatenate(vd, axis=0), axis=0, keepdims=True
        )
        return jnp.dot(v2, gt_ref[k_cols(n), :], preferred_element_type=F32)

    def score_side(n, d_all):
        ds = []
        for h in range(heads):
            dp = merge(near, d_all[:, h * rows:(h + 1) * rows], nb)
            at = slice(n * span + h * rows, n * span + (h + 1) * rows)
            p = p_ref[:, at].astype(F32)
            delta = jnp.sum(p * dp, axis=0, keepdims=True)
            ds_b = (p * (dp - delta)).astype(BF16)
            ds_ref[:, at] = ds_b
            ds.append(split(near_b, far_b, ds_b, nb))
        return jnp.concatenate(ds, axis=1)

    def key_side(n, ds2):
        k_grad = (lax.dot_general(qt_ref[k_cols(n), :], ds2, ACROSS, preferred_element_type=F32) * scale).T
        grad_ref[:, k_cols(n)] = k_grad[:rows].astype(BF16)
        far_ref[:, k_cols(n)] = k_grad[rows:].astype(BF16)
        scale_ref[n:n + 1, :] = jnp.sum(k_grad[:rows] * dclip_ref[:, k_cols(n)], axis=0, keepdims=True) + jnp.sum(
            k_grad[rows:] * kdclip_ref[:, k_cols(n)], axis=0, keepdims=True
        )

    ahead, behind = value_side(0), None
    for n in range(kv_heads):
        d_all, ahead = ahead, value_side(n + 1) if n + 1 < kv_heads else None
        ds2 = score_side(n, d_all)
        if behind is not None:
            key_side(n - 1, behind)
        behind = ds2
    key_side(kv_heads - 1, behind)
    part = scale_ref[...].astype(BF16)

    def spread(i, carry):
        spread_ref[i] = part
        return carry

    lax.fori_loop(0, spread_ref.shape[0], spread, 0, unroll=8)


def output_kernel(nb, p_ref, ds_ref, k2_ref, v2_ref, grad_ref, slope_hbm, *rest):
    backs, rest = rest[:nb], rest[nb:]
    out_hbm, gq_hbm, gk_hbm, gv_hbm, out_ref, gq_ref, gk_ref, gv_ref, slope_ref, back_ref, sems, more_sems = rest
    loads = [pltpu.make_async_copy(slope_hbm, slope_ref, more_sems.at[2])]
    loads += [pltpu.make_async_copy(back, back_ref.at[d], more_sems.at[3 + d]) for d, back in enumerate(backs)]
    for copy in loads:
        copy.start()
    kv_heads = sems.shape[1]
    rows, group = out_ref.shape[0], out_ref.shape[1] // kv_heads
    hd = k2_ref.shape[1] // kv_heads
    heads = group // hd
    near_b = near_mask(rows).astype(F32).astype(BF16)
    far_b = 1.0 - near_b

    def copies(n):
        cols = pl.ds(pl.multiple_of(n * group, group), group)
        return (
            pltpu.make_async_copy(out_ref.at[:, cols], out_hbm.at[:, cols], sems.at[0, n]),
            pltpu.make_async_copy(gq_ref.at[:, cols], gq_hbm.at[:, cols], sems.at[1, n]),
        )

    def step(n, carry):
        cols = pl.ds(pl.multiple_of(n * hd, hd), hd)
        for left, right, dst, scale in ((v2_ref, p_ref, out_ref, None), (k2_ref, ds_ref, gq_ref, hd ** -0.5)):
            at = pl.ds(pl.multiple_of(n * heads * rows, rows), heads * rows)
            x = right[:, at]
            x2 = jnp.concatenate(
                [split(near_b, far_b, x[:, h * rows:(h + 1) * rows], nb) for h in range(heads)], axis=1
            )
            y = jnp.dot(left[:, cols].T, x2, preferred_element_type=F32)
            y = (y if scale is None else y * scale).astype(BF16)
            for h in range(heads):
                dst[:, pl.ds(pl.multiple_of(n * group + h * hd, hd), hd)] = y[:, h * rows:(h + 1) * rows].T
        for copy in copies(n):
            copy.start()
        return carry

    lax.fori_loop(0, kv_heads, step, 0, unroll=True)
    for copy in loads:
        copy.wait()
    stores = []
    width = gk_ref.shape[1]
    for side, ref, dst in ((0, gk_ref, gk_hbm), (1, gv_ref, gv_hbm)):
        at = slice(side * width, (side + 1) * width)
        total = grad_ref[:, at].astype(F32)
        for d in range(nb):
            total = total + back_ref[d, :, at].astype(F32)
        ref[...] = (total * slope_ref[:, at]).astype(BF16)
        stores.append(pltpu.make_async_copy(ref, dst, more_sems.at[side]))
        stores[-1].start()
    for n in range(kv_heads):
        for copy in copies(n):
            copy.wait()
    for copy in stores:
        copy.wait()


def total_kernel(parts_ref, after_ref, out_ref):
    del after_ref
    out_ref[...] = jnp.sum(parts_ref[...].astype(F32), axis=0)


def on_device(sizes, queries, keys, values, grad_out, quant_scale, doc_lengths):
    dp_count, seq_count = sizes
    count = dp_count * seq_count
    nb = max(1, seq_count // 2)
    rows, width = keys.shape
    kv_heads, hd = quant_scale.shape[1], quant_scale.shape[2]
    heads = queries.shape[1] // hd
    vmem = pl.BlockSpec(memory_space=pltpu.VMEM)
    hbm = pl.BlockSpec(memory_space=pltpu.HBM)
    params = pltpu.CompilerParams(vmem_limit_bytes=36 * 1024 * 1024)
    shape = jax.ShapeDtypeStruct
    work = rows * rows * queries.shape[1]

    def call(kernel, name, flops, args, outs, in_specs=None, out_specs=None, scratch=()):
        return pl.pallas_call(
            kernel,
            out_shape=outs,
            in_specs=in_specs or [vmem] * len(args),
            out_specs=out_specs or (vmem,) * len(outs),
            scratch_shapes=scratch,
            compiler_params=params,
            cost_estimate=pl.CostEstimate(flops=flops, bytes_accessed=16 * rows * width, transcendentals=0),
            name=name,
        )(*args)

    def shift(array, d):
        return lax.ppermute(array, "seq", [(r, (r + d) % seq_count) for r in range(seq_count)])

    def unshift(array, d):
        return lax.ppermute(array, "seq", [((r + d) % seq_count, r) for r in range(seq_count)])

    def pinned(*arrays):
        return [pltpu.with_memory_space_constraint(x, pltpu.HBM) for x in arrays]

    far_k = [shift(keys, d) for d in range(1, nb + 1)]
    quants, slopes, dclips, bias, clips = call(
        functools.partial(prep_kernel, nb),
        "prep",
        100 * rows * width,
        pinned(keys, values, quant_scale, doc_lengths),
        (
            shape((rows, 2 * width), BF16),
            pltpu.HBM((rows, 2 * width), F32),
            shape((rows, 2 * width), F32),
            shape((nb * rows, rows), F32),
            shape(quant_scale.shape, F32),
        ),
        in_specs=[hbm] * 4,
        out_specs=(vmem, hbm, vmem, vmem, vmem),
        scratch=[
            pltpu.VMEM(keys.shape, BF16),
            pltpu.VMEM(values.shape, BF16),
            pltpu.SMEM(doc_lengths.shape, jnp.int32),
            pltpu.VMEM((rows, 2 * width), F32),
            pltpu.SemaphoreType.DMA((5,)),
        ],
    )
    late_values, bias = lax.optimization_barrier((values, bias))
    far_v = [shift(late_values, d) for d in range(1, nb + 1)]
    qt, gt = call(
        functools.partial(turn_kernel, kv_heads),
        "turn",
        work,
        pinned(queries, grad_out),
        (shape((width, heads // kv_heads * rows), BF16), shape((width, heads // kv_heads * rows), BF16)),
        in_specs=[hbm] * 2,
        scratch=[
            pltpu.VMEM(queries.shape, BF16),
            pltpu.VMEM(queries.shape, BF16),
            pltpu.SemaphoreType.DMA((2, kv_heads)),
        ],
    )
    p, k2, kdclips, v_grads = call(
        functools.partial(score_kernel, nb),
        "score",
        4 * (nb + 1) * work,
        (qt, gt, quants, bias, clips, *far_k),
        (
            shape((nb * rows, heads * rows), BF16),
            shape(((nb + 1) * rows, width), BF16),
            shape((nb * rows, width), F32),
            shape(((nb + 1) * rows, width), F32),
        ),
    )
    ds, v2, grads, far_grads, spread = call(
        functools.partial(grad_kernel, nb),
        "grad",
        4 * (nb + 1) * work,
        (qt, gt, quants, dclips, clips, p, kdclips, v_grads, *far_v),
        (
            shape((nb * rows, heads * rows), BF16),
            shape(((nb + 1) * rows, width), BF16),
            shape((rows, 2 * width), BF16),
            shape((nb * rows, 2 * width), BF16),
            pltpu.VMEM((count, 2 * kv_heads, hd), BF16),
        ),
        scratch=[pltpu.VMEM((2 * kv_heads, hd), F32)],
    )
    backs = []
    for d in range(1, nb + 1):
        at = far_order(nb).index(d) * rows
        backs.append(unshift(lax.slice_in_dim(far_grads, at, at + rows, axis=0), d))
    parts = lax.all_to_all(
        spread,
        ("dp", "seq"),
        split_axis=0,
        concat_axis=0,
        axis_index_groups=[list(reversed(range(count)))],
        tiled=True,
    )
    attn_out, grad_queries, grad_keys, grad_values = call(
        functools.partial(output_kernel, nb),
        "output",
        4 * (nb + 1) * work,
        (p, ds, k2, v2, grads, *pinned(slopes), *backs),
        (
            shape(queries.shape, BF16),
            shape(queries.shape, BF16),
            shape((rows, width), BF16),
            shape((rows, width), BF16),
        ),
        in_specs=[vmem] * 5 + [hbm] + [pl.BlockSpec(memory_space=pl.ANY)] * nb,
        out_specs=(hbm,) * 4,
        scratch=[
            pltpu.VMEM(queries.shape, BF16),
            pltpu.VMEM(queries.shape, BF16),
            pltpu.VMEM((rows, width), BF16),
            pltpu.VMEM((rows, width), BF16),
            pltpu.VMEM((rows, 2 * width), F32),
            pltpu.VMEM((nb, rows, 2 * width), BF16),
            pltpu.SemaphoreType.DMA((2, kv_heads)),
            pltpu.SemaphoreType.DMA((3 + nb,)),
        ],
    )
    (grad_scale,) = call(
        total_kernel,
        "total",
        parts.size,
        (parts, *pinned(grad_keys)),
        (shape(parts.shape[1:], F32),),
        in_specs=[vmem, hbm],
    )
    return (attn_out, grad_queries, grad_keys, grad_values, grad_scale.reshape(quant_scale.shape))


def solution(mesh):
    rows = P(("dp", "seq"), None)
    return jax.shard_map(
        functools.partial(on_device, (mesh.shape["dp"], mesh.shape["seq"])),
        mesh=mesh,
        in_specs=(rows, rows, rows, rows, P(), P("dp", None)),
        out_specs=(rows, rows, rows, rows, P()),
        check_vma=False,
    )
```

```python
import functools
import math

import jax
import jax.numpy as jnp
from jax import lax
from jax.experimental import pallas as pl
from jax.experimental.pallas import tpu as pltpu
from jax.sharding import PartitionSpec as P

F32 = jnp.float32
BF16 = jnp.bfloat16
LEVELS = 127.0
NEG = -1e30


def sin_cos_half(u):
    r = (u - jnp.round(u)) * math.pi
    z = r * r
    s = z * (1.0 / 6227020800.0) - 1.0 / 39916800.0
    for c in (1.0 / 362880.0, -1.0 / 5040.0, 1.0 / 120.0, -1.0 / 6.0, 1.0):
        s = s * z + c
    s = s * r
    k = z * (1.0 / 479001600.0) - 1.0 / 3628800.0
    for c in (1.0 / 40320.0, -1.0 / 720.0, 1.0 / 24.0, -0.5, 1.0):
        k = k * z + c
    return s, k


def quant_parts(x, clip):
    inv = 1.0 / clip
    ratio = x * inv
    t = jnp.tanh(ratio)
    u = LEVELS * t
    s, k = sin_cos_half(u)
    level = u - s * k * (1.0 / math.pi)
    unit = level * (1.0 / LEVELS)
    slope = (2.0 * s * s) * (1.0 - t * t)
    return clip * unit, slope, unit - slope * ratio


def prep_kernel(nb, q_hbm, g_hbm, key_hbm, value_hbm, clip_hbm, len_hbm, qt_ref, gt_ref, quant_ref, slope_hbm,
                dclip_ref, bias_ref, clip_out, part_a_ref, part_b_ref, q_ref, g_ref, key_ref, value_ref, len_ref, slope_ref, sems):
    small = [
        pltpu.make_async_copy(src, dst, sems.at[i])
        for i, (src, dst) in enumerate(
            ((len_hbm, len_ref), (clip_hbm, clip_out), (key_hbm, key_ref), (value_hbm, value_ref))
        )
    ]
    large = [
        pltpu.make_async_copy(q_hbm, q_ref, sems.at[4]),
        pltpu.make_async_copy(g_hbm, g_ref, sems.at[5]),
    ]
    for copy in small + large:
        copy.start()
    rows = key_ref.shape[0]
    kv_heads, hd = clip_out.shape[1], clip_out.shape[2]
    group = q_ref.shape[1] // kv_heads
    base = lax.axis_index("seq") * rows
    for copy in small:
        copy.wait()
    half = part_a_ref.shape[1]
    part_a_ref[...] = value_ref[:, :half]
    part_b_ref[...] = value_ref[:, half:]
    for side, src in ((0, key_ref), (1, value_ref)):
        for n in range(kv_heads):
            x = src[:, n * hd:(n + 1) * hd].astype(F32)
            q, slope, dclip = quant_parts(x, clip_out[side, n:n + 1, :])
            at = slice((side * kv_heads + n) * hd, (side * kv_heads + n + 1) * hd)
            quant_ref[:, at] = q.astype(BF16)
            slope_ref[:, at] = slope
            dclip_ref[:, at] = dclip
    slope_copy = pltpu.make_async_copy(slope_ref, slope_hbm, sems.at[6])
    slope_copy.start()
    key = lax.broadcasted_iota(jnp.int32, (rows, rows), 0)
    row = lax.broadcasted_iota(jnp.int32, (rows, rows), 1)
    start = jnp.zeros((rows, rows), jnp.int32)
    end = jnp.int32(0)
    for d in range(len_ref.shape[1]):
        end = end + len_ref[0, d]
        start = jnp.where(row + base >= end, end, start)
    for b in range(nb):
        pos = jnp.where(key <= row, key, key - nb * rows) if b == 0 else key - b * rows
        bias_ref[b * rows:(b + 1) * rows, :] = jnp.where(pos + base >= start, 0.0, NEG)
    for copy, src, dst in zip(large, (q_ref, g_ref), (qt_ref, gt_ref)):
        copy.wait()
        for n in range(kv_heads):
            for h in range(group // hd):
                at = n * group + h * hd
                dst[n * hd:(n + 1) * hd, h * rows:(h + 1) * rows] = src[:, at:at + hd].T
    slope_copy.wait()


ACROSS = (((1,), (1,)), ((), ()))


def far_order(nb):
    return [nb] + list(range(1, nb))


def near_mask(rows):
    key = lax.broadcasted_iota(jnp.int32, (rows, rows), 0)
    row = lax.broadcasted_iota(jnp.int32, (rows, rows), 1)
    return key <= row


def merge(near, x, nb):
    rows = near.shape[0]
    first = jnp.where(near, x[:rows], x[rows:2 * rows])
    return jnp.concatenate([first, x[2 * rows:]], axis=0) if nb > 1 else first


def split(near_b, far_b, x, nb):
    rows = near_b.shape[0]
    parts = [x[:rows] * near_b, x[:rows] * far_b]
    if nb > 1:
        parts.append(x[rows:])
    return jnp.concatenate(parts, axis=0)


def score_kernel(nb, qt_ref, gt_ref, quant_ref, bias_ref, clip_ref, *rest):
    far, (p_ref, k2_ref, dclip_ref, vgrad_ref) = rest[:nb], rest[nb:]
    kv_heads, hd = clip_ref.shape[1], clip_ref.shape[2]
    rows, span = bias_ref.shape[1], qt_ref.shape[1]
    factor = hd ** -0.5 * math.log2(math.e)
    near = near_mask(rows)
    near_b = near.astype(F32).astype(BF16)
    far_b = 1.0 - near_b

    bias = bias_ref[...]

    def scores(n):
        cols = slice(n * hd, (n + 1) * hd)
        ks = [quant_ref[:, cols]]
        for j, d in enumerate(far_order(nb)):
            q, _, dclip = quant_parts(far[d - 1][:, cols].astype(F32), clip_ref[0, n:n + 1, :])
            ks.append(q.astype(BF16))
            dclip_ref[j * rows:(j + 1) * rows, cols] = dclip
        k2 = jnp.concatenate(ks, axis=0)
        k2_ref[:, cols] = k2
        return jnp.dot(k2, qt_ref[cols, :], preferred_element_type=F32)

    def softmax(n, s_all):
        ps = []
        for h in range(span // rows):
            s = merge(near, s_all[:, h * rows:(h + 1) * rows], nb) * factor + bias
            w = jnp.exp2(s - jnp.max(s, axis=0, keepdims=True))
            p = (w * (1.0 / jnp.sum(w, axis=0, keepdims=True))).astype(BF16)
            p_ref[:, n * span + h * rows:n * span + (h + 1) * rows] = p
            ps.append(split(near_b, far_b, p, nb))
        return jnp.concatenate(ps, axis=1)

    def value_grad(n, p2):
        cols = slice(n * hd, (n + 1) * hd)
        vgrad_ref[:, cols] = lax.dot_general(gt_ref[cols, :], p2, ACROSS, preferred_element_type=F32).T

    ahead, behind = scores(0), None
    for n in range(kv_heads):
        s_all, ahead = ahead, scores(n + 1) if n + 1 < kv_heads else None
        p2 = softmax(n, s_all)
        if behind is not None:
            value_grad(n - 1, behind)
        behind = p2
    value_grad(kv_heads - 1, behind)


def grad_kernel(nb, lo, last, qt_ref, gt_ref, quant_ref, dclip_ref, clip_ref, p_ref, kdclip_ref, vgrad_ref, *rest):
    far_v, rest = rest[:nb], rest[nb:]
    if last:
        before, (ds_ref, v2_ref, grad_ref, far_ref, spread_ref, scale_ref) = rest[:3], rest[3:]
    else:
        ds_ref, v2_ref, grad_ref, far_ref, scale_ref = rest
    kv_heads, hd = clip_ref.shape[1], clip_ref.shape[2]
    rows, span = dclip_ref.shape[0], gt_ref.shape[1]
    heads = span // rows
    width = kv_heads * hd
    count = v2_ref.shape[1] // hd
    scale = hd ** -0.5
    near = near_mask(rows)
    near_b = near.astype(F32).astype(BF16)
    far_b = 1.0 - near_b

    def head_cols(j, first=0):
        return slice(first + j * hd, first + (j + 1) * hd)

    k_at = [lo + j if last else j for j in range(count)]
    v_at = [(kv_heads if last else count) + k_at[j] for j in range(count)]

    def value_side(j):
        n = lo + j
        v_grad = vgrad_ref[:, head_cols(n)]
        vs, vd = [quant_ref[:, head_cols(n, width)]], [dclip_ref[:, head_cols(n, width)]]
        for d in far_order(nb):
            q, _, dc = quant_parts(far_v[d - 1][:, head_cols(j)].astype(F32), clip_ref[1, n:n + 1, :])
            vs.append(q.astype(BF16))
            vd.append(dc)
        v2 = jnp.concatenate(vs, axis=0)
        v2_ref[:, head_cols(j)] = v2
        grad_ref[:, head_cols(v_at[j])] = v_grad[:rows].astype(BF16)
        far_ref[:, head_cols(v_at[j])] = v_grad[rows:].astype(BF16)
        scale_ref[v_at[j]:v_at[j] + 1, :] = jnp.sum(v_grad * jnp.concatenate(vd, axis=0), axis=0, keepdims=True)
        return jnp.dot(v2, gt_ref[head_cols(n), :], preferred_element_type=F32)

    def score_side(j, d_all):
        ds = []
        for h in range(heads):
            dp = merge(near, d_all[:, h * rows:(h + 1) * rows], nb)
            at = (lo + j) * span + h * rows
            p = p_ref[:, at:at + rows].astype(F32)
            delta = jnp.sum(p * dp, axis=0, keepdims=True)
            ds_b = (p * (dp - delta)).astype(BF16)
            ds_ref[:, j * span + h * rows:j * span + (h + 1) * rows] = ds_b
            ds.append(split(near_b, far_b, ds_b, nb))
        return jnp.concatenate(ds, axis=1)

    def key_side(j, ds2):
        n = lo + j
        k_grad = (lax.dot_general(qt_ref[head_cols(n), :], ds2, ACROSS, preferred_element_type=F32) * scale).T
        grad_ref[:, head_cols(k_at[j])] = k_grad[:rows].astype(BF16)
        far_ref[:, head_cols(k_at[j])] = k_grad[rows:].astype(BF16)
        scale_ref[k_at[j]:k_at[j] + 1, :] = jnp.sum(
            k_grad[:rows] * dclip_ref[:, head_cols(n)], axis=0, keepdims=True
        ) + jnp.sum(k_grad[rows:] * kdclip_ref[:, head_cols(n)], axis=0, keepdims=True)

    if last:
        for src, dst in zip(before[:2], (grad_ref, far_ref)):
            dst[:, :lo * hd] = src[:, :lo * hd]
            dst[:, width:width + lo * hd] = src[:, lo * hd:]
        scale_ref[:lo, :] = before[2][:lo, :]
        scale_ref[kv_heads:kv_heads + lo, :] = before[2][lo:, :]
    ahead, behind = value_side(0), None
    for j in range(count):
        d_all, ahead = ahead, value_side(j + 1) if j + 1 < count else None
        ds2 = score_side(j, d_all)
        if behind is not None:
            key_side(j - 1, behind)
        behind = ds2
    key_side(count - 1, behind)
    if last:
        part = scale_ref[...].astype(BF16)

        def spread(i, carry):
            spread_ref[i] = part
            return carry

        lax.fori_loop(0, spread_ref.shape[0], spread, 0, unroll=8)


def output_kernel(nb, p_ref, ds_a_ref, ds_b_ref, k2_ref, v2_a_ref, v2_b_ref, grad_ref, slope_hbm, *rest):
    backs, rest = rest[:nb], rest[nb:]
    out_hbm, gq_hbm, gk_hbm, gv_hbm, out_ref, gq_ref, gk_ref, gv_ref, slope_ref, back_ref, sems, more_sems = rest
    loads = [pltpu.make_async_copy(slope_hbm, slope_ref, more_sems.at[2])]
    loads += [pltpu.make_async_copy(back, back_ref.at[d], more_sems.at[3 + d]) for d, back in enumerate(backs)]
    for copy in loads:
        copy.start()
    kv_heads = sems.shape[1]
    rows, group = out_ref.shape[0], out_ref.shape[1] // kv_heads
    hd = k2_ref.shape[1] // kv_heads
    heads = group // hd
    near_b = near_mask(rows).astype(F32).astype(BF16)
    far_b = 1.0 - near_b

    def copies(n):
        cols = pl.ds(pl.multiple_of(n * group, group), group)
        return (
            pltpu.make_async_copy(out_ref.at[:, cols], out_hbm.at[:, cols], sems.at[0, n]),
            pltpu.make_async_copy(gq_ref.at[:, cols], gq_hbm.at[:, cols], sems.at[1, n]),
        )

    half = ds_a_ref.shape[1] // (heads * rows)
    for n in range(kv_heads):
        ds_ref, v2_ref, j = (ds_a_ref, v2_a_ref, n) if n < half else (ds_b_ref, v2_b_ref, n - half)
        for left, at, right, to, dst, scale in (
            (v2_ref, j, p_ref, n, out_ref, None),
            (k2_ref, n, ds_ref, j, gq_ref, hd ** -0.5),
        ):
            x = right[:, to * heads * rows:(to + 1) * heads * rows]
            x2 = jnp.concatenate(
                [split(near_b, far_b, x[:, h * rows:(h + 1) * rows], nb) for h in range(heads)], axis=1
            )
            y = jnp.dot(left[:, at * hd:(at + 1) * hd].T, x2, preferred_element_type=F32)
            y = (y if scale is None else y * scale).astype(BF16)
            for h in range(heads):
                first = n * group + h * hd
                dst[:, first:first + hd] = y[:, h * rows:(h + 1) * rows].T
        for copy in copies(n):
            copy.start()
    for copy in loads:
        copy.wait()
    stores = []
    width = gk_ref.shape[1]
    for side, ref, dst in ((0, gk_ref, gk_hbm), (1, gv_ref, gv_hbm)):
        at = slice(side * width, (side + 1) * width)
        total = grad_ref[:, at].astype(F32)
        for d in range(nb):
            total = total + back_ref[d, :, at].astype(F32)
        ref[...] = (total * slope_ref[:, at]).astype(BF16)
        stores.append(pltpu.make_async_copy(ref, dst, more_sems.at[side]))
        stores[-1].start()
    for n in range(kv_heads):
        for copy in copies(n):
            copy.wait()
    for copy in stores:
        copy.wait()


def total_kernel(parts_ref, after_ref, out_ref):
    del after_ref
    out_ref[...] = jnp.sum(parts_ref[...].astype(F32), axis=0)


def on_device(sizes, queries, keys, values, grad_out, quant_scale, doc_lengths):
    dp_count, seq_count = sizes
    count = dp_count * seq_count
    nb = max(1, seq_count // 2)
    rows, width = keys.shape
    kv_heads, hd = quant_scale.shape[1], quant_scale.shape[2]
    heads = queries.shape[1] // hd
    vmem = pl.BlockSpec(memory_space=pltpu.VMEM)
    hbm = pl.BlockSpec(memory_space=pltpu.HBM)
    params = pltpu.CompilerParams(vmem_limit_bytes=36 * 1024 * 1024)
    shape = jax.ShapeDtypeStruct
    work = rows * rows * queries.shape[1]

    def call(kernel, name, flops, args, outs, in_specs=None, out_specs=None, scratch=()):
        return pl.pallas_call(
            kernel,
            out_shape=outs,
            in_specs=in_specs or [vmem] * len(args),
            out_specs=out_specs or (vmem,) * len(outs),
            scratch_shapes=scratch,
            compiler_params=params,
            cost_estimate=pl.CostEstimate(flops=flops, bytes_accessed=16 * rows * width, transcendentals=0),
            name=name,
        )(*args)

    def shift(array, d):
        return lax.ppermute(array, "seq", [(r, (r + d) % seq_count) for r in range(seq_count)])

    def unshift(array, d):
        return lax.ppermute(array, "seq", [((r + d) % seq_count, r) for r in range(seq_count)])

    def pinned(*arrays):
        return [pltpu.with_memory_space_constraint(x, pltpu.HBM) for x in arrays]

    far_k = [shift(keys, d) for d in range(1, nb + 1)]
    turned = shape((width, heads // kv_heads * rows), BF16)
    half = kv_heads // 2 * hd
    qt, gt, quants, slopes, dclips, bias, clips, part_a, part_b = call(
        functools.partial(prep_kernel, nb),
        "prep",
        2 * work,
        pinned(queries, grad_out, keys, values, quant_scale, doc_lengths),
        (
            turned,
            turned,
            shape((rows, 2 * width), BF16),
            pltpu.HBM((rows, 2 * width), F32),
            shape((rows, 2 * width), F32),
            shape((nb * rows, rows), F32),
            shape(quant_scale.shape, F32),
            shape((rows, half), BF16),
            shape((rows, width - half), BF16),
        ),
        in_specs=[hbm] * 6,
        out_specs=(vmem,) * 3 + (hbm,) + (vmem,) * 5,
        scratch=[
            pltpu.VMEM(queries.shape, BF16),
            pltpu.VMEM(queries.shape, BF16),
            pltpu.VMEM(keys.shape, BF16),
            pltpu.VMEM(values.shape, BF16),
            pltpu.SMEM(doc_lengths.shape, jnp.int32),
            pltpu.VMEM((rows, 2 * width), F32),
            pltpu.SemaphoreType.DMA((7,)),
        ],
    )
    far_a = [shift(part_a, d) for d in range(1, nb + 1)]
    far_b = [shift(part_b, d) for d in range(1, nb + 1)]
    p, k2, kdclips, v_grads = call(
        functools.partial(score_kernel, nb),
        "score",
        4 * (nb + 1) * work,
        (qt, gt, quants, bias, clips, *far_k),
        (
            shape((nb * rows, heads * rows), BF16),
            shape(((nb + 1) * rows, width), BF16),
            shape((nb * rows, width), F32),
            shape(((nb + 1) * rows, width), F32),
        ),
    )
    common = (qt, gt, quants, dclips, clips, p, kdclips, v_grads)
    span = turned.shape[1]
    ds_a, v2_a, *before = call(
        functools.partial(grad_kernel, nb, 0, False),
        "grad_a",
        2 * (nb + 1) * work,
        (*common, *far_a),
        (
            shape((nb * rows, half // hd * span), BF16),
            shape(((nb + 1) * rows, half), BF16),
            shape((rows, 2 * half), BF16),
            shape((nb * rows, 2 * half), BF16),
            shape((2 * half // hd, hd), F32),
        ),
    )
    ds_b, v2_b, grads, far_grads, spread = call(
        functools.partial(grad_kernel, nb, half // hd, True),
        "grad_b",
        2 * (nb + 1) * work,
        (*common, *far_b, *before),
        (
            shape((nb * rows, (width - half) // hd * span), BF16),
            shape(((nb + 1) * rows, width - half), BF16),
            shape((rows, 2 * width), BF16),
            shape((nb * rows, 2 * width), BF16),
            pltpu.VMEM((count, 2 * kv_heads, hd), BF16),
        ),
        scratch=[pltpu.VMEM((2 * kv_heads, hd), F32)],
    )
    backs = []
    for d in range(1, nb + 1):
        at = far_order(nb).index(d) * rows
        backs.append(unshift(lax.slice_in_dim(far_grads, at, at + rows, axis=0), d))
    parts = lax.all_to_all(
        spread,
        ("dp", "seq"),
        split_axis=0,
        concat_axis=0,
        axis_index_groups=[list(reversed(range(count)))],
        tiled=True,
    )
    attn_out, grad_queries, grad_keys, grad_values = call(
        functools.partial(output_kernel, nb),
        "output",
        4 * (nb + 1) * work,
        (p, ds_a, ds_b, k2, v2_a, v2_b, grads, *pinned(slopes), *backs),
        (
            shape(queries.shape, BF16),
            shape(queries.shape, BF16),
            shape((rows, width), BF16),
            shape((rows, width), BF16),
        ),
        in_specs=[vmem] * 7 + [hbm] + [pl.BlockSpec(memory_space=pl.ANY)] * nb,
        out_specs=(hbm,) * 4,
        scratch=[
            pltpu.VMEM(queries.shape, BF16),
            pltpu.VMEM(queries.shape, BF16),
            pltpu.VMEM((rows, width), BF16),
            pltpu.VMEM((rows, width), BF16),
            pltpu.VMEM((rows, 2 * width), F32),
            pltpu.VMEM((nb, rows, 2 * width), BF16),
            pltpu.SemaphoreType.DMA((2, kv_heads)),
            pltpu.SemaphoreType.DMA((3 + nb,)),
        ],
    )
    (grad_scale,) = call(
        total_kernel,
        "total",
        parts.size,
        (parts, *pinned(grad_keys)),
        (shape(parts.shape[1:], F32),),
        in_specs=[vmem, hbm],
    )
    return (attn_out, grad_queries, grad_keys, grad_values, grad_scale.reshape(quant_scale.shape))


def solution(mesh):
    rows = P(("dp", "seq"), None)
    return jax.shard_map(
        functools.partial(on_device, (mesh.shape["dp"], mesh.shape["seq"])),
        mesh=mesh,
        in_specs=(rows, rows, rows, rows, P(), P("dp", None)),
        out_specs=(rows, rows, rows, rows, P()),
        check_vma=False,
    )
```

```python
import functools
import math

import jax
import jax.numpy as jnp
from jax import lax
from jax.experimental import pallas as pl
from jax.experimental.pallas import tpu as pltpu
from jax.sharding import PartitionSpec as P

F32 = jnp.float32
BF16 = jnp.bfloat16
LEVELS = 127.0
NEG = -1e30


def sin_cos_half(u):
    r = (u - jnp.round(u)) * math.pi
    z = r * r
    s = z * (1.0 / 6227020800.0) - 1.0 / 39916800.0
    for c in (1.0 / 362880.0, -1.0 / 5040.0, 1.0 / 120.0, -1.0 / 6.0, 1.0):
        s = s * z + c
    s = s * r
    k = z * (1.0 / 479001600.0) - 1.0 / 3628800.0
    for c in (1.0 / 40320.0, -1.0 / 720.0, 1.0 / 24.0, -0.5, 1.0):
        k = k * z + c
    return s, k


def quant_parts(x, clip):
    inv = 1.0 / clip
    ratio = x * inv
    t = jnp.tanh(ratio)
    u = LEVELS * t
    s, k = sin_cos_half(u)
    level = u - s * k * (1.0 / math.pi)
    unit = level * (1.0 / LEVELS)
    slope = (2.0 * s * s) * (1.0 - t * t)
    return clip * unit, slope, unit - slope * ratio


def prep_kernel(nb, q_hbm, g_hbm, key_hbm, value_hbm, clip_hbm, len_hbm, qt_ref, gt_ref, quant_ref, slope_hbm,
                dclip_ref, bias_ref, clip_out, part_a_ref, part_b_ref, q_ref, g_ref, key_ref, value_ref, len_ref, slope_ref, sems):
    small = [
        pltpu.make_async_copy(src, dst, sems.at[i])
        for i, (src, dst) in enumerate(
            ((len_hbm, len_ref), (clip_hbm, clip_out), (key_hbm, key_ref), (value_hbm, value_ref))
        )
    ]
    large = [
        pltpu.make_async_copy(q_hbm, q_ref, sems.at[4]),
        pltpu.make_async_copy(g_hbm, g_ref, sems.at[5]),
    ]
    for copy in small + large:
        copy.start()
    rows = key_ref.shape[0]
    kv_heads, hd = clip_out.shape[1], clip_out.shape[2]
    group = q_ref.shape[1] // kv_heads
    base = lax.axis_index("seq") * rows
    for copy in small:
        copy.wait()
    half = part_a_ref.shape[1]
    part_a_ref[...] = value_ref[:, :half]
    part_b_ref[...] = value_ref[:, half:]
    for side, src in ((0, key_ref), (1, value_ref)):
        for n in range(kv_heads):
            x = src[:, n * hd:(n + 1) * hd].astype(F32)
            q, slope, dclip = quant_parts(x, clip_out[side, n:n + 1, :])
            at = slice((side * kv_heads + n) * hd, (side * kv_heads + n + 1) * hd)
            quant_ref[:, at] = q.astype(BF16)
            slope_ref[:, at] = slope
            dclip_ref[:, at] = dclip
    slope_copy = pltpu.make_async_copy(slope_ref, slope_hbm, sems.at[6])
    slope_copy.start()
    key = lax.broadcasted_iota(jnp.int32, (rows, rows), 0)
    row = lax.broadcasted_iota(jnp.int32, (rows, rows), 1)
    start = jnp.zeros((rows, rows), jnp.int32)
    end = jnp.int32(0)
    for d in range(len_ref.shape[1]):
        end = end + len_ref[0, d]
        start = jnp.where(row + base >= end, end, start)
    for b in range(nb):
        pos = jnp.where(key <= row, key, key - nb * rows) if b == 0 else key - b * rows
        bias_ref[b * rows:(b + 1) * rows, :] = jnp.where(pos + base >= start, 0.0, NEG)
    for copy, src, dst in zip(large, (q_ref, g_ref), (qt_ref, gt_ref)):
        copy.wait()
        for n in range(kv_heads):
            for h in range(group // hd):
                at = n * group + h * hd
                dst[n * hd:(n + 1) * hd, h * rows:(h + 1) * rows] = src[:, at:at + hd].T
    slope_copy.wait()


ACROSS = (((1,), (1,)), ((), ()))


def far_order(nb):
    return [nb] + list(range(1, nb))


def near_mask(rows):
    key = lax.broadcasted_iota(jnp.int32, (rows, rows), 0)
    row = lax.broadcasted_iota(jnp.int32, (rows, rows), 1)
    return key <= row


def merge(near, x, nb):
    rows = near.shape[0]
    first = jnp.where(near, x[:rows], x[rows:2 * rows])
    return jnp.concatenate([first, x[2 * rows:]], axis=0) if nb > 1 else first


def split(near_b, far_b, x, nb):
    rows = near_b.shape[0]
    parts = [x[:rows] * near_b, x[:rows] * far_b]
    if nb > 1:
        parts.append(x[rows:])
    return jnp.concatenate(parts, axis=0)


def score_kernel(nb, qt_ref, gt_ref, quant_ref, bias_ref, clip_ref, *rest):
    far, (p_ref, k2_ref, dclip_ref, vgrad_ref) = rest[:nb], rest[nb:]
    kv_heads, hd = clip_ref.shape[1], clip_ref.shape[2]
    rows, span = bias_ref.shape[1], qt_ref.shape[1]
    factor = hd ** -0.5 * math.log2(math.e)
    near = near_mask(rows)
    near_b = near.astype(F32).astype(BF16)
    far_b = 1.0 - near_b

    bias = bias_ref[...]

    def scores(n):
        cols = slice(n * hd, (n + 1) * hd)
        ks = [quant_ref[:, cols]]
        for j, d in enumerate(far_order(nb)):
            q, _, dclip = quant_parts(far[d - 1][:, cols].astype(F32), clip_ref[0, n:n + 1, :])
            ks.append(q.astype(BF16))
            dclip_ref[j * rows:(j + 1) * rows, cols] = dclip
        k2 = jnp.concatenate(ks, axis=0)
        k2_ref[:, cols] = k2
        return jnp.dot(k2, qt_ref[cols, :], preferred_element_type=F32)

    def softmax(n, s_all):
        ps = []
        for h in range(span // rows):
            s = merge(near, s_all[:, h * rows:(h + 1) * rows], nb) * factor + bias
            w = jnp.exp2(s - jnp.max(s, axis=0, keepdims=True))
            p = (w * (1.0 / jnp.sum(w, axis=0, keepdims=True))).astype(BF16)
            p_ref[:, n * span + h * rows:n * span + (h + 1) * rows] = p
            ps.append(split(near_b, far_b, p, nb))
        return jnp.concatenate(ps, axis=1)

    def value_grad(n, p2):
        cols = slice(n * hd, (n + 1) * hd)
        vgrad_ref[:, cols] = lax.dot_general(gt_ref[cols, :], p2, ACROSS, preferred_element_type=F32).T

    ahead, behind = scores(0), None
    for n in range(kv_heads):
        s_all, ahead = ahead, scores(n + 1) if n + 1 < kv_heads else None
        p2 = softmax(n, s_all)
        if behind is not None:
            value_grad(n - 1, behind)
        behind = p2
    value_grad(kv_heads - 1, behind)


def grad_kernel(nb, lo, last, qt_ref, gt_ref, quant_ref, dclip_ref, clip_ref, p_ref, kdclip_ref, vgrad_ref, *rest):
    far_v, rest = rest[:nb], rest[nb:]
    if last:
        before_ref, ds_ref, v2_ref, grad_ref, far_ref, spread_ref, scale_ref = rest
    else:
        ds_ref, v2_ref, grad_ref, far_ref, scale_ref = rest
    kv_heads, hd = clip_ref.shape[1], clip_ref.shape[2]
    rows, span = dclip_ref.shape[0], gt_ref.shape[1]
    heads = span // rows
    width = kv_heads * hd
    count = v2_ref.shape[1] // hd
    scale = hd ** -0.5
    near = near_mask(rows)
    near_b = near.astype(F32).astype(BF16)
    far_b = 1.0 - near_b

    def head_cols(j, first=0):
        return slice(first + j * hd, first + (j + 1) * hd)

    k_row, v_row = (lo, kv_heads + lo) if last else (0, count)

    def value_side(j):
        n = lo + j
        v_grad = vgrad_ref[:, head_cols(n)]
        vs, vd = [quant_ref[:, head_cols(n, width)]], [dclip_ref[:, head_cols(n, width)]]
        for d in far_order(nb):
            q, _, dc = quant_parts(far_v[d - 1][:, head_cols(j)].astype(F32), clip_ref[1, n:n + 1, :])
            vs.append(q.astype(BF16))
            vd.append(dc)
        v2 = jnp.concatenate(vs, axis=0)
        v2_ref[:, head_cols(j)] = v2
        grad_ref[:, head_cols(count + j)] = v_grad[:rows].astype(BF16)
        far_ref[:, head_cols(count + j)] = v_grad[rows:].astype(BF16)
        scale_ref[v_row + j:v_row + j + 1, :] = jnp.sum(v_grad * jnp.concatenate(vd, axis=0), axis=0, keepdims=True)
        return jnp.dot(v2, gt_ref[head_cols(n), :], preferred_element_type=F32)

    def score_side(j, d_all):
        ds = []
        for h in range(heads):
            dp = merge(near, d_all[:, h * rows:(h + 1) * rows], nb)
            at = (lo + j) * span + h * rows
            p = p_ref[:, at:at + rows].astype(F32)
            delta = jnp.sum(p * dp, axis=0, keepdims=True)
            ds_b = (p * (dp - delta)).astype(BF16)
            ds_ref[:, j * span + h * rows:j * span + (h + 1) * rows] = ds_b
            ds.append(split(near_b, far_b, ds_b, nb))
        return jnp.concatenate(ds, axis=1)

    def key_side(j, ds2):
        n = lo + j
        k_grad = (lax.dot_general(qt_ref[head_cols(n), :], ds2, ACROSS, preferred_element_type=F32) * scale).T
        grad_ref[:, head_cols(j)] = k_grad[:rows].astype(BF16)
        far_ref[:, head_cols(j)] = k_grad[rows:].astype(BF16)
        scale_ref[k_row + j:k_row + j + 1, :] = jnp.sum(
            k_grad[:rows] * dclip_ref[:, head_cols(n)], axis=0, keepdims=True
        ) + jnp.sum(k_grad[rows:] * kdclip_ref[:, head_cols(n)], axis=0, keepdims=True)

    if last:
        scale_ref[:lo, :] = before_ref[:lo, :]
        scale_ref[kv_heads:kv_heads + lo, :] = before_ref[lo:, :]
    ahead, behind = value_side(0), None
    for j in range(count):
        d_all, ahead = ahead, value_side(j + 1) if j + 1 < count else None
        ds2 = score_side(j, d_all)
        if behind is not None:
            key_side(j - 1, behind)
        behind = ds2
    key_side(count - 1, behind)
    if last:
        part = scale_ref[...].astype(BF16)

        def spread(i, carry):
            spread_ref[i] = part
            return carry

        lax.fori_loop(0, spread_ref.shape[0], spread, 0, unroll=8)


def slope_loads(lo_col, slope_hbm, slope_ref, sems):
    half, width = slope_ref.shape[1] // 2, slope_hbm.shape[1] // 2
    return [
        pltpu.make_async_copy(
            slope_hbm.at[:, side * width + lo_col:side * width + lo_col + half],
            slope_ref.at[:, side * half:(side + 1) * half],
            sems.at[side],
        )
        for side in range(2)
    ]


def finish_part(nb, grad_ref, backs, slope_ref, outs):
    half = outs[0].shape[1]
    for side, out in enumerate(outs):
        at = slice(side * half, (side + 1) * half)
        total = grad_ref[:, at].astype(F32)
        for back in backs:
            total = total + back[:, at].astype(F32)
        out[...] = (total * slope_ref[:, at]).astype(BF16)


def part_stores(lo_col, refs, dsts, sems):
    half = refs[0].shape[1]
    return [
        pltpu.make_async_copy(ref, dst.at[:, lo_col:lo_col + half], sems.at[2 + side])
        for side, (ref, dst) in enumerate(zip(refs, dsts))
    ]


def output_kernel(nb, kv_heads, lo, finish, p_ref, ds_ref, k2_ref, v2_ref, *rest):
    if finish:
        grad_ref, slope_hbm, backs, rest = rest[0], rest[1], rest[2:2 + nb], rest[2 + nb:]
        out_hbm, gq_hbm, gk_hbm, gv_hbm, out_ref, gq_ref, sems, gk_ref, gv_ref, slope_ref, more_sems = rest
        loads = slope_loads(0, slope_hbm, slope_ref, more_sems)
        for copy in loads:
            copy.start()
    else:
        _, _, out_hbm, gq_hbm, out_ref, gq_ref, sems = rest
    hd = k2_ref.shape[1] // kv_heads
    rows, group = out_ref.shape[0], out_hbm.shape[1] // kv_heads
    heads = group // hd
    span = heads * rows
    near_b = near_mask(rows).astype(F32).astype(BF16)
    far_b = 1.0 - near_b
    stores = []
    for j in range(v2_ref.shape[1] // hd):
        n = lo + j
        for side, (left, at, right, to, dst, scale) in enumerate(
            ((v2_ref, j, p_ref, n, out_ref, None), (k2_ref, n, ds_ref, j, gq_ref, hd ** -0.5))
        ):
            x = right[:, to * span:(to + 1) * span]
            x2 = jnp.concatenate(
                [split(near_b, far_b, x[:, h * rows:(h + 1) * rows], nb) for h in range(heads)], axis=1
            )
            y = jnp.dot(left[:, at * hd:(at + 1) * hd].T, x2, preferred_element_type=F32)
            y = (y if scale is None else y * scale).astype(BF16)
            for h in range(heads):
                first = j * group + h * hd
                dst[:, first:first + hd] = y[:, h * rows:(h + 1) * rows].T
            stores.append(
                pltpu.make_async_copy(
                    dst.at[:, j * group:(j + 1) * group],
                    (out_hbm, gq_hbm)[side].at[:, n * group:(n + 1) * group],
                    sems.at[side, j],
                )
            )
            stores[-1].start()
    if finish:
        for copy in loads:
            copy.wait()
        finish_part(nb, grad_ref, backs, slope_ref, (gk_ref, gv_ref))
        more = part_stores(0, (gk_ref, gv_ref), (gk_hbm, gv_hbm), more_sems)
        for copy in more:
            copy.start()
        stores += more
    for copy in stores:
        copy.wait()


def finish_kernel(nb, lo_col, grad_ref, slope_hbm, *rest):
    backs, (_, _, gk_hbm, gv_hbm, gk_ref, gv_ref, slope_ref, sems) = rest[:nb], rest[nb:]
    loads = slope_loads(lo_col, slope_hbm, slope_ref, sems)
    for copy in loads:
        copy.start()
    for copy in loads:
        copy.wait()
    finish_part(nb, grad_ref, backs, slope_ref, (gk_ref, gv_ref))
    stores = part_stores(lo_col, (gk_ref, gv_ref), (gk_hbm, gv_hbm), sems)
    for copy in stores:
        copy.start()
    for copy in stores:
        copy.wait()


def total_kernel(parts_ref, after_ref, out_ref):
    del after_ref
    out_ref[...] = jnp.sum(parts_ref[...].astype(F32), axis=0)


def on_device(sizes, queries, keys, values, grad_out, quant_scale, doc_lengths):
    dp_count, seq_count = sizes
    count = dp_count * seq_count
    nb = max(1, seq_count // 2)
    rows, width = keys.shape
    kv_heads, hd = quant_scale.shape[1], quant_scale.shape[2]
    heads = queries.shape[1] // hd
    vmem = pl.BlockSpec(memory_space=pltpu.VMEM)
    hbm = pl.BlockSpec(memory_space=pltpu.HBM)
    params = pltpu.CompilerParams(vmem_limit_bytes=36 * 1024 * 1024)
    shape = jax.ShapeDtypeStruct
    work = rows * rows * queries.shape[1]

    def call(kernel, name, flops, args, outs, in_specs=None, out_specs=None, scratch=(), aliases=None):
        return pl.pallas_call(
            kernel,
            out_shape=outs,
            in_specs=in_specs or [vmem] * len(args),
            out_specs=out_specs or (vmem,) * len(outs),
            scratch_shapes=scratch,
            input_output_aliases=aliases or {},
            compiler_params=params,
            cost_estimate=pl.CostEstimate(flops=flops, bytes_accessed=16 * rows * width, transcendentals=0),
            name=name,
        )(*args)

    def shift(array, d):
        return lax.ppermute(array, "seq", [(r, (r + d) % seq_count) for r in range(seq_count)])

    def unshift(array, d):
        return lax.ppermute(array, "seq", [((r + d) % seq_count, r) for r in range(seq_count)])

    def pinned(*arrays):
        return [pltpu.with_memory_space_constraint(x, pltpu.HBM) for x in arrays]

    def give_back(far_grads):
        order = far_order(nb)
        pieces = [lax.slice_in_dim(far_grads, order.index(d) * rows, (order.index(d) + 1) * rows) for d in range(1, nb + 1)]
        return [unshift(piece, d) for d, piece in zip(range(1, nb + 1), pieces)]

    far_k = [shift(keys, d) for d in range(1, nb + 1)]
    turned = shape((width, heads // kv_heads * rows), BF16)
    half = kv_heads // 2 * hd
    qt, gt, quants, slopes, dclips, bias, clips, part_a, part_b = call(
        functools.partial(prep_kernel, nb),
        "prep",
        2 * work,
        pinned(queries, grad_out, keys, values, quant_scale, doc_lengths),
        (
            turned,
            turned,
            shape((rows, 2 * width), BF16),
            pltpu.HBM((rows, 2 * width), F32),
            shape((rows, 2 * width), F32),
            shape((nb * rows, rows), F32),
            shape(quant_scale.shape, F32),
            shape((rows, half), BF16),
            shape((rows, width - half), BF16),
        ),
        in_specs=[hbm] * 6,
        out_specs=(vmem,) * 3 + (hbm,) + (vmem,) * 5,
        scratch=[
            pltpu.VMEM(queries.shape, BF16),
            pltpu.VMEM(queries.shape, BF16),
            pltpu.VMEM(keys.shape, BF16),
            pltpu.VMEM(values.shape, BF16),
            pltpu.SMEM(doc_lengths.shape, jnp.int32),
            pltpu.VMEM((rows, 2 * width), F32),
            pltpu.SemaphoreType.DMA((7,)),
        ],
    )
    far_a = [shift(part_a, d) for d in range(1, nb + 1)]
    far_b = [shift(part_b, d) for d in range(1, nb + 1)]
    p, k2, kdclips, v_grads = call(
        functools.partial(score_kernel, nb),
        "score",
        4 * (nb + 1) * work,
        (qt, gt, quants, bias, clips, *far_k),
        (
            shape((nb * rows, heads * rows), BF16),
            shape(((nb + 1) * rows, width), BF16),
            shape((nb * rows, width), F32),
            shape(((nb + 1) * rows, width), F32),
        ),
    )
    common = (qt, gt, quants, dclips, clips, p, kdclips, v_grads)
    span = turned.shape[1]
    ds_a, v2_a, grads_a, far_grads_a, scale_a = call(
        functools.partial(grad_kernel, nb, 0, False),
        "grad_a",
        2 * (nb + 1) * work,
        (*common, *far_a),
        (
            shape((nb * rows, half // hd * span), BF16),
            shape(((nb + 1) * rows, half), BF16),
            shape((rows, 2 * half), BF16),
            shape((nb * rows, 2 * half), BF16),
            shape((2 * half // hd, hd), F32),
        ),
    )
    backs_a = give_back(far_grads_a)
    ds_b, v2_b, grads_b, far_grads_b, spread = call(
        functools.partial(grad_kernel, nb, half // hd, True),
        "grad_b",
        2 * (nb + 1) * work,
        (*common, *far_b, scale_a),
        (
            shape((nb * rows, half // hd * span), BF16),
            shape(((nb + 1) * rows, half), BF16),
            shape((rows, 2 * half), BF16),
            shape((nb * rows, 2 * half), BF16),
            pltpu.VMEM((count, 2 * kv_heads, hd), BF16),
        ),
        scratch=[pltpu.VMEM((2 * kv_heads, hd), F32)],
    )
    parts = lax.all_to_all(spread, ("dp", "seq"), split_axis=0, concat_axis=0, tiled=True)
    out_scratch = [
        pltpu.VMEM((rows, queries.shape[1] // 2), BF16),
        pltpu.VMEM((rows, queries.shape[1] // 2), BF16),
        pltpu.SemaphoreType.DMA((2, half // hd)),
    ]
    finish_scratch = [
        pltpu.VMEM((rows, half), BF16),
        pltpu.VMEM((rows, half), BF16),
        pltpu.VMEM((rows, 2 * half), F32),
        pltpu.SemaphoreType.DMA((4,)),
    ]
    attn_out, grad_queries, grad_keys, grad_values = call(
        functools.partial(output_kernel, nb, kv_heads, 0, True),
        "output_a",
        2 * (nb + 1) * work,
        (p, ds_a, k2, v2_a, grads_a, *pinned(slopes), *backs_a),
        (
            shape(queries.shape, BF16),
            shape(queries.shape, BF16),
            shape((rows, width), BF16),
            shape((rows, width), BF16),
        ),
        in_specs=[vmem] * 5 + [hbm] + [vmem] * nb,
        out_specs=(hbm,) * 4,
        scratch=out_scratch + finish_scratch,
    )
    far_grads_b, grad_keys = lax.optimization_barrier((far_grads_b, grad_keys))
    backs_b = give_back(far_grads_b)
    attn_out, grad_queries = call(
        functools.partial(output_kernel, nb, kv_heads, half // hd, False),
        "output_b",
        2 * (nb + 1) * work,
        (p, ds_b, k2, v2_b, *pinned(attn_out, grad_queries)),
        (shape(queries.shape, BF16), shape(queries.shape, BF16)),
        in_specs=[vmem] * 4 + [hbm] * 2,
        out_specs=(hbm,) * 2,
        scratch=out_scratch,
        aliases={4: 0, 5: 1},
    )
    grad_keys, grad_values = call(
        functools.partial(finish_kernel, nb, half),
        "finish_b",
        6 * rows * width,
        (grads_b, *pinned(slopes), *backs_b, *pinned(grad_keys, grad_values)),
        (shape((rows, width), BF16), shape((rows, width), BF16)),
        in_specs=[vmem, hbm] + [vmem] * nb + [hbm] * 2,
        out_specs=(hbm,) * 2,
        scratch=finish_scratch,
        aliases={2 + nb: 0, 3 + nb: 1},
    )
    (grad_scale,) = call(
        total_kernel,
        "total",
        parts.size,
        (parts, *pinned(grad_keys)),
        (shape(parts.shape[1:], F32),),
        in_specs=[vmem, hbm],
    )
    return (attn_out, grad_queries, grad_keys, grad_values, grad_scale.reshape(quant_scale.shape))


def solution(mesh):
    rows = P(("dp", "seq"), None)
    return jax.shard_map(
        functools.partial(on_device, (mesh.shape["dp"], mesh.shape["seq"])),
        mesh=mesh,
        in_specs=(rows, rows, rows, rows, P(), P("dp", None)),
        out_specs=(rows, rows, rows, rows, P()),
        check_vma=False,
    )
```

```python
import functools
import math

import jax
import jax.numpy as jnp
from jax import lax
from jax.experimental import pallas as pl
from jax.experimental.pallas import tpu as pltpu
from jax.sharding import PartitionSpec as P

F32 = jnp.float32
BF16 = jnp.bfloat16
LEVELS = 127.0
NEG = -1e30


def sin_cos_half(u):
    r = (u - jnp.round(u)) * math.pi
    z = r * r
    s = z * (1.0 / 6227020800.0) - 1.0 / 39916800.0
    for c in (1.0 / 362880.0, -1.0 / 5040.0, 1.0 / 120.0, -1.0 / 6.0, 1.0):
        s = s * z + c
    s = s * r
    k = z * (1.0 / 479001600.0) - 1.0 / 3628800.0
    for c in (1.0 / 40320.0, -1.0 / 720.0, 1.0 / 24.0, -0.5, 1.0):
        k = k * z + c
    return s, k


def quant_parts(x, clip):
    inv = 1.0 / clip
    ratio = x * inv
    t = jnp.tanh(ratio)
    u = LEVELS * t
    s, k = sin_cos_half(u)
    level = u - s * k * (1.0 / math.pi)
    unit = level * (1.0 / LEVELS)
    slope = (2.0 * s * s) * (1.0 - t * t)
    return clip * unit, slope, unit - slope * ratio


def prep_kernel(nb, q_hbm, g_hbm, key_hbm, value_hbm, clip_hbm, len_hbm, q_ref, g_ref, quant_ref, slope_hbm,
                dclip_ref, bias_ref, clip_out, part_a_ref, part_b_ref, key_ref, value_ref, len_ref, slope_ref, sems):
    small = [
        pltpu.make_async_copy(src, dst, sems.at[i])
        for i, (src, dst) in enumerate(
            ((len_hbm, len_ref), (clip_hbm, clip_out), (key_hbm, key_ref), (value_hbm, value_ref))
        )
    ]
    large = [
        pltpu.make_async_copy(q_hbm, q_ref, sems.at[4]),
        pltpu.make_async_copy(g_hbm, g_ref, sems.at[5]),
    ]
    for copy in small + large:
        copy.start()
    rows = key_ref.shape[0]
    kv_heads, hd = clip_out.shape[1], clip_out.shape[2]
    group = q_ref.shape[1] // kv_heads
    base = lax.axis_index("seq") * rows
    for copy in small:
        copy.wait()
    half = part_a_ref.shape[1]
    part_a_ref[...] = value_ref[:, :half]
    part_b_ref[...] = value_ref[:, half:]
    for side, src in ((0, key_ref), (1, value_ref)):
        for n in range(kv_heads):
            x = src[:, n * hd:(n + 1) * hd].astype(F32)
            q, slope, dclip = quant_parts(x, clip_out[side, n:n + 1, :])
            at = slice((side * kv_heads + n) * hd, (side * kv_heads + n + 1) * hd)
            quant_ref[:, at] = q.astype(BF16)
            slope_ref[:, at] = slope
            dclip_ref[:, at] = dclip
    slope_copy = pltpu.make_async_copy(slope_ref, slope_hbm, sems.at[6])
    slope_copy.start()
    key = lax.broadcasted_iota(jnp.int32, (rows, rows), 0)
    row = lax.broadcasted_iota(jnp.int32, (rows, rows), 1)
    start = jnp.zeros((rows, rows), jnp.int32)
    end = jnp.int32(0)
    for d in range(len_ref.shape[1]):
        end = end + len_ref[0, d]
        start = jnp.where(row + base >= end, end, start)
    for b in range(nb):
        pos = jnp.where(key <= row, key, key - nb * rows) if b == 0 else key - b * rows
        bias_ref[b * rows:(b + 1) * rows, :] = jnp.where(pos + base >= start, 0.0, NEG)
    for copy in large:
        copy.wait()
    slope_copy.wait()


def turn_kernel(kv_heads, q_ref, g_ref, qt_ref, gt_ref):
    rows, group = q_ref.shape[0], q_ref.shape[1] // kv_heads
    hd = qt_ref.shape[0] // kv_heads
    for src, dst in ((q_ref, qt_ref), (g_ref, gt_ref)):
        for n in range(kv_heads):
            for h in range(group // hd):
                at = n * group + h * hd
                dst[n * hd:(n + 1) * hd, h * rows:(h + 1) * rows] = src[:, at:at + hd].T


ACROSS = (((1,), (1,)), ((), ()))


def far_order(nb):
    return [nb] + list(range(1, nb))


def near_mask(rows):
    key = lax.broadcasted_iota(jnp.int32, (rows, rows), 0)
    row = lax.broadcasted_iota(jnp.int32, (rows, rows), 1)
    return key <= row


def merge(near, x, nb):
    rows = near.shape[0]
    first = jnp.where(near, x[:rows], x[rows:2 * rows])
    return jnp.concatenate([first, x[2 * rows:]], axis=0) if nb > 1 else first


def split(near_b, far_b, x, nb):
    rows = near_b.shape[0]
    parts = [x[:rows] * near_b, x[:rows] * far_b]
    if nb > 1:
        parts.append(x[rows:])
    return jnp.concatenate(parts, axis=0)


def score_kernel(nb, qt_ref, gt_ref, quant_ref, bias_ref, clip_ref, *rest):
    far, (p_ref, k2_ref, dclip_ref, vgrad_ref) = rest[:nb], rest[nb:]
    kv_heads, hd = clip_ref.shape[1], clip_ref.shape[2]
    rows, span = bias_ref.shape[1], qt_ref.shape[1]
    factor = hd ** -0.5 * math.log2(math.e)
    near = near_mask(rows)
    near_b = near.astype(F32).astype(BF16)
    far_b = 1.0 - near_b

    bias = bias_ref[...]

    def scores(n):
        cols = slice(n * hd, (n + 1) * hd)
        ks = [quant_ref[:, cols]]
        for j, d in enumerate(far_order(nb)):
            q, _, dclip = quant_parts(far[d - 1][:, cols].astype(F32), clip_ref[0, n:n + 1, :])
            ks.append(q.astype(BF16))
            dclip_ref[j * rows:(j + 1) * rows, cols] = dclip
        k2 = jnp.concatenate(ks, axis=0)
        k2_ref[:, cols] = k2
        return jnp.dot(k2, qt_ref[cols, :], preferred_element_type=F32)

    def softmax(n, s_all):
        ps = []
        for h in range(span // rows):
            s = merge(near, s_all[:, h * rows:(h + 1) * rows], nb) * factor + bias
            w = jnp.exp2(s - jnp.max(s, axis=0, keepdims=True))
            p = (w * (1.0 / jnp.sum(w, axis=0, keepdims=True))).astype(BF16)
            p_ref[:, n * span + h * rows:n * span + (h + 1) * rows] = p
            ps.append(split(near_b, far_b, p, nb))
        return jnp.concatenate(ps, axis=1)

    def value_grad(n, p2):
        cols = slice(n * hd, (n + 1) * hd)
        vgrad_ref[:, cols] = lax.dot_general(gt_ref[cols, :], p2, ACROSS, preferred_element_type=F32).T

    ahead, behind = scores(0), None
    for n in range(kv_heads):
        s_all, ahead = ahead, scores(n + 1) if n + 1 < kv_heads else None
        p2 = softmax(n, s_all)
        if behind is not None:
            value_grad(n - 1, behind)
        behind = p2
    value_grad(kv_heads - 1, behind)


def grad_kernel(nb, lo, last, qt_ref, gt_ref, quant_ref, dclip_ref, clip_ref, p_ref, kdclip_ref, vgrad_ref, *rest):
    far_v, rest = rest[:nb], rest[nb:]
    if last:
        before, (ds_ref, v2_ref, grad_ref, far_ref, spread_ref, scale_ref) = rest[:3], rest[3:]
    else:
        ds_ref, v2_ref, grad_ref, far_ref, scale_ref = rest
    kv_heads, hd = clip_ref.shape[1], clip_ref.shape[2]
    rows, span = dclip_ref.shape[0], gt_ref.shape[1]
    heads = span // rows
    width = kv_heads * hd
    count = v2_ref.shape[1] // hd
    scale = hd ** -0.5
    near = near_mask(rows)
    near_b = near.astype(F32).astype(BF16)
    far_b = 1.0 - near_b

    def head_cols(j, first=0):
        return slice(first + j * hd, first + (j + 1) * hd)

    k_at = [lo + j if last else j for j in range(count)]
    v_at = [(kv_heads if last else count) + k_at[j] for j in range(count)]

    def value_side(j):
        n = lo + j
        v_grad = vgrad_ref[:, head_cols(n)]
        vs, vd = [quant_ref[:, head_cols(n, width)]], [dclip_ref[:, head_cols(n, width)]]
        for d in far_order(nb):
            q, _, dc = quant_parts(far_v[d - 1][:, head_cols(j)].astype(F32), clip_ref[1, n:n + 1, :])
            vs.append(q.astype(BF16))
            vd.append(dc)
        v2 = jnp.concatenate(vs, axis=0)
        v2_ref[:, head_cols(j)] = v2
        grad_ref[:, head_cols(v_at[j])] = v_grad[:rows].astype(BF16)
        far_ref[:, head_cols(v_at[j])] = v_grad[rows:].astype(BF16)
        scale_ref[v_at[j]:v_at[j] + 1, :] = jnp.sum(v_grad * jnp.concatenate(vd, axis=0), axis=0, keepdims=True)
        return jnp.dot(v2, gt_ref[head_cols(n), :], preferred_element_type=F32)

    def score_side(j, d_all):
        ds = []
        for h in range(heads):
            dp = merge(near, d_all[:, h * rows:(h + 1) * rows], nb)
            at = (lo + j) * span + h * rows
            p = p_ref[:, at:at + rows].astype(F32)
            delta = jnp.sum(p * dp, axis=0, keepdims=True)
            ds_b = (p * (dp - delta)).astype(BF16)
            ds_ref[:, j * span + h * rows:j * span + (h + 1) * rows] = ds_b
            ds.append(split(near_b, far_b, ds_b, nb))
        return jnp.concatenate(ds, axis=1)

    def key_side(j, ds2):
        n = lo + j
        k_grad = (lax.dot_general(qt_ref[head_cols(n), :], ds2, ACROSS, preferred_element_type=F32) * scale).T
        grad_ref[:, head_cols(k_at[j])] = k_grad[:rows].astype(BF16)
        far_ref[:, head_cols(k_at[j])] = k_grad[rows:].astype(BF16)
        scale_ref[k_at[j]:k_at[j] + 1, :] = jnp.sum(
            k_grad[:rows] * dclip_ref[:, head_cols(n)], axis=0, keepdims=True
        ) + jnp.sum(k_grad[rows:] * kdclip_ref[:, head_cols(n)], axis=0, keepdims=True)

    if last:
        for src, dst in zip(before[:2], (grad_ref, far_ref)):
            dst[:, :lo * hd] = src[:, :lo * hd]
            dst[:, width:width + lo * hd] = src[:, lo * hd:]
        scale_ref[:lo, :] = before[2][:lo, :]
        scale_ref[kv_heads:kv_heads + lo, :] = before[2][lo:, :]
    ahead, behind = value_side(0), None
    for j in range(count):
        d_all, ahead = ahead, value_side(j + 1) if j + 1 < count else None
        ds2 = score_side(j, d_all)
        if behind is not None:
            key_side(j - 1, behind)
        behind = ds2
    key_side(count - 1, behind)
    if last:
        spread_ref[...] = jnp.broadcast_to(scale_ref[...].astype(BF16)[None], spread_ref.shape)


def output_kernel(nb, p_ref, ds_a_ref, ds_b_ref, k2_ref, v2_a_ref, v2_b_ref, grad_ref, slope_hbm, *rest):
    backs, rest = rest[:nb], rest[nb:]
    out_hbm, gq_hbm, gk_hbm, gv_hbm, out_ref, gq_ref, gk_ref, gv_ref, slope_ref, back_ref, sems, more_sems = rest
    loads = [pltpu.make_async_copy(slope_hbm, slope_ref, more_sems.at[2])]
    loads += [pltpu.make_async_copy(back, back_ref.at[d], more_sems.at[3 + d]) for d, back in enumerate(backs)]
    for copy in loads:
        copy.start()
    kv_heads = sems.shape[1]
    rows, group = out_ref.shape[0], out_ref.shape[1] // kv_heads
    hd = k2_ref.shape[1] // kv_heads
    heads = group // hd
    near_b = near_mask(rows).astype(F32).astype(BF16)
    far_b = 1.0 - near_b

    def copies(n):
        cols = pl.ds(pl.multiple_of(n * group, group), group)
        return (
            pltpu.make_async_copy(out_ref.at[:, cols], out_hbm.at[:, cols], sems.at[0, n]),
            pltpu.make_async_copy(gq_ref.at[:, cols], gq_hbm.at[:, cols], sems.at[1, n]),
        )

    half = ds_a_ref.shape[1] // (heads * rows)
    for n in range(kv_heads):
        ds_ref, v2_ref, j = (ds_a_ref, v2_a_ref, n) if n < half else (ds_b_ref, v2_b_ref, n - half)
        for left, at, right, to, dst, scale in (
            (v2_ref, j, p_ref, n, out_ref, None),
            (k2_ref, n, ds_ref, j, gq_ref, hd ** -0.5),
        ):
            x = right[:, to * heads * rows:(to + 1) * heads * rows]
            x2 = jnp.concatenate(
                [split(near_b, far_b, x[:, h * rows:(h + 1) * rows], nb) for h in range(heads)], axis=1
            )
            y = jnp.dot(left[:, at * hd:(at + 1) * hd].T, x2, preferred_element_type=F32)
            y = (y if scale is None else y * scale).astype(BF16)
            for h in range(heads):
                first = n * group + h * hd
                dst[:, first:first + hd] = y[:, h * rows:(h + 1) * rows].T
        for copy in copies(n):
            copy.start()
    for copy in loads:
        copy.wait()
    stores = []
    width = gk_ref.shape[1]
    for side, ref, dst in ((0, gk_ref, gk_hbm), (1, gv_ref, gv_hbm)):
        at = slice(side * width, (side + 1) * width)
        total = grad_ref[:, at].astype(F32)
        for d in range(nb):
            total = total + back_ref[d, :, at].astype(F32)
        ref[...] = (total * slope_ref[:, at]).astype(BF16)
        stores.append(pltpu.make_async_copy(ref, dst, more_sems.at[side]))
        stores[-1].start()
    for n in range(kv_heads):
        for copy in copies(n):
            copy.wait()
    for copy in stores:
        copy.wait()


def total_kernel(parts_ref, after_ref, out_ref):
    del after_ref
    out_ref[...] = jnp.sum(parts_ref[...].astype(F32), axis=0)


def on_device(sizes, queries, keys, values, grad_out, quant_scale, doc_lengths):
    dp_count, seq_count = sizes
    count = dp_count * seq_count
    nb = max(1, seq_count // 2)
    rows, width = keys.shape
    kv_heads, hd = quant_scale.shape[1], quant_scale.shape[2]
    heads = queries.shape[1] // hd
    vmem = pl.BlockSpec(memory_space=pltpu.VMEM)
    hbm = pl.BlockSpec(memory_space=pltpu.HBM)
    params = pltpu.CompilerParams(vmem_limit_bytes=36 * 1024 * 1024)
    shape = jax.ShapeDtypeStruct
    work = rows * rows * queries.shape[1]

    def call(kernel, name, flops, args, outs, in_specs=None, out_specs=None, scratch=()):
        return pl.pallas_call(
            kernel,
            out_shape=outs,
            in_specs=in_specs or [vmem] * len(args),
            out_specs=out_specs or (vmem,) * len(outs),
            scratch_shapes=scratch,
            compiler_params=params,
            cost_estimate=pl.CostEstimate(flops=flops, bytes_accessed=16 * rows * width, transcendentals=0),
            name=name,
        )(*args)

    def shift(array, d):
        return lax.ppermute(array, "seq", [(r, (r + d) % seq_count) for r in range(seq_count)])

    def unshift(array, d):
        return lax.ppermute(array, "seq", [((r + d) % seq_count, r) for r in range(seq_count)])

    def pinned(*arrays):
        return [pltpu.with_memory_space_constraint(x, pltpu.HBM) for x in arrays]

    far_k = [shift(keys, d) for d in range(1, nb + 1)]
    turned = shape((width, heads // kv_heads * rows), BF16)
    half = kv_heads // 2 * hd
    q, g, quants, slopes, dclips, bias, clips, part_a, part_b = call(
        functools.partial(prep_kernel, nb),
        "prep",
        2 * work,
        pinned(queries, grad_out, keys, values, quant_scale, doc_lengths),
        (
            shape(queries.shape, BF16),
            shape(queries.shape, BF16),
            shape((rows, 2 * width), BF16),
            pltpu.HBM((rows, 2 * width), F32),
            shape((rows, 2 * width), F32),
            shape((nb * rows, rows), F32),
            shape(quant_scale.shape, F32),
            shape((rows, half), BF16),
            shape((rows, width - half), BF16),
        ),
        in_specs=[hbm] * 6,
        out_specs=(vmem,) * 3 + (hbm,) + (vmem,) * 5,
        scratch=[
            pltpu.VMEM(keys.shape, BF16),
            pltpu.VMEM(values.shape, BF16),
            pltpu.SMEM(doc_lengths.shape, jnp.int32),
            pltpu.VMEM((rows, 2 * width), F32),
            pltpu.SemaphoreType.DMA((7,)),
        ],
    )
    far_a = [shift(part_a, d) for d in range(1, nb + 1)]
    far_b = [shift(part_b, d) for d in range(1, nb + 1)]
    qt, gt = call(functools.partial(turn_kernel, kv_heads), "turn", work, (q, g), (turned, turned))
    p, k2, kdclips, v_grads = call(
        functools.partial(score_kernel, nb),
        "score",
        4 * (nb + 1) * work,
        (qt, gt, quants, bias, clips, *far_k),
        (
            shape((nb * rows, heads * rows), BF16),
            shape(((nb + 1) * rows, width), BF16),
            shape((nb * rows, width), F32),
            shape(((nb + 1) * rows, width), F32),
        ),
    )
    common = (qt, gt, quants, dclips, clips, p, kdclips, v_grads)
    span = turned.shape[1]
    ds_a, v2_a, *before = call(
        functools.partial(grad_kernel, nb, 0, False),
        "grad_a",
        2 * (nb + 1) * work,
        (*common, *far_a),
        (
            shape((nb * rows, half // hd * span), BF16),
            shape(((nb + 1) * rows, half), BF16),
            shape((rows, 2 * half), BF16),
            shape((nb * rows, 2 * half), BF16),
            shape((2 * half // hd, hd), F32),
        ),
    )
    ds_b, v2_b, grads, far_grads, spread = call(
        functools.partial(grad_kernel, nb, half // hd, True),
        "grad_b",
        2 * (nb + 1) * work,
        (*common, *far_b, *before),
        (
            shape((nb * rows, (width - half) // hd * span), BF16),
            shape(((nb + 1) * rows, width - half), BF16),
            shape((rows, 2 * width), BF16),
            shape((nb * rows, 2 * width), BF16),
            pltpu.VMEM((count, 2 * kv_heads, hd), BF16),
        ),
        scratch=[pltpu.VMEM((2 * kv_heads, hd), F32)],
    )
    backs = []
    for d in range(1, nb + 1):
        at = far_order(nb).index(d) * rows
        backs.append(unshift(lax.slice_in_dim(far_grads, at, at + rows, axis=0), d))
    parts = lax.all_to_all(
        spread,
        ("dp", "seq"),
        split_axis=0,
        concat_axis=0,
        axis_index_groups=[list(reversed(range(count)))],
        tiled=True,
    )
    attn_out, grad_queries, grad_keys, grad_values = call(
        functools.partial(output_kernel, nb),
        "output",
        4 * (nb + 1) * work,
        (p, ds_a, ds_b, k2, v2_a, v2_b, grads, *pinned(slopes), *backs),
        (
            shape(queries.shape, BF16),
            shape(queries.shape, BF16),
            shape((rows, width), BF16),
            shape((rows, width), BF16),
        ),
        in_specs=[vmem] * 7 + [hbm] + [pl.BlockSpec(memory_space=pl.ANY)] * nb,
        out_specs=(hbm,) * 4,
        scratch=[
            pltpu.VMEM(queries.shape, BF16),
            pltpu.VMEM(queries.shape, BF16),
            pltpu.VMEM((rows, width), BF16),
            pltpu.VMEM((rows, width), BF16),
            pltpu.VMEM((rows, 2 * width), F32),
            pltpu.VMEM((nb, rows, 2 * width), BF16),
            pltpu.SemaphoreType.DMA((2, kv_heads)),
            pltpu.SemaphoreType.DMA((3 + nb,)),
        ],
    )
    (grad_scale,) = call(
        total_kernel,
        "total",
        parts.size,
        (parts, *pinned(grad_keys)),
        (shape(parts.shape[1:], F32),),
        in_specs=[vmem, hbm],
    )
    return (attn_out, grad_queries, grad_keys, grad_values, grad_scale.reshape(quant_scale.shape))


def solution(mesh):
    rows = P(("dp", "seq"), None)
    return jax.shard_map(
        functools.partial(on_device, (mesh.shape["dp"], mesh.shape["seq"])),
        mesh=mesh,
        in_specs=(rows, rows, rows, rows, P(), P("dp", None)),
        out_specs=(rows, rows, rows, rows, P()),
        check_vma=False,
    )
```

```python
import functools
import math

import jax
import jax.numpy as jnp
from jax import lax
from jax.experimental import pallas as pl
from jax.experimental.pallas import tpu as pltpu
from jax.sharding import PartitionSpec as P

F32 = jnp.float32
BF16 = jnp.bfloat16
LEVELS = 127.0
NEG = -1e30


def sin_cos_half(u):
    r = (u - jnp.round(u)) * math.pi
    z = r * r
    s = z * (1.0 / 6227020800.0) - 1.0 / 39916800.0
    for c in (1.0 / 362880.0, -1.0 / 5040.0, 1.0 / 120.0, -1.0 / 6.0, 1.0):
        s = s * z + c
    s = s * r
    k = z * (1.0 / 479001600.0) - 1.0 / 3628800.0
    for c in (1.0 / 40320.0, -1.0 / 720.0, 1.0 / 24.0, -0.5, 1.0):
        k = k * z + c
    return s, k


def quant_parts(x, clip):
    inv = 1.0 / clip
    ratio = x * inv
    t = jnp.tanh(ratio)
    u = LEVELS * t
    s, k = sin_cos_half(u)
    level = u - s * k * (1.0 / math.pi)
    unit = level * (1.0 / LEVELS)
    slope = (2.0 * s * s) * (1.0 - t * t)
    return clip * unit, slope, unit - slope * ratio


def prep_kernel(nb, q_hbm, g_hbm, key_hbm, value_hbm, clip_hbm, len_hbm, qt_ref, gt_ref, quant_ref, slope_hbm,
                dclip_ref, bias_ref, clip_out, q_ref, g_ref, key_ref, value_ref, len_ref, slope_ref, sems):
    small = [
        pltpu.make_async_copy(src, dst, sems.at[i])
        for i, (src, dst) in enumerate(
            ((len_hbm, len_ref), (clip_hbm, clip_out), (key_hbm, key_ref), (value_hbm, value_ref))
        )
    ]
    large = [
        pltpu.make_async_copy(q_hbm, q_ref, sems.at[4]),
        pltpu.make_async_copy(g_hbm, g_ref, sems.at[5]),
    ]
    for copy in small + large:
        copy.start()
    rows = key_ref.shape[0]
    kv_heads, hd = clip_out.shape[1], clip_out.shape[2]
    group = q_ref.shape[1] // kv_heads
    base = lax.axis_index("seq") * rows
    for copy in small:
        copy.wait()
    for side, src in ((0, key_ref), (1, value_ref)):
        for n in range(kv_heads):
            x = src[:, n * hd:(n + 1) * hd].astype(F32)
            q, slope, dclip = quant_parts(x, clip_out[side, n:n + 1, :])
            at = slice((side * kv_heads + n) * hd, (side * kv_heads + n + 1) * hd)
            quant_ref[:, at] = q.astype(BF16)
            slope_ref[:, at] = slope
            dclip_ref[:, at] = dclip
    slope_copy = pltpu.make_async_copy(slope_ref, slope_hbm, sems.at[6])
    slope_copy.start()
    key = lax.broadcasted_iota(jnp.int32, (rows, rows), 0)
    row = lax.broadcasted_iota(jnp.int32, (rows, rows), 1)
    start = jnp.zeros((rows, rows), jnp.int32)
    end = jnp.int32(0)
    for d in range(len_ref.shape[1]):
        end = end + len_ref[0, d]
        start = jnp.where(row + base >= end, end, start)
    for b in range(nb):
        pos = jnp.where(key <= row, key, key - nb * rows) if b == 0 else key - b * rows
        bias_ref[b * rows:(b + 1) * rows, :] = jnp.where(pos + base >= start, 0.0, NEG)
    for copy, src, dst in zip(large, (q_ref, g_ref), (qt_ref, gt_ref)):
        copy.wait()
        for n in range(kv_heads):
            for h in range(group // hd):
                at = n * group + h * hd
                dst[n * hd:(n + 1) * hd, h * rows:(h + 1) * rows] = src[:, at:at + hd].T
    slope_copy.wait()


ACROSS = (((1,), (1,)), ((), ()))


def far_order(nb):
    return [nb] + list(range(1, nb))


def near_mask(rows):
    key = lax.broadcasted_iota(jnp.int32, (rows, rows), 0)
    row = lax.broadcasted_iota(jnp.int32, (rows, rows), 1)
    return key <= row


def merge(near, x, nb):
    rows = near.shape[0]
    first = jnp.where(near, x[:rows], x[rows:2 * rows])
    return jnp.concatenate([first, x[2 * rows:]], axis=0) if nb > 1 else first


def split(near_b, far_b, x, nb):
    rows = near_b.shape[0]
    parts = [x[:rows] * near_b, x[:rows] * far_b]
    if nb > 1:
        parts.append(x[rows:])
    return jnp.concatenate(parts, axis=0)


def score_kernel(nb, qt_ref, quant_ref, bias_ref, clip_ref, *rest):
    far, (p_ref, k2_ref, dclip_ref) = rest[:nb], rest[nb:]
    kv_heads, hd = clip_ref.shape[1], clip_ref.shape[2]
    rows, span = bias_ref.shape[1], qt_ref.shape[1]
    factor = hd ** -0.5 * math.log2(math.e)
    near = near_mask(rows)

    bias = bias_ref[...]

    def scores(n):
        cols = slice(n * hd, (n + 1) * hd)
        ks = [quant_ref[:, cols]]
        for j, d in enumerate(far_order(nb)):
            q, _, dclip = quant_parts(far[d - 1][:, cols].astype(F32), clip_ref[0, n:n + 1, :])
            ks.append(q.astype(BF16))
            dclip_ref[j * rows:(j + 1) * rows, cols] = dclip
        k2 = jnp.concatenate(ks, axis=0)
        k2_ref[:, cols] = k2
        return jnp.dot(k2, qt_ref[cols, :], preferred_element_type=F32)

    ahead = scores(0)
    for n in range(kv_heads):
        s_all, ahead = ahead, scores(n + 1) if n + 1 < kv_heads else None
        for h in range(span // rows):
            s = merge(near, s_all[:, h * rows:(h + 1) * rows], nb) * factor + bias
            w = jnp.exp2(s - jnp.max(s, axis=0, keepdims=True))
            p = w * (1.0 / jnp.sum(w, axis=0, keepdims=True))
            p_ref[:, n * span + h * rows:n * span + (h + 1) * rows] = p.astype(BF16)


def grad_kernel(nb, qt_ref, gt_ref, quant_ref, dclip_ref, clip_ref, p_ref, kdclip_ref, *rest):
    far_v, (ds_ref, v2_ref, grad_ref, far_ref, scale_ref) = rest[:nb], rest[nb:]
    kv_heads, hd = clip_ref.shape[1], clip_ref.shape[2]
    rows, span = dclip_ref.shape[0], gt_ref.shape[1]
    heads = span // rows
    width = kv_heads * hd
    scale = hd ** -0.5
    near = near_mask(rows)
    near_b = near.astype(F32).astype(BF16)
    far_b = 1.0 - near_b

    def k_cols(n):
        return slice(n * hd, (n + 1) * hd)

    def v_cols(n):
        return slice(width + n * hd, width + (n + 1) * hd)

    def value_side(n):
        p2 = jnp.concatenate(
            [split(near_b, far_b, p_ref[:, n * span + h * rows:n * span + (h + 1) * rows], nb) for h in range(heads)],
            axis=1,
        )
        v_grad = lax.dot_general(gt_ref[k_cols(n), :], p2, ACROSS, preferred_element_type=F32).T
        vs, vd = [quant_ref[:, v_cols(n)]], [dclip_ref[:, v_cols(n)]]
        for d in far_order(nb):
            q, _, dc = quant_parts(far_v[d - 1][:, k_cols(n)].astype(F32), clip_ref[1, n:n + 1, :])
            vs.append(q.astype(BF16))
            vd.append(dc)
        v2 = jnp.concatenate(vs, axis=0)
        v2_ref[:, k_cols(n)] = v2
        grad_ref[:, v_cols(n)] = v_grad[:rows].astype(BF16)
        far_ref[:, v_cols(n)] = v_grad[rows:].astype(BF16)
        scale_ref[kv_heads + n:kv_heads + n + 1, :] = jnp.sum(
            v_grad * jnp.concatenate(vd, axis=0), axis=0, keepdims=True
        )
        return jnp.dot(v2, gt_ref[k_cols(n), :], preferred_element_type=F32)

    def score_side(n, d_all):
        ds = []
        for h in range(heads):
            dp = merge(near, d_all[:, h * rows:(h + 1) * rows], nb)
            at = slice(n * span + h * rows, n * span + (h + 1) * rows)
            p = p_ref[:, at].astype(F32)
            delta = jnp.sum(p * dp, axis=0, keepdims=True)
            ds_b = (p * (dp - delta)).astype(BF16)
            ds_ref[:, at] = ds_b
            ds.append(split(near_b, far_b, ds_b, nb))
        return jnp.concatenate(ds, axis=1)

    def key_side(n, ds2):
        k_grad = (lax.dot_general(qt_ref[k_cols(n), :], ds2, ACROSS, preferred_element_type=F32) * scale).T
        grad_ref[:, k_cols(n)] = k_grad[:rows].astype(BF16)
        far_ref[:, k_cols(n)] = k_grad[rows:].astype(BF16)
        scale_ref[n:n + 1, :] = jnp.sum(k_grad[:rows] * dclip_ref[:, k_cols(n)], axis=0, keepdims=True) + jnp.sum(
            k_grad[rows:] * kdclip_ref[:, k_cols(n)], axis=0, keepdims=True
        )

    ahead, behind = value_side(0), None
    for n in range(kv_heads):
        d_all, ahead = ahead, value_side(n + 1) if n + 1 < kv_heads else None
        ds2 = score_side(n, d_all)
        if behind is not None:
            key_side(n - 1, behind)
        behind = ds2
    key_side(kv_heads - 1, behind)


def output_kernel(nb, p_ref, ds_ref, k2_ref, v2_ref, grad_ref, slope_hbm, *rest):
    backs, rest = rest[:nb], rest[nb:]
    out_hbm, gq_hbm, gk_hbm, gv_hbm, out_ref, gq_ref, gk_ref, gv_ref, slope_ref, back_ref, sems, more_sems = rest
    loads = [pltpu.make_async_copy(slope_hbm, slope_ref, more_sems.at[2])]
    loads += [pltpu.make_async_copy(back, back_ref.at[d], more_sems.at[3 + d]) for d, back in enumerate(backs)]
    for copy in loads:
        copy.start()
    kv_heads = sems.shape[1]
    rows, group = out_ref.shape[0], out_ref.shape[1] // kv_heads
    hd = k2_ref.shape[1] // kv_heads
    heads = group // hd
    near_b = near_mask(rows).astype(F32).astype(BF16)
    far_b = 1.0 - near_b

    def copies(n):
        cols = pl.ds(pl.multiple_of(n * group, group), group)
        return (
            pltpu.make_async_copy(out_ref.at[:, cols], out_hbm.at[:, cols], sems.at[0, n]),
            pltpu.make_async_copy(gq_ref.at[:, cols], gq_hbm.at[:, cols], sems.at[1, n]),
        )

    def step(n, carry):
        cols = pl.ds(pl.multiple_of(n * hd, hd), hd)
        for left, right, dst, scale in ((v2_ref, p_ref, out_ref, None), (k2_ref, ds_ref, gq_ref, hd ** -0.5)):
            at = pl.ds(pl.multiple_of(n * heads * rows, rows), heads * rows)
            x = right[:, at]
            x2 = jnp.concatenate(
                [split(near_b, far_b, x[:, h * rows:(h + 1) * rows], nb) for h in range(heads)], axis=1
            )
            y = jnp.dot(left[:, cols].T, x2, preferred_element_type=F32)
            y = (y if scale is None else y * scale).astype(BF16)
            for h in range(heads):
                dst[:, pl.ds(pl.multiple_of(n * group + h * hd, hd), hd)] = y[:, h * rows:(h + 1) * rows].T
        for copy in copies(n):
            copy.start()
        return carry

    lax.fori_loop(0, kv_heads, step, 0, unroll=True)
    for copy in loads:
        copy.wait()
    stores = []
    width = gk_ref.shape[1]
    for side, ref, dst in ((0, gk_ref, gk_hbm), (1, gv_ref, gv_hbm)):
        at = slice(side * width, (side + 1) * width)
        total = grad_ref[:, at].astype(F32)
        for d in range(nb):
            total = total + back_ref[d, :, at].astype(F32)
        ref[...] = (total * slope_ref[:, at]).astype(BF16)
        stores.append(pltpu.make_async_copy(ref, dst, more_sems.at[side]))
        stores[-1].start()
    for n in range(kv_heads):
        for copy in copies(n):
            copy.wait()
    for copy in stores:
        copy.wait()


def plane_sums(part, count):
    axes = ("dp", "seq")
    size = min(8, count)

    def exchange(array, mask):
        return lax.ppermute(array, axes, [(i, i ^ mask) for i in range(count)])

    bits = [1 << b for b in range(size.bit_length() - 1, count.bit_length() - 1)]
    if len(bits) % 2:
        part = part + exchange(part, bits[0])
        bits = bits[1:]
    for low, high in zip(bits[::2], bits[1::2]):
        far, mid, near = exchange(part, low | high), exchange(part, high), exchange(part, low)
        part = (part + near) + (mid + far)
    groups = [list(range(first, first + size)) for first in range(0, count, size)]
    copies = jnp.broadcast_to(part.astype(BF16)[None], (size,) + part.shape)
    return lax.all_to_all(copies, axes, split_axis=0, concat_axis=0, axis_index_groups=groups, tiled=True), part


def total_kernel(parts_ref, after_ref, out_ref):
    del after_ref
    out_ref[...] = jnp.sum(parts_ref[...].astype(F32), axis=0)


def on_device(sizes, queries, keys, values, grad_out, quant_scale, doc_lengths):
    dp_count, seq_count = sizes
    count = dp_count * seq_count
    nb = max(1, seq_count // 2)
    rows, width = keys.shape
    kv_heads, hd = quant_scale.shape[1], quant_scale.shape[2]
    heads = queries.shape[1] // hd
    vmem = pl.BlockSpec(memory_space=pltpu.VMEM)
    hbm = pl.BlockSpec(memory_space=pltpu.HBM)
    params = pltpu.CompilerParams(vmem_limit_bytes=36 * 1024 * 1024)
    shape = jax.ShapeDtypeStruct
    work = rows * rows * queries.shape[1]

    def call(kernel, name, flops, args, outs, in_specs=None, out_specs=None, scratch=()):
        return pl.pallas_call(
            kernel,
            out_shape=outs,
            in_specs=in_specs or [vmem] * len(args),
            out_specs=out_specs or (vmem,) * len(outs),
            scratch_shapes=scratch,
            compiler_params=params,
            cost_estimate=pl.CostEstimate(flops=flops, bytes_accessed=16 * rows * width, transcendentals=0),
            name=name,
        )(*args)

    def shift(array, d):
        return lax.ppermute(array, "seq", [(r, (r + d) % seq_count) for r in range(seq_count)])

    def unshift(array, d):
        return lax.ppermute(array, "seq", [((r + d) % seq_count, r) for r in range(seq_count)])

    far_k = [shift(keys, d) for d in range(1, nb + 1)]
    far_v = [shift(values, d) for d in range(1, nb + 1)]

    raw = (queries, grad_out, keys, values, quant_scale, doc_lengths)
    qt, gt, quants, slopes, dclips, bias, clips = call(
        functools.partial(prep_kernel, nb),
        "prep",
        2 * work,
        [pltpu.with_memory_space_constraint(x, pltpu.HBM) for x in raw],
        (
            shape((width, heads // kv_heads * rows), BF16),
            shape((width, heads // kv_heads * rows), BF16),
            shape((rows, 2 * width), BF16),
            pltpu.HBM((rows, 2 * width), F32),
            shape((rows, 2 * width), F32),
            shape((nb * rows, rows), F32),
            shape(quant_scale.shape, F32),
        ),
        in_specs=[hbm] * 6,
        out_specs=(vmem, vmem, vmem, hbm, vmem, vmem, vmem),
        scratch=[
            pltpu.VMEM(queries.shape, BF16),
            pltpu.VMEM(queries.shape, BF16),
            pltpu.VMEM(keys.shape, BF16),
            pltpu.VMEM(values.shape, BF16),
            pltpu.SMEM(doc_lengths.shape, jnp.int32),
            pltpu.VMEM((rows, 2 * width), F32),
            pltpu.SemaphoreType.DMA((7,)),
        ],
    )
    p, k2, kdclips = call(
        functools.partial(score_kernel, nb),
        "score",
        2 * (nb + 1) * work,
        (qt, quants, bias, clips, *far_k),
        (
            shape((nb * rows, heads * rows), BF16),
            shape(((nb + 1) * rows, width), BF16),
            shape((nb * rows, width), F32),
        ),
    )
    ds, v2, grads, far_grads, scale_part = call(
        functools.partial(grad_kernel, nb),
        "grad",
        6 * (nb + 1) * work,
        (qt, gt, quants, dclips, clips, p, kdclips, *far_v),
        (
            shape((nb * rows, heads * rows), BF16),
            shape(((nb + 1) * rows, width), BF16),
            shape((rows, 2 * width), BF16),
            shape((nb * rows, 2 * width), BF16),
            shape((2 * kv_heads, hd), F32),
        ),
    )
    backs = []
    for d in range(1, nb + 1):
        at = far_order(nb).index(d) * rows
        backs.append(unshift(lax.slice_in_dim(far_grads, at, at + rows, axis=0), d))
    parts, plane_part = plane_sums(scale_part, count)
    k2, _ = lax.optimization_barrier((k2, plane_part))
    pinned = pltpu.with_memory_space_constraint(slopes, pltpu.HBM)
    attn_out, grad_queries, grad_keys, grad_values = call(
        functools.partial(output_kernel, nb),
        "output",
        4 * (nb + 1) * work,
        (p, ds, k2, v2, grads, pinned, *backs),
        (
            shape(queries.shape, BF16),
            shape(queries.shape, BF16),
            shape((rows, width), BF16),
            shape((rows, width), BF16),
        ),
        in_specs=[vmem] * 5 + [hbm] + [pl.BlockSpec(memory_space=pl.ANY)] * nb,
        out_specs=(hbm,) * 4,
        scratch=[
            pltpu.VMEM(queries.shape, BF16),
            pltpu.VMEM(queries.shape, BF16),
            pltpu.VMEM((rows, width), BF16),
            pltpu.VMEM((rows, width), BF16),
            pltpu.VMEM((rows, 2 * width), F32),
            pltpu.VMEM((nb, rows, 2 * width), BF16),
            pltpu.SemaphoreType.DMA((2, kv_heads)),
            pltpu.SemaphoreType.DMA((3 + nb,)),
        ],
    )
    (grad_scale,) = call(
        total_kernel,
        "total",
        parts.size,
        (parts, pltpu.with_memory_space_constraint(grad_keys, pltpu.HBM)),
        (shape(parts.shape[1:], F32),),
        in_specs=[vmem, hbm],
    )
    return (attn_out, grad_queries, grad_keys, grad_values, grad_scale.reshape(quant_scale.shape))


def solution(mesh):
    rows = P(("dp", "seq"), None)
    return jax.shard_map(
        functools.partial(on_device, (mesh.shape["dp"], mesh.shape["seq"])),
        mesh=mesh,
        in_specs=(rows, rows, rows, rows, P(), P("dp", None)),
        out_specs=(rows, rows, rows, rows, P()),
        check_vma=False,
    )
```

```python
import functools
import math

import jax
import jax.numpy as jnp
from jax import lax
from jax.experimental import pallas as pl
from jax.experimental.pallas import tpu as pltpu
from jax.sharding import PartitionSpec as P

F32 = jnp.float32
BF16 = jnp.bfloat16
LEVELS = 127.0
NEG = -1e30


def sin_cos_half(u):
    r = (u - jnp.round(u)) * math.pi
    z = r * r
    s = z * (1.0 / 6227020800.0) - 1.0 / 39916800.0
    for c in (1.0 / 362880.0, -1.0 / 5040.0, 1.0 / 120.0, -1.0 / 6.0, 1.0):
        s = s * z + c
    s = s * r
    k = z * (1.0 / 479001600.0) - 1.0 / 3628800.0
    for c in (1.0 / 40320.0, -1.0 / 720.0, 1.0 / 24.0, -0.5, 1.0):
        k = k * z + c
    return s, k


def quant_parts(x, clip):
    inv = 1.0 / clip
    ratio = x * inv
    t = jnp.tanh(ratio)
    u = LEVELS * t
    s, k = sin_cos_half(u)
    level = u - s * k * (1.0 / math.pi)
    unit = level * (1.0 / LEVELS)
    slope = (2.0 * s * s) * (1.0 - t * t)
    return clip * unit, slope, unit - slope * ratio


def prep_kernel(nb, q_hbm, g_hbm, key_hbm, value_hbm, clip_hbm, len_hbm, qt_ref, gt_ref, quant_ref, slope_hbm,
                dclip_ref, bias_ref, clip_out, q_ref, g_ref, key_ref, value_ref, len_ref, slope_ref, sems):
    small = [
        pltpu.make_async_copy(src, dst, sems.at[i])
        for i, (src, dst) in enumerate(
            ((len_hbm, len_ref), (clip_hbm, clip_out), (key_hbm, key_ref), (value_hbm, value_ref))
        )
    ]
    large = [
        pltpu.make_async_copy(q_hbm, q_ref, sems.at[4]),
        pltpu.make_async_copy(g_hbm, g_ref, sems.at[5]),
    ]
    for copy in small + large:
        copy.start()
    rows = key_ref.shape[0]
    kv_heads, hd = clip_out.shape[1], clip_out.shape[2]
    group = q_ref.shape[1] // kv_heads
    base = lax.axis_index("seq") * rows
    for copy in small:
        copy.wait()
    for side, src in ((0, key_ref), (1, value_ref)):
        for n in range(kv_heads):
            x = src[:, n * hd:(n + 1) * hd].astype(F32)
            q, slope, dclip = quant_parts(x, clip_out[side, n:n + 1, :])
            at = slice((side * kv_heads + n) * hd, (side * kv_heads + n + 1) * hd)
            quant_ref[:, at] = q.astype(BF16)
            slope_ref[:, at] = slope
            dclip_ref[:, at] = dclip
    slope_copy = pltpu.make_async_copy(slope_ref, slope_hbm, sems.at[6])
    slope_copy.start()
    key = lax.broadcasted_iota(jnp.int32, (rows, rows), 0)
    row = lax.broadcasted_iota(jnp.int32, (rows, rows), 1)
    start = jnp.zeros((rows, rows), jnp.int32)
    end = jnp.int32(0)
    for d in range(len_ref.shape[1]):
        end = end + len_ref[0, d]
        start = jnp.where(row + base >= end, end, start)
    for b in range(nb):
        pos = jnp.where(key <= row, key, key - nb * rows) if b == 0 else key - b * rows
        bias_ref[b * rows:(b + 1) * rows, :] = jnp.where(pos + base >= start, 0.0, NEG)
    for copy, src, dst in zip(large, (q_ref, g_ref), (qt_ref, gt_ref)):
        copy.wait()
        for n in range(kv_heads):
            for h in range(group // hd):
                at = n * group + h * hd
                dst[n * hd:(n + 1) * hd, h * rows:(h + 1) * rows] = src[:, at:at + hd].T
    slope_copy.wait()


def far_order(nb):
    return [nb] + list(range(1, nb))


def near_mask(rows):
    key = lax.broadcasted_iota(jnp.int32, (rows, rows), 0)
    row = lax.broadcasted_iota(jnp.int32, (rows, rows), 1)
    return key <= row


def merge(near, x, nb):
    rows = near.shape[0]
    first = jnp.where(near, x[:rows], x[rows:2 * rows])
    return jnp.concatenate([first, x[2 * rows:]], axis=0) if nb > 1 else first


def split(near_b, far_b, x, nb):
    rows = near_b.shape[0]
    parts = [x[:rows] * near_b, x[:rows] * far_b]
    if nb > 1:
        parts.append(x[rows:])
    return jnp.concatenate(parts, axis=0)


def score_kernel(nb, qt_ref, quant_ref, bias_ref, clip_ref, *rest):
    far, (p_ref, k2_ref, dclip_ref) = rest[:nb], rest[nb:]
    kv_heads, hd = clip_ref.shape[1], clip_ref.shape[2]
    rows, span = bias_ref.shape[1], qt_ref.shape[1]
    factor = hd ** -0.5 * math.log2(math.e)
    near = near_mask(rows)

    bias = bias_ref[...]

    def scores(n):
        cols = slice(n * hd, (n + 1) * hd)
        ks = [quant_ref[:, cols]]
        for j, d in enumerate(far_order(nb)):
            q, _, dclip = quant_parts(far[d - 1][:, cols].astype(F32), clip_ref[0, n:n + 1, :])
            ks.append(q.astype(BF16))
            dclip_ref[j * rows:(j + 1) * rows, cols] = dclip
        k2 = jnp.concatenate(ks, axis=0)
        k2_ref[:, cols] = k2
        return jnp.dot(k2, qt_ref[cols, :], preferred_element_type=F32)

    ahead = scores(0)
    for n in range(kv_heads):
        s_all, ahead = ahead, scores(n + 1) if n + 1 < kv_heads else None
        for h in range(span // rows):
            s = merge(near, s_all[:, h * rows:(h + 1) * rows], nb) * factor + bias
            w = jnp.exp2(s - jnp.max(s, axis=0, keepdims=True))
            p = w * (1.0 / jnp.sum(w, axis=0, keepdims=True))
            p_ref[:, n * span + h * rows:n * span + (h + 1) * rows] = p.astype(BF16)


def grad_kernel(nb, q_ref, g_ref, gt_ref, quant_ref, dclip_ref, clip_ref, p_ref, kdclip_ref, *rest):
    far_v, (ds_ref, v2_ref, grad_ref, far_ref, spread_ref, scale_ref) = rest[:nb], rest[nb:]
    kv_heads, hd = clip_ref.shape[1], clip_ref.shape[2]
    rows, span = dclip_ref.shape[0], gt_ref.shape[1]
    heads = span // rows
    width = kv_heads * hd
    scale = hd ** -0.5
    near = near_mask(rows)
    near_b = near.astype(F32).astype(BF16)
    far_b = 1.0 - near_b

    def k_cols(n):
        return slice(n * hd, (n + 1) * hd)

    def v_cols(n):
        return slice(width + n * hd, width + (n + 1) * hd)

    def stacked(ref, n):
        return jnp.concatenate(
            [ref[:, (n * heads + h) * hd:(n * heads + h + 1) * hd] for h in range(heads)], axis=0
        )

    def value_side(n):
        p2 = jnp.concatenate(
            [split(near_b, far_b, p_ref[:, n * span + h * rows:n * span + (h + 1) * rows], nb) for h in range(heads)],
            axis=1,
        )
        v_grad = jnp.dot(p2, stacked(g_ref, n), preferred_element_type=F32)
        vs, vd = [quant_ref[:, v_cols(n)]], [dclip_ref[:, v_cols(n)]]
        for d in far_order(nb):
            q, _, dc = quant_parts(far_v[d - 1][:, k_cols(n)].astype(F32), clip_ref[1, n:n + 1, :])
            vs.append(q.astype(BF16))
            vd.append(dc)
        v2 = jnp.concatenate(vs, axis=0)
        v2_ref[:, k_cols(n)] = v2
        grad_ref[:, v_cols(n)] = v_grad[:rows].astype(BF16)
        far_ref[:, v_cols(n)] = v_grad[rows:].astype(BF16)
        scale_ref[kv_heads + n:kv_heads + n + 1, :] = jnp.sum(
            v_grad * jnp.concatenate(vd, axis=0), axis=0, keepdims=True
        )
        return jnp.dot(v2, gt_ref[k_cols(n), :], preferred_element_type=F32)

    def score_side(n, d_all):
        ds = []
        for h in range(heads):
            dp = merge(near, d_all[:, h * rows:(h + 1) * rows], nb)
            at = slice(n * span + h * rows, n * span + (h + 1) * rows)
            p = p_ref[:, at].astype(F32)
            delta = jnp.sum(p * dp, axis=0, keepdims=True)
            ds_b = (p * (dp - delta)).astype(BF16)
            ds_ref[:, at] = ds_b
            ds.append(split(near_b, far_b, ds_b, nb))
        return jnp.concatenate(ds, axis=1)

    def key_side(n, ds2):
        k_grad = jnp.dot(ds2, stacked(q_ref, n), preferred_element_type=F32) * scale
        grad_ref[:, k_cols(n)] = k_grad[:rows].astype(BF16)
        far_ref[:, k_cols(n)] = k_grad[rows:].astype(BF16)
        scale_ref[n:n + 1, :] = jnp.sum(k_grad[:rows] * dclip_ref[:, k_cols(n)], axis=0, keepdims=True) + jnp.sum(
            k_grad[rows:] * kdclip_ref[:, k_cols(n)], axis=0, keepdims=True
        )

    ahead, behind = value_side(0), None
    for n in range(kv_heads):
        d_all, ahead = ahead, value_side(n + 1) if n + 1 < kv_heads else None
        ds2 = score_side(n, d_all)
        if behind is not None:
            key_side(n - 1, behind)
        behind = ds2
    key_side(kv_heads - 1, behind)
    part = scale_ref[...].astype(BF16)

    def spread(i, carry):
        spread_ref[i] = part
        return carry

    lax.fori_loop(0, spread_ref.shape[0], spread, 0, unroll=8)


def output_kernel(nb, p_ref, ds_ref, k2_ref, v2_ref, grad_ref, slope_hbm, *rest):
    backs, rest = rest[:nb], rest[nb:]
    out_hbm, gq_hbm, gk_hbm, gv_hbm, out_ref, gq_ref, gk_ref, gv_ref, slope_ref, back_ref, sems, more_sems = rest
    loads = [pltpu.make_async_copy(slope_hbm, slope_ref, more_sems.at[2])]
    loads += [pltpu.make_async_copy(back, back_ref.at[d], more_sems.at[3 + d]) for d, back in enumerate(backs)]
    for copy in loads:
        copy.start()
    kv_heads = sems.shape[1]
    rows, group = out_ref.shape[0], out_ref.shape[1] // kv_heads
    hd = k2_ref.shape[1] // kv_heads
    heads = group // hd
    near_b = near_mask(rows).astype(F32).astype(BF16)
    far_b = 1.0 - near_b

    def copies(n):
        cols = pl.ds(pl.multiple_of(n * group, group), group)
        return (
            pltpu.make_async_copy(out_ref.at[:, cols], out_hbm.at[:, cols], sems.at[0, n]),
            pltpu.make_async_copy(gq_ref.at[:, cols], gq_hbm.at[:, cols], sems.at[1, n]),
        )

    def step(n, carry):
        cols = pl.ds(pl.multiple_of(n * hd, hd), hd)
        for left, right, dst, scale in ((v2_ref, p_ref, out_ref, None), (k2_ref, ds_ref, gq_ref, hd ** -0.5)):
            at = pl.ds(pl.multiple_of(n * heads * rows, rows), heads * rows)
            x = right[:, at]
            x2 = jnp.concatenate(
                [split(near_b, far_b, x[:, h * rows:(h + 1) * rows], nb) for h in range(heads)], axis=1
            )
            y = jnp.dot(left[:, cols].T, x2, preferred_element_type=F32)
            y = (y if scale is None else y * scale).astype(BF16)
            for h in range(heads):
                dst[:, pl.ds(pl.multiple_of(n * group + h * hd, hd), hd)] = y[:, h * rows:(h + 1) * rows].T
        for copy in copies(n):
            copy.start()
        return carry

    lax.fori_loop(0, kv_heads, step, 0, unroll=True)
    for copy in loads:
        copy.wait()
    stores = []
    width = gk_ref.shape[1]
    for side, ref, dst in ((0, gk_ref, gk_hbm), (1, gv_ref, gv_hbm)):
        at = slice(side * width, (side + 1) * width)
        total = grad_ref[:, at].astype(F32)
        for d in range(nb):
            total = total + back_ref[d, :, at].astype(F32)
        ref[...] = (total * slope_ref[:, at]).astype(BF16)
        stores.append(pltpu.make_async_copy(ref, dst, more_sems.at[side]))
        stores[-1].start()
    for n in range(kv_heads):
        for copy in copies(n):
            copy.wait()
    for copy in stores:
        copy.wait()


def total_kernel(parts_ref, after_ref, out_ref):
    del after_ref
    out_ref[...] = jnp.sum(parts_ref[...].astype(F32), axis=0)


def on_device(sizes, queries, keys, values, grad_out, quant_scale, doc_lengths):
    dp_count, seq_count = sizes
    count = dp_count * seq_count
    nb = max(1, seq_count // 2)
    rows, width = keys.shape
    kv_heads, hd = quant_scale.shape[1], quant_scale.shape[2]
    heads = queries.shape[1] // hd
    vmem = pl.BlockSpec(memory_space=pltpu.VMEM)
    hbm = pl.BlockSpec(memory_space=pltpu.HBM)
    params = pltpu.CompilerParams(vmem_limit_bytes=36 * 1024 * 1024)
    shape = jax.ShapeDtypeStruct
    work = rows * rows * queries.shape[1]

    def call(kernel, name, flops, args, outs, in_specs=None, out_specs=None, scratch=()):
        return pl.pallas_call(
            kernel,
            out_shape=outs,
            in_specs=in_specs or [vmem] * len(args),
            out_specs=out_specs or (vmem,) * len(outs),
            scratch_shapes=scratch,
            compiler_params=params,
            cost_estimate=pl.CostEstimate(flops=flops, bytes_accessed=16 * rows * width, transcendentals=0),
            name=name,
        )(*args)

    def shift(array, d):
        return lax.ppermute(array, "seq", [(r, (r + d) % seq_count) for r in range(seq_count)])

    def unshift(array, d):
        return lax.ppermute(array, "seq", [((r + d) % seq_count, r) for r in range(seq_count)])

    far_k = [shift(keys, d) for d in range(1, nb + 1)]
    far_v = [shift(values, d) for d in range(1, nb + 1)]

    raw = (queries, grad_out, keys, values, quant_scale, doc_lengths)
    qt, gt, quants, slopes, dclips, bias, clips, q, g = call(
        functools.partial(prep_kernel, nb),
        "prep",
        2 * work,
        [pltpu.with_memory_space_constraint(x, pltpu.HBM) for x in raw],
        (
            shape((width, heads // kv_heads * rows), BF16),
            shape((width, heads // kv_heads * rows), BF16),
            shape((rows, 2 * width), BF16),
            pltpu.HBM((rows, 2 * width), F32),
            shape((rows, 2 * width), F32),
            shape((nb * rows, rows), F32),
            shape(quant_scale.shape, F32),
            shape(queries.shape, BF16),
            shape(queries.shape, BF16),
        ),
        in_specs=[hbm] * 6,
        out_specs=(vmem, vmem, vmem, hbm, vmem, vmem, vmem, vmem, vmem),
        scratch=[
            pltpu.VMEM(keys.shape, BF16),
            pltpu.VMEM(values.shape, BF16),
            pltpu.SMEM(doc_lengths.shape, jnp.int32),
            pltpu.VMEM((rows, 2 * width), F32),
            pltpu.SemaphoreType.DMA((7,)),
        ],
    )
    p, k2, kdclips = call(
        functools.partial(score_kernel, nb),
        "score",
        2 * (nb + 1) * work,
        (qt, quants, bias, clips, *far_k),
        (
            shape((nb * rows, heads * rows), BF16),
            shape(((nb + 1) * rows, width), BF16),
            shape((nb * rows, width), F32),
        ),
    )
    ds, v2, grads, far_grads, spread = call(
        functools.partial(grad_kernel, nb),
        "grad",
        6 * (nb + 1) * work,
        (q, g, gt, quants, dclips, clips, p, kdclips, *far_v),
        (
            shape((nb * rows, heads * rows), BF16),
            shape(((nb + 1) * rows, width), BF16),
            shape((rows, 2 * width), BF16),
            shape((nb * rows, 2 * width), BF16),
            pltpu.VMEM((count, 2 * kv_heads, hd), BF16),
        ),
        scratch=[pltpu.VMEM((2 * kv_heads, hd), F32)],
    )
    backs = []
    for d in range(1, nb + 1):
        at = far_order(nb).index(d) * rows
        backs.append(unshift(lax.slice_in_dim(far_grads, at, at + rows, axis=0), d))
    parts = lax.all_to_all(
        spread,
        ("dp", "seq"),
        split_axis=0,
        concat_axis=0,
        axis_index_groups=[list(reversed(range(count)))],
        tiled=True,
    )
    pinned = pltpu.with_memory_space_constraint(slopes, pltpu.HBM)
    attn_out, grad_queries, grad_keys, grad_values = call(
        functools.partial(output_kernel, nb),
        "output",
        4 * (nb + 1) * work,
        (p, ds, k2, v2, grads, pinned, *backs),
        (
            shape(queries.shape, BF16),
            shape(queries.shape, BF16),
            shape((rows, width), BF16),
            shape((rows, width), BF16),
        ),
        in_specs=[vmem] * 5 + [hbm] + [pl.BlockSpec(memory_space=pl.ANY)] * nb,
        out_specs=(hbm,) * 4,
        scratch=[
            pltpu.VMEM(queries.shape, BF16),
            pltpu.VMEM(queries.shape, BF16),
            pltpu.VMEM((rows, width), BF16),
            pltpu.VMEM((rows, width), BF16),
            pltpu.VMEM((rows, 2 * width), F32),
            pltpu.VMEM((nb, rows, 2 * width), BF16),
            pltpu.SemaphoreType.DMA((2, kv_heads)),
            pltpu.SemaphoreType.DMA((3 + nb,)),
        ],
    )
    (grad_scale,) = call(
        total_kernel,
        "total",
        parts.size,
        (parts, pltpu.with_memory_space_constraint(grad_keys, pltpu.HBM)),
        (shape(parts.shape[1:], F32),),
        in_specs=[vmem, hbm],
    )
    return (attn_out, grad_queries, grad_keys, grad_values, grad_scale.reshape(quant_scale.shape))


def solution(mesh):
    rows = P(("dp", "seq"), None)
    return jax.shard_map(
        functools.partial(on_device, (mesh.shape["dp"], mesh.shape["seq"])),
        mesh=mesh,
        in_specs=(rows, rows, rows, rows, P(), P("dp", None)),
        out_specs=(rows, rows, rows, rows, P()),
        check_vma=False,
    )
```

```python
import functools
import math

import jax
import jax.numpy as jnp
from jax import lax
from jax.experimental import pallas as pl
from jax.experimental.pallas import tpu as pltpu
from jax.sharding import PartitionSpec as P

F32 = jnp.float32
BF16 = jnp.bfloat16
LEVELS = 127.0
NEG = -1e30


def sin_cos_half(u):
    r = (u - jnp.round(u)) * math.pi
    z = r * r
    s = z * (1.0 / 6227020800.0) - 1.0 / 39916800.0
    for c in (1.0 / 362880.0, -1.0 / 5040.0, 1.0 / 120.0, -1.0 / 6.0, 1.0):
        s = s * z + c
    s = s * r
    k = z * (1.0 / 479001600.0) - 1.0 / 3628800.0
    for c in (1.0 / 40320.0, -1.0 / 720.0, 1.0 / 24.0, -0.5, 1.0):
        k = k * z + c
    return s, k


def quant_parts(x, clip):
    inv = 1.0 / clip
    ratio = x * inv
    t = jnp.tanh(ratio)
    u = LEVELS * t
    s, k = sin_cos_half(u)
    level = u - s * k * (1.0 / math.pi)
    unit = level * (1.0 / LEVELS)
    slope = (2.0 * s * s) * (1.0 - t * t)
    return clip * unit, slope, unit - slope * ratio


def prep_kernel(nb, q_hbm, g_hbm, key_hbm, value_hbm, clip_hbm, len_hbm, qt_ref, gt_ref, quant_ref, slope_hbm,
                dclip_ref, bias_ref, clip_out, q_ref, g_ref, key_ref, value_ref, len_ref, slope_ref, sems):
    small = [
        pltpu.make_async_copy(src, dst, sems.at[i])
        for i, (src, dst) in enumerate(
            ((len_hbm, len_ref), (clip_hbm, clip_out), (key_hbm, key_ref), (value_hbm, value_ref))
        )
    ]
    large = [
        pltpu.make_async_copy(q_hbm, q_ref, sems.at[4]),
        pltpu.make_async_copy(g_hbm, g_ref, sems.at[5]),
    ]
    for copy in small + large:
        copy.start()
    rows = key_ref.shape[0]
    kv_heads, hd = clip_out.shape[1], clip_out.shape[2]
    group = q_ref.shape[1] // kv_heads
    base = lax.axis_index("seq") * rows
    for copy in small:
        copy.wait()
    for side, src in ((0, key_ref), (1, value_ref)):
        for n in range(kv_heads):
            x = src[:, n * hd:(n + 1) * hd].astype(F32)
            q, slope, dclip = quant_parts(x, clip_out[side, n:n + 1, :])
            at = slice((side * kv_heads + n) * hd, (side * kv_heads + n + 1) * hd)
            quant_ref[:, at] = q.astype(BF16)
            slope_ref[:, at] = slope
            dclip_ref[:, at] = dclip
    slope_copy = pltpu.make_async_copy(slope_ref, slope_hbm, sems.at[6])
    slope_copy.start()
    key = lax.broadcasted_iota(jnp.int32, (rows, rows), 0)
    row = lax.broadcasted_iota(jnp.int32, (rows, rows), 1)
    start = jnp.zeros((rows, rows), jnp.int32)
    end = jnp.int32(0)
    for d in range(len_ref.shape[1]):
        end = end + len_ref[0, d]
        start = jnp.where(row + base >= end, end, start)
    for b in range(nb):
        pos = jnp.where(key <= row, key, key - nb * rows) if b == 0 else key - b * rows
        bias_ref[b * rows:(b + 1) * rows, :] = jnp.where(pos + base >= start, 0.0, NEG)
    for copy, src, dst in zip(large, (q_ref, g_ref), (qt_ref, gt_ref)):
        copy.wait()
        for n in range(kv_heads):
            for h in range(group // hd):
                at = n * group + h * hd
                dst[n * hd:(n + 1) * hd, h * rows:(h + 1) * rows] = src[:, at:at + hd].T
    slope_copy.wait()


ACROSS = (((1,), (1,)), ((), ()))


def far_order(nb):
    return [nb] + list(range(1, nb))


def near_mask(rows):
    key = lax.broadcasted_iota(jnp.int32, (rows, rows), 0)
    row = lax.broadcasted_iota(jnp.int32, (rows, rows), 1)
    return key <= row


def merge(near, x, nb):
    rows = near.shape[0]
    first = jnp.where(near, x[:rows], x[rows:2 * rows])
    return jnp.concatenate([first, x[2 * rows:]], axis=0) if nb > 1 else first


def split(near_b, far_b, x, nb):
    rows = near_b.shape[0]
    parts = [x[:rows] * near_b, x[:rows] * far_b]
    if nb > 1:
        parts.append(x[rows:])
    return jnp.concatenate(parts, axis=0)


def score_kernel(nb, qt_ref, quant_ref, bias_ref, clip_ref, *rest):
    far, (p_ref, k2_ref, dclip_ref) = rest[:nb], rest[nb:]
    kv_heads, hd = clip_ref.shape[1], clip_ref.shape[2]
    rows, span = bias_ref.shape[1], qt_ref.shape[1]
    factor = hd ** -0.5 * math.log2(math.e)
    near = near_mask(rows)

    bias = bias_ref[...]

    def scores(n):
        cols = slice(n * hd, (n + 1) * hd)
        ks = [quant_ref[:, cols]]
        for j, d in enumerate(far_order(nb)):
            q, _, dclip = quant_parts(far[d - 1][:, cols].astype(F32), clip_ref[0, n:n + 1, :])
            ks.append(q.astype(BF16))
            dclip_ref[j * rows:(j + 1) * rows, cols] = dclip
        k2 = jnp.concatenate(ks, axis=0)
        k2_ref[:, cols] = k2
        return jnp.dot(k2, qt_ref[cols, :], preferred_element_type=F32)

    ahead = scores(0)
    for n in range(kv_heads):
        s_all, ahead = ahead, scores(n + 1) if n + 1 < kv_heads else None
        for h in range(span // rows):
            s = merge(near, s_all[:, h * rows:(h + 1) * rows], nb) * factor + bias
            w = jnp.exp2(s - jnp.max(s, axis=0, keepdims=True))
            p = w * (1.0 / jnp.sum(w, axis=0, keepdims=True))
            p_ref[:, n * span + h * rows:n * span + (h + 1) * rows] = p.astype(BF16)


def grad_kernel(nb, qt_ref, gt_ref, quant_ref, dclip_ref, clip_ref, p_ref, kdclip_ref, *rest):
    far_v, (ds_ref, v2_ref, grad_ref, far_ref, spread_ref, scale_ref) = rest[:nb], rest[nb:]
    kv_heads, hd = clip_ref.shape[1], clip_ref.shape[2]
    rows, span = dclip_ref.shape[0], gt_ref.shape[1]
    heads = span // rows
    width = kv_heads * hd
    scale = hd ** -0.5
    near = near_mask(rows)
    near_b = near.astype(F32).astype(BF16)
    far_b = 1.0 - near_b

    def k_cols(n):
        return slice(n * hd, (n + 1) * hd)

    def v_cols(n):
        return slice(width + n * hd, width + (n + 1) * hd)

    def value_side(n):
        p2 = jnp.concatenate(
            [split(near_b, far_b, p_ref[:, n * span + h * rows:n * span + (h + 1) * rows], nb) for h in range(heads)],
            axis=1,
        )
        v_grad = lax.dot_general(gt_ref[k_cols(n), :], p2, ACROSS, preferred_element_type=F32).T
        vs, vd = [quant_ref[:, v_cols(n)]], [dclip_ref[:, v_cols(n)]]
        for d in far_order(nb):
            q, _, dc = quant_parts(far_v[d - 1][:, k_cols(n)].astype(F32), clip_ref[1, n:n + 1, :])
            vs.append(q.astype(BF16))
            vd.append(dc)
        v2 = jnp.concatenate(vs, axis=0)
        v2_ref[:, k_cols(n)] = v2
        grad_ref[:, v_cols(n)] = v_grad[:rows].astype(BF16)
        far_ref[:, v_cols(n)] = v_grad[rows:].astype(BF16)
        scale_ref[kv_heads + n:kv_heads + n + 1, :] = jnp.sum(
            v_grad * jnp.concatenate(vd, axis=0), axis=0, keepdims=True
        )
        return jnp.dot(v2, gt_ref[k_cols(n), :], preferred_element_type=F32)

    def score_side(n, d_all):
        ds = []
        for h in range(heads):
            dp = merge(near, d_all[:, h * rows:(h + 1) * rows], nb)
            at = slice(n * span + h * rows, n * span + (h + 1) * rows)
            p = p_ref[:, at].astype(F32)
            delta = jnp.sum(p * dp, axis=0, keepdims=True)
            ds_b = (p * (dp - delta)).astype(BF16)
            ds_ref[:, at] = ds_b
            ds.append(split(near_b, far_b, ds_b, nb))
        return jnp.concatenate(ds, axis=1)

    def key_side(n, ds2):
        k_grad = (lax.dot_general(qt_ref[k_cols(n), :], ds2, ACROSS, preferred_element_type=F32) * scale).T
        grad_ref[:, k_cols(n)] = k_grad[:rows].astype(BF16)
        far_ref[:, k_cols(n)] = k_grad[rows:].astype(BF16)
        scale_ref[n:n + 1, :] = jnp.sum(k_grad[:rows] * dclip_ref[:, k_cols(n)], axis=0, keepdims=True) + jnp.sum(
            k_grad[rows:] * kdclip_ref[:, k_cols(n)], axis=0, keepdims=True
        )

    ahead, behind = value_side(0), None
    for n in range(kv_heads):
        d_all, ahead = ahead, value_side(n + 1) if n + 1 < kv_heads else None
        ds2 = score_side(n, d_all)
        if behind is not None:
            key_side(n - 1, behind)
        behind = ds2
    key_side(kv_heads - 1, behind)
    part = scale_ref[...].astype(BF16)

    def spread(i, carry):
        spread_ref[i] = part
        return carry

    lax.fori_loop(0, spread_ref.shape[0], spread, 0, unroll=8)


def output_kernel(nb, p_ref, ds_ref, k2_ref, v2_ref, grad_ref, slope_hbm, *rest):
    backs, rest = rest[:nb], rest[nb:]
    out_hbm, gq_hbm, gk_hbm, gv_hbm, out_ref, gq_ref, gk_ref, gv_ref, slope_ref, back_ref, sems, more_sems = rest
    loads = [pltpu.make_async_copy(slope_hbm, slope_ref, more_sems.at[2])]
    loads += [pltpu.make_async_copy(back, back_ref.at[d], more_sems.at[3 + d]) for d, back in enumerate(backs)]
    for copy in loads:
        copy.start()
    kv_heads = sems.shape[1]
    rows, group = out_ref.shape[0], out_ref.shape[1] // kv_heads
    hd = k2_ref.shape[1] // kv_heads
    heads = group // hd
    near_b = near_mask(rows).astype(F32).astype(BF16)
    far_b = 1.0 - near_b

    def copies(n):
        cols = pl.ds(pl.multiple_of(n * group, group), group)
        return (
            pltpu.make_async_copy(out_ref.at[:, cols], out_hbm.at[:, cols], sems.at[0, n]),
            pltpu.make_async_copy(gq_ref.at[:, cols], gq_hbm.at[:, cols], sems.at[1, n]),
        )

    def step(n, carry):
        cols = pl.ds(pl.multiple_of(n * hd, hd), hd)
        for left, right, dst, scale in ((v2_ref, p_ref, out_ref, None), (k2_ref, ds_ref, gq_ref, hd ** -0.5)):
            at = pl.ds(pl.multiple_of(n * heads * rows, rows), heads * rows)
            x = right[:, at]
            x2 = jnp.concatenate(
                [split(near_b, far_b, x[:, h * rows:(h + 1) * rows], nb) for h in range(heads)], axis=1
            )
            y = jnp.dot(left[:, cols].T, x2, preferred_element_type=F32)
            y = (y if scale is None else y * scale).astype(BF16)
            for h in range(heads):
                dst[:, pl.ds(pl.multiple_of(n * group + h * hd, hd), hd)] = y[:, h * rows:(h + 1) * rows].T
        for copy in copies(n):
            copy.start()
        return carry

    lax.fori_loop(0, kv_heads, step, 0, unroll=True)
    for copy in loads:
        copy.wait()
    stores = []
    width = gk_ref.shape[1]
    for side, ref, dst in ((0, gk_ref, gk_hbm), (1, gv_ref, gv_hbm)):
        at = slice(side * width, (side + 1) * width)
        total = grad_ref[:, at].astype(F32)
        for d in range(nb):
            total = total + back_ref[d, :, at].astype(F32)
        ref[...] = (total * slope_ref[:, at]).astype(BF16)
        stores.append(pltpu.make_async_copy(ref, dst, more_sems.at[side]))
        stores[-1].start()
    for n in range(kv_heads):
        for copy in copies(n):
            copy.wait()
    for copy in stores:
        copy.wait()


def total_kernel(parts_ref, after_ref, out_ref):
    del after_ref
    out_ref[...] = jnp.sum(parts_ref[...].astype(F32), axis=0)


def on_device(sizes, queries, keys, values, grad_out, quant_scale, doc_lengths):
    dp_count, seq_count = sizes
    count = dp_count * seq_count
    nb = max(1, seq_count // 2)
    rows, width = keys.shape
    kv_heads, hd = quant_scale.shape[1], quant_scale.shape[2]
    heads = queries.shape[1] // hd
    vmem = pl.BlockSpec(memory_space=pltpu.VMEM)
    hbm = pl.BlockSpec(memory_space=pltpu.HBM)
    params = pltpu.CompilerParams(vmem_limit_bytes=36 * 1024 * 1024)
    shape = jax.ShapeDtypeStruct
    work = rows * rows * queries.shape[1]

    def call(kernel, name, flops, args, outs, in_specs=None, out_specs=None, scratch=()):
        return pl.pallas_call(
            kernel,
            out_shape=outs,
            in_specs=in_specs or [vmem] * len(args),
            out_specs=out_specs or (vmem,) * len(outs),
            scratch_shapes=scratch,
            compiler_params=params,
            cost_estimate=pl.CostEstimate(flops=flops, bytes_accessed=16 * rows * width, transcendentals=0),
            name=name,
        )(*args)

    def shift(array, d):
        return lax.ppermute(array, "seq", [(r, (r + d) % seq_count) for r in range(seq_count)])

    def unshift(array, d):
        return lax.ppermute(array, "seq", [((r + d) % seq_count, r) for r in range(seq_count)])

    def shift_up(array, d):
        return lax.ppermute(array, "seq", [(r, r + d) for r in range(seq_count - d)])

    far_k = [shift(keys, d) for d in range(1, nb + 1)]
    far_v = [shift_up(values, d) for d in range(1, nb + 1)]

    raw = (queries, grad_out, keys, values, quant_scale, doc_lengths)
    qt, gt, quants, slopes, dclips, bias, clips = call(
        functools.partial(prep_kernel, nb),
        "prep",
        2 * work,
        [pltpu.with_memory_space_constraint(x, pltpu.HBM) for x in raw],
        (
            shape((width, heads // kv_heads * rows), BF16),
            shape((width, heads // kv_heads * rows), BF16),
            shape((rows, 2 * width), BF16),
            pltpu.HBM((rows, 2 * width), F32),
            shape((rows, 2 * width), F32),
            shape((nb * rows, rows), F32),
            shape(quant_scale.shape, F32),
        ),
        in_specs=[hbm] * 6,
        out_specs=(vmem, vmem, vmem, hbm, vmem, vmem, vmem),
        scratch=[
            pltpu.VMEM(queries.shape, BF16),
            pltpu.VMEM(queries.shape, BF16),
            pltpu.VMEM(keys.shape, BF16),
            pltpu.VMEM(values.shape, BF16),
            pltpu.SMEM(doc_lengths.shape, jnp.int32),
            pltpu.VMEM((rows, 2 * width), F32),
            pltpu.SemaphoreType.DMA((7,)),
        ],
    )
    p, k2, kdclips = call(
        functools.partial(score_kernel, nb),
        "score",
        2 * (nb + 1) * work,
        (qt, quants, bias, clips, *far_k),
        (
            shape((nb * rows, heads * rows), BF16),
            shape(((nb + 1) * rows, width), BF16),
            shape((nb * rows, width), F32),
        ),
    )
    ds, v2, grads, far_grads, spread = call(
        functools.partial(grad_kernel, nb),
        "grad",
        6 * (nb + 1) * work,
        (qt, gt, quants, dclips, clips, p, kdclips, *far_v),
        (
            shape((nb * rows, heads * rows), BF16),
            shape(((nb + 1) * rows, width), BF16),
            shape((rows, 2 * width), BF16),
            shape((nb * rows, 2 * width), BF16),
            pltpu.VMEM((count, 2 * kv_heads, hd), BF16),
        ),
        scratch=[pltpu.VMEM((2 * kv_heads, hd), F32)],
    )
    backs = []
    for d in range(1, nb + 1):
        at = far_order(nb).index(d) * rows
        backs.append(unshift(lax.slice_in_dim(far_grads, at, at + rows, axis=0), d))
    parts = lax.all_to_all(
        spread,
        ("dp", "seq"),
        split_axis=0,
        concat_axis=0,
        axis_index_groups=[list(reversed(range(count)))],
        tiled=True,
    )
    pinned = pltpu.with_memory_space_constraint(slopes, pltpu.HBM)
    attn_out, grad_queries, grad_keys, grad_values = call(
        functools.partial(output_kernel, nb),
        "output",
        4 * (nb + 1) * work,
        (p, ds, k2, v2, grads, pinned, *backs),
        (
            shape(queries.shape, BF16),
            shape(queries.shape, BF16),
            shape((rows, width), BF16),
            shape((rows, width), BF16),
        ),
        in_specs=[vmem] * 5 + [hbm] + [pl.BlockSpec(memory_space=pl.ANY)] * nb,
        out_specs=(hbm,) * 4,
        scratch=[
            pltpu.VMEM(queries.shape, BF16),
            pltpu.VMEM(queries.shape, BF16),
            pltpu.VMEM((rows, width), BF16),
            pltpu.VMEM((rows, width), BF16),
            pltpu.VMEM((rows, 2 * width), F32),
            pltpu.VMEM((nb, rows, 2 * width), BF16),
            pltpu.SemaphoreType.DMA((2, kv_heads)),
            pltpu.SemaphoreType.DMA((3 + nb,)),
        ],
    )
    (grad_scale,) = call(
        total_kernel,
        "total",
        parts.size,
        (parts, pltpu.with_memory_space_constraint(grad_keys, pltpu.HBM)),
        (shape(parts.shape[1:], F32),),
        in_specs=[vmem, hbm],
    )
    return (attn_out, grad_queries, grad_keys, grad_values, grad_scale.reshape(quant_scale.shape))


def solution(mesh):
    rows = P(("dp", "seq"), None)
    return jax.shard_map(
        functools.partial(on_device, (mesh.shape["dp"], mesh.shape["seq"])),
        mesh=mesh,
        in_specs=(rows, rows, rows, rows, P(), P("dp", None)),
        out_specs=(rows, rows, rows, rows, P()),
        check_vma=False,
    )
```

```python
import functools
import math

import jax
import jax.numpy as jnp
from jax import lax
from jax.experimental import pallas as pl
from jax.experimental.pallas import tpu as pltpu
from jax.sharding import PartitionSpec as P

F32 = jnp.float32
BF16 = jnp.bfloat16
LEVELS = 127.0
NEG = -1e30


def sin_cos_half(u):
    r = (u - jnp.round(u)) * math.pi
    z = r * r
    s = z * (1.0 / 6227020800.0) - 1.0 / 39916800.0
    for c in (1.0 / 362880.0, -1.0 / 5040.0, 1.0 / 120.0, -1.0 / 6.0, 1.0):
        s = s * z + c
    s = s * r
    k = z * (1.0 / 479001600.0) - 1.0 / 3628800.0
    for c in (1.0 / 40320.0, -1.0 / 720.0, 1.0 / 24.0, -0.5, 1.0):
        k = k * z + c
    return s, k


def quant_parts(x, clip):
    inv = 1.0 / clip
    ratio = x * inv
    t = jnp.tanh(ratio)
    u = LEVELS * t
    s, k = sin_cos_half(u)
    level = u - s * k * (1.0 / math.pi)
    unit = level * (1.0 / LEVELS)
    slope = (2.0 * s * s) * (1.0 - t * t)
    return clip * unit, slope, unit - slope * ratio


def prep_kernel(nb, q_hbm, g_hbm, key_hbm, value_hbm, clip_hbm, len_hbm, qt_ref, gt_ref, quant_ref, slope_hbm,
                dclip_ref, bias_ref, clip_out, q_ref, g_ref, key_ref, value_ref, len_ref, slope_ref, sems):
    small = [
        pltpu.make_async_copy(src, dst, sems.at[i])
        for i, (src, dst) in enumerate(
            ((len_hbm, len_ref), (clip_hbm, clip_out), (key_hbm, key_ref), (value_hbm, value_ref))
        )
    ]
    large = [
        pltpu.make_async_copy(q_hbm, q_ref, sems.at[4]),
        pltpu.make_async_copy(g_hbm, g_ref, sems.at[5]),
    ]
    for copy in small + large:
        copy.start()
    rows = key_ref.shape[0]
    kv_heads, hd = clip_out.shape[1], clip_out.shape[2]
    group = q_ref.shape[1] // kv_heads
    base = lax.axis_index("seq") * rows
    for copy in small:
        copy.wait()
    for side, src in ((0, key_ref), (1, value_ref)):
        for n in range(kv_heads):
            x = src[:, n * hd:(n + 1) * hd].astype(F32)
            q, slope, dclip = quant_parts(x, clip_out[side, n:n + 1, :])
            at = slice((side * kv_heads + n) * hd, (side * kv_heads + n + 1) * hd)
            quant_ref[:, at] = q.astype(BF16)
            slope_ref[:, at] = slope
            dclip_ref[:, at] = dclip
    slope_copy = pltpu.make_async_copy(slope_ref, slope_hbm, sems.at[6])
    slope_copy.start()
    key = lax.broadcasted_iota(jnp.int32, (rows, rows), 0)
    row = lax.broadcasted_iota(jnp.int32, (rows, rows), 1)
    start = jnp.zeros((rows, rows), jnp.int32)
    end = jnp.int32(0)
    for d in range(len_ref.shape[1]):
        end = end + len_ref[0, d]
        start = jnp.where(row + base >= end, end, start)
    for b in range(nb):
        pos = jnp.where(key <= row, key, key - nb * rows) if b == 0 else key - b * rows
        bias_ref[b * rows:(b + 1) * rows, :] = jnp.where(pos + base >= start, 0.0, NEG)
    for copy, src, dst in zip(large, (q_ref, g_ref), (qt_ref, gt_ref)):
        copy.wait()
        for n in range(kv_heads):
            for h in range(group // hd):
                at = n * group + h * hd
                dst[n * hd:(n + 1) * hd, h * rows:(h + 1) * rows] = src[:, at:at + hd].T
    slope_copy.wait()


ACROSS = (((1,), (1,)), ((), ()))


def far_order(nb):
    return [nb] + list(range(1, nb))


def near_mask(rows):
    key = lax.broadcasted_iota(jnp.int32, (rows, rows), 0)
    row = lax.broadcasted_iota(jnp.int32, (rows, rows), 1)
    return key <= row


def merge(near, x, nb):
    rows = near.shape[0]
    first = jnp.where(near, x[:rows], x[rows:2 * rows])
    return jnp.concatenate([first, x[2 * rows:]], axis=0) if nb > 1 else first


def split(near_b, far_b, x, nb):
    rows = near_b.shape[0]
    parts = [x[:rows] * near_b, x[:rows] * far_b]
    if nb > 1:
        parts.append(x[rows:])
    return jnp.concatenate(parts, axis=0)


def score_kernel(nb, qt_ref, quant_ref, bias_ref, clip_ref, *rest):
    far, (p_ref, k2_ref, dclip_ref) = rest[:nb], rest[nb:]
    kv_heads, hd = clip_ref.shape[1], clip_ref.shape[2]
    rows, span = bias_ref.shape[1], qt_ref.shape[1]
    factor = hd ** -0.5 * math.log2(math.e)
    near = near_mask(rows)

    bias = bias_ref[...]

    def scores(n):
        cols = slice(n * hd, (n + 1) * hd)
        ks = [quant_ref[:, cols]]
        for j, d in enumerate(far_order(nb)):
            q, _, dclip = quant_parts(far[d - 1][:, cols].astype(F32), clip_ref[0, n:n + 1, :])
            ks.append(q.astype(BF16))
            dclip_ref[j * rows:(j + 1) * rows, cols] = dclip
        k2 = jnp.concatenate(ks, axis=0)
        k2_ref[:, cols] = k2
        return jnp.dot(k2, qt_ref[cols, :], preferred_element_type=F32)

    ahead = scores(0)
    for n in range(kv_heads):
        s_all, ahead = ahead, scores(n + 1) if n + 1 < kv_heads else None
        for h in range(span // rows):
            s = merge(near, s_all[:, h * rows:(h + 1) * rows], nb) * factor + bias
            w = jnp.exp2(s - jnp.max(s, axis=0, keepdims=True))
            p = w * (1.0 / jnp.sum(w, axis=0, keepdims=True))
            p_ref[:, n * span + h * rows:n * span + (h + 1) * rows] = p.astype(BF16)


def grad_kernel(nb, qt_ref, gt_ref, quant_ref, dclip_ref, clip_ref, p_ref, kdclip_ref, *rest):
    far_v, (ds_ref, v2_ref, grad_ref, far_k_ref, far_v_ref, spread_ref, scale_ref) = rest[:nb], rest[nb:]
    kv_heads, hd = clip_ref.shape[1], clip_ref.shape[2]
    rows, span = dclip_ref.shape[0], gt_ref.shape[1]
    heads = span // rows
    width = kv_heads * hd
    scale = hd ** -0.5
    near = near_mask(rows)
    near_b = near.astype(F32).astype(BF16)
    far_b = 1.0 - near_b

    def k_cols(n):
        return slice(n * hd, (n + 1) * hd)

    def v_cols(n):
        return slice(width + n * hd, width + (n + 1) * hd)

    def value_side(n):
        p2 = jnp.concatenate(
            [split(near_b, far_b, p_ref[:, n * span + h * rows:n * span + (h + 1) * rows], nb) for h in range(heads)],
            axis=1,
        )
        v_grad = lax.dot_general(gt_ref[k_cols(n), :], p2, ACROSS, preferred_element_type=F32).T
        vs, vd = [quant_ref[:, v_cols(n)]], [dclip_ref[:, v_cols(n)]]
        for d in far_order(nb):
            q, _, dc = quant_parts(far_v[d - 1][:, k_cols(n)].astype(F32), clip_ref[1, n:n + 1, :])
            vs.append(q.astype(BF16))
            vd.append(dc)
        v2 = jnp.concatenate(vs, axis=0)
        v2_ref[:, k_cols(n)] = v2
        grad_ref[:, v_cols(n)] = v_grad[:rows].astype(BF16)
        far_v_ref[:, k_cols(n)] = v_grad[rows:].astype(BF16)
        scale_ref[kv_heads + n:kv_heads + n + 1, :] = jnp.sum(
            v_grad * jnp.concatenate(vd, axis=0), axis=0, keepdims=True
        )
        return jnp.dot(v2, gt_ref[k_cols(n), :], preferred_element_type=F32)

    def score_side(n, d_all):
        ds = []
        for h in range(heads):
            dp = merge(near, d_all[:, h * rows:(h + 1) * rows], nb)
            at = slice(n * span + h * rows, n * span + (h + 1) * rows)
            p = p_ref[:, at].astype(F32)
            delta = jnp.sum(p * dp, axis=0, keepdims=True)
            ds_b = (p * (dp - delta)).astype(BF16)
            ds_ref[:, at] = ds_b
            ds.append(split(near_b, far_b, ds_b, nb))
        return jnp.concatenate(ds, axis=1)

    def key_side(n, ds2):
        k_grad = (lax.dot_general(qt_ref[k_cols(n), :], ds2, ACROSS, preferred_element_type=F32) * scale).T
        grad_ref[:, k_cols(n)] = k_grad[:rows].astype(BF16)
        far_k_ref[:, k_cols(n)] = k_grad[rows:].astype(BF16)
        scale_ref[n:n + 1, :] = jnp.sum(k_grad[:rows] * dclip_ref[:, k_cols(n)], axis=0, keepdims=True) + jnp.sum(
            k_grad[rows:] * kdclip_ref[:, k_cols(n)], axis=0, keepdims=True
        )

    ahead, behind = value_side(0), None
    for n in range(kv_heads):
        d_all, ahead = ahead, value_side(n + 1) if n + 1 < kv_heads else None
        ds2 = score_side(n, d_all)
        if behind is not None:
            key_side(n - 1, behind)
        behind = ds2
    key_side(kv_heads - 1, behind)
    part = scale_ref[...].astype(BF16)

    def spread(i, carry):
        spread_ref[i] = part
        return carry

    lax.fori_loop(0, spread_ref.shape[0], spread, 0, unroll=8)


def output_kernel(nb, p_ref, ds_ref, k2_ref, v2_ref, out_hbm, gq_hbm, out_ref, gq_ref, sems):
    kv_heads = sems.shape[1]
    rows, group = out_ref.shape[0], out_ref.shape[1] // kv_heads
    hd = k2_ref.shape[1] // kv_heads
    heads = group // hd
    near_b = near_mask(rows).astype(F32).astype(BF16)
    far_b = 1.0 - near_b

    def copies(n):
        cols = pl.ds(pl.multiple_of(n * group, group), group)
        return (
            pltpu.make_async_copy(out_ref.at[:, cols], out_hbm.at[:, cols], sems.at[0, n]),
            pltpu.make_async_copy(gq_ref.at[:, cols], gq_hbm.at[:, cols], sems.at[1, n]),
        )

    def step(n, carry):
        cols = pl.ds(pl.multiple_of(n * hd, hd), hd)
        for left, right, dst, scale in ((v2_ref, p_ref, out_ref, None), (k2_ref, ds_ref, gq_ref, hd ** -0.5)):
            at = pl.ds(pl.multiple_of(n * heads * rows, rows), heads * rows)
            x = right[:, at]
            x2 = jnp.concatenate(
                [split(near_b, far_b, x[:, h * rows:(h + 1) * rows], nb) for h in range(heads)], axis=1
            )
            y = jnp.dot(left[:, cols].T, x2, preferred_element_type=F32)
            y = (y if scale is None else y * scale).astype(BF16)
            for h in range(heads):
                dst[:, pl.ds(pl.multiple_of(n * group + h * hd, hd), hd)] = y[:, h * rows:(h + 1) * rows].T
        for copy in copies(n):
            copy.start()
        return carry

    lax.fori_loop(0, kv_heads, step, 0, unroll=True)
    for n in range(kv_heads):
        for copy in copies(n):
            copy.wait()


def finish_kernel(nb, parts_ref, grad_ref, slope_hbm, *rest):
    backs, (gk_ref, gv_ref, gs_ref, slope_ref, sem) = rest[:2 * nb], rest[2 * nb:]
    load = pltpu.make_async_copy(slope_hbm, slope_ref, sem)
    load.start()
    gs_ref[...] = jnp.sum(parts_ref[...].astype(F32), axis=0)
    width = gk_ref.shape[1]
    load.wait()
    for side, out in ((0, gk_ref), (1, gv_ref)):
        at = slice(side * width, (side + 1) * width)
        total = grad_ref[:, at].astype(F32)
        for back in backs[side * nb:(side + 1) * nb]:
            total = total + back[...].astype(F32)
        out[...] = (total * slope_ref[:, at]).astype(BF16)


def on_device(sizes, queries, keys, values, grad_out, quant_scale, doc_lengths):
    dp_count, seq_count = sizes
    count = dp_count * seq_count
    nb = max(1, seq_count // 2)
    rows, width = keys.shape
    kv_heads, hd = quant_scale.shape[1], quant_scale.shape[2]
    heads = queries.shape[1] // hd
    vmem = pl.BlockSpec(memory_space=pltpu.VMEM)
    hbm = pl.BlockSpec(memory_space=pltpu.HBM)
    params = pltpu.CompilerParams(vmem_limit_bytes=36 * 1024 * 1024)
    shape = jax.ShapeDtypeStruct
    work = rows * rows * queries.shape[1]

    def call(kernel, name, flops, args, outs, in_specs=None, out_specs=None, scratch=()):
        return pl.pallas_call(
            kernel,
            out_shape=outs,
            in_specs=in_specs or [vmem] * len(args),
            out_specs=out_specs or (vmem,) * len(outs),
            scratch_shapes=scratch,
            compiler_params=params,
            cost_estimate=pl.CostEstimate(flops=flops, bytes_accessed=16 * rows * width, transcendentals=0),
            name=name,
        )(*args)

    def shift(array, d):
        return lax.ppermute(array, "seq", [(r, (r + d) % seq_count) for r in range(seq_count)])

    def unshift(array, d):
        return lax.ppermute(array, "seq", [((r + d) % seq_count, r) for r in range(seq_count)])

    far_k = [shift(keys, d) for d in range(1, nb + 1)]
    far_v = [shift(values, d) for d in range(1, nb + 1)]

    raw = (queries, grad_out, keys, values, quant_scale, doc_lengths)
    qt, gt, quants, slopes, dclips, bias, clips = call(
        functools.partial(prep_kernel, nb),
        "prep",
        2 * work,
        [pltpu.with_memory_space_constraint(x, pltpu.HBM) for x in raw],
        (
            shape((width, heads // kv_heads * rows), BF16),
            shape((width, heads // kv_heads * rows), BF16),
            shape((rows, 2 * width), BF16),
            pltpu.HBM((rows, 2 * width), F32),
            shape((rows, 2 * width), F32),
            shape((nb * rows, rows), F32),
            shape(quant_scale.shape, F32),
        ),
        in_specs=[hbm] * 6,
        out_specs=(vmem, vmem, vmem, hbm, vmem, vmem, vmem),
        scratch=[
            pltpu.VMEM(queries.shape, BF16),
            pltpu.VMEM(queries.shape, BF16),
            pltpu.VMEM(keys.shape, BF16),
            pltpu.VMEM(values.shape, BF16),
            pltpu.SMEM(doc_lengths.shape, jnp.int32),
            pltpu.VMEM((rows, 2 * width), F32),
            pltpu.SemaphoreType.DMA((7,)),
        ],
    )
    p, k2, kdclips = call(
        functools.partial(score_kernel, nb),
        "score",
        2 * (nb + 1) * work,
        (qt, quants, bias, clips, *far_k),
        (
            shape((nb * rows, heads * rows), BF16),
            shape(((nb + 1) * rows, width), BF16),
            shape((nb * rows, width), F32),
        ),
    )
    ds, v2, grads, *far_grads, spread = call(
        functools.partial(grad_kernel, nb),
        "grad",
        6 * (nb + 1) * work,
        (qt, gt, quants, dclips, clips, p, kdclips, *far_v),
        (
            shape((nb * rows, heads * rows), BF16),
            shape(((nb + 1) * rows, width), BF16),
            shape((rows, 2 * width), BF16),
            shape((nb * rows, width), BF16),
            shape((nb * rows, width), BF16),
            pltpu.VMEM((count, 2 * kv_heads, hd), BF16),
        ),
        scratch=[pltpu.VMEM((2 * kv_heads, hd), F32)],
    )
    parts = lax.all_to_all(spread, ("dp", "seq"), split_axis=0, concat_axis=0, tiled=True)
    backs = []
    for array in far_grads:
        for d in range(1, nb + 1):
            at = far_order(nb).index(d) * rows
            backs.append(unshift(lax.slice_in_dim(array, at, at + rows, axis=0), d))
    attn_out, grad_queries = call(
        functools.partial(output_kernel, nb),
        "output",
        4 * (nb + 1) * work,
        (p, ds, k2, v2),
        (shape(queries.shape, BF16), shape(queries.shape, BF16)),
        out_specs=(hbm, hbm),
        scratch=[
            pltpu.VMEM(queries.shape, BF16),
            pltpu.VMEM(queries.shape, BF16),
            pltpu.SemaphoreType.DMA((2, kv_heads)),
        ],
    )
    grad_keys, grad_values, grad_scale = call(
        functools.partial(finish_kernel, nb),
        "finish",
        6 * rows * width,
        (parts, grads, pltpu.with_memory_space_constraint(slopes, pltpu.HBM), *backs),
        (shape((rows, width), BF16), shape((rows, width), BF16), shape(parts.shape[1:], F32)),
        in_specs=[vmem, vmem, hbm] + [vmem] * (2 * nb),
        scratch=[pltpu.VMEM((rows, 2 * width), F32), pltpu.SemaphoreType.DMA(())],
    )
    return (attn_out, grad_queries, grad_keys, grad_values, grad_scale.reshape(quant_scale.shape))


def solution(mesh):
    rows = P(("dp", "seq"), None)
    return jax.shard_map(
        functools.partial(on_device, (mesh.shape["dp"], mesh.shape["seq"])),
        mesh=mesh,
        in_specs=(rows, rows, rows, rows, P(), P("dp", None)),
        out_specs=(rows, rows, rows, rows, P()),
        check_vma=False,
    )
```

```python
import functools
import math

import jax
import jax.numpy as jnp
from jax import lax
from jax.experimental import pallas as pl
from jax.experimental.pallas import tpu as pltpu
from jax.sharding import PartitionSpec as P

F32 = jnp.float32
BF16 = jnp.bfloat16
LEVELS = 127.0
NEG = -1e30


def sin_cos_half(u):
    r = (u - jnp.round(u)) * math.pi
    z = r * r
    s = z * (1.0 / 6227020800.0) - 1.0 / 39916800.0
    for c in (1.0 / 362880.0, -1.0 / 5040.0, 1.0 / 120.0, -1.0 / 6.0, 1.0):
        s = s * z + c
    s = s * r
    k = z * (1.0 / 479001600.0) - 1.0 / 3628800.0
    for c in (1.0 / 40320.0, -1.0 / 720.0, 1.0 / 24.0, -0.5, 1.0):
        k = k * z + c
    return s, k


def quant_parts(x, clip):
    inv = 1.0 / clip
    ratio = x * inv
    t = jnp.tanh(ratio)
    u = LEVELS * t
    s, k = sin_cos_half(u)
    level = u - s * k * (1.0 / math.pi)
    unit = level * (1.0 / LEVELS)
    slope = (2.0 * s * s) * (1.0 - t * t)
    return clip * unit, slope, unit - slope * ratio


def prep_kernel(nb, q_hbm, g_hbm, key_hbm, value_hbm, clip_hbm, len_hbm, qt_ref, gt_ref, quant_ref, slope_hbm,
                dclip_ref, bias_ref, clip_out, q_ref, g_ref, key_ref, value_ref, len_ref, slope_ref, sems):
    small = [
        pltpu.make_async_copy(src, dst, sems.at[i])
        for i, (src, dst) in enumerate(
            ((len_hbm, len_ref), (clip_hbm, clip_out), (key_hbm, key_ref), (value_hbm, value_ref))
        )
    ]
    large = [
        pltpu.make_async_copy(q_hbm, q_ref, sems.at[4]),
        pltpu.make_async_copy(g_hbm, g_ref, sems.at[5]),
    ]
    for copy in small + large:
        copy.start()
    rows = key_ref.shape[0]
    kv_heads, hd = clip_out.shape[1], clip_out.shape[2]
    group = q_ref.shape[1] // kv_heads
    base = lax.axis_index("seq") * rows
    for copy in small:
        copy.wait()
    for side, src in ((0, key_ref), (1, value_ref)):
        for n in range(kv_heads):
            x = src[:, n * hd:(n + 1) * hd].astype(F32)
            q, slope, dclip = quant_parts(x, clip_out[side, n:n + 1, :])
            at = slice((side * kv_heads + n) * hd, (side * kv_heads + n + 1) * hd)
            quant_ref[:, at] = q.astype(BF16)
            slope_ref[:, at] = slope
            dclip_ref[:, at] = dclip
    slope_copy = pltpu.make_async_copy(slope_ref, slope_hbm, sems.at[6])
    slope_copy.start()
    key = lax.broadcasted_iota(jnp.int32, (rows, rows), 0)
    row = lax.broadcasted_iota(jnp.int32, (rows, rows), 1)
    start = jnp.zeros((rows, rows), jnp.int32)
    end = jnp.int32(0)
    for d in range(len_ref.shape[1]):
        end = end + len_ref[0, d]
        start = jnp.where(row + base >= end, end, start)
    for b in range(nb):
        pos = jnp.where(key <= row, key, key - nb * rows) if b == 0 else key - b * rows
        bias_ref[b * rows:(b + 1) * rows, :] = jnp.where(pos + base >= start, 0.0, NEG)
    for copy, src, dst in zip(large, (q_ref, g_ref), (qt_ref, gt_ref)):
        copy.wait()
        for n in range(kv_heads):
            for h in range(group // hd):
                at = n * group + h * hd
                dst[n * hd:(n + 1) * hd, h * rows:(h + 1) * rows] = src[:, at:at + hd].T
    slope_copy.wait()


ACROSS = (((1,), (1,)), ((), ()))


def far_order(nb):
    return [nb] + list(range(1, nb))


def near_mask(rows):
    key = lax.broadcasted_iota(jnp.int32, (rows, rows), 0)
    row = lax.broadcasted_iota(jnp.int32, (rows, rows), 1)
    return key <= row


def merge(near, x, nb):
    rows = near.shape[0]
    first = jnp.where(near, x[:rows], x[rows:2 * rows])
    return jnp.concatenate([first, x[2 * rows:]], axis=0) if nb > 1 else first


def split(near_b, x, nb):
    rows = near_b.shape[0]
    own = x[:rows] * near_b
    parts = [own, x[:rows] - own]
    if nb > 1:
        parts.append(x[rows:])
    return jnp.concatenate(parts, axis=0)


def score_kernel(nb, qt_ref, quant_ref, bias_ref, clip_ref, *rest):
    far, (p_ref, k2_ref, dclip_ref) = rest[:nb], rest[nb:]
    kv_heads, hd = clip_ref.shape[1], clip_ref.shape[2]
    rows, span = bias_ref.shape[1], qt_ref.shape[1]
    factor = hd ** -0.5 * math.log2(math.e)
    near = near_mask(rows)

    bias = bias_ref[...]

    def scores(n):
        cols = slice(n * hd, (n + 1) * hd)
        ks = [quant_ref[:, cols]]
        for j, d in enumerate(far_order(nb)):
            q, _, dclip = quant_parts(far[d - 1][:, cols].astype(F32), clip_ref[0, n:n + 1, :])
            ks.append(q.astype(BF16))
            dclip_ref[j * rows:(j + 1) * rows, cols] = dclip
        k2 = jnp.concatenate(ks, axis=0)
        k2_ref[:, cols] = k2
        return jnp.dot(k2, qt_ref[cols, :], preferred_element_type=F32)

    ahead = scores(0)
    for n in range(kv_heads):
        s_all, ahead = ahead, scores(n + 1) if n + 1 < kv_heads else None
        for h in range(span // rows):
            s = merge(near, s_all[:, h * rows:(h + 1) * rows], nb) * factor + bias
            w = jnp.exp2(s - jnp.max(s, axis=0, keepdims=True))
            p = w * (1.0 / jnp.sum(w, axis=0, keepdims=True))
            p_ref[:, n * span + h * rows:n * span + (h + 1) * rows] = p.astype(BF16)


def grad_kernel(nb, qt_ref, gt_ref, quant_ref, dclip_ref, clip_ref, p_ref, kdclip_ref, *rest):
    far_v, (ds_ref, v2_ref, grad_ref, far_ref, spread_ref, scale_ref) = rest[:nb], rest[nb:]
    kv_heads, hd = clip_ref.shape[1], clip_ref.shape[2]
    rows, span = dclip_ref.shape[0], gt_ref.shape[1]
    heads = span // rows
    width = kv_heads * hd
    scale = hd ** -0.5
    near = near_mask(rows)
    near_b = near.astype(F32).astype(BF16)

    def k_cols(n):
        return slice(n * hd, (n + 1) * hd)

    def v_cols(n):
        return slice(width + n * hd, width + (n + 1) * hd)

    def value_side(n):
        p2 = jnp.concatenate(
            [split(near_b, p_ref[:, n * span + h * rows:n * span + (h + 1) * rows], nb) for h in range(heads)],
            axis=1,
        )
        v_grad = lax.dot_general(gt_ref[k_cols(n), :], p2, ACROSS, preferred_element_type=F32).T
        vs, vd = [quant_ref[:, v_cols(n)]], [dclip_ref[:, v_cols(n)]]
        for d in far_order(nb):
            q, _, dc = quant_parts(far_v[d - 1][:, k_cols(n)].astype(F32), clip_ref[1, n:n + 1, :])
            vs.append(q.astype(BF16))
            vd.append(dc)
        v2 = jnp.concatenate(vs, axis=0)
        v2_ref[:, k_cols(n)] = v2
        grad_ref[:, v_cols(n)] = v_grad[:rows].astype(BF16)
        far_ref[:, v_cols(n)] = v_grad[rows:].astype(BF16)
        scale_ref[kv_heads + n:kv_heads + n + 1, :] = jnp.sum(
            v_grad * jnp.concatenate(vd, axis=0), axis=0, keepdims=True
        )
        return jnp.dot(v2, gt_ref[k_cols(n), :], preferred_element_type=F32)

    def score_side(n, d_all):
        ds = []
        for h in range(heads):
            dp = merge(near, d_all[:, h * rows:(h + 1) * rows], nb)
            at = slice(n * span + h * rows, n * span + (h + 1) * rows)
            p = p_ref[:, at].astype(F32)
            delta = jnp.sum(p * dp, axis=0, keepdims=True)
            ds_b = (p * (dp - delta)).astype(BF16)
            ds_ref[:, at] = ds_b
            ds.append(split(near_b, ds_b, nb))
        return jnp.concatenate(ds, axis=1)

    def key_side(n, ds2):
        k_grad = (lax.dot_general(qt_ref[k_cols(n), :], ds2, ACROSS, preferred_element_type=F32) * scale).T
        grad_ref[:, k_cols(n)] = k_grad[:rows].astype(BF16)
        far_ref[:, k_cols(n)] = k_grad[rows:].astype(BF16)
        scale_ref[n:n + 1, :] = jnp.sum(k_grad[:rows] * dclip_ref[:, k_cols(n)], axis=0, keepdims=True) + jnp.sum(
            k_grad[rows:] * kdclip_ref[:, k_cols(n)], axis=0, keepdims=True
        )

    ahead, behind = value_side(0), None
    for n in range(kv_heads):
        d_all, ahead = ahead, value_side(n + 1) if n + 1 < kv_heads else None
        ds2 = score_side(n, d_all)
        if behind is not None:
            key_side(n - 1, behind)
        behind = ds2
    key_side(kv_heads - 1, behind)
    part = scale_ref[...].astype(BF16)

    def spread(i, carry):
        spread_ref[i] = part
        return carry

    lax.fori_loop(0, spread_ref.shape[0], spread, 0, unroll=8)


def output_kernel(nb, p_ref, ds_ref, k2_ref, v2_ref, grad_ref, slope_hbm, *rest):
    backs, rest = rest[:nb], rest[nb:]
    out_hbm, gq_hbm, gk_hbm, gv_hbm, out_ref, gq_ref, gk_ref, gv_ref, slope_ref, back_ref, sems, more_sems = rest
    loads = [pltpu.make_async_copy(slope_hbm, slope_ref, more_sems.at[2])]
    loads += [pltpu.make_async_copy(back, back_ref.at[d], more_sems.at[3 + d]) for d, back in enumerate(backs)]
    for copy in loads:
        copy.start()
    kv_heads = sems.shape[1]
    rows, group = out_ref.shape[0], out_ref.shape[1] // kv_heads
    hd = k2_ref.shape[1] // kv_heads
    heads = group // hd
    near_b = near_mask(rows).astype(F32).astype(BF16)

    def copies(n):
        cols = pl.ds(pl.multiple_of(n * group, group), group)
        return (
            pltpu.make_async_copy(out_ref.at[:, cols], out_hbm.at[:, cols], sems.at[0, n]),
            pltpu.make_async_copy(gq_ref.at[:, cols], gq_hbm.at[:, cols], sems.at[1, n]),
        )

    def step(n, carry):
        cols = pl.ds(pl.multiple_of(n * hd, hd), hd)
        for left, right, dst, scale in ((v2_ref, p_ref, out_ref, None), (k2_ref, ds_ref, gq_ref, hd ** -0.5)):
            at = pl.ds(pl.multiple_of(n * heads * rows, rows), heads * rows)
            x = right[:, at]
            x2 = jnp.concatenate(
                [split(near_b, x[:, h * rows:(h + 1) * rows], nb) for h in range(heads)], axis=1
            )
            y = jnp.dot(left[:, cols].T, x2, preferred_element_type=F32)
            y = (y if scale is None else y * scale).astype(BF16)
            for h in range(heads):
                dst[:, pl.ds(pl.multiple_of(n * group + h * hd, hd), hd)] = y[:, h * rows:(h + 1) * rows].T
        for copy in copies(n):
            copy.start()
        return carry

    lax.fori_loop(0, kv_heads, step, 0, unroll=True)
    for copy in loads:
        copy.wait()
    stores = []
    width = gk_ref.shape[1]
    for side, ref, dst in ((0, gk_ref, gk_hbm), (1, gv_ref, gv_hbm)):
        at = slice(side * width, (side + 1) * width)
        total = grad_ref[:, at].astype(F32)
        for d in range(nb):
            total = total + back_ref[d, :, at].astype(F32)
        ref[...] = (total * slope_ref[:, at]).astype(BF16)
        stores.append(pltpu.make_async_copy(ref, dst, more_sems.at[side]))
        stores[-1].start()
    for n in range(kv_heads):
        for copy in copies(n):
            copy.wait()
    for copy in stores:
        copy.wait()


def total_kernel(parts_ref, after_ref, out_ref):
    del after_ref
    out_ref[...] = jnp.sum(parts_ref[...].astype(F32), axis=0)


def on_device(sizes, queries, keys, values, grad_out, quant_scale, doc_lengths):
    dp_count, seq_count = sizes
    count = dp_count * seq_count
    nb = max(1, seq_count // 2)
    rows, width = keys.shape
    kv_heads, hd = quant_scale.shape[1], quant_scale.shape[2]
    heads = queries.shape[1] // hd
    vmem = pl.BlockSpec(memory_space=pltpu.VMEM)
    hbm = pl.BlockSpec(memory_space=pltpu.HBM)
    params = pltpu.CompilerParams(vmem_limit_bytes=36 * 1024 * 1024)
    shape = jax.ShapeDtypeStruct
    work = rows * rows * queries.shape[1]

    def call(kernel, name, flops, args, outs, in_specs=None, out_specs=None, scratch=()):
        return pl.pallas_call(
            kernel,
            out_shape=outs,
            in_specs=in_specs or [vmem] * len(args),
            out_specs=out_specs or (vmem,) * len(outs),
            scratch_shapes=scratch,
            compiler_params=params,
            cost_estimate=pl.CostEstimate(flops=flops, bytes_accessed=16 * rows * width, transcendentals=0),
            name=name,
        )(*args)

    def shift(array, d):
        return lax.ppermute(array, "seq", [(r, (r + d) % seq_count) for r in range(seq_count)])

    def unshift(array, d):
        return lax.ppermute(array, "seq", [((r + d) % seq_count, r) for r in range(seq_count)])

    far_k = [shift(keys, d) for d in range(1, nb + 1)]
    far_v = [shift(values, d) for d in range(1, nb + 1)]

    raw = (queries, grad_out, keys, values, quant_scale, doc_lengths)
    qt, gt, quants, slopes, dclips, bias, clips = call(
        functools.partial(prep_kernel, nb),
        "prep",
        2 * work,
        [pltpu.with_memory_space_constraint(x, pltpu.HBM) for x in raw],
        (
            shape((width, heads // kv_heads * rows), BF16),
            shape((width, heads // kv_heads * rows), BF16),
            shape((rows, 2 * width), BF16),
            pltpu.HBM((rows, 2 * width), F32),
            shape((rows, 2 * width), F32),
            shape((nb * rows, rows), F32),
            shape(quant_scale.shape, F32),
        ),
        in_specs=[hbm] * 6,
        out_specs=(vmem, vmem, vmem, hbm, vmem, vmem, vmem),
        scratch=[
            pltpu.VMEM(queries.shape, BF16),
            pltpu.VMEM(queries.shape, BF16),
            pltpu.VMEM(keys.shape, BF16),
            pltpu.VMEM(values.shape, BF16),
            pltpu.SMEM(doc_lengths.shape, jnp.int32),
            pltpu.VMEM((rows, 2 * width), F32),
            pltpu.SemaphoreType.DMA((7,)),
        ],
    )
    p, k2, kdclips = call(
        functools.partial(score_kernel, nb),
        "score",
        2 * (nb + 1) * work,
        (qt, quants, bias, clips, *far_k),
        (
            shape((nb * rows, heads * rows), BF16),
            shape(((nb + 1) * rows, width), BF16),
            shape((nb * rows, width), F32),
        ),
    )
    ds, v2, grads, far_grads, spread = call(
        functools.partial(grad_kernel, nb),
        "grad",
        6 * (nb + 1) * work,
        (qt, gt, quants, dclips, clips, p, kdclips, *far_v),
        (
            shape((nb * rows, heads * rows), BF16),
            shape(((nb + 1) * rows, width), BF16),
            shape((rows, 2 * width), BF16),
            shape((nb * rows, 2 * width), BF16),
            pltpu.VMEM((count, 2 * kv_heads, hd), BF16),
        ),
        scratch=[pltpu.VMEM((2 * kv_heads, hd), F32)],
    )
    backs = []
    for d in range(1, nb + 1):
        at = far_order(nb).index(d) * rows
        backs.append(unshift(lax.slice_in_dim(far_grads, at, at + rows, axis=0), d))
    parts = lax.all_to_all(
        spread,
        ("dp", "seq"),
        split_axis=0,
        concat_axis=0,
        axis_index_groups=[list(reversed(range(count)))],
        tiled=True,
    )
    pinned = pltpu.with_memory_space_constraint(slopes, pltpu.HBM)
    attn_out, grad_queries, grad_keys, grad_values = call(
        functools.partial(output_kernel, nb),
        "output",
        4 * (nb + 1) * work,
        (p, ds, k2, v2, grads, pinned, *backs),
        (
            shape(queries.shape, BF16),
            shape(queries.shape, BF16),
            shape((rows, width), BF16),
            shape((rows, width), BF16),
        ),
        in_specs=[vmem] * 5 + [hbm] + [pl.BlockSpec(memory_space=pl.ANY)] * nb,
        out_specs=(hbm,) * 4,
        scratch=[
            pltpu.VMEM(queries.shape, BF16),
            pltpu.VMEM(queries.shape, BF16),
            pltpu.VMEM((rows, width), BF16),
            pltpu.VMEM((rows, width), BF16),
            pltpu.VMEM((rows, 2 * width), F32),
            pltpu.VMEM((nb, rows, 2 * width), BF16),
            pltpu.SemaphoreType.DMA((2, kv_heads)),
            pltpu.SemaphoreType.DMA((3 + nb,)),
        ],
    )
    (grad_scale,) = call(
        total_kernel,
        "total",
        parts.size,
        (parts, pltpu.with_memory_space_constraint(grad_keys, pltpu.HBM)),
        (shape(parts.shape[1:], F32),),
        in_specs=[vmem, hbm],
    )
    return (attn_out, grad_queries, grad_keys, grad_values, grad_scale.reshape(quant_scale.shape))


def solution(mesh):
    rows = P(("dp", "seq"), None)
    return jax.shard_map(
        functools.partial(on_device, (mesh.shape["dp"], mesh.shape["seq"])),
        mesh=mesh,
        in_specs=(rows, rows, rows, rows, P(), P("dp", None)),
        out_specs=(rows, rows, rows, rows, P()),
        check_vma=False,
    )
```

```python
import functools
import math

import jax
import jax.numpy as jnp
from jax import lax
from jax.experimental import pallas as pl
from jax.experimental.pallas import tpu as pltpu
from jax.sharding import PartitionSpec as P

F32 = jnp.float32
BF16 = jnp.bfloat16
LEVELS = 127.0
NEG = -1e30


def sin_cos_half(u):
    r = (u - jnp.round(u)) * math.pi
    z = r * r
    s = z * (1.0 / 6227020800.0) - 1.0 / 39916800.0
    for c in (1.0 / 362880.0, -1.0 / 5040.0, 1.0 / 120.0, -1.0 / 6.0, 1.0):
        s = s * z + c
    s = s * r
    k = z * (1.0 / 479001600.0) - 1.0 / 3628800.0
    for c in (1.0 / 40320.0, -1.0 / 720.0, 1.0 / 24.0, -0.5, 1.0):
        k = k * z + c
    return s, k


def quant_parts(x, clip):
    inv = 1.0 / clip
    ratio = x * inv
    t = jnp.tanh(ratio)
    u = LEVELS * t
    s, k = sin_cos_half(u)
    level = u - s * k * (1.0 / math.pi)
    unit = level * (1.0 / LEVELS)
    slope = (2.0 * s * s) * (1.0 - t * t)
    return clip * unit, slope, unit - slope * ratio


def prep_kernel(nb, q_hbm, g_hbm, key_hbm, value_hbm, clip_hbm, len_hbm, qt_ref, gt_ref, quant_ref, slope_hbm,
                dclip_ref, bias_ref, clip_out, q_ref, g_ref, key_ref, value_ref, len_ref, slope_ref, sems):
    small = [
        pltpu.make_async_copy(src, dst, sems.at[i])
        for i, (src, dst) in enumerate(
            ((len_hbm, len_ref), (clip_hbm, clip_out), (key_hbm, key_ref), (value_hbm, value_ref))
        )
    ]
    large = [
        pltpu.make_async_copy(q_hbm, q_ref, sems.at[4]),
        pltpu.make_async_copy(g_hbm, g_ref, sems.at[5]),
    ]
    for copy in small + large:
        copy.start()
    rows = key_ref.shape[0]
    kv_heads, hd = clip_out.shape[1], clip_out.shape[2]
    group = q_ref.shape[1] // kv_heads
    base = lax.axis_index("seq") * rows
    for copy in small:
        copy.wait()
    for side, src in ((0, key_ref), (1, value_ref)):
        for n in range(kv_heads):
            x = src[:, n * hd:(n + 1) * hd].astype(F32)
            q, slope, dclip = quant_parts(x, clip_out[side, n:n + 1, :])
            at = slice((side * kv_heads + n) * hd, (side * kv_heads + n + 1) * hd)
            quant_ref[:, at] = q.astype(BF16)
            slope_ref[:, at] = slope
            dclip_ref[:, at] = dclip
    slope_copy = pltpu.make_async_copy(slope_ref, slope_hbm, sems.at[6])
    slope_copy.start()
    key = lax.broadcasted_iota(jnp.int32, (rows, rows), 0)
    row = lax.broadcasted_iota(jnp.int32, (rows, rows), 1)
    start = jnp.zeros((rows, rows), jnp.int32)
    end = jnp.int32(0)
    for d in range(len_ref.shape[1]):
        end = end + len_ref[0, d]
        start = jnp.where(row + base >= end, end, start)
    for b in range(nb):
        pos = jnp.where(key <= row, key, key - nb * rows) if b == 0 else key - b * rows
        bias_ref[b * rows:(b + 1) * rows, :] = jnp.where(pos + base >= start, 0.0, NEG)
    for copy, src, dst in zip(large, (q_ref, g_ref), (qt_ref, gt_ref)):
        copy.wait()
        for n in range(kv_heads):
            for h in range(group // hd):
                at = n * group + h * hd
                dst[n * hd:(n + 1) * hd, h * rows:(h + 1) * rows] = src[:, at:at + hd].T
    slope_copy.wait()


ACROSS = (((1,), (1,)), ((), ()))


def far_order(nb):
    return [nb] + list(range(1, nb))


def near_mask(rows):
    key = lax.broadcasted_iota(jnp.int32, (rows, rows), 0)
    row = lax.broadcasted_iota(jnp.int32, (rows, rows), 1)
    return key <= row


def merge(near, x, nb):
    rows = near.shape[0]
    first = jnp.where(near, x[:rows], x[rows:2 * rows])
    return jnp.concatenate([first, x[2 * rows:]], axis=0) if nb > 1 else first


def split(near_b, far_b, x, nb):
    rows = near_b.shape[0]
    parts = [x[:rows] * near_b, x[:rows] * far_b]
    if nb > 1:
        parts.append(x[rows:])
    return jnp.concatenate(parts, axis=0)


def score_kernel(nb, qt_ref, quant_ref, bias_ref, clip_ref, *rest):
    far, (p_ref, k2_ref, dclip_ref) = rest[:nb], rest[nb:]
    kv_heads, hd = clip_ref.shape[1], clip_ref.shape[2]
    rows, span = bias_ref.shape[1], qt_ref.shape[1]
    factor = hd ** -0.5 * math.log2(math.e)
    near = near_mask(rows)

    bias = bias_ref[...]

    def scores(n):
        cols = slice(n * hd, (n + 1) * hd)
        ks = [quant_ref[:, cols]]
        for j, d in enumerate(far_order(nb)):
            q, _, dclip = quant_parts(far[d - 1][:, cols].astype(F32), clip_ref[0, n:n + 1, :])
            ks.append(q.astype(BF16))
            dclip_ref[j * rows:(j + 1) * rows, cols] = dclip
        k2 = jnp.concatenate(ks, axis=0)
        k2_ref[:, cols] = k2
        return jnp.dot(k2, qt_ref[cols, :], preferred_element_type=F32)

    ahead = scores(0)
    for n in range(kv_heads):
        s_all, ahead = ahead, scores(n + 1) if n + 1 < kv_heads else None
        for h in range(span // rows):
            s = merge(near, s_all[:, h * rows:(h + 1) * rows], nb) * factor + bias
            w = jnp.exp2(s - jnp.max(s, axis=0, keepdims=True))
            p = w * (1.0 / jnp.sum(w, axis=0, keepdims=True))
            p_ref[:, n * span + h * rows:n * span + (h + 1) * rows] = p.astype(BF16)


def grad_kernel(nb, qt_ref, gt_ref, quant_ref, dclip_ref, clip_ref, p_ref, kdclip_ref, *rest):
    far_v, (ds_ref, v2_ref, grad_ref, far_ref, spread_ref, scale_ref) = rest[:nb], rest[nb:]
    kv_heads, hd = clip_ref.shape[1], clip_ref.shape[2]
    rows, span = dclip_ref.shape[0], gt_ref.shape[1]
    heads = span // rows
    width = kv_heads * hd
    scale = hd ** -0.5
    near = near_mask(rows)
    near_b = near.astype(F32).astype(BF16)
    far_b = 1.0 - near_b

    def k_cols(n):
        return slice(n * hd, (n + 1) * hd)

    def v_cols(n):
        return slice(width + n * hd, width + (n + 1) * hd)

    vdclips = {}

    def value_side(n):
        vs, vd = [quant_ref[:, v_cols(n)]], [dclip_ref[:, v_cols(n)]]
        for d in far_order(nb):
            q, _, dc = quant_parts(far_v[d - 1][:, k_cols(n)].astype(F32), clip_ref[1, n:n + 1, :])
            vs.append(q.astype(BF16))
            vd.append(dc)
        vdclips[n] = vd
        v2 = jnp.concatenate(vs, axis=0)
        v2_ref[:, k_cols(n)] = v2
        return jnp.dot(v2, gt_ref[k_cols(n), :], preferred_element_type=F32)

    def value_grad(n):
        p2 = jnp.concatenate(
            [split(near_b, far_b, p_ref[:, n * span + h * rows:n * span + (h + 1) * rows], nb) for h in range(heads)],
            axis=1,
        )
        v_grad = lax.dot_general(gt_ref[k_cols(n), :], p2, ACROSS, preferred_element_type=F32).T
        grad_ref[:, v_cols(n)] = v_grad[:rows].astype(BF16)
        far_ref[:, v_cols(n)] = v_grad[rows:].astype(BF16)
        scale_ref[kv_heads + n:kv_heads + n + 1, :] = jnp.sum(
            v_grad * jnp.concatenate(vdclips[n], axis=0), axis=0, keepdims=True
        )

    def score_side(n, d_all):
        ds = []
        for h in range(heads):
            dp = merge(near, d_all[:, h * rows:(h + 1) * rows], nb)
            at = slice(n * span + h * rows, n * span + (h + 1) * rows)
            p = p_ref[:, at].astype(F32)
            delta = jnp.sum(p * dp, axis=0, keepdims=True)
            ds_b = (p * (dp - delta)).astype(BF16)
            ds_ref[:, at] = ds_b
            ds.append(split(near_b, far_b, ds_b, nb))
        return jnp.concatenate(ds, axis=1)

    def key_side(n, ds2):
        k_grad = (lax.dot_general(qt_ref[k_cols(n), :], ds2, ACROSS, preferred_element_type=F32) * scale).T
        grad_ref[:, k_cols(n)] = k_grad[:rows].astype(BF16)
        far_ref[:, k_cols(n)] = k_grad[rows:].astype(BF16)
        scale_ref[n:n + 1, :] = jnp.sum(k_grad[:rows] * dclip_ref[:, k_cols(n)], axis=0, keepdims=True) + jnp.sum(
            k_grad[rows:] * kdclip_ref[:, k_cols(n)], axis=0, keepdims=True
        )

    ahead, behind = value_side(0), None
    for n in range(kv_heads):
        d_all, ahead = ahead, value_side(n + 1) if n + 1 < kv_heads else None
        value_grad(n)
        ds2 = score_side(n, d_all)
        if behind is not None:
            key_side(n - 1, behind)
        behind = ds2
    key_side(kv_heads - 1, behind)
    part = scale_ref[...].astype(BF16)

    def spread(i, carry):
        spread_ref[i] = part
        return carry

    lax.fori_loop(0, spread_ref.shape[0], spread, 0, unroll=8)


def output_kernel(nb, p_ref, ds_ref, k2_ref, v2_ref, grad_ref, slope_hbm, *rest):
    backs, rest = rest[:nb], rest[nb:]
    out_hbm, gq_hbm, gk_hbm, gv_hbm, out_ref, gq_ref, gk_ref, gv_ref, slope_ref, back_ref, sems, more_sems = rest
    loads = [pltpu.make_async_copy(slope_hbm, slope_ref, more_sems.at[2])]
    loads += [pltpu.make_async_copy(back, back_ref.at[d], more_sems.at[3 + d]) for d, back in enumerate(backs)]
    for copy in loads:
        copy.start()
    kv_heads = sems.shape[1]
    rows, group = out_ref.shape[0], out_ref.shape[1] // kv_heads
    hd = k2_ref.shape[1] // kv_heads
    heads = group // hd
    near_b = near_mask(rows).astype(F32).astype(BF16)
    far_b = 1.0 - near_b

    def copies(n):
        cols = pl.ds(pl.multiple_of(n * group, group), group)
        return (
            pltpu.make_async_copy(out_ref.at[:, cols], out_hbm.at[:, cols], sems.at[0, n]),
            pltpu.make_async_copy(gq_ref.at[:, cols], gq_hbm.at[:, cols], sems.at[1, n]),
        )

    def step(n, carry):
        cols = pl.ds(pl.multiple_of(n * hd, hd), hd)
        for left, right, dst, scale in ((v2_ref, p_ref, out_ref, None), (k2_ref, ds_ref, gq_ref, hd ** -0.5)):
            at = pl.ds(pl.multiple_of(n * heads * rows, rows), heads * rows)
            x = right[:, at]
            x2 = jnp.concatenate(
                [split(near_b, far_b, x[:, h * rows:(h + 1) * rows], nb) for h in range(heads)], axis=1
            )
            y = jnp.dot(left[:, cols].T, x2, preferred_element_type=F32)
            y = (y if scale is None else y * scale).astype(BF16)
            for h in range(heads):
                dst[:, pl.ds(pl.multiple_of(n * group + h * hd, hd), hd)] = y[:, h * rows:(h + 1) * rows].T
        for copy in copies(n):
            copy.start()
        return carry

    lax.fori_loop(0, kv_heads, step, 0, unroll=True)
    for copy in loads:
        copy.wait()
    stores = []
    width = gk_ref.shape[1]
    for side, ref, dst in ((0, gk_ref, gk_hbm), (1, gv_ref, gv_hbm)):
        at = slice(side * width, (side + 1) * width)
        total = grad_ref[:, at].astype(F32)
        for d in range(nb):
            total = total + back_ref[d, :, at].astype(F32)
        ref[...] = (total * slope_ref[:, at]).astype(BF16)
        stores.append(pltpu.make_async_copy(ref, dst, more_sems.at[side]))
        stores[-1].start()
    for n in range(kv_heads):
        for copy in copies(n):
            copy.wait()
    for copy in stores:
        copy.wait()


def total_kernel(parts_ref, after_ref, out_ref):
    del after_ref
    out_ref[...] = jnp.sum(parts_ref[...].astype(F32), axis=0)


def on_device(sizes, queries, keys, values, grad_out, quant_scale, doc_lengths):
    dp_count, seq_count = sizes
    count = dp_count * seq_count
    nb = max(1, seq_count // 2)
    rows, width = keys.shape
    kv_heads, hd = quant_scale.shape[1], quant_scale.shape[2]
    heads = queries.shape[1] // hd
    vmem = pl.BlockSpec(memory_space=pltpu.VMEM)
    hbm = pl.BlockSpec(memory_space=pltpu.HBM)
    params = pltpu.CompilerParams(vmem_limit_bytes=36 * 1024 * 1024)
    shape = jax.ShapeDtypeStruct
    work = rows * rows * queries.shape[1]

    def call(kernel, name, flops, args, outs, in_specs=None, out_specs=None, scratch=()):
        return pl.pallas_call(
            kernel,
            out_shape=outs,
            in_specs=in_specs or [vmem] * len(args),
            out_specs=out_specs or (vmem,) * len(outs),
            scratch_shapes=scratch,
            compiler_params=params,
            cost_estimate=pl.CostEstimate(flops=flops, bytes_accessed=16 * rows * width, transcendentals=0),
            name=name,
        )(*args)

    def shift(array, d):
        return lax.ppermute(array, "seq", [(r, (r + d) % seq_count) for r in range(seq_count)])

    def unshift(array, d):
        return lax.ppermute(array, "seq", [((r + d) % seq_count, r) for r in range(seq_count)])

    far_k = [shift(keys, d) for d in range(1, nb + 1)]
    far_v = [shift(values, d) for d in range(1, nb + 1)]

    raw = (queries, grad_out, keys, values, quant_scale, doc_lengths)
    qt, gt, quants, slopes, dclips, bias, clips = call(
        functools.partial(prep_kernel, nb),
        "prep",
        2 * work,
        [pltpu.with_memory_space_constraint(x, pltpu.HBM) for x in raw],
        (
            shape((width, heads // kv_heads * rows), BF16),
            shape((width, heads // kv_heads * rows), BF16),
            shape((rows, 2 * width), BF16),
            pltpu.HBM((rows, 2 * width), F32),
            shape((rows, 2 * width), F32),
            shape((nb * rows, rows), F32),
            shape(quant_scale.shape, F32),
        ),
        in_specs=[hbm] * 6,
        out_specs=(vmem, vmem, vmem, hbm, vmem, vmem, vmem),
        scratch=[
            pltpu.VMEM(queries.shape, BF16),
            pltpu.VMEM(queries.shape, BF16),
            pltpu.VMEM(keys.shape, BF16),
            pltpu.VMEM(values.shape, BF16),
            pltpu.SMEM(doc_lengths.shape, jnp.int32),
            pltpu.VMEM((rows, 2 * width), F32),
            pltpu.SemaphoreType.DMA((7,)),
        ],
    )
    p, k2, kdclips = call(
        functools.partial(score_kernel, nb),
        "score",
        2 * (nb + 1) * work,
        (qt, quants, bias, clips, *far_k),
        (
            shape((nb * rows, heads * rows), BF16),
            shape(((nb + 1) * rows, width), BF16),
            shape((nb * rows, width), F32),
        ),
    )
    ds, v2, grads, far_grads, spread = call(
        functools.partial(grad_kernel, nb),
        "grad",
        6 * (nb + 1) * work,
        (qt, gt, quants, dclips, clips, p, kdclips, *far_v),
        (
            shape((nb * rows, heads * rows), BF16),
            shape(((nb + 1) * rows, width), BF16),
            shape((rows, 2 * width), BF16),
            shape((nb * rows, 2 * width), BF16),
            pltpu.VMEM((count, 2 * kv_heads, hd), BF16),
        ),
        scratch=[pltpu.VMEM((2 * kv_heads, hd), F32)],
    )
    backs = []
    for d in range(1, nb + 1):
        at = far_order(nb).index(d) * rows
        backs.append(unshift(lax.slice_in_dim(far_grads, at, at + rows, axis=0), d))
    parts = lax.all_to_all(
        spread,
        ("dp", "seq"),
        split_axis=0,
        concat_axis=0,
        axis_index_groups=[list(reversed(range(count)))],
        tiled=True,
    )
    pinned = pltpu.with_memory_space_constraint(slopes, pltpu.HBM)
    attn_out, grad_queries, grad_keys, grad_values = call(
        functools.partial(output_kernel, nb),
        "output",
        4 * (nb + 1) * work,
        (p, ds, k2, v2, grads, pinned, *backs),
        (
            shape(queries.shape, BF16),
            shape(queries.shape, BF16),
            shape((rows, width), BF16),
            shape((rows, width), BF16),
        ),
        in_specs=[vmem] * 5 + [hbm] + [pl.BlockSpec(memory_space=pl.ANY)] * nb,
        out_specs=(hbm,) * 4,
        scratch=[
            pltpu.VMEM(queries.shape, BF16),
            pltpu.VMEM(queries.shape, BF16),
            pltpu.VMEM((rows, width), BF16),
            pltpu.VMEM((rows, width), BF16),
            pltpu.VMEM((rows, 2 * width), F32),
            pltpu.VMEM((nb, rows, 2 * width), BF16),
            pltpu.SemaphoreType.DMA((2, kv_heads)),
            pltpu.SemaphoreType.DMA((3 + nb,)),
        ],
    )
    (grad_scale,) = call(
        total_kernel,
        "total",
        parts.size,
        (parts, pltpu.with_memory_space_constraint(grad_keys, pltpu.HBM)),
        (shape(parts.shape[1:], F32),),
        in_specs=[vmem, hbm],
    )
    return (attn_out, grad_queries, grad_keys, grad_values, grad_scale.reshape(quant_scale.shape))


def solution(mesh):
    rows = P(("dp", "seq"), None)
    return jax.shard_map(
        functools.partial(on_device, (mesh.shape["dp"], mesh.shape["seq"])),
        mesh=mesh,
        in_specs=(rows, rows, rows, rows, P(), P("dp", None)),
        out_specs=(rows, rows, rows, rows, P()),
        check_vma=False,
    )
```

```python
import functools
import math

import jax
import jax.numpy as jnp
from jax import lax
from jax.experimental import pallas as pl
from jax.experimental.pallas import tpu as pltpu
from jax.sharding import PartitionSpec as P

F32 = jnp.float32
BF16 = jnp.bfloat16
LEVELS = 127.0
NEG = -1e30


def sin_cos_half(u):
    r = (u - jnp.round(u)) * math.pi
    z = r * r
    s = z * (1.0 / 6227020800.0) - 1.0 / 39916800.0
    for c in (1.0 / 362880.0, -1.0 / 5040.0, 1.0 / 120.0, -1.0 / 6.0, 1.0):
        s = s * z + c
    s = s * r
    k = z * (1.0 / 479001600.0) - 1.0 / 3628800.0
    for c in (1.0 / 40320.0, -1.0 / 720.0, 1.0 / 24.0, -0.5, 1.0):
        k = k * z + c
    return s, k


def quant_parts(x, clip):
    inv = 1.0 / clip
    ratio = x * inv
    t = jnp.tanh(ratio)
    u = LEVELS * t
    s, k = sin_cos_half(u)
    level = u - s * k * (1.0 / math.pi)
    unit = level * (1.0 / LEVELS)
    slope = (2.0 * s * s) * (1.0 - t * t)
    return clip * unit, slope, unit - slope * ratio


def prep_kernel(nb, q_hbm, g_hbm, key_hbm, value_hbm, clip_hbm, len_hbm, qt_ref, gt_ref, quant_ref, slope_hbm,
                dclip_ref, bias_ref, clip_out, q_ref, g_ref, key_ref, value_ref, len_ref, slope_ref, sems):
    small = [
        pltpu.make_async_copy(src, dst, sems.at[i])
        for i, (src, dst) in enumerate(
            ((len_hbm, len_ref), (clip_hbm, clip_out), (key_hbm, key_ref), (value_hbm, value_ref))
        )
    ]
    large = [
        pltpu.make_async_copy(q_hbm, q_ref, sems.at[4]),
        pltpu.make_async_copy(g_hbm, g_ref, sems.at[5]),
    ]
    for copy in small + large:
        copy.start()
    rows = key_ref.shape[0]
    kv_heads, hd = clip_out.shape[1], clip_out.shape[2]
    group = q_ref.shape[1] // kv_heads
    base = lax.axis_index("seq") * rows
    for copy in small:
        copy.wait()
    for side, src in ((0, key_ref), (1, value_ref)):
        for n in range(kv_heads):
            x = src[:, n * hd:(n + 1) * hd].astype(F32)
            q, slope, dclip = quant_parts(x, clip_out[side, n:n + 1, :])
            at = slice((side * kv_heads + n) * hd, (side * kv_heads + n + 1) * hd)
            quant_ref[:, at] = q.astype(BF16)
            slope_ref[:, at] = slope
            dclip_ref[:, at] = dclip
    slope_copy = pltpu.make_async_copy(slope_ref, slope_hbm, sems.at[6])
    slope_copy.start()
    key = lax.broadcasted_iota(jnp.int32, (rows, rows), 0)
    row = lax.broadcasted_iota(jnp.int32, (rows, rows), 1)
    start = jnp.zeros((rows, rows), jnp.int32)
    end = jnp.int32(0)
    for d in range(len_ref.shape[1]):
        end = end + len_ref[0, d]
        start = jnp.where(row + base >= end, end, start)
    for b in range(nb):
        pos = jnp.where(key <= row, key, key - nb * rows) if b == 0 else key - b * rows
        bias_ref[b * rows:(b + 1) * rows, :] = jnp.where(pos + base >= start, 0.0, NEG)
    for copy, src, dst in zip(large, (q_ref, g_ref), (qt_ref, gt_ref)):
        copy.wait()
        for n in range(kv_heads):
            for h in range(group // hd):
                at = n * group + h * hd
                dst[n * hd:(n + 1) * hd, h * rows:(h + 1) * rows] = src[:, at:at + hd].T
    slope_copy.wait()


ACROSS = (((1,), (1,)), ((), ()))


def far_order(nb):
    return [nb] + list(range(1, nb))


def near_mask(rows):
    key = lax.broadcasted_iota(jnp.int32, (rows, rows), 0)
    row = lax.broadcasted_iota(jnp.int32, (rows, rows), 1)
    return key <= row


def merge(near, x, nb):
    rows = near.shape[0]
    first = jnp.where(near, x[:rows], x[rows:2 * rows])
    return jnp.concatenate([first, x[2 * rows:]], axis=0) if nb > 1 else first


def split(near_b, x, nb):
    rows = near_b.shape[0]
    own = x[:rows] * near_b
    parts = [own, x[:rows] - own]
    if nb > 1:
        parts.append(x[rows:])
    return jnp.concatenate(parts, axis=0)


def score_kernel(nb, qt_ref, quant_ref, bias_ref, clip_ref, *rest):
    far, (p_ref, k2_ref, dclip_ref) = rest[:nb], rest[nb:]
    kv_heads, hd = clip_ref.shape[1], clip_ref.shape[2]
    rows, span = bias_ref.shape[1], qt_ref.shape[1]
    factor = hd ** -0.5 * math.log2(math.e)
    near = near_mask(rows)

    bias = bias_ref[...]

    def scores(n):
        cols = slice(n * hd, (n + 1) * hd)
        ks = [quant_ref[:, cols]]
        for j, d in enumerate(far_order(nb)):
            q, _, dclip = quant_parts(far[d - 1][:, cols].astype(F32), clip_ref[0, n:n + 1, :])
            ks.append(q.astype(BF16))
            dclip_ref[j * rows:(j + 1) * rows, cols] = dclip
        k2 = jnp.concatenate(ks, axis=0)
        k2_ref[:, cols] = k2
        return jnp.dot(k2, qt_ref[cols, :], preferred_element_type=F32)

    ahead = scores(0)
    for n in range(kv_heads):
        s_all, ahead = ahead, scores(n + 1) if n + 1 < kv_heads else None
        for h in range(span // rows):
            s = merge(near, s_all[:, h * rows:(h + 1) * rows], nb) * factor + bias
            w = jnp.exp2(s - jnp.max(s, axis=0, keepdims=True))
            p = w * (1.0 / jnp.sum(w, axis=0, keepdims=True))
            p_ref[:, n * span + h * rows:n * span + (h + 1) * rows] = p.astype(BF16)


def grad_kernel(nb, qt_ref, gt_ref, quant_ref, dclip_ref, clip_ref, p_ref, kdclip_ref, *rest):
    far_v, (ds_ref, v2_ref, grad_ref, far_ref, spread_ref, scale_ref) = rest[:nb], rest[nb:]
    kv_heads, hd = clip_ref.shape[1], clip_ref.shape[2]
    rows, span = dclip_ref.shape[0], gt_ref.shape[1]
    heads = span // rows
    width = kv_heads * hd
    scale = hd ** -0.5
    near = near_mask(rows)
    near_b = near.astype(F32).astype(BF16)

    def k_cols(n):
        return slice(n * hd, (n + 1) * hd)

    def v_cols(n):
        return slice(width + n * hd, width + (n + 1) * hd)

    vdclips = {}

    def value_side(n):
        vs, vd = [quant_ref[:, v_cols(n)]], [dclip_ref[:, v_cols(n)]]
        for d in far_order(nb):
            q, _, dc = quant_parts(far_v[d - 1][:, k_cols(n)].astype(F32), clip_ref[1, n:n + 1, :])
            vs.append(q.astype(BF16))
            vd.append(dc)
        vdclips[n] = vd
        v2 = jnp.concatenate(vs, axis=0)
        v2_ref[:, k_cols(n)] = v2
        return jnp.dot(v2, gt_ref[k_cols(n), :], preferred_element_type=F32)

    def value_grad(n):
        p2 = jnp.concatenate(
            [split(near_b, p_ref[:, n * span + h * rows:n * span + (h + 1) * rows], nb) for h in range(heads)],
            axis=1,
        )
        v_grad = lax.dot_general(gt_ref[k_cols(n), :], p2, ACROSS, preferred_element_type=F32).T
        grad_ref[:, v_cols(n)] = v_grad[:rows].astype(BF16)
        far_ref[:, v_cols(n)] = v_grad[rows:].astype(BF16)
        scale_ref[kv_heads + n:kv_heads + n + 1, :] = jnp.sum(
            v_grad * jnp.concatenate(vdclips[n], axis=0), axis=0, keepdims=True
        )

    def score_side(n, d_all):
        ds = []
        for h in range(heads):
            dp = merge(near, d_all[:, h * rows:(h + 1) * rows], nb)
            at = slice(n * span + h * rows, n * span + (h + 1) * rows)
            p = p_ref[:, at].astype(F32)
            delta = jnp.sum(p * dp, axis=0, keepdims=True)
            ds_b = (p * (dp - delta)).astype(BF16)
            ds_ref[:, at] = ds_b
            ds.append(split(near_b, ds_b, nb))
        return jnp.concatenate(ds, axis=1)

    def key_side(n, ds2):
        k_grad = (lax.dot_general(qt_ref[k_cols(n), :], ds2, ACROSS, preferred_element_type=F32) * scale).T
        grad_ref[:, k_cols(n)] = k_grad[:rows].astype(BF16)
        far_ref[:, k_cols(n)] = k_grad[rows:].astype(BF16)
        scale_ref[n:n + 1, :] = jnp.sum(k_grad[:rows] * dclip_ref[:, k_cols(n)], axis=0, keepdims=True) + jnp.sum(
            k_grad[rows:] * kdclip_ref[:, k_cols(n)], axis=0, keepdims=True
        )

    ahead, behind = value_side(0), None
    for n in range(kv_heads):
        d_all, ahead = ahead, value_side(n + 1) if n + 1 < kv_heads else None
        value_grad(n)
        ds2 = score_side(n, d_all)
        if behind is not None:
            key_side(n - 1, behind)
        behind = ds2
    key_side(kv_heads - 1, behind)
    part = scale_ref[...].astype(BF16)

    def spread(i, carry):
        spread_ref[i] = part
        return carry

    lax.fori_loop(0, spread_ref.shape[0], spread, 0, unroll=8)


def output_kernel(nb, p_ref, ds_ref, k2_ref, v2_ref, grad_ref, slope_hbm, *rest):
    backs, rest = rest[:nb], rest[nb:]
    out_hbm, gq_hbm, gk_hbm, gv_hbm, out_ref, gq_ref, gk_ref, gv_ref, slope_ref, back_ref, sems, more_sems = rest
    loads = [pltpu.make_async_copy(slope_hbm, slope_ref, more_sems.at[2])]
    loads += [pltpu.make_async_copy(back, back_ref.at[d], more_sems.at[3 + d]) for d, back in enumerate(backs)]
    for copy in loads:
        copy.start()
    kv_heads = sems.shape[1]
    rows, group = out_ref.shape[0], out_ref.shape[1] // kv_heads
    hd = k2_ref.shape[1] // kv_heads
    heads = group // hd
    near_b = near_mask(rows).astype(F32).astype(BF16)

    def copies(n):
        cols = pl.ds(pl.multiple_of(n * group, group), group)
        return (
            pltpu.make_async_copy(out_ref.at[:, cols], out_hbm.at[:, cols], sems.at[0, n]),
            pltpu.make_async_copy(gq_ref.at[:, cols], gq_hbm.at[:, cols], sems.at[1, n]),
        )

    def step(n, carry):
        cols = pl.ds(pl.multiple_of(n * hd, hd), hd)
        for left, right, dst, scale in ((v2_ref, p_ref, out_ref, None), (k2_ref, ds_ref, gq_ref, hd ** -0.5)):
            at = pl.ds(pl.multiple_of(n * heads * rows, rows), heads * rows)
            x = right[:, at]
            x2 = jnp.concatenate(
                [split(near_b, x[:, h * rows:(h + 1) * rows], nb) for h in range(heads)], axis=1
            )
            y = jnp.dot(left[:, cols].T, x2, preferred_element_type=F32)
            y = (y if scale is None else y * scale).astype(BF16)
            for h in range(heads):
                dst[:, pl.ds(pl.multiple_of(n * group + h * hd, hd), hd)] = y[:, h * rows:(h + 1) * rows].T
        for copy in copies(n):
            copy.start()
        return carry

    lax.fori_loop(0, kv_heads, step, 0, unroll=True)
    for copy in loads:
        copy.wait()
    stores = []
    width = gk_ref.shape[1]
    for side, ref, dst in ((0, gk_ref, gk_hbm), (1, gv_ref, gv_hbm)):
        at = slice(side * width, (side + 1) * width)
        total = grad_ref[:, at].astype(F32)
        for d in range(nb):
            total = total + back_ref[d, :, at].astype(F32)
        ref[...] = (total * slope_ref[:, at]).astype(BF16)
        stores.append(pltpu.make_async_copy(ref, dst, more_sems.at[side]))
        stores[-1].start()
    for n in range(kv_heads):
        for copy in copies(n):
            copy.wait()
    for copy in stores:
        copy.wait()


def total_kernel(parts_ref, after_ref, out_ref):
    del after_ref
    out_ref[...] = jnp.sum(parts_ref[...].astype(F32), axis=0)


def on_device(sizes, queries, keys, values, grad_out, quant_scale, doc_lengths):
    dp_count, seq_count = sizes
    count = dp_count * seq_count
    nb = max(1, seq_count // 2)
    rows, width = keys.shape
    kv_heads, hd = quant_scale.shape[1], quant_scale.shape[2]
    heads = queries.shape[1] // hd
    vmem = pl.BlockSpec(memory_space=pltpu.VMEM)
    hbm = pl.BlockSpec(memory_space=pltpu.HBM)
    params = pltpu.CompilerParams(vmem_limit_bytes=36 * 1024 * 1024)
    shape = jax.ShapeDtypeStruct
    work = rows * rows * queries.shape[1]

    def call(kernel, name, flops, args, outs, in_specs=None, out_specs=None, scratch=()):
        return pl.pallas_call(
            kernel,
            out_shape=outs,
            in_specs=in_specs or [vmem] * len(args),
            out_specs=out_specs or (vmem,) * len(outs),
            scratch_shapes=scratch,
            compiler_params=params,
            cost_estimate=pl.CostEstimate(flops=flops, bytes_accessed=16 * rows * width, transcendentals=0),
            name=name,
        )(*args)

    def shift(array, d):
        return lax.ppermute(array, "seq", [(r, (r + d) % seq_count) for r in range(seq_count)])

    def unshift(array, d):
        return lax.ppermute(array, "seq", [((r + d) % seq_count, r) for r in range(seq_count)])

    far_k = [shift(keys, d) for d in range(1, nb + 1)]
    far_v = [shift(values, d) for d in range(1, nb + 1)]

    raw = (queries, grad_out, keys, values, quant_scale, doc_lengths)
    qt, gt, quants, slopes, dclips, bias, clips = call(
        functools.partial(prep_kernel, nb),
        "prep",
        2 * work,
        [pltpu.with_memory_space_constraint(x, pltpu.HBM) for x in raw],
        (
            shape((width, heads // kv_heads * rows), BF16),
            shape((width, heads // kv_heads * rows), BF16),
            shape((rows, 2 * width), BF16),
            pltpu.HBM((rows, 2 * width), F32),
            shape((rows, 2 * width), F32),
            shape((nb * rows, rows), F32),
            shape(quant_scale.shape, F32),
        ),
        in_specs=[hbm] * 6,
        out_specs=(vmem, vmem, vmem, hbm, vmem, vmem, vmem),
        scratch=[
            pltpu.VMEM(queries.shape, BF16),
            pltpu.VMEM(queries.shape, BF16),
            pltpu.VMEM(keys.shape, BF16),
            pltpu.VMEM(values.shape, BF16),
            pltpu.SMEM(doc_lengths.shape, jnp.int32),
            pltpu.VMEM((rows, 2 * width), F32),
            pltpu.SemaphoreType.DMA((7,)),
        ],
    )
    p, k2, kdclips = call(
        functools.partial(score_kernel, nb),
        "score",
        2 * (nb + 1) * work,
        (qt, quants, bias, clips, *far_k),
        (
            shape((nb * rows, heads * rows), BF16),
            shape(((nb + 1) * rows, width), BF16),
            shape((nb * rows, width), F32),
        ),
    )
    ds, v2, grads, far_grads, spread = call(
        functools.partial(grad_kernel, nb),
        "grad",
        6 * (nb + 1) * work,
        (qt, gt, quants, dclips, clips, p, kdclips, *far_v),
        (
            shape((nb * rows, heads * rows), BF16),
            shape(((nb + 1) * rows, width), BF16),
            shape((rows, 2 * width), BF16),
            shape((nb * rows, 2 * width), BF16),
            pltpu.VMEM((count, 2 * kv_heads, hd), BF16),
        ),
        scratch=[pltpu.VMEM((2 * kv_heads, hd), F32)],
    )
    backs = []
    for d in range(1, nb + 1):
        at = far_order(nb).index(d) * rows
        backs.append(unshift(lax.slice_in_dim(far_grads, at, at + rows, axis=0), d))
    parts = lax.all_to_all(
        spread,
        ("dp", "seq"),
        split_axis=0,
        concat_axis=0,
        axis_index_groups=[list(reversed(range(count)))],
        tiled=True,
    )
    pinned = pltpu.with_memory_space_constraint(slopes, pltpu.HBM)
    attn_out, grad_queries, grad_keys, grad_values = call(
        functools.partial(output_kernel, nb),
        "output",
        4 * (nb + 1) * work,
        (p, ds, k2, v2, grads, pinned, *backs),
        (
            shape(queries.shape, BF16),
            shape(queries.shape, BF16),
            shape((rows, width), BF16),
            shape((rows, width), BF16),
        ),
        in_specs=[vmem] * 5 + [hbm] + [pl.BlockSpec(memory_space=pl.ANY)] * nb,
        out_specs=(hbm,) * 4,
        scratch=[
            pltpu.VMEM(queries.shape, BF16),
            pltpu.VMEM(queries.shape, BF16),
            pltpu.VMEM((rows, width), BF16),
            pltpu.VMEM((rows, width), BF16),
            pltpu.VMEM((rows, 2 * width), F32),
            pltpu.VMEM((nb, rows, 2 * width), BF16),
            pltpu.SemaphoreType.DMA((2, kv_heads)),
            pltpu.SemaphoreType.DMA((3 + nb,)),
        ],
    )
    (grad_scale,) = call(
        total_kernel,
        "total",
        parts.size,
        (parts, pltpu.with_memory_space_constraint(grad_keys, pltpu.HBM)),
        (shape(parts.shape[1:], F32),),
        in_specs=[vmem, hbm],
    )
    return (attn_out, grad_queries, grad_keys, grad_values, grad_scale.reshape(quant_scale.shape))


def solution(mesh):
    rows = P(("dp", "seq"), None)
    return jax.shard_map(
        functools.partial(on_device, (mesh.shape["dp"], mesh.shape["seq"])),
        mesh=mesh,
        in_specs=(rows, rows, rows, rows, P(), P("dp", None)),
        out_specs=(rows, rows, rows, rows, P()),
        check_vma=False,
    )
```
